32 devices in a mesh: rep: 2 (over y), pd: 4 (over x, core), tp: 4 (over z).
Axes of the slice: x: 2, y: 2, z: 4, core: 2. Of those that a mesh axis runs over, the one named last changes fastest.
Arguments:
- prompt_query: bfloat16 [4096, 4096], P(('rep', 'pd', 'tp')), parts along dimension 0, may hold values from -200 to 200
- prompt_key: bfloat16 [4096, 512], P(('rep', 'pd', 'tp')), parts along dimension 0, may hold values from -6 to 6
- prompt_value: bfloat16 [4096, 512], P(('rep', 'pd', 'tp')), parts along dimension 0, may hold values from -6 to 6
- prompt_lengths: int32 [8, 4], P('rep'), parts along dimension 0, may hold values from 1 to 16, 32 in all within a row
- decode_slot: int32 [32], P('rep'), parts along dimension 0, may hold values from 0 to 15, as said below
- decoded_query: bfloat16 [32, 2, 4096], P(('rep', 'pd')), parts along dimension 0, may hold values from -200 to 200
- decoded_key: bfloat16 [32, 2, 512], P(('rep', 'pd')), parts along dimension 0, may hold values from -6 to 6
- decoded_value: bfloat16 [32, 2, 512], P(('rep', 'pd')), parts along dimension 0, may hold values from -6 to 6
Outputs:
- pre_out: bfloat16 [4096, 4096], P(('rep', 'pd', 'tp')), parts along dimension 0
- dec_out: bfloat16 [32, 2, 4096], P(('rep', 'pd')), parts along dimension 0
The draws below stay inside these ranges and needn't reach their ends.
There are 2 independent parts, one for each index of `rep`. The reference program is written for one: setup_inputs(seed, part) draws one part's arguments, and reference() takes and returns one part's arrays. A program takes and returns all parts, laid end to end along the dimension named above; each array names one. Nothing has to cross between parts.
Inputs may be any that keep to these rules, and one draw needn't show every extreme that they name: `prompt_lengths`: each row sums to 32; its largest entry is exactly 16. `decode_slot`: A permutation of the 16 request numbers onto the decode slots; the 4 requests of one prefill group go to 4 different decode groups.
All inputs are finite; a program needn't handle non-finite values.
Results may differ from the reference program's by a relative error of at most 0.014.
Values may be sent and summed in bfloat16 or wider, within the bound.
No kernel may reach another device: no remote copies, remote signals or barrier semaphores. Data moves between devices by JAX's collectives and lax.ppermute only.
A program may use at most 64 MiB of HBM per device.

```python
import math
import jax
import jax.numpy as jnp
import numpy as np
from jax import lax

QUERY_HEADS = 32
KEY_VALUE_HEADS = 4
HEAD_SIZE = 128
TOK = 128
PAGE = 16
GROUP_REQUESTS = 4
DECODE_STEPS = 2
GROUPED_TOKENS = 512
EVERY_TOKEN = 2048
REQUEST_TOTAL = 16
N_PD = 4
N_TP = 4


def shared_prompt_keys(key):
    return jnp.clip(jax.random.normal(jax.random.fold_in(key, 101), (EVERY_TOKEN, KEY_VALUE_HEADS * HEAD_SIZE), jnp.float32), -6.0, 6.0)


def shared_fresh_keys(key):
    return jnp.clip(jax.random.normal(jax.random.fold_in(key, 202), (REQUEST_TOTAL * DECODE_STEPS, KEY_VALUE_HEADS * HEAD_SIZE), jnp.float32), -6.0, 6.0)


def drawn_queries(key, row_range):
    drawn = jnp.clip(jax.random.normal(key, (row_range, QUERY_HEADS * HEAD_SIZE), jnp.float32), -6.0, 6.0)
    return drawn


def draw_prompt_key(key, part):
    return shared_prompt_keys(key).astype(jnp.bfloat16)


def draw_prompt_query(key, part):
    key = jax.random.fold_in(key, 2)
    return drawn_queries(key, EVERY_TOKEN).astype(jnp.bfloat16)


def draw_decoded_key(key, part):
    return shared_fresh_keys(key).reshape(REQUEST_TOTAL, DECODE_STEPS, KEY_VALUE_HEADS * HEAD_SIZE).astype(jnp.bfloat16)


def draw_decoded_query(key, part):
    key = jax.random.fold_in(key, 4)
    return drawn_queries(key, REQUEST_TOTAL * DECODE_STEPS).reshape(REQUEST_TOTAL, DECODE_STEPS, QUERY_HEADS * HEAD_SIZE).astype(jnp.bfloat16)


def draw_decode_slot(key, part):
    key = jax.random.fold_in(key, 9)
    first_index, second, third = jax.random.split(key, 3)
    offsets = jax.random.permutation(first_index, N_PD)[:GROUP_REQUESTS]
    relabel = jax.random.permutation(second, N_PD)
    places = jax.random.permutation(third, GROUP_REQUESTS)
    sources = jnp.arange(N_PD, dtype=jnp.int32)[:, None]
    target = relabel[(sources + offsets[None, :]) % N_PD]
    return (target * GROUP_REQUESTS + places[None, :]).reshape(REQUEST_TOTAL).astype(jnp.int32)


def level_of(key, extent, pieces, low, top_value):
    factor_of, own = 1.0, jax.random.fold_in(key, 6)
    for position, blocks in pieces:
        heights = jnp.exp(jax.random.uniform(jax.random.fold_in(own, position), (blocks,), jnp.float32, low / len(pieces), top_value / len(pieces)))
        factor_of = factor_of * jnp.repeat(heights, extent[position] // blocks).reshape([-1 if axis == position else 1 for axis in range(len(extent))])
    return factor_of


def split_up(count, total, bound, lean):
    loads = [(1 << 20) // math.isqrt(rank ** lean) + 1 for rank in range(2, count + 1)]
    rest, holding = total - bound - (count - 1), [1] * (count - 1)
    while rest > 0:
        candidates = [i for i in range(count - 1) if holding[i] < bound]
        mass, budget = sum([loads[i] for i in candidates]), rest
        for i in candidates:
            more = min(bound - holding[i], max(1, budget * loads[i] // mass), rest)
            holding[i] = holding[i] + more
            rest = rest - more
    return np.array([bound] + holding)


def ragged(rng, amount, total, reach, skew):
    if amount == 2:
        one = jax.random.randint(rng, (), max(1, total - reach), min(reach, total - 1) + 1)
        return jnp.stack([one, total - one])
    lengths = jnp.asarray(split_up(amount, total, reach, skew), jnp.int32)
    twos = (amount - 1) // 2
    giver, sink = lengths[1:1 + 2 * twos:2], lengths[2:2 + 2 * twos:2]
    margin = jnp.minimum(giver - 1, reach - sink)
    shifted = jax.random.randint(jax.random.fold_in(rng, 1), (twos,), 0, 1 << 20) % (margin + 1)
    lengths = lengths.at[1:1 + 2 * twos:2].set(giver - shifted).at[2:2 + 2 * twos:2].set(sink + shifted)
    return lengths[jax.random.permutation(jax.random.fold_in(rng, 2), amount)]


def centred(own_key, extent, scale, most, shards=(), kind=jnp.bfloat16):
    factor_of = level_of(own_key, extent, shards, -0.22, 0.18) if shards else 1.0
    array = jax.random.normal(own_key, extent, jnp.float32) * scale * factor_of
    return jnp.minimum(jnp.maximum(array, -most), most).astype(kind)


def setup_inputs(seed: int = 0, part: int = 0) -> dict:
    splits = jax.random.split(jax.random.key(seed), 9)
    own_keys = jax.random.split(jax.random.fold_in(splits[8], part), 9)
    prompt_query = draw_prompt_query(jax.random.fold_in(jax.random.fold_in(splits[8], part), 71), part)
    prompt_key = draw_prompt_key(jax.random.fold_in(jax.random.fold_in(splits[8], part), 71), part)
    prompt_value = centred(own_keys[2], (EVERY_TOKEN, KEY_VALUE_HEADS * HEAD_SIZE), 1.0, 6.0, ((0, 16),))
    prompt_lengths = jax.vmap(lambda own: ragged(own, GROUP_REQUESTS, GROUPED_TOKENS // PAGE, GROUPED_TOKENS // (2 * PAGE), 2))(jax.random.split(own_keys[3], N_PD)).reshape((N_PD, GROUP_REQUESTS)).astype(jnp.int32)
    decode_slot = draw_decode_slot(jax.random.fold_in(jax.random.fold_in(splits[8], part), 71), part)
    decoded_query = draw_decoded_query(jax.random.fold_in(jax.random.fold_in(splits[8], part), 71), part)
    decoded_key = draw_decoded_key(jax.random.fold_in(jax.random.fold_in(splits[8], part), 71), part)
    decoded_value = centred(own_keys[7], (REQUEST_TOTAL, DECODE_STEPS, KEY_VALUE_HEADS * HEAD_SIZE), 1.0, 6.0, ((0, 4),))
    return {"prompt_query": prompt_query, "prompt_key": prompt_key, "prompt_value": prompt_value, "prompt_lengths": prompt_lengths, "decode_slot": decode_slot, "decoded_query": decoded_query, "decoded_key": decoded_key, "decoded_value": decoded_value}


NEGATIVE_FILL = -1e+30

def segment_of(positions, ends_row):
    return lax.optimization_barrier(jnp.sum((positions[:, None] >= ends_row[None, :]).astype(jnp.int32), axis=1))

def to_positions(row_range):
    page_count = TOK // PAGE
    columns = row_range.shape[1]
    return row_range.reshape(N_TP, page_count, PAGE, columns).transpose(1, 0, 2, 3).reshape(GROUPED_TOKENS, columns)

def from_positions(row_range):
    page_count = TOK // PAGE
    columns = row_range.shape[1]
    return row_range.reshape(page_count, N_TP, PAGE, columns).transpose(1, 0, 2, 3).reshape(GROUPED_TOKENS, columns)

def prefill_group(query_rows, key_array, value_array, ends_row):
    group_number = QUERY_HEADS // KEY_VALUE_HEADS
    scale = 1.0 / math.sqrt(HEAD_SIZE)
    token_count = query_rows.shape[0]
    query_block = min(512, token_count)
    key_width = min(token_count, token_count // 2 + query_block)
    positions = jnp.arange(token_count, dtype=jnp.int32)
    segments = segment_of(positions, ends_row)
    reshaped_array = query_rows.reshape(token_count // query_block, query_block, KEY_VALUE_HEADS, group_number, HEAD_SIZE)

    def one_block(index):
        query_row_block = reshaped_array[index].astype(jnp.float32)
        first_index = jnp.clip(index * query_block + query_block - key_width, 0, token_count - key_width).astype(jnp.int32)
        key_row_block = lax.dynamic_slice_in_dim(key_array, first_index, key_width, 0).reshape(key_width, KEY_VALUE_HEADS, HEAD_SIZE).astype(jnp.float32)
        value_row_block = lax.dynamic_slice_in_dim(value_array, first_index, key_width, 0).reshape(key_width, KEY_VALUE_HEADS, HEAD_SIZE).astype(jnp.float32)
        kpos = first_index + jnp.arange(key_width, dtype=jnp.int32)
        kseg = lax.dynamic_slice_in_dim(segments, first_index, key_width, 0)
        qstart = (index * query_block).astype(jnp.int32)
        qpos = qstart + jnp.arange(query_block, dtype=jnp.int32)
        qseg = lax.dynamic_slice_in_dim(segments, qstart, query_block, 0)
        allowed = (kpos[None, :] <= qpos[:, None]) & (kseg[None, :] == qseg[:, None])
        scores = jnp.einsum('tkgd,skd->kgts', query_row_block, key_row_block) * scale
        scores = jnp.where(allowed, scores, NEGATIVE_FILL)
        top = lax.optimization_barrier(jnp.max(scores, axis=-1, keepdims=True))
        weights = jnp.where(allowed, jnp.exp(scores - top), 0.0)
        total = lax.optimization_barrier(jnp.sum(weights, axis=-1))
        rounded = lax.optimization_barrier(weights.astype(jnp.bfloat16)).astype(jnp.float32)
        mixed = jnp.einsum('kgts,skd->tkgd', rounded, value_row_block) / total.transpose(2, 0, 1)[..., None]
        return mixed.reshape(query_block, QUERY_HEADS * HEAD_SIZE).astype(jnp.bfloat16)
    blocks = lax.map(one_block, jnp.arange(token_count // query_block, dtype=jnp.int32))
    return blocks.reshape(token_count, QUERY_HEADS * HEAD_SIZE)

def reference(prompt_query, prompt_key, prompt_value, prompt_lengths, decode_slot, decoded_query, decoded_key, decoded_value):
    group_number = QUERY_HEADS // KEY_VALUE_HEADS
    scale = 1.0 / math.sqrt(HEAD_SIZE)
    ends_all = (jnp.cumsum(prompt_lengths, axis=1) * PAGE).astype(jnp.int32)
    starts_all = (ends_all - prompt_lengths * PAGE).astype(jnp.int32)
    query_array = prompt_query.reshape(N_PD, GROUPED_TOKENS, QUERY_HEADS * HEAD_SIZE)
    key_array = prompt_key.reshape(N_PD, GROUPED_TOKENS, KEY_VALUE_HEADS * HEAD_SIZE)
    value_array = prompt_value.reshape(N_PD, GROUPED_TOKENS, KEY_VALUE_HEADS * HEAD_SIZE)

    def group_fn(group):
        ordered = prefill_group(to_positions(query_array[group]), to_positions(key_array[group]), to_positions(value_array[group]), ends_all[group])
        return from_positions(ordered)
    pre_out = lax.map(group_fn, jnp.arange(N_PD, dtype=jnp.int32)).reshape(EVERY_TOKEN, QUERY_HEADS * HEAD_SIZE)
    numbers = jnp.arange(REQUEST_TOTAL, dtype=jnp.int32)
    steps_idx = jnp.arange(DECODE_STEPS, dtype=jnp.int32)
    kpos = jnp.arange(GROUPED_TOKENS, dtype=jnp.int32)

    def slot_fn(slot_number):
        request = jnp.sum(jnp.where(decode_slot == slot_number, numbers, 0)).astype(jnp.int32)
        group = request // GROUP_REQUESTS
        order = request % GROUP_REQUESTS
        lower = starts_all[group, order]
        upper = ends_all[group, order]
        prompt_key_rows = to_positions(key_array[group]).astype(jnp.float32)
        prompt_value_rows = to_positions(value_array[group]).astype(jnp.float32)
        complete_keys = jnp.concatenate([prompt_key_rows, decoded_key[slot_number].astype(jnp.float32)], axis=0).reshape(GROUPED_TOKENS + DECODE_STEPS, KEY_VALUE_HEADS, HEAD_SIZE)
        complete_values = jnp.concatenate([prompt_value_rows, decoded_value[slot_number].astype(jnp.float32)], axis=0).reshape(GROUPED_TOKENS + DECODE_STEPS, KEY_VALUE_HEADS, HEAD_SIZE)
        in_prompt = (kpos >= lower) & (kpos < upper)
        prompt_mask = jnp.broadcast_to(in_prompt[None, :], (DECODE_STEPS, GROUPED_TOKENS))
        new_mask = steps_idx[None, :] <= steps_idx[:, None]
        mask = jnp.concatenate([prompt_mask, new_mask], axis=1)
        query_row_block = decoded_query[slot_number].astype(jnp.float32).reshape(DECODE_STEPS, KEY_VALUE_HEADS, group_number, HEAD_SIZE)
        scores = jnp.einsum('skgd,rkd->kgsr', query_row_block, complete_keys) * scale
        scores = jnp.where(mask[None, None], scores, NEGATIVE_FILL)
        top = lax.optimization_barrier(jnp.max(scores, axis=-1, keepdims=True))
        weights = jnp.where(mask[None, None], jnp.exp(scores - top), 0.0)
        total = lax.optimization_barrier(jnp.sum(weights, axis=-1))
        rounded = lax.optimization_barrier(weights.astype(jnp.bfloat16)).astype(jnp.float32)
        mixed = jnp.einsum('kgsr,rkd->skgd', rounded, complete_values) / total.transpose(2, 0, 1)[..., None]
        return mixed.reshape(DECODE_STEPS, QUERY_HEADS * HEAD_SIZE).astype(jnp.bfloat16)
    dec_out = lax.map(slot_fn, numbers)
    return (pre_out, dec_out)
```

```python
import math

import jax
import jax.numpy as jnp
from jax import lax
from jax.experimental import pallas as pl
from jax.experimental.pallas import tpu as pltpu
from jax.sharding import PartitionSpec as P

QUERY_HEADS = 32
KEY_VALUE_HEADS = 4
HEAD_SIZE = 128
PAGE = 16
GROUP_REQUESTS = 4
DECODE_STEPS = 2
HEADS_PER_KV = QUERY_HEADS // KEY_VALUE_HEADS
KV_WIDTH = KEY_VALUE_HEADS * HEAD_SIZE
Q_WIDTH = QUERY_HEADS * HEAD_SIZE
DECODE_ROWS = GROUP_REQUESTS * DECODE_STEPS
PADDED_ROWS = 16
CHUNK = 4

MASKED = -1e30
EXPONENT = math.log2(math.e) / math.sqrt(HEAD_SIZE)


def scores_of(queries, keys):
    return lax.dot_general(
        queries, keys, (((1,), (1,)), ((), ())), preferred_element_type=jnp.float32
    )


def with_ones(values):
    return jnp.concatenate([values, jnp.ones_like(values)], axis=1)


def key_positions(shape, member, width, first_shard):
    column = lax.broadcasted_iota(jnp.int32, shape, 1)
    rows = shape[1] // CHUNK if width >= CHUNK else shape[1] // width
    shard = column // rows
    offset = column - shard * rows
    source = member - (first_shard + shard)
    source = jnp.where(source < 0, source + width, source)
    return (offset // PAGE * width + source) * PAGE + offset % PAGE


def request_ends(lengths_ref, group):
    ends = []
    total = jnp.int32(0)
    for r in range(GROUP_REQUESTS):
        total = total + lengths_ref[group, r] * PAGE
        ends.append(total)
    return ends


def fold(state, scores_list, values_list):
    top = None
    for scores in scores_list:
        part = jnp.max(scores, axis=1, keepdims=True)
        top = part if top is None else jnp.maximum(top, part)
    if state is not None:
        top = jnp.maximum(top, state[0])
    acc = None
    for scores, values in zip(scores_list, values_list):
        weights = jnp.exp2((scores - top) * EXPONENT).astype(jnp.bfloat16)
        part = jnp.dot(weights, values, preferred_element_type=jnp.float32)
        acc = part if acc is None else acc + part
    if state is not None:
        acc = acc + state[1] * jnp.exp2((state[0] - top) * EXPONENT)
    return top, acc


def normalised(state):
    acc = state[1]
    return (acc[:, :HEAD_SIZE] / acc[:, HEAD_SIZE:]).astype(jnp.bfloat16)


def prefill_kernel(width, lengths_ref, where_ref, q_ref, *refs):
    k_refs, v_refs, out_ref, bias_ref = refs[:width], refs[width : 2 * width], refs[-2], refs[-1]
    tokens = q_ref.shape[0]
    half = tokens // 2
    group, member = where_ref[0], where_ref[1]
    per_chunk = min(CHUNK, width)
    chunks = width // per_chunk

    @pl.when(pl.program_id(0) == 0)
    def _():
        ends = request_ends(lengths_ref, group)
        offset = lax.broadcasted_iota(jnp.int32, (tokens, 1), 0)
        qpos = (offset // PAGE * width + member) * PAGE + offset % PAGE
        low = jnp.zeros_like(qpos)
        for end in ends:
            low = jnp.where(qpos >= end, end, low)
        for c in range(chunks):
            kpos = key_positions((tokens, per_chunk * tokens), member, width, c * per_chunk)
            bias_ref[c] = jnp.where((kpos >= low) & (kpos <= qpos), 0.0, MASKED)

    for first, keys in ((0, half), (half, tokens)):
        rows = pl.ds(first, half)
        chunk_data = []
        for c in range(chunks):
            span = range(c * per_chunk, (c + 1) * per_chunk)
            k_all = jnp.concatenate([k_refs[s][:keys, :] for s in span], axis=0)
            v_all = with_ones(jnp.concatenate([v_refs[s][:keys, :] for s in span], axis=0))
            bias = jnp.concatenate(
                [bias_ref[c, rows, i * tokens : i * tokens + keys] for i in range(per_chunk)], axis=1
            )
            chunk_data.append((k_all, v_all, bias))
        for head in range(HEADS_PER_KV):
            columns = slice(head * HEAD_SIZE, (head + 1) * HEAD_SIZE)
            queries = q_ref[rows, columns]
            state = None
            for k_all, v_all, bias in chunk_data:
                state = fold(state, [scores_of(queries, k_all) + bias], [v_all])
            out_ref[rows, columns] = normalised(state)


def decode_kernel(width, lengths_ref, where_ref, q_ref, fresh_k_ref, fresh_v_ref, *refs):
    k_refs, v_refs, out_ref = refs[:width], refs[width : 2 * width], refs[-1]
    tokens = k_refs[0].shape[0]
    group, member = where_ref[0], where_ref[1]
    per_chunk = min(CHUNK, width)
    chunks = width // per_chunk
    count = HEADS_PER_KV * PADDED_ROWS
    ends = request_ends(lengths_ref, group)
    row = lax.broadcasted_iota(jnp.int32, (count, 1), 0) % PADDED_ROWS
    request = row // DECODE_STEPS
    low = jnp.zeros_like(row)
    high = jnp.zeros_like(row) + ends[0]
    for r in range(1, GROUP_REQUESTS):
        low = jnp.where(request == r, ends[r - 1], low)
        high = jnp.where(request == r, ends[r], high)
    queries = jnp.concatenate(
        [q_ref[:, h * HEAD_SIZE : (h + 1) * HEAD_SIZE] for h in range(HEADS_PER_KV)], axis=0
    )
    column = lax.broadcasted_iota(jnp.int32, (count, PADDED_ROWS), 1)
    fresh = (column // DECODE_STEPS == request) & (column % DECODE_STEPS <= row % DECODE_STEPS)
    fresh_scores = jnp.where(fresh, scores_of(queries, fresh_k_ref[...]), MASKED)
    fresh_values = with_ones(fresh_v_ref[...])
    state = None
    for c in range(chunks):
        span = range(c * per_chunk, (c + 1) * per_chunk)
        k_all = jnp.concatenate([k_refs[s][...] for s in span], axis=0)
        v_all = with_ones(jnp.concatenate([v_refs[s][...] for s in span], axis=0))
        kpos = key_positions((count, per_chunk * tokens), member, width, c * per_chunk)
        scores = jnp.where((kpos >= low) & (kpos < high), scores_of(queries, k_all), MASKED)
        if c == 0:
            state = fold(state, [scores, fresh_scores], [v_all, fresh_values])
        else:
            state = fold(state, [scores], [v_all])
    out = normalised(state)
    for h in range(HEADS_PER_KV):
        out_ref[:, h * HEAD_SIZE : (h + 1) * HEAD_SIZE] = out[
            h * PADDED_ROWS : (h + 1) * PADDED_ROWS
        ]


def call_prefill(lengths, where, query, keys, values):
    tokens = query.shape[0]
    width = len(keys)
    per_chunk = min(CHUNK, width)
    kv_spec = pl.BlockSpec((tokens, HEAD_SIZE), lambda h: (0, h))
    q_spec = pl.BlockSpec((tokens, HEADS_PER_KV * HEAD_SIZE), lambda h: (0, h))
    return pl.pallas_call(
        lambda *refs: prefill_kernel(width, *refs),
        grid=(KEY_VALUE_HEADS,),
        in_specs=[pl.BlockSpec(memory_space=pltpu.SMEM)] * 2 + [q_spec] + [kv_spec] * (2 * width),
        out_specs=q_spec,
        out_shape=jax.ShapeDtypeStruct(query.shape, jnp.bfloat16),
        scratch_shapes=[
            pltpu.VMEM((width // per_chunk, tokens, per_chunk * tokens), jnp.float32)
        ],
        compiler_params=pltpu.CompilerParams(vmem_limit_bytes=32 * 1024 * 1024),
        cost_estimate=pl.CostEstimate(
            flops=4 * tokens * tokens * width * Q_WIDTH,
            bytes_accessed=4 * tokens * Q_WIDTH + 4 * width * tokens * KV_WIDTH,
            transcendentals=tokens * tokens * width * QUERY_HEADS,
        ),
        name="prefill_attention",
    )(lengths, where, query, *keys, *values)


def call_decode(lengths, where, rows, keys, values):
    tokens = keys[0].shape[0]
    width = len(keys)
    heads = HEADS_PER_KV * HEAD_SIZE
    kv_spec = pl.BlockSpec((tokens, HEAD_SIZE), lambda h: (0, h))
    q_spec = pl.BlockSpec((PADDED_ROWS, heads), lambda h: (0, h))
    first_k, first_v = Q_WIDTH // HEAD_SIZE, (Q_WIDTH + KV_WIDTH) // HEAD_SIZE
    return pl.pallas_call(
        lambda *refs: decode_kernel(width, *refs),
        grid=(KEY_VALUE_HEADS,),
        in_specs=[pl.BlockSpec(memory_space=pltpu.SMEM)] * 2
        + [
            q_spec,
            pl.BlockSpec((PADDED_ROWS, HEAD_SIZE), lambda h: (0, first_k + h)),
            pl.BlockSpec((PADDED_ROWS, HEAD_SIZE), lambda h: (0, first_v + h)),
        ]
        + [kv_spec] * (2 * width),
        out_specs=q_spec,
        out_shape=jax.ShapeDtypeStruct((PADDED_ROWS, Q_WIDTH), jnp.bfloat16),
        compiler_params=pltpu.CompilerParams(vmem_limit_bytes=32 * 1024 * 1024),
        cost_estimate=pl.CostEstimate(
            flops=4 * PADDED_ROWS * tokens * width * Q_WIDTH,
            bytes_accessed=4 * width * tokens * KV_WIDTH,
            transcendentals=PADDED_ROWS * tokens * width * QUERY_HEADS,
        ),
        name="decode_attention",
    )(lengths, where, rows, rows, rows, *keys, *values)


def ring(size, step):
    return [(i, (i + step) % size) for i in range(size)]


def chosen(picks, rows):
    return jnp.dot(picks.astype(jnp.bfloat16), rows, preferred_element_type=jnp.float32).astype(
        jnp.bfloat16
    )


def body(
    prompt_query,
    prompt_key,
    prompt_value,
    prompt_lengths,
    decode_slot,
    decoded_query,
    decoded_key,
    decoded_value,
):
    tp_size = lax.axis_size("tp")
    pd_size = lax.axis_size("pd")
    my_group = lax.axis_index("pd")
    member = lax.axis_index("tp")
    where = jnp.stack([my_group, member]).astype(jnp.int32)

    keys, values = [prompt_key], [prompt_value]
    for _ in range(1, tp_size):
        keys.append(lax.ppermute(keys[-1], "tp", ring(tp_size, 1)))
        values.append(lax.ppermute(values[-1], "tp", ring(tp_size, 1)))

    own = jnp.concatenate([decoded_query, decoded_key, decoded_value], axis=2).reshape(
        DECODE_ROWS, Q_WIDTH + 2 * KV_WIDTH
    )
    blocks = [own] + [lax.ppermute(own, "pd", ring(pd_size, k)) for k in range(1, pd_size)]
    everyone = jnp.concatenate(blocks, axis=0)

    slots = lax.dynamic_slice_in_dim(decode_slot, my_group * GROUP_REQUESTS, GROUP_REQUESTS, 0)
    block_of = (my_group - slots // GROUP_REQUESTS) % pd_size
    place_of = slots % GROUP_REQUESTS
    row = jnp.arange(PADDED_ROWS, dtype=jnp.int32)
    step = row % DECODE_STEPS
    at = jnp.repeat(
        block_of * DECODE_ROWS + place_of * DECODE_STEPS, DECODE_STEPS, total_repeat_length=DECODE_ROWS
    )
    at = jnp.concatenate([at, jnp.full((PADDED_ROWS - DECODE_ROWS,), -DECODE_STEPS, jnp.int32)]) + step
    picks = at[:, None] == jnp.arange(pd_size * DECODE_ROWS, dtype=jnp.int32)[None, :]
    rows = chosen(picks, everyone)

    dec = call_decode(prompt_lengths, where, rows, keys, values)

    sent = []
    for k in range(pd_size):
        out_row = jnp.arange(DECODE_STEPS, dtype=jnp.int32)
        match = (block_of == (-k) % pd_size if k else block_of == 0)
        match = jnp.repeat(match, DECODE_STEPS, total_repeat_length=DECODE_ROWS)
        match = jnp.concatenate([match, jnp.zeros((PADDED_ROWS - DECODE_ROWS,), bool)])
        sent.append(match[None, :] & (step[None, :] == out_row[:, None]))
    outgoing = chosen(jnp.concatenate(sent, axis=0), dec)
    arrived = [outgoing[:DECODE_STEPS]]
    for k in range(1, pd_size):
        part = outgoing[k * DECODE_STEPS : (k + 1) * DECODE_STEPS]
        arrived.append(lax.ppermute(part, "pd", ring(pd_size, k)))

    pre_out = call_prefill(prompt_lengths, where, prompt_query, keys, values)

    numbers = jnp.arange(decode_slot.shape[0], dtype=jnp.int32)
    wanted = my_group * GROUP_REQUESTS + jnp.arange(GROUP_REQUESTS, dtype=jnp.int32)
    owner = jnp.sum(
        jnp.where(decode_slot[None, :] == wanted[:, None], numbers[None, :] // GROUP_REQUESTS, 0), axis=1
    )
    from_block = (my_group - owner) % pd_size
    dec_out = jnp.zeros((GROUP_REQUESTS, DECODE_STEPS, Q_WIDTH), jnp.bfloat16)
    for k in range(pd_size):
        dec_out = jnp.where((from_block == k)[:, None, None], arrived[k][None], dec_out)
    return (pre_out, dec_out)


def solution(mesh):
    placed = (
        P(("rep", "pd", "tp"), None),
        P(("rep", "pd", "tp"), None),
        P(("rep", "pd", "tp"), None),
        P("rep", None),
        P("rep"),
        P(("rep", "pd"), None, None),
        P(("rep", "pd"), None, None),
        P(("rep", "pd"), None, None),
    )
    return jax.shard_map(
        body,
        mesh=mesh,
        in_specs=placed,
        out_specs=(P(("rep", "pd", "tp"), None), P(("rep", "pd"), None, None)),
        check_vma=False,
    )
```

```python
import math

import jax
import jax.numpy as jnp
from jax import lax
from jax.experimental import pallas as pl
from jax.experimental.pallas import tpu as pltpu
from jax.sharding import PartitionSpec as P

QUERY_HEADS = 32
KEY_VALUE_HEADS = 4
HEAD_SIZE = 128
PAGE = 16
GROUP_REQUESTS = 4
DECODE_STEPS = 2
HEADS_PER_KV = QUERY_HEADS // KEY_VALUE_HEADS
KV_WIDTH = KEY_VALUE_HEADS * HEAD_SIZE
Q_WIDTH = QUERY_HEADS * HEAD_SIZE
Q_BLOCK = HEADS_PER_KV * HEAD_SIZE
DECODE_ROWS = GROUP_REQUESTS * DECODE_STEPS
PADDED_ROWS = 16
STACKED = HEADS_PER_KV * PADDED_ROWS
MIB = 1024 * 1024

MASKED = -1e30
EXPONENT = math.log2(math.e) / math.sqrt(HEAD_SIZE)

VMEM = pl.BlockSpec(memory_space=pltpu.VMEM)
SMEM = pl.BlockSpec(memory_space=pltpu.SMEM)


def scores_of(queries, keys):
    return lax.dot_general(
        queries, keys, (((1,), (1,)), ((), ())), preferred_element_type=jnp.float32
    )


def product(left, right):
    return jnp.dot(left, right, preferred_element_type=jnp.float32)


def iota(shape, axis):
    return lax.broadcasted_iota(jnp.int32, shape, axis)


def key_positions(rows, member, width):
    column = iota((1, width * rows), 1)
    shift = column // rows
    offset = column - shift * rows
    source = member - shift
    source = jnp.where(source < 0, source + width, source)
    return (offset // PAGE * width + source) * PAGE + offset % PAGE


def request_ends(lengths_ref, group):
    ends = []
    total = jnp.int32(0)
    for r in range(GROUP_REQUESTS):
        total = total + lengths_ref[group, r] * PAGE
        ends.append(total)
    return ends


def collect(table, refs, member, out_ref):
    rows = refs[0].shape[0]
    for shift, (right, left) in enumerate(table):
        part = refs[right][...]
        if left != right:
            part = jnp.where(member >= shift, part, refs[left][...])
        out_ref[shift * rows : (shift + 1) * rows, : part.shape[1]] = part


def parts_of(ref, width, tokens, keys, columns):
    if keys == tokens:
        return ref[:, columns]
    return jnp.concatenate([ref[s * tokens : s * tokens + keys, columns] for s in range(width)], axis=0)


def head_group(width):
    return max(1, min(HEADS_PER_KV, HEADS_PER_KV * 4 // width))


def weights_kernel(table, pd_size, lengths_ref, where_ref, slots_ref, q_ref, *refs):
    width = len(table)
    k_count = len(refs) - pd_size - 7
    block_refs, k_refs = refs[:pd_size], refs[pd_size : pd_size + k_count]
    low_ref, high_ref, dec_ref, fresh_ref, fresh_v_ref, keys_ref, rows_ref = refs[pd_size + k_count :]
    tokens = q_ref.shape[0]
    half = tokens // 2
    group, member = where_ref[0], where_ref[1]
    ends = request_ends(lengths_ref, group)
    h = pl.program_id(0)

    @pl.when(h == 0)
    def _():
        collect(table, k_refs, member, keys_ref)
        row = iota((PADDED_ROWS, DECODE_ROWS), 0)
        column = iota((PADDED_ROWS, DECODE_ROWS), 1)
        total = None
        for k in range(pd_size):
            pick = column < 0
            for r in range(GROUP_REQUESTS):
                slot = slots_ref[group * GROUP_REQUESTS + r]
                back = group - slot // GROUP_REQUESTS
                back = jnp.where(back < 0, back + pd_size, back)
                first = jnp.where(back == k, slot % GROUP_REQUESTS * DECODE_STEPS, -DECODE_ROWS * 4)
                pick = pick | (
                    (row // DECODE_STEPS == r) & (column == first + row - r * DECODE_STEPS)
                )
            part = product(pick.astype(jnp.float32).astype(jnp.bfloat16), block_refs[k][...])
            total = part if total is None else total + part
        total = total.astype(jnp.bfloat16)
        rows_ref[...] = total[:, : Q_WIDTH + KV_WIDTH]
        fresh_v_ref[...] = total[:, Q_WIDTH + KV_WIDTH :]

    columns = pl.ds(pl.multiple_of(h * HEAD_SIZE, HEAD_SIZE), HEAD_SIZE)

    row = iota((STACKED, 1), 0) % PADDED_ROWS
    request = row // DECODE_STEPS
    low = jnp.zeros_like(row)
    high = jnp.zeros_like(row) + ends[0]
    for r in range(1, GROUP_REQUESTS):
        low = jnp.where(request == r, ends[r - 1], low)
        high = jnp.where(request == r, ends[r], high)
    first = h * Q_BLOCK
    queries = jnp.concatenate(
        [
            rows_ref[:, pl.ds(pl.multiple_of(first + g * HEAD_SIZE, HEAD_SIZE), HEAD_SIZE)]
            for g in range(HEADS_PER_KV)
        ],
        axis=0,
    )
    column = iota((STACKED, PADDED_ROWS), 1)
    fresh = (column // DECODE_STEPS == request) & (column % DECODE_STEPS <= row % DECODE_STEPS)
    fresh_columns = pl.ds(pl.multiple_of(Q_WIDTH + h * HEAD_SIZE, HEAD_SIZE), HEAD_SIZE)
    fresh_scores = jnp.where(fresh, scores_of(queries, rows_ref[:, fresh_columns]), MASKED)
    kpos = key_positions(tokens, member, width)
    scores = jnp.where(
        (kpos >= low) & (kpos < high), scores_of(queries, keys_ref[:, columns]), MASKED
    )
    top = jnp.maximum(
        jnp.max(scores, axis=1, keepdims=True), jnp.max(fresh_scores, axis=1, keepdims=True)
    )
    dec_ref[0] = jnp.exp2((scores - top) * EXPONENT).astype(jnp.bfloat16)
    fresh_ref[0] = jnp.exp2((fresh_scores - top) * EXPONENT).astype(jnp.bfloat16)

    together = head_group(width)
    for start, keys, out_ref in ((0, half, low_ref), (half, tokens, high_ref)):
        offset = start + iota((half, 1), 0)
        qpos = (offset // PAGE * width + member) * PAGE + offset % PAGE
        low = jnp.zeros_like(qpos)
        for end in ends:
            low = jnp.where(qpos >= end, end, low)
        kpos = key_positions(keys, member, width)
        bias = jnp.where((kpos >= low) & (kpos <= qpos), 0.0, MASKED)
        k_all = parts_of(keys_ref, width, tokens, keys, columns)
        for g in range(0, HEADS_PER_KV, together):
            queries = jnp.concatenate(
                [
                    q_ref[
                        start : start + half,
                        pl.ds(pl.multiple_of(first + i * HEAD_SIZE, HEAD_SIZE), HEAD_SIZE),
                    ]
                    for i in range(g, g + together)
                ],
                axis=0,
            )
            scores = scores_of(queries, k_all).reshape(together, half, width * keys) + bias[None]
            top = jnp.max(scores, axis=2, keepdims=True)
            weights = jnp.exp2((scores - top) * EXPONENT).astype(jnp.bfloat16)
            out_ref[0, g * half : (g + together) * half, :] = weights.reshape(
                together * half, width * keys
            )


def decode_kernel(table, pd_size, where_ref, slots_ref, dec_ref, fresh_ref, fresh_v_ref, *refs):
    width = len(table)
    v_refs, out_refs, values_ref = refs[: -pd_size - 1], refs[-pd_size - 1 : -1], refs[-1]
    group, member = where_ref[0], where_ref[1]
    collect(table, v_refs, member, values_ref)
    ones = jnp.ones((values_ref.shape[0], HEAD_SIZE), jnp.bfloat16)
    fresh_ones = jnp.ones((PADDED_ROWS, HEAD_SIZE), jnp.bfloat16)
    row = iota((8, PADDED_ROWS), 0)
    column = iota((8, PADDED_ROWS), 1)
    picks = []
    for k in range(pd_size):
        target = group + k
        target = jnp.where(target >= pd_size, target - pd_size, target)
        pick = column < 0
        for r in range(GROUP_REQUESTS):
            mine = slots_ref[group * GROUP_REQUESTS + r] // GROUP_REQUESTS == target
            first = jnp.where(mine, r * DECODE_STEPS, -PADDED_ROWS * 4)
            pick = pick | ((row < DECODE_STEPS) & (column == first + row))
        picks.append(pick.astype(jnp.float32).astype(jnp.bfloat16))
    for h in range(KEY_VALUE_HEADS):
        columns = slice(h * HEAD_SIZE, (h + 1) * HEAD_SIZE)
        acc = product(dec_ref[h], jnp.concatenate([values_ref[:, columns], ones], axis=1))
        acc += product(fresh_ref[h], jnp.concatenate([fresh_v_ref[:, columns], fresh_ones], axis=1))
        out = (acc[:, :HEAD_SIZE] / acc[:, HEAD_SIZE:]).astype(jnp.bfloat16)
        out = jnp.concatenate(
            [out[g * PADDED_ROWS : (g + 1) * PADDED_ROWS] for g in range(HEADS_PER_KV)], axis=1
        )
        for k in range(pd_size):
            sent = product(picks[k], out).astype(jnp.bfloat16)
            out_refs[k][:, h * Q_BLOCK : (h + 1) * Q_BLOCK] = sent[:DECODE_STEPS]


def prefill_kernel(table, where_ref, low_ref, high_ref, *refs):
    width = len(table)
    v_refs, (out_ref, values_ref, done_ref, sem) = refs[:-4], refs[-4:]
    tokens = v_refs[0].shape[0]
    half = tokens // 2
    collect(table, v_refs, where_ref[1], values_ref)
    copies = []
    for h in range(KEY_VALUE_HEADS):
        columns = slice(h * HEAD_SIZE, (h + 1) * HEAD_SIZE)
        for start, keys, p_ref in ((0, half, low_ref), (half, tokens, high_ref)):
            values = parts_of(values_ref, width, tokens, keys, columns)
            acc = product(p_ref[h], jnp.concatenate([values, jnp.ones_like(values)], axis=1))
            out = (acc[:, :HEAD_SIZE] / acc[:, HEAD_SIZE:]).astype(jnp.bfloat16)
            for g in range(HEADS_PER_KV):
                done_ref[
                    start : start + half, h * Q_BLOCK + g * HEAD_SIZE : h * Q_BLOCK + (g + 1) * HEAD_SIZE
                ] = out[g * half : (g + 1) * half]
        span = pl.ds(h * Q_BLOCK, Q_BLOCK)
        copy = pltpu.make_async_copy(done_ref.at[:, span], out_ref.at[:, span], sem.at[h])
        copy.start()
        copies.append(copy)
    for copy in copies:
        copy.wait()


def call_weights(table, lengths, where, slots, query, blocks, keys):
    tokens, width = query.shape[0], len(table)
    half, every = tokens // 2, width * tokens
    stacked = HEADS_PER_KV * half
    shapes = [
        (KEY_VALUE_HEADS, stacked, width * half),
        (KEY_VALUE_HEADS, stacked, every),
        (KEY_VALUE_HEADS, STACKED, every),
        (KEY_VALUE_HEADS, STACKED, PADDED_ROWS),
    ]
    return pl.pallas_call(
        lambda *refs: weights_kernel(table, len(blocks), *refs),
        grid=(KEY_VALUE_HEADS,),
        in_specs=[SMEM] * 3 + [VMEM] * (1 + len(blocks) + len(keys)),
        out_specs=[pl.BlockSpec((1,) + s[1:], lambda h: (h, 0, 0)) for s in shapes] + [VMEM],
        out_shape=[jax.ShapeDtypeStruct(s, jnp.bfloat16) for s in shapes]
        + [jax.ShapeDtypeStruct((PADDED_ROWS, KV_WIDTH), jnp.bfloat16)],
        scratch_shapes=[
            pltpu.VMEM((every, KV_WIDTH), jnp.bfloat16),
            pltpu.VMEM((PADDED_ROWS, Q_WIDTH + KV_WIDTH), jnp.bfloat16),
        ],
        compiler_params=pltpu.CompilerParams(vmem_limit_bytes=(28 + width) * MIB),
        cost_estimate=pl.CostEstimate(
            flops=2 * tokens * every * Q_WIDTH,
            bytes_accessed=2 * tokens * Q_WIDTH + 2 * every * KV_WIDTH,
            transcendentals=tokens * every * QUERY_HEADS,
        ),
        name="weights",
    )(lengths, where, slots, query, *blocks, *keys)


def call_decode(table, pd_size, where, slots, weights, values):
    _, _, dec, fresh, fresh_v = weights
    every = dec.shape[2]
    return pl.pallas_call(
        lambda *refs: decode_kernel(table, pd_size, *refs),
        in_specs=[SMEM] * 2 + [VMEM] * (3 + len(values)),
        out_specs=[VMEM] * pd_size,
        out_shape=[jax.ShapeDtypeStruct((DECODE_STEPS, Q_WIDTH), jnp.bfloat16)] * pd_size,
        scratch_shapes=[pltpu.VMEM((every, KV_WIDTH), jnp.bfloat16)],
        compiler_params=pltpu.CompilerParams(vmem_limit_bytes=(28 + len(table)) * MIB),
        cost_estimate=pl.CostEstimate(
            flops=2 * PADDED_ROWS * every * Q_WIDTH,
            bytes_accessed=2 * every * KV_WIDTH,
            transcendentals=0,
        ),
        name="decode_values",
    )(where, slots, dec, fresh, fresh_v, *values)


def call_prefill(table, where, weights, values):
    low, high = weights[0], weights[1]
    tokens = values[0].shape[0]
    every = high.shape[2]
    return pl.pallas_call(
        lambda *refs: prefill_kernel(table, *refs),
        in_specs=[SMEM] + [VMEM] * (2 + len(values)),
        out_specs=pl.BlockSpec(memory_space=pl.ANY),
        out_shape=jax.ShapeDtypeStruct((tokens, Q_WIDTH), jnp.bfloat16),
        scratch_shapes=[
            pltpu.VMEM((every, KV_WIDTH), jnp.bfloat16),
            pltpu.VMEM((tokens, Q_WIDTH), jnp.bfloat16),
            pltpu.SemaphoreType.DMA((KEY_VALUE_HEADS,)),
        ],
        compiler_params=pltpu.CompilerParams(vmem_limit_bytes=(28 + len(table)) * MIB),
        cost_estimate=pl.CostEstimate(
            flops=2 * tokens * every * Q_WIDTH,
            bytes_accessed=4 * tokens * Q_WIDTH + 2 * every * KV_WIDTH,
            transcendentals=0,
        ),
        name="prefill_values",
    )(where, low, high, *values)


def ring(size, step):
    return [(i, (i + step) % size) for i in range(size)]


def line_exchange(own, size):
    arrays, right, left = [own], {0: 0}, {0: 0}

    def send(place, pairs):
        arrays.append(lax.ppermute(arrays[place], "tp", pairs))
        return len(arrays) - 1

    for d in sorted(range(1, size), key=lambda d: (d > 2, d != 2, d)):
        if d <= 2 and 2 * d == size:
            right[d] = left[d] = send(0, ring(size, d))
        elif d > 2 and right[d - 1] == left[d - 1] and 2 * d > size + 1:
            pairs = [(i, i + 1) for i in range(d - 1, size - 1)]
            right[d] = left[d] = send(right[d - 1], pairs + [(i, i - 1) for i in range(1, size - d + 1)])
        else:
            hop = min(d, 2) if d <= 2 else 1
            first = 0 if d <= 2 else d - 1
            right[d] = send(0 if d <= 2 else right[d - 1], [(i, i + hop) for i in range(first, size - hop)])
            left[d] = send(0 if d <= 2 else left[d - 1], [(i, i - hop) for i in range(hop, size - first)])
    return arrays, [(right[s], left[(size - s) % size]) for s in range(size)]


def body(
    prompt_query,
    prompt_key,
    prompt_value,
    prompt_lengths,
    decode_slot,
    decoded_query,
    decoded_key,
    decoded_value,
):
    tp_size = lax.axis_size("tp")
    pd_size = lax.axis_size("pd")
    my_group = lax.axis_index("pd")
    member = lax.axis_index("tp")
    where = jnp.stack([my_group, member]).astype(jnp.int32)

    keys, table = line_exchange(prompt_key, tp_size)
    values, _ = line_exchange(prompt_value, tp_size)

    own = jnp.concatenate([decoded_query, decoded_key, decoded_value], axis=2).reshape(
        DECODE_ROWS, Q_WIDTH + 2 * KV_WIDTH
    )
    own, _ = lax.optimization_barrier((own, keys[1]))
    blocks = [own] + [lax.ppermute(own, "pd", ring(pd_size, k)) for k in range(1, pd_size)]

    weights = call_weights(table, prompt_lengths, where, decode_slot, prompt_query, blocks, keys)
    outgoing = call_decode(table, pd_size, where, decode_slot, weights, values)
    arrived = [outgoing[0]]
    for k in range(1, pd_size):
        arrived.append(lax.ppermute(outgoing[k], "pd", ring(pd_size, k)))
    pre_out = call_prefill(table, where, weights, values)

    numbers = jnp.arange(decode_slot.shape[0], dtype=jnp.int32)
    wanted = my_group * GROUP_REQUESTS + jnp.arange(GROUP_REQUESTS, dtype=jnp.int32)
    owner = jnp.sum(
        jnp.where(decode_slot[None, :] == wanted[:, None], numbers[None, :] // GROUP_REQUESTS, 0), axis=1
    )
    from_block = (my_group - owner) % pd_size
    dec_out = jnp.zeros((GROUP_REQUESTS, DECODE_STEPS, Q_WIDTH), jnp.bfloat16)
    for k in range(pd_size):
        dec_out = jnp.where((from_block == k)[:, None, None], arrived[k][None], dec_out)
    return (pre_out, dec_out)


def solution(mesh):
    placed = (
        P(("rep", "pd", "tp"), None),
        P(("rep", "pd", "tp"), None),
        P(("rep", "pd", "tp"), None),
        P("rep", None),
        P("rep"),
        P(("rep", "pd"), None, None),
        P(("rep", "pd"), None, None),
        P(("rep", "pd"), None, None),
    )
    return jax.shard_map(
        body,
        mesh=mesh,
        in_specs=placed,
        out_specs=(P(("rep", "pd", "tp"), None), P(("rep", "pd"), None, None)),
        check_vma=False,
    )
```

```python
import math

import jax
import jax.numpy as jnp
import numpy as np
from jax import lax
from jax.experimental import pallas as pl
from jax.experimental.pallas import tpu as pltpu
from jax.sharding import PartitionSpec as P

QUERY_HEADS = 32
KEY_VALUE_HEADS = 4
HEAD_SIZE = 128
PAGE = 16
GROUP_REQUESTS = 4
DECODE_STEPS = 2
HEADS_PER_KV = QUERY_HEADS // KEY_VALUE_HEADS
KV_WIDTH = KEY_VALUE_HEADS * HEAD_SIZE
Q_WIDTH = QUERY_HEADS * HEAD_SIZE
Q_BLOCK = HEADS_PER_KV * HEAD_SIZE
DECODE_ROWS = GROUP_REQUESTS * DECODE_STEPS
PADDED_ROWS = 16
STACKED = HEADS_PER_KV * PADDED_ROWS
MIB = 1024 * 1024

MASKED = -1e30
EXPONENT = math.log2(math.e) / math.sqrt(HEAD_SIZE)

VMEM = pl.BlockSpec(memory_space=pltpu.VMEM)
SMEM = pl.BlockSpec(memory_space=pltpu.SMEM)


class Exchange:
    def __init__(self, size):
        self.size = size
        self.steps = []
        got = [[] for _ in range(size)]
        last = [0, 0]
        for d in range(1, size):
            made = [None, None]
            for odd in (0, 1):
                pairs = []
                for i in range(odd, size - 1, 2):
                    if i >= d - 1:
                        pairs.append((i, i + 1))
                    if i + 1 <= size - d:
                        pairs.append((i + 1, i))
                if pairs:
                    self.steps.append((last[1 - odd], pairs))
                    made[odd] = len(self.steps)
                    for src, dst in pairs:
                        got[dst].append((made[odd], dst - d if src < dst else dst + d))
            last = made
        self.choice = np.array([[b for b, _ in g] for g in got], np.int32)
        self.source = np.array([[s for _, s in g] for g in got], np.int32)
        self.candidates = [sorted(set(self.choice[:, j])) for j in range(size - 1)]

    def run(self, own, axis, meanwhile):
        arrays = [own]
        extra = None
        for operand, pairs in self.steps:
            if len(arrays) == len(self.steps):
                arrays, extra = lax.optimization_barrier((arrays, extra))
            arrays.append(lax.ppermute(arrays[operand], axis, pairs))
            if len(arrays) == 2:
                arrays[1], extra = meanwhile(arrays[1])
        return arrays, extra

    def table(self):
        return np.concatenate([self.choice, self.source], axis=1)


def scores_of(queries, keys):
    return lax.dot_general(
        queries, keys, (((1,), (1,)), ((), ())), preferred_element_type=jnp.float32
    )


def product(left, right):
    return jnp.dot(left, right, preferred_element_type=jnp.float32)


def iota(shape, axis):
    return lax.broadcasted_iota(jnp.int32, shape, axis)


def span(start, size):
    if isinstance(start, int):
        return slice(start, start + size)
    return pl.ds(pl.multiple_of(start, size), size)


def with_ones(values):
    return jnp.concatenate([values, jnp.ones_like(values)], axis=1)


def page_position(offset, member, width):
    return (offset // PAGE * width + member) * PAGE + offset % PAGE


def key_positions(rows, sources, width):
    column = iota((1, len(sources) * rows), 1)
    part = column // rows
    source = jnp.zeros_like(column) + sources[0]
    for b in range(1, len(sources)):
        source = jnp.where(part == b, sources[b], source)
    return page_position(column - part * rows, source, width)


class Facts:
    def __init__(self, ref, width):
        self.width = width
        self.group, self.member = ref[0], ref[1]
        self.slots = [ref[2 + r] for r in range(GROUP_REQUESTS)]
        first = 2 + GROUP_REQUESTS
        self.ends = []
        total = jnp.int32(0)
        for r in range(GROUP_REQUESTS):
            total = total + ref[first + r] * PAGE
            self.ends.append(total)
        first += GROUP_REQUESTS
        self.choice = [ref[first + j] for j in range(width - 1)]
        self.source = [ref[first + width - 1 + j] for j in range(width - 1)]


def facts_row(plan, lengths, slots):
    group, member = lax.axis_index("pd"), lax.axis_index("tp")
    return jnp.concatenate(
        [
            jnp.stack([group, member]).astype(jnp.int32),
            lax.dynamic_slice_in_dim(slots, group * GROUP_REQUESTS, GROUP_REQUESTS, 0),
            lax.dynamic_index_in_dim(lengths, group, 0, keepdims=False),
            lax.dynamic_index_in_dim(jnp.asarray(plan.table()), member, 0, keepdims=False),
        ]
    )


def causal_bias(start, rows, keys, sources, ends, member, width):
    qpos = page_position(start + iota((rows, 1), 0), member, width)
    low = jnp.zeros_like(qpos)
    for end in ends:
        low = jnp.where(qpos >= end, end, low)
    kpos = key_positions(keys, sources, width)
    return jnp.where((kpos >= low) & (kpos <= qpos), 0.0, MASKED)


def request_mask(ends, keys, sources, width):
    request = iota((STACKED, 1), 0) % PADDED_ROWS // DECODE_STEPS
    low = jnp.zeros_like(request)
    high = jnp.zeros_like(request) + ends[0]
    for r in range(1, GROUP_REQUESTS):
        low = jnp.where(request == r, ends[r - 1], low)
        high = jnp.where(request == r, ends[r], high)
    kpos = key_positions(keys, sources, width)
    return (kpos >= low) & (kpos < high)


def stacked_heads(ref, rows, first, count):
    return jnp.concatenate(
        [ref[rows, span(first + i * HEAD_SIZE, HEAD_SIZE)] for i in range(count)], axis=0
    )


def slot_rows(plan, slot, facts, refs, rows):
    names = plan.candidates[slot]
    part = refs[names[0]][rows, :]
    for name in names[1:]:
        part = jnp.where(facts.choice[slot] == name, refs[name][rows, :], part)
    return part


def each_kv_head(width, step):
    if width <= 8:
        for h in range(KEY_VALUE_HEADS):
            step(h)
    else:
        lax.fori_loop(0, KEY_VALUE_HEADS, lambda h, c: (step(h), c)[1], 0)


def first_kernel(plan, pd_size, facts_ref, q_ref, *refs):
    width = plan.size
    block_refs, refs = refs[:pd_size], refs[pd_size:]
    count = len(refs) - 8
    kv_refs = refs[:count]
    acc_ref, top_ref, dec_acc_ref, dec_top_ref, queries_ref, keys_ref, values_ref, fresh_ref = refs[count:]
    tokens = q_ref.shape[0]
    half = tokens // 2
    facts = Facts(facts_ref, width)
    group, member, ends = facts.group, facts.member, facts.ends
    sources = [member] + facts.source[:-1]
    for out, rows in ((keys_ref, slice(0, tokens)), (values_ref, slice(tokens, 2 * tokens))):
        out[:tokens, :] = kv_refs[0][rows, :]
        for j in range(width - 2):
            out[(j + 1) * tokens : (j + 2) * tokens, :] = slot_rows(plan, j, facts, kv_refs, rows)

    row = iota((PADDED_ROWS, DECODE_ROWS), 0)
    column = iota((PADDED_ROWS, DECODE_ROWS), 1)
    total = None
    for k in range(pd_size):
        pick = column < 0
        for r in range(GROUP_REQUESTS):
            slot = facts.slots[r]
            back = group - slot // GROUP_REQUESTS
            back = jnp.where(back < 0, back + pd_size, back)
            first = jnp.where(back == k, slot % GROUP_REQUESTS * DECODE_STEPS, -DECODE_ROWS * 4)
            pick = pick | ((row // DECODE_STEPS == r) & (column == first + row - r * DECODE_STEPS))
        part = product(pick.astype(jnp.float32).astype(jnp.bfloat16), block_refs[k][...])
        total = part if total is None else total + part
    total = total.astype(jnp.bfloat16)
    queries_ref[...] = total[:, :Q_WIDTH]
    fresh_ref[...] = total[:, Q_WIDTH:]

    row = iota((STACKED, PADDED_ROWS), 0) % PADDED_ROWS
    column = iota((STACKED, PADDED_ROWS), 1)
    fresh_mask = (column // DECODE_STEPS == row // DECODE_STEPS) & (
        column % DECODE_STEPS <= row % DECODE_STEPS
    )
    mask = request_mask(ends, tokens, sources, width)
    spans = ((0, half), (half, tokens))
    biases = [causal_bias(s, half, keys, sources, ends, member, width) for s, keys in spans]
    together = max(1, min(HEADS_PER_KV, HEADS_PER_KV * 4 // width))

    def step(h):
        columns = span(h * HEAD_SIZE, HEAD_SIZE)
        first = h * Q_BLOCK
        queries = stacked_heads(queries_ref, slice(None), first, HEADS_PER_KV)
        fresh_scores = jnp.where(fresh_mask, scores_of(queries, fresh_ref[:, columns]), MASKED)
        scores = jnp.where(mask, scores_of(queries, keys_ref[:, columns]), MASKED)
        top = jnp.maximum(
            jnp.max(scores, axis=1, keepdims=True), jnp.max(fresh_scores, axis=1, keepdims=True)
        )
        weights = jnp.exp2((scores - top) * EXPONENT).astype(jnp.bfloat16)
        fresh_weights = jnp.exp2((fresh_scores - top) * EXPONENT).astype(jnp.bfloat16)
        fresh_values = fresh_ref[:, span(KV_WIDTH + h * HEAD_SIZE, HEAD_SIZE)]
        dec_acc_ref[h] = product(weights, with_ones(values_ref[:, columns])) + product(
            fresh_weights, with_ones(fresh_values)
        )
        dec_top_ref[h] = top
        for (start, keys), bias in zip(spans, biases):
            parts = [slice(b * tokens, b * tokens + keys) for b in range(width - 1)]
            k_all = jnp.concatenate([keys_ref[p, columns] for p in parts], axis=0)
            v_all = with_ones(jnp.concatenate([values_ref[p, columns] for p in parts], axis=0))
            for g in range(0, HEADS_PER_KV, together):
                queries = stacked_heads(
                    q_ref, slice(start, start + half), first + g * HEAD_SIZE, together
                )
                scores = scores_of(queries, k_all).reshape(together, half, bias.shape[1]) + bias[None]
                top = jnp.max(scores, axis=2, keepdims=True)
                weights = jnp.exp2((scores - top) * EXPONENT).astype(jnp.bfloat16)
                rows = slice(
                    start * HEADS_PER_KV + g * half, start * HEADS_PER_KV + (g + together) * half
                )
                acc_ref[h, rows, :] = product(weights.reshape(together * half, bias.shape[1]), v_all)
                top_ref[h, rows, :] = top.reshape(together * half, 1)

    each_kv_head(width, step)


def merge(acc, old_top, scores, values):
    top = jnp.maximum(old_top, jnp.max(scores, axis=1, keepdims=True))
    weights = jnp.exp2((scores - top) * EXPONENT).astype(jnp.bfloat16)
    acc = acc * jnp.exp2((old_top - top) * EXPONENT) + product(weights, with_ones(values))
    return (acc[:, :HEAD_SIZE] / acc[:, HEAD_SIZE:]).astype(jnp.bfloat16)


def decode_kernel(plan, pd_size, facts_ref, *refs):
    width = plan.size
    acc_ref, top_ref, queries_ref = refs[:3]
    kv_refs, out_refs = refs[3:-pd_size], refs[-pd_size:]
    tokens = kv_refs[-1].shape[0] // 2
    facts = Facts(facts_ref, width)
    group = facts.group
    refs = dict(zip(plan.candidates[-1], kv_refs))
    slot = width - 2
    keys = slot_rows(plan, slot, facts, refs, slice(0, tokens))
    values = slot_rows(plan, slot, facts, refs, slice(tokens, 2 * tokens))
    mask = request_mask(facts.ends, tokens, facts.source[-1:], width)
    row = iota((8, PADDED_ROWS), 0)
    column = iota((8, PADDED_ROWS), 1)
    picks = []
    for k in range(pd_size):
        target = group + k
        target = jnp.where(target >= pd_size, target - pd_size, target)
        pick = column < 0
        for r in range(GROUP_REQUESTS):
            mine = facts.slots[r] // GROUP_REQUESTS == target
            first = jnp.where(mine, r * DECODE_STEPS, -PADDED_ROWS * 4)
            pick = pick | ((row < DECODE_STEPS) & (column == first + row))
        picks.append(pick.astype(jnp.float32).astype(jnp.bfloat16))
    for h in range(KEY_VALUE_HEADS):
        columns = slice(h * HEAD_SIZE, (h + 1) * HEAD_SIZE)
        queries = stacked_heads(queries_ref, slice(None), h * Q_BLOCK, HEADS_PER_KV)
        scores = jnp.where(mask, scores_of(queries, keys[:, columns]), MASKED)
        out = merge(acc_ref[h], top_ref[h], scores, values[:, columns])
        out = jnp.concatenate(
            [out[g * PADDED_ROWS : (g + 1) * PADDED_ROWS] for g in range(HEADS_PER_KV)], axis=1
        )
        for k in range(pd_size):
            sent = product(picks[k], out).astype(jnp.bfloat16)
            out_refs[k][:, h * Q_BLOCK : (h + 1) * Q_BLOCK] = sent[:DECODE_STEPS]


def prefill_kernel(plan, facts_ref, q_ref, acc_ref, top_ref, *refs):
    width = plan.size
    kv_refs, (out_ref, done_ref, sem) = refs[:-3], refs[-3:]
    tokens = q_ref.shape[0]
    half = tokens // 2
    facts = Facts(facts_ref, width)
    refs = dict(zip(plan.candidates[-1], kv_refs))
    slot = width - 2
    keys = slot_rows(plan, slot, facts, refs, slice(0, tokens))
    values = slot_rows(plan, slot, facts, refs, slice(tokens, 2 * tokens))
    biases = [
        causal_bias(s, half, tokens, facts.source[-1:], facts.ends, facts.member, width)
        for s in (0, half)
    ]
    copies = []
    for h in range(KEY_VALUE_HEADS):
        columns = slice(h * HEAD_SIZE, (h + 1) * HEAD_SIZE)
        for start, bias in zip((0, half), biases):
            queries = stacked_heads(q_ref, slice(start, start + half), h * Q_BLOCK, HEADS_PER_KV)
            scores = scores_of(queries, keys[:, columns]).reshape(HEADS_PER_KV, half, tokens)
            scores = (scores + bias[None]).reshape(HEADS_PER_KV * half, tokens)
            rows = slice(start * HEADS_PER_KV, (start + half) * HEADS_PER_KV)
            out = merge(acc_ref[h, rows, :], top_ref[h, rows, :], scores, values[:, columns])
            for g in range(HEADS_PER_KV):
                done_ref[
                    start : start + half, h * Q_BLOCK + g * HEAD_SIZE : h * Q_BLOCK + (g + 1) * HEAD_SIZE
                ] = out[g * half : (g + 1) * half]
        part = pl.ds(h * Q_BLOCK, Q_BLOCK)
        copy = pltpu.make_async_copy(done_ref.at[:, part], out_ref.at[:, part], sem.at[h])
        copy.start()
        copies.append(copy)
    for copy in copies:
        copy.wait()


def load(array):
    def kernel(in_ref, out_ref, sem):
        copy = pltpu.make_async_copy(in_ref, out_ref, sem)
        copy.start()
        copy.wait()

    return pl.pallas_call(
        kernel,
        in_specs=[pl.BlockSpec(memory_space=pl.ANY)],
        out_specs=VMEM,
        out_shape=jax.ShapeDtypeStruct(array.shape, array.dtype),
        scratch_shapes=[pltpu.SemaphoreType.DMA],
        cost_estimate=pl.CostEstimate(flops=0, bytes_accessed=4 * array.size, transcendentals=0),
        name="load_queries",
    )(array)


def cost(rows, keys, exps):
    return pl.CostEstimate(
        flops=4 * rows * keys * Q_WIDTH, bytes_accessed=4 * rows * Q_WIDTH, transcendentals=exps
    )


def call_first(plan, facts, query, blocks, arrays):
    tokens, width = query.shape[0], plan.size
    every = (width - 1) * tokens
    rows = HEADS_PER_KV * tokens
    f32 = jnp.float32
    shapes = [
        jax.ShapeDtypeStruct((KEY_VALUE_HEADS, rows, 2 * HEAD_SIZE), f32),
        jax.ShapeDtypeStruct((KEY_VALUE_HEADS, rows, 1), f32),
        jax.ShapeDtypeStruct((KEY_VALUE_HEADS, STACKED, 2 * HEAD_SIZE), f32),
        jax.ShapeDtypeStruct((KEY_VALUE_HEADS, STACKED, 1), f32),
        jax.ShapeDtypeStruct((PADDED_ROWS, Q_WIDTH), jnp.bfloat16),
    ]
    needed = arrays[: 1 + max(max(c) for c in plan.candidates[:-1])]
    return pl.pallas_call(
        lambda *refs: first_kernel(plan, len(blocks), *refs),
        in_specs=[SMEM] + [VMEM] * (1 + len(blocks) + len(needed)),
        out_specs=[VMEM] * len(shapes),
        out_shape=shapes,
        scratch_shapes=[
            pltpu.VMEM((every, KV_WIDTH), jnp.bfloat16),
            pltpu.VMEM((every, KV_WIDTH), jnp.bfloat16),
            pltpu.VMEM((PADDED_ROWS, 2 * KV_WIDTH), jnp.bfloat16),
        ],
        compiler_params=pltpu.CompilerParams(vmem_limit_bytes=(28 + width) * MIB),
        cost_estimate=cost(tokens, every, tokens * every * QUERY_HEADS),
        name="first_shards",
    )(facts, query, *blocks, *needed)


def call_decode(plan, pd_size, facts, state, arrays):
    last = [arrays[b] for b in plan.candidates[-1]]
    tokens = last[0].shape[0] // 2
    return pl.pallas_call(
        lambda *refs: decode_kernel(plan, pd_size, *refs),
        in_specs=[SMEM] + [VMEM] * (3 + len(last)),
        out_specs=[VMEM] * pd_size,
        out_shape=[jax.ShapeDtypeStruct((DECODE_STEPS, Q_WIDTH), jnp.bfloat16)] * pd_size,
        compiler_params=pltpu.CompilerParams(vmem_limit_bytes=32 * MIB),
        cost_estimate=cost(PADDED_ROWS, tokens, PADDED_ROWS * tokens * QUERY_HEADS),
        name="last_shard_decode",
    )(facts, *state[2:], *last)


def call_prefill(plan, facts, query, state, arrays):
    last = [arrays[b] for b in plan.candidates[-1]]
    tokens = query.shape[0]
    return pl.pallas_call(
        lambda *refs: prefill_kernel(plan, *refs),
        in_specs=[SMEM] + [VMEM] * (3 + len(last)),
        out_specs=pl.BlockSpec(memory_space=pl.ANY),
        out_shape=jax.ShapeDtypeStruct((tokens, Q_WIDTH), jnp.bfloat16),
        scratch_shapes=[
            pltpu.VMEM((tokens, Q_WIDTH), jnp.bfloat16),
            pltpu.SemaphoreType.DMA((KEY_VALUE_HEADS,)),
        ],
        compiler_params=pltpu.CompilerParams(vmem_limit_bytes=32 * MIB),
        cost_estimate=cost(tokens, tokens, tokens * tokens * QUERY_HEADS),
        name="last_shard_prefill",
    )(facts, query, *state[:2], *last)


def ring(size, step):
    return [(i, (i + step) % size) for i in range(size)]


def body(
    prompt_query,
    prompt_key,
    prompt_value,
    prompt_lengths,
    decode_slot,
    decoded_query,
    decoded_key,
    decoded_value,
):
    plan = Exchange(lax.axis_size("tp"))
    pd_size = lax.axis_size("pd")
    my_group = lax.axis_index("pd")
    kv = jnp.concatenate([prompt_key, prompt_value], axis=0)
    def gather(buffer):
        buffer, rows, query, facts = lax.optimization_barrier(
            (buffer, own, load(prompt_query), facts_row(plan, prompt_lengths, decode_slot))
        )
        blocks = [rows] + [lax.ppermute(rows, "pd", ring(pd_size, k)) for k in range(1, pd_size)]
        return buffer, (facts, query, blocks)

    kv, decoded_query = lax.optimization_barrier((kv, decoded_query))
    own = jnp.concatenate([decoded_query, decoded_key, decoded_value], axis=2).reshape(
        DECODE_ROWS, Q_WIDTH + 2 * KV_WIDTH
    )
    arrays, (facts, query, blocks) = plan.run(kv, "tp", gather)

    state = call_first(plan, facts, query, blocks, arrays)
    outgoing = call_decode(plan, pd_size, facts, state, arrays)
    arrived = [outgoing[0]]
    for k in range(1, pd_size):
        arrived.append(lax.ppermute(outgoing[k], "pd", ring(pd_size, k)))
    pre_out = call_prefill(plan, facts, query, state, arrays)

    numbers = jnp.arange(decode_slot.shape[0], dtype=jnp.int32)
    wanted = my_group * GROUP_REQUESTS + jnp.arange(GROUP_REQUESTS, dtype=jnp.int32)
    owner = jnp.sum(
        jnp.where(decode_slot[None, :] == wanted[:, None], numbers[None, :] // GROUP_REQUESTS, 0), axis=1
    )
    from_block = (my_group - owner) % pd_size
    dec_out = jnp.zeros((GROUP_REQUESTS, DECODE_STEPS, Q_WIDTH), jnp.bfloat16)
    for k in range(pd_size):
        dec_out = jnp.where((from_block == k)[:, None, None], arrived[k][None], dec_out)
    return (pre_out, dec_out)


def solution(mesh):
    placed = (
        P(("rep", "pd", "tp"), None),
        P(("rep", "pd", "tp"), None),
        P(("rep", "pd", "tp"), None),
        P("rep", None),
        P("rep"),
        P(("rep", "pd"), None, None),
        P(("rep", "pd"), None, None),
        P(("rep", "pd"), None, None),
    )
    return jax.shard_map(
        body,
        mesh=mesh,
        in_specs=placed,
        out_specs=(P(("rep", "pd", "tp"), None), P(("rep", "pd"), None, None)),
        check_vma=False,
    )
```

```python
import math

import jax
import jax.numpy as jnp
import numpy as np
from jax import lax
from jax.experimental import pallas as pl
from jax.experimental.pallas import tpu as pltpu
from jax.sharding import PartitionSpec as P

QUERY_HEADS = 32
KEY_VALUE_HEADS = 4
HEAD_SIZE = 128
PAGE = 16
GROUP_REQUESTS = 4
DECODE_STEPS = 2
HEADS_PER_KV = QUERY_HEADS // KEY_VALUE_HEADS
KV_WIDTH = KEY_VALUE_HEADS * HEAD_SIZE
Q_WIDTH = QUERY_HEADS * HEAD_SIZE
Q_BLOCK = HEADS_PER_KV * HEAD_SIZE
DECODE_ROWS = GROUP_REQUESTS * DECODE_STEPS
PADDED_ROWS = 16
STACKED = HEADS_PER_KV * PADDED_ROWS
MIB = 1024 * 1024

MASKED = -1e30
LIMIT = 60.0
EXPONENT = math.log2(math.e) / math.sqrt(HEAD_SIZE)

VMEM = pl.BlockSpec(memory_space=pltpu.VMEM)
SMEM = pl.BlockSpec(memory_space=pltpu.SMEM)
ANY = pl.BlockSpec(memory_space=pl.ANY)


class Ring:
    def __init__(self, size):
        self.size = size
        order = [0] + list(range(1, size, 2)) + [i for i in range(size - 1, 0, -1) if i % 2 == 0]
        self.pairs = [(order[i], order[(i + 1) % size]) for i in range(size)]
        place = {m: i for i, m in enumerate(order)}
        self.source = np.array(
            [[order[(place[m] - s) % size] for s in range(size)] for m in range(size)], np.int32
        )

    def step(self, array):
        return lax.ppermute(array, "tp", self.pairs)


def scores_of(queries, keys):
    return lax.dot_general(
        queries, keys, (((1,), (1,)), ((), ())), preferred_element_type=jnp.float32
    )


def product(left, right):
    return jnp.dot(left, right, preferred_element_type=jnp.float32)


def iota(shape, axis):
    return lax.broadcasted_iota(jnp.int32, shape, axis)


def span(start, size):
    if isinstance(start, int):
        return slice(start, start + size)
    return pl.ds(pl.multiple_of(start, size), size)


def with_ones(values):
    return jnp.concatenate([values, jnp.ones_like(values)], axis=1)


def page_position(offset, member, width):
    return (offset // PAGE * width + member) * PAGE + offset % PAGE


def key_positions(rows, sources, width):
    column = iota((1, len(sources) * rows), 1)
    part = column // rows
    source = jnp.zeros_like(column) + sources[0]
    for b in range(1, len(sources)):
        source = jnp.where(part == b, sources[b], source)
    return page_position(column - part * rows, source, width)


class Facts:
    def __init__(self, ref, width):
        self.width = width
        self.group, self.member = ref[0], ref[1]
        self.slots = [ref[2 + r] for r in range(GROUP_REQUESTS)]
        first = 2 + GROUP_REQUESTS
        self.ends = []
        total = jnp.int32(0)
        for r in range(GROUP_REQUESTS):
            total = total + ref[first + r] * PAGE
            self.ends.append(total)
        first += GROUP_REQUESTS
        self.source = [ref[first + s] for s in range(width)]


def facts_row(plan, lengths, slots):
    group, member = lax.axis_index("pd"), lax.axis_index("tp")
    return jnp.concatenate(
        [
            jnp.stack([group, member]).astype(jnp.int32),
            lax.dynamic_slice_in_dim(slots, group * GROUP_REQUESTS, GROUP_REQUESTS, 0),
            lax.dynamic_index_in_dim(lengths, group, 0, keepdims=False),
            lax.dynamic_index_in_dim(jnp.asarray(plan.source), member, 0, keepdims=False),
        ]
    )


def causal_bias(start, rows, keys, sources, ends, member, width):
    qpos = page_position(start + iota((rows, 1), 0), member, width)
    low = jnp.zeros_like(qpos)
    for end in ends:
        low = jnp.where(qpos >= end, end, low)
    kpos = key_positions(keys, sources, width)
    return jnp.where((kpos >= low) & (kpos <= qpos), 0.0, MASKED)


def request_mask(ends, keys, sources, width):
    request = iota((STACKED, 1), 0) % PADDED_ROWS // DECODE_STEPS
    low = jnp.zeros_like(request)
    high = jnp.zeros_like(request) + ends[0]
    for r in range(1, GROUP_REQUESTS):
        low = jnp.where(request == r, ends[r - 1], low)
        high = jnp.where(request == r, ends[r], high)
    kpos = key_positions(keys, sources, width)
    return (kpos >= low) & (kpos < high)


def stacked_heads(ref, rows, first, count):
    return jnp.concatenate(
        [ref[rows, span(first + i * HEAD_SIZE, HEAD_SIZE)] for i in range(count)], axis=0
    )


def each_kv_head(width, step):
    if width <= 8:
        for h in range(KEY_VALUE_HEADS):
            step(h)
    else:
        lax.fori_loop(0, KEY_VALUE_HEADS, lambda h, c: (step(h), c)[1], 0)


def first_kernel(plan, pd_size, facts_ref, q_hbm_ref, *refs):
    width = plan.size
    kv_refs, refs = refs[: width - 1], refs[width - 1 :]
    block_refs, refs = refs[:pd_size], refs[pd_size:]
    acc_ref, top_ref, dec_acc_ref, dec_top_ref, queries_ref, q_ref, fresh_ref, sem = refs
    copies = []
    for h in range(KEY_VALUE_HEADS):
        part = pl.ds(h * Q_BLOCK, Q_BLOCK)
        copies.append(pltpu.make_async_copy(q_hbm_ref.at[:, part], q_ref.at[:, part], sem.at[h]))
    for copy in copies:
        copy.start()
    tokens = q_ref.shape[0]
    half = tokens // 2
    facts = Facts(facts_ref, width)
    group, member, ends = facts.group, facts.member, facts.ends
    sources = facts.source[:-1]

    row = iota((PADDED_ROWS, DECODE_ROWS), 0)
    column = iota((PADDED_ROWS, DECODE_ROWS), 1)
    total = None
    for k in range(pd_size):
        pick = column < 0
        for r in range(GROUP_REQUESTS):
            slot = facts.slots[r]
            back = group - slot // GROUP_REQUESTS
            back = jnp.where(back < 0, back + pd_size, back)
            first = jnp.where(back == k, slot % GROUP_REQUESTS * DECODE_STEPS, -DECODE_ROWS * 4)
            pick = pick | ((row // DECODE_STEPS == r) & (column == first + row - r * DECODE_STEPS))
        part = product(pick.astype(jnp.float32).astype(jnp.bfloat16), block_refs[k][...])
        total = part if total is None else total + part
    total = total.astype(jnp.bfloat16)
    queries_ref[...] = total[:, :Q_WIDTH]
    fresh_ref[...] = total[:, Q_WIDTH:]

    row = iota((STACKED, PADDED_ROWS), 0) % PADDED_ROWS
    column = iota((STACKED, PADDED_ROWS), 1)
    fresh_mask = (column // DECODE_STEPS == row // DECODE_STEPS) & (
        column % DECODE_STEPS <= row % DECODE_STEPS
    )
    mask = request_mask(ends, tokens, sources, width)
    spans = ((0, half), (half, tokens))
    biases = [causal_bias(s, half, keys, sources, ends, member, width) for s, keys in spans]
    together = max(1, min(HEADS_PER_KV, HEADS_PER_KV * 4 // width))

    def step(h):
        columns = span(h * HEAD_SIZE, HEAD_SIZE)
        first = h * Q_BLOCK
        queries = stacked_heads(queries_ref, slice(None), first, HEADS_PER_KV)
        fresh_scores = jnp.where(fresh_mask, scores_of(queries, fresh_ref[:, columns]), MASKED)
        k_all = jnp.concatenate([ref[:tokens, columns] for ref in kv_refs], axis=0)
        v_all = with_ones(jnp.concatenate([ref[tokens:, columns] for ref in kv_refs], axis=0))
        scores = jnp.where(mask, scores_of(queries, k_all), MASKED)
        top = jnp.maximum(
            jnp.max(scores, axis=1, keepdims=True), jnp.max(fresh_scores, axis=1, keepdims=True)
        )
        weights = jnp.exp2((scores - top) * EXPONENT).astype(jnp.bfloat16)
        fresh_weights = jnp.exp2((fresh_scores - top) * EXPONENT).astype(jnp.bfloat16)
        fresh_values = fresh_ref[:, span(KV_WIDTH + h * HEAD_SIZE, HEAD_SIZE)]
        dec_acc_ref[h] = product(weights, v_all) + product(fresh_weights, with_ones(fresh_values))
        dec_top_ref[h] = jnp.broadcast_to(top, (STACKED, HEAD_SIZE))
        for (start, keys), bias in zip(spans, biases):
            if keys < tokens:
                k_part = jnp.concatenate([ref[:keys, columns] for ref in kv_refs], axis=0)
                v_part = with_ones(jnp.concatenate([ref[tokens : tokens + keys, columns] for ref in kv_refs], axis=0))
            else:
                k_part, v_part = k_all, v_all
            for g in range(0, HEADS_PER_KV, together):
                queries = stacked_heads(
                    q_ref, slice(start, start + half), first + g * HEAD_SIZE, together
                )
                scores = scores_of(queries, k_part).reshape(together, half, bias.shape[1]) + bias[None]
                top = jnp.max(scores, axis=2, keepdims=True)
                weights = jnp.exp2((scores - top) * EXPONENT).astype(jnp.bfloat16)
                rows = slice(
                    start * HEADS_PER_KV + g * half, start * HEADS_PER_KV + (g + together) * half
                )
                acc_ref[h, rows, :] = product(weights.reshape(together * half, bias.shape[1]), v_part)
                top_ref[h, rows, :] = jnp.broadcast_to(top, (together, half, HEAD_SIZE)).reshape(
                    together * half, HEAD_SIZE
                )

    for copy in copies:
        copy.wait()
    each_kv_head(width, step)


def divided(acc):
    return (acc[:, :HEAD_SIZE] / acc[:, HEAD_SIZE:]).astype(jnp.bfloat16)


def merge(acc, old_top, scores, values):
    top = jnp.maximum(old_top, jnp.max(scores, axis=1, keepdims=True))
    weights = jnp.exp2((scores - top) * EXPONENT).astype(jnp.bfloat16)
    factor = jnp.exp2((old_top - top) * EXPONENT)
    return acc * jnp.concatenate([factor, factor], axis=1) + product(weights, with_ones(values))


def decode_kernel(plan, pd_size, facts_ref, acc_ref, top_ref, queries_ref, kv_ref, out_ref):
    width = plan.size
    tokens = kv_ref.shape[0] // 2
    facts = Facts(facts_ref, width)
    mask = request_mask(facts.ends, tokens, facts.source[-1:], width)
    row = iota((PADDED_ROWS, PADDED_ROWS), 0)
    column = iota((PADDED_ROWS, PADDED_ROWS), 1)
    pick = column < 0
    for r in range(GROUP_REQUESTS):
        ahead = facts.slots[r] // GROUP_REQUESTS - facts.group
        ahead = jnp.where(ahead < 0, ahead + pd_size, ahead)
        pick = pick | (
            (column // DECODE_STEPS == r) & (row == ahead * DECODE_STEPS + column - r * DECODE_STEPS)
        )
    pick = pick.astype(jnp.float32).astype(jnp.bfloat16)
    heads = range(KEY_VALUE_HEADS)
    columns = [slice(h * HEAD_SIZE, (h + 1) * HEAD_SIZE) for h in heads]
    scores = [
        scores_of(stacked_heads(queries_ref, slice(None), h * Q_BLOCK, HEADS_PER_KV), kv_ref[:tokens, columns[h]])
        for h in heads
    ]
    scores = [jnp.where(mask, s, MASKED) for s in scores]
    out = [divided(merge(acc_ref[h], top_ref[h], scores[h], kv_ref[tokens:, columns[h]])) for h in heads]
    out = jnp.concatenate(
        [o[g * PADDED_ROWS : (g + 1) * PADDED_ROWS] for o in out for g in range(HEADS_PER_KV)], axis=1
    )
    out_ref[...] = product(pick, out).astype(jnp.bfloat16)


def prefill_kernel(plan, facts_ref, q_ref, acc_ref, top_ref, kv_ref, out_ref, done_ref, sem):
    width = plan.size
    tokens = q_ref.shape[0]
    half = tokens // 2
    facts = Facts(facts_ref, width)
    biases = [
        causal_bias(s, half, tokens, facts.source[-1:], facts.ends, facts.member, width)
        for s in (0, half)
    ]

    def finish(rescale):
        copies = []
        worst = jnp.full((half, tokens), MASKED, jnp.float32)
        for h in range(KEY_VALUE_HEADS):
            columns = slice(h * HEAD_SIZE, (h + 1) * HEAD_SIZE)
            keys, values = kv_ref[:tokens, columns], kv_ref[tokens:, columns]
            for start, bias in zip((0, half), biases):
                queries = stacked_heads(q_ref, slice(start, start + half), h * Q_BLOCK, HEADS_PER_KV)
                scores = scores_of(queries, keys).reshape(HEADS_PER_KV, half, tokens) + bias[None]
                rows = slice(start * HEADS_PER_KV, (start + half) * HEADS_PER_KV)
                if rescale:
                    scores = scores.reshape(HEADS_PER_KV * half, tokens)
                    acc = merge(acc_ref[h, rows, :], top_ref[h, rows, :], scores, values)
                else:
                    above = scores - top_ref[h, rows, :].reshape(HEADS_PER_KV, half, tokens)
                    worst = jnp.maximum(worst, jnp.max(above, axis=0))
                    weights = jnp.exp2(above * EXPONENT).astype(jnp.bfloat16)
                    weights = weights.reshape(HEADS_PER_KV * half, tokens)
                    acc = acc_ref[h, rows, :] + product(weights, with_ones(values))
                out = divided(acc)
                for g in range(HEADS_PER_KV):
                    done_ref[
                        start : start + half,
                        h * Q_BLOCK + g * HEAD_SIZE : h * Q_BLOCK + (g + 1) * HEAD_SIZE,
                    ] = out[g * half : (g + 1) * half]
            part = pl.ds(h * Q_BLOCK, Q_BLOCK)
            copy = pltpu.make_async_copy(done_ref.at[:, part], out_ref.at[:, part], sem.at[h])
            copy.start()
            copies.append(copy)
        for copy in copies:
            copy.wait()
        return jnp.max(worst)

    @pl.when(finish(False) * EXPONENT > LIMIT)
    def _():
        finish(True)


def cost(rows, keys, exps):
    return pl.CostEstimate(
        flops=32 * rows * keys * Q_WIDTH, bytes_accessed=4 * rows * Q_WIDTH, transcendentals=exps
    )


def call_first(plan, facts, query, blocks, pieces):
    tokens, width = query.shape[0], plan.size
    rows = HEADS_PER_KV * tokens
    f32, bf16 = jnp.float32, jnp.bfloat16
    shapes = [
        jax.ShapeDtypeStruct((KEY_VALUE_HEADS, rows, 2 * HEAD_SIZE), f32),
        jax.ShapeDtypeStruct((KEY_VALUE_HEADS, rows, HEAD_SIZE), f32),
        jax.ShapeDtypeStruct((KEY_VALUE_HEADS, STACKED, 2 * HEAD_SIZE), f32),
        jax.ShapeDtypeStruct((KEY_VALUE_HEADS, STACKED, HEAD_SIZE), f32),
        jax.ShapeDtypeStruct((PADDED_ROWS, Q_WIDTH), bf16),
    ]
    every = (width - 1) * tokens
    return pl.pallas_call(
        lambda *refs: first_kernel(plan, len(blocks), *refs),
        in_specs=[SMEM, ANY] + [VMEM] * (len(blocks) + width - 1),
        out_specs=[VMEM] * len(shapes),
        out_shape=shapes,
        scratch_shapes=[
            pltpu.VMEM((tokens, Q_WIDTH), bf16),
            pltpu.VMEM((PADDED_ROWS, 2 * KV_WIDTH), bf16),
            pltpu.SemaphoreType.DMA((KEY_VALUE_HEADS,)),
        ],
        compiler_params=pltpu.CompilerParams(vmem_limit_bytes=(28 + width) * MIB),
        cost_estimate=cost(tokens, every, tokens * every * QUERY_HEADS),
        name="first_shards",
    )(facts, query, *pieces, *blocks)


def call_decode(plan, pd_size, facts, state, piece):
    tokens = piece.shape[0] // 2
    return pl.pallas_call(
        lambda *refs: decode_kernel(plan, pd_size, *refs),
        in_specs=[SMEM] + [VMEM] * 4,
        out_specs=VMEM,
        out_shape=jax.ShapeDtypeStruct((PADDED_ROWS, Q_WIDTH), jnp.bfloat16),
        compiler_params=pltpu.CompilerParams(vmem_limit_bytes=32 * MIB),
        cost_estimate=cost(PADDED_ROWS, tokens, PADDED_ROWS * tokens * QUERY_HEADS),
        name="last_shard_decode",
    )(facts, *state[2:], piece)


def call_prefill(plan, facts, query, state, piece):
    tokens = query.shape[0]
    return pl.pallas_call(
        lambda *refs: prefill_kernel(plan, *refs),
        in_specs=[SMEM] + [VMEM] * 4,
        out_specs=ANY,
        out_shape=jax.ShapeDtypeStruct((tokens, Q_WIDTH), jnp.bfloat16),
        scratch_shapes=[
            pltpu.VMEM((tokens, Q_WIDTH), jnp.bfloat16),
            pltpu.SemaphoreType.DMA((KEY_VALUE_HEADS,)),
        ],
        compiler_params=pltpu.CompilerParams(vmem_limit_bytes=32 * MIB),
        cost_estimate=cost(tokens, tokens, tokens * tokens * QUERY_HEADS),
        name="last_shard_prefill",
    )(facts, query, *state[:2], piece)


def ring(size, step):
    return [(i, (i + step) % size) for i in range(size)]


def body(
    prompt_query,
    prompt_key,
    prompt_value,
    prompt_lengths,
    decode_slot,
    decoded_query,
    decoded_key,
    decoded_value,
):
    plan = Ring(lax.axis_size("tp"))
    pd_size = lax.axis_size("pd")
    my_group = lax.axis_index("pd")
    facts = facts_row(plan, prompt_lengths, decode_slot)
    pieces, blocks = [jnp.concatenate([prompt_key, prompt_value], axis=0)], None
    pieces[0], decoded_query = lax.optimization_barrier((pieces[0], decoded_query))
    own = jnp.concatenate([decoded_query, decoded_key, decoded_value], axis=2).reshape(
        DECODE_ROWS, Q_WIDTH + 2 * KV_WIDTH
    )
    for s in range(1, plan.size):
        if s == 2:
            pieces[1], own, facts = lax.optimization_barrier((pieces[1], own, facts))
        if s == plan.size - 1:
            pieces, blocks = lax.optimization_barrier((pieces, blocks))
        pieces.append(plan.step(pieces[-1]))
        if s == 2:
            blocks = [own] + [lax.ppermute(own, "pd", ring(pd_size, k)) for k in range(1, pd_size)]

    state = call_first(plan, facts, prompt_query, blocks, pieces[:-1])
    outgoing = call_decode(plan, pd_size, facts, state, pieces[-1])
    arrived = [outgoing[:DECODE_STEPS]]
    for k in range(1, pd_size):
        part = outgoing[k * DECODE_STEPS : (k + 1) * DECODE_STEPS]
        arrived.append(lax.ppermute(part, "pd", ring(pd_size, k)))
    pre_out = call_prefill(plan, facts, prompt_query, state, pieces[-1])

    numbers = jnp.arange(decode_slot.shape[0], dtype=jnp.int32)
    wanted = my_group * GROUP_REQUESTS + jnp.arange(GROUP_REQUESTS, dtype=jnp.int32)
    owner = jnp.sum(
        jnp.where(decode_slot[None, :] == wanted[:, None], numbers[None, :] // GROUP_REQUESTS, 0), axis=1
    )
    from_block = (my_group - owner) % pd_size
    dec_out = jnp.zeros((GROUP_REQUESTS, DECODE_STEPS, Q_WIDTH), jnp.bfloat16)
    for k in range(pd_size):
        dec_out = jnp.where((from_block == k)[:, None, None], arrived[k][None], dec_out)
    return (pre_out, dec_out)


def solution(mesh):
    placed = (
        P(("rep", "pd", "tp"), None),
        P(("rep", "pd", "tp"), None),
        P(("rep", "pd", "tp"), None),
        P("rep", None),
        P("rep"),
        P(("rep", "pd"), None, None),
        P(("rep", "pd"), None, None),
        P(("rep", "pd"), None, None),
    )
    return jax.shard_map(
        body,
        mesh=mesh,
        in_specs=placed,
        out_specs=(P(("rep", "pd", "tp"), None), P(("rep", "pd"), None, None)),
        check_vma=False,
    )
```

```python
import math

import jax
import jax.numpy as jnp
import numpy as np
from jax import lax
from jax.experimental import pallas as pl
from jax.experimental.pallas import tpu as pltpu
from jax.sharding import PartitionSpec as P

QUERY_HEADS = 32
KEY_VALUE_HEADS = 4
HEAD_SIZE = 128
PAGE = 16
GROUP_REQUESTS = 4
DECODE_STEPS = 2
HEADS_PER_KV = QUERY_HEADS // KEY_VALUE_HEADS
KV_WIDTH = KEY_VALUE_HEADS * HEAD_SIZE
Q_WIDTH = QUERY_HEADS * HEAD_SIZE
Q_BLOCK = HEADS_PER_KV * HEAD_SIZE
DECODE_ROWS = GROUP_REQUESTS * DECODE_STEPS
PADDED_ROWS = 16
STACKED = HEADS_PER_KV * PADDED_ROWS
MIB = 1024 * 1024

MASKED = -1e30
LIMIT = 60.0
EXPONENT = math.log2(math.e) / math.sqrt(HEAD_SIZE)

VMEM = pl.BlockSpec(memory_space=pltpu.VMEM)
SMEM = pl.BlockSpec(memory_space=pltpu.SMEM)
ANY = pl.BlockSpec(memory_space=pl.ANY)


class Ring:
    def __init__(self, size):
        self.size = size
        order = [0] + list(range(1, size, 2)) + [i for i in range(size - 1, 0, -1) if i % 2 == 0]
        self.pairs = [(order[i], order[(i + 1) % size]) for i in range(size)]
        place = {m: i for i, m in enumerate(order)}
        self.source = np.array(
            [[order[(place[m] - s) % size] for s in range(size)] for m in range(size)], np.int32
        )

    def steps(self, arrays):
        groups = lax.axis_size("pd")
        return [
            lax.ppermute(
                array,
                ("pd", "tp"),
                [
                    (g * self.size + a, g * self.size + b)
                    for g in range(parity, groups, 2)
                    for a, b in self.pairs
                ],
            )
            for parity, array in enumerate(arrays)
        ]


def mine(group, refs, rows, columns):
    even, odd = refs
    return jnp.where(group % 2 == 0, even[rows, columns], odd[rows, columns])


def scores_of(queries, keys):
    return lax.dot_general(
        queries, keys, (((1,), (1,)), ((), ())), preferred_element_type=jnp.float32
    )


def product(left, right):
    return jnp.dot(left, right, preferred_element_type=jnp.float32)


def iota(shape, axis):
    return lax.broadcasted_iota(jnp.int32, shape, axis)


def span(start, size):
    if isinstance(start, int):
        return slice(start, start + size)
    return pl.ds(pl.multiple_of(start, size), size)


def with_ones(values):
    return jnp.concatenate([values, jnp.ones_like(values)], axis=1)


def page_position(offset, member, width):
    return (offset // PAGE * width + member) * PAGE + offset % PAGE


def key_positions(rows, sources, width):
    column = iota((1, len(sources) * rows), 1)
    part = column // rows
    source = jnp.zeros_like(column) + sources[0]
    for b in range(1, len(sources)):
        source = jnp.where(part == b, sources[b], source)
    return page_position(column - part * rows, source, width)


class Facts:
    def __init__(self, ref, width):
        self.width = width
        self.group, self.member = ref[0], ref[1]
        self.slots = [ref[2 + r] for r in range(GROUP_REQUESTS)]
        first = 2 + GROUP_REQUESTS
        self.ends = []
        total = jnp.int32(0)
        for r in range(GROUP_REQUESTS):
            total = total + ref[first + r] * PAGE
            self.ends.append(total)
        first += GROUP_REQUESTS
        self.source = [ref[first + s] for s in range(width)]


def facts_row(plan, lengths, slots):
    group, member = lax.axis_index("pd"), lax.axis_index("tp")
    return jnp.concatenate(
        [
            jnp.stack([group, member]).astype(jnp.int32),
            lax.dynamic_slice_in_dim(slots, group * GROUP_REQUESTS, GROUP_REQUESTS, 0),
            lax.dynamic_index_in_dim(lengths, group, 0, keepdims=False),
            lax.dynamic_index_in_dim(jnp.asarray(plan.source), member, 0, keepdims=False),
        ]
    )


def causal_bias(start, rows, keys, sources, ends, member, width):
    qpos = page_position(start + iota((rows, 1), 0), member, width)
    low = jnp.zeros_like(qpos)
    for end in ends:
        low = jnp.where(qpos >= end, end, low)
    kpos = key_positions(keys, sources, width)
    return jnp.where((kpos >= low) & (kpos <= qpos), 0.0, MASKED)


def request_mask(ends, keys, sources, width):
    request = iota((STACKED, 1), 0) % PADDED_ROWS // DECODE_STEPS
    low = jnp.zeros_like(request)
    high = jnp.zeros_like(request) + ends[0]
    for r in range(1, GROUP_REQUESTS):
        low = jnp.where(request == r, ends[r - 1], low)
        high = jnp.where(request == r, ends[r], high)
    kpos = key_positions(keys, sources, width)
    return (kpos >= low) & (kpos < high)


def stacked_heads(ref, rows, first, count):
    return jnp.concatenate(
        [ref[rows, span(first + i * HEAD_SIZE, HEAD_SIZE)] for i in range(count)], axis=0
    )


def each_kv_head(width, step):
    if width <= 8:
        for h in range(KEY_VALUE_HEADS):
            step(h)
    else:
        lax.fori_loop(0, KEY_VALUE_HEADS, lambda h, c: (step(h), c)[1], 0)


def first_kernel(plan, pd_size, facts_ref, q_hbm_ref, *refs):
    width = plan.size
    own_ref, kv_refs, refs = refs[0], refs[1 : 2 * width - 3], refs[2 * width - 3 :]
    block_refs, refs = refs[:pd_size], refs[pd_size:]
    acc_ref, top_ref, dec_acc_ref, dec_top_ref, queries_ref, q_ref, fresh_ref, sem = refs
    got_refs = [(kv_refs[2 * i], kv_refs[2 * i + 1]) for i in range(width - 2)]
    copies = []
    for h in range(KEY_VALUE_HEADS):
        part = pl.ds(h * Q_BLOCK, Q_BLOCK)
        copies.append(pltpu.make_async_copy(q_hbm_ref.at[:, part], q_ref.at[:, part], sem.at[h]))
    for copy in copies:
        copy.start()
    tokens = q_ref.shape[0]
    half = tokens // 2
    facts = Facts(facts_ref, width)
    group, member, ends = facts.group, facts.member, facts.ends
    sources = facts.source[:-1]

    row = iota((PADDED_ROWS, DECODE_ROWS), 0)
    column = iota((PADDED_ROWS, DECODE_ROWS), 1)
    total = None
    for k in range(pd_size):
        pick = column < 0
        for r in range(GROUP_REQUESTS):
            slot = facts.slots[r]
            back = group - slot // GROUP_REQUESTS
            back = jnp.where(back < 0, back + pd_size, back)
            first = jnp.where(back == k, slot % GROUP_REQUESTS * DECODE_STEPS, -DECODE_ROWS * 4)
            pick = pick | ((row // DECODE_STEPS == r) & (column == first + row - r * DECODE_STEPS))
        part = product(pick.astype(jnp.float32).astype(jnp.bfloat16), block_refs[k][...])
        total = part if total is None else total + part
    total = total.astype(jnp.bfloat16)
    queries_ref[...] = total[:, :Q_WIDTH]
    fresh_ref[...] = total[:, Q_WIDTH:]

    row = iota((STACKED, PADDED_ROWS), 0) % PADDED_ROWS
    column = iota((STACKED, PADDED_ROWS), 1)
    fresh_mask = (column // DECODE_STEPS == row // DECODE_STEPS) & (
        column % DECODE_STEPS <= row % DECODE_STEPS
    )
    mask = request_mask(ends, tokens, sources, width)
    spans = ((0, half), (half, tokens))
    biases = [causal_bias(s, half, keys, sources, ends, member, width) for s, keys in spans]
    together = max(1, min(HEADS_PER_KV, HEADS_PER_KV * 4 // width))

    def step(h):
        columns = span(h * HEAD_SIZE, HEAD_SIZE)
        first = h * Q_BLOCK
        queries = stacked_heads(queries_ref, slice(None), first, HEADS_PER_KV)
        fresh_scores = jnp.where(fresh_mask, scores_of(queries, fresh_ref[:, columns]), MASKED)
        k_parts, v_parts = (
            [own_ref[rows, columns]] + [mine(group, refs, rows, columns) for refs in got_refs]
            for rows in (slice(0, tokens), slice(tokens, 2 * tokens))
        )
        k_all = jnp.concatenate(k_parts, axis=0)
        v_all = with_ones(jnp.concatenate(v_parts, axis=0))
        scores = jnp.where(mask, scores_of(queries, k_all), MASKED)
        top = jnp.maximum(
            jnp.max(scores, axis=1, keepdims=True), jnp.max(fresh_scores, axis=1, keepdims=True)
        )
        weights = jnp.exp2((scores - top) * EXPONENT).astype(jnp.bfloat16)
        fresh_weights = jnp.exp2((fresh_scores - top) * EXPONENT).astype(jnp.bfloat16)
        fresh_values = fresh_ref[:, span(KV_WIDTH + h * HEAD_SIZE, HEAD_SIZE)]
        dec_acc_ref[h] = product(weights, v_all) + product(fresh_weights, with_ones(fresh_values))
        dec_top_ref[h] = jnp.broadcast_to(top, (STACKED, HEAD_SIZE))
        for (start, keys), bias in zip(spans, biases):
            if keys < tokens:
                k_part = jnp.concatenate([part[:keys] for part in k_parts], axis=0)
                v_part = with_ones(jnp.concatenate([part[:keys] for part in v_parts], axis=0))
            else:
                k_part, v_part = k_all, v_all
            for g in range(0, HEADS_PER_KV, together):
                queries = stacked_heads(
                    q_ref, slice(start, start + half), first + g * HEAD_SIZE, together
                )
                scores = scores_of(queries, k_part).reshape(together, half, bias.shape[1]) + bias[None]
                top = jnp.max(scores, axis=2, keepdims=True)
                weights = jnp.exp2((scores - top) * EXPONENT).astype(jnp.bfloat16)
                rows = slice(
                    start * HEADS_PER_KV + g * half, start * HEADS_PER_KV + (g + together) * half
                )
                acc_ref[h, rows, :] = product(weights.reshape(together * half, bias.shape[1]), v_part)
                top_ref[h, rows, :] = jnp.broadcast_to(top, (together, half, HEAD_SIZE)).reshape(
                    together * half, HEAD_SIZE
                )

    for copy in copies:
        copy.wait()
    each_kv_head(width, step)


def divided(acc):
    return (acc[:, :HEAD_SIZE] / acc[:, HEAD_SIZE:]).astype(jnp.bfloat16)


def merge(acc, old_top, scores, values):
    top = jnp.maximum(old_top, jnp.max(scores, axis=1, keepdims=True))
    weights = jnp.exp2((scores - top) * EXPONENT).astype(jnp.bfloat16)
    factor = jnp.exp2((old_top - top) * EXPONENT)
    return acc * jnp.concatenate([factor, factor], axis=1) + product(weights, with_ones(values))


def decode_kernel(plan, pd_size, facts_ref, acc_ref, top_ref, queries_ref, even_ref, odd_ref, out_ref):
    width = plan.size
    tokens = even_ref.shape[0] // 2
    facts = Facts(facts_ref, width)
    k_part, v_part = (
        mine(facts.group, (even_ref, odd_ref), rows, slice(None))
        for rows in (slice(0, tokens), slice(tokens, 2 * tokens))
    )
    mask = request_mask(facts.ends, tokens, facts.source[-1:], width)
    row = iota((PADDED_ROWS, PADDED_ROWS), 0)
    column = iota((PADDED_ROWS, PADDED_ROWS), 1)
    pick = column < 0
    for r in range(GROUP_REQUESTS):
        ahead = facts.slots[r] // GROUP_REQUESTS - facts.group
        ahead = jnp.where(ahead < 0, ahead + pd_size, ahead)
        pick = pick | (
            (column // DECODE_STEPS == r) & (row == ahead * DECODE_STEPS + column - r * DECODE_STEPS)
        )
    pick = pick.astype(jnp.float32).astype(jnp.bfloat16)
    heads = range(KEY_VALUE_HEADS)
    columns = [slice(h * HEAD_SIZE, (h + 1) * HEAD_SIZE) for h in heads]
    scores = [
        scores_of(stacked_heads(queries_ref, slice(None), h * Q_BLOCK, HEADS_PER_KV), k_part[:, columns[h]])
        for h in heads
    ]
    scores = [jnp.where(mask, s, MASKED) for s in scores]
    out = [divided(merge(acc_ref[h], top_ref[h], scores[h], v_part[:, columns[h]])) for h in heads]
    out = jnp.concatenate(
        [o[g * PADDED_ROWS : (g + 1) * PADDED_ROWS] for o in out for g in range(HEADS_PER_KV)], axis=1
    )
    out_ref[...] = product(pick, out).astype(jnp.bfloat16)


def prefill_kernel(plan, facts_ref, q_ref, acc_ref, top_ref, even_ref, odd_ref, out_ref, done_ref, sem):
    width = plan.size
    tokens = q_ref.shape[0]
    half = tokens // 2
    facts = Facts(facts_ref, width)
    biases = [
        causal_bias(s, half, tokens, facts.source[-1:], facts.ends, facts.member, width)
        for s in (0, half)
    ]

    def finish(rescale):
        copies = []
        worst = jnp.full((half, tokens), MASKED, jnp.float32)
        for h in range(KEY_VALUE_HEADS):
            columns = slice(h * HEAD_SIZE, (h + 1) * HEAD_SIZE)
            keys, values = (
                mine(facts.group, (even_ref, odd_ref), rows, columns)
                for rows in (slice(0, tokens), slice(tokens, 2 * tokens))
            )
            for start, bias in zip((0, half), biases):
                queries = stacked_heads(q_ref, slice(start, start + half), h * Q_BLOCK, HEADS_PER_KV)
                scores = scores_of(queries, keys).reshape(HEADS_PER_KV, half, tokens) + bias[None]
                rows = slice(start * HEADS_PER_KV, (start + half) * HEADS_PER_KV)
                if rescale:
                    scores = scores.reshape(HEADS_PER_KV * half, tokens)
                    acc = merge(acc_ref[h, rows, :], top_ref[h, rows, :], scores, values)
                else:
                    above = scores - top_ref[h, rows, :].reshape(HEADS_PER_KV, half, tokens)
                    worst = jnp.maximum(worst, jnp.max(above, axis=0))
                    weights = jnp.exp2(above * EXPONENT).astype(jnp.bfloat16)
                    weights = weights.reshape(HEADS_PER_KV * half, tokens)
                    acc = acc_ref[h, rows, :] + product(weights, with_ones(values))
                out = divided(acc)
                for g in range(HEADS_PER_KV):
                    done_ref[
                        start : start + half,
                        h * Q_BLOCK + g * HEAD_SIZE : h * Q_BLOCK + (g + 1) * HEAD_SIZE,
                    ] = out[g * half : (g + 1) * half]
            part = pl.ds(h * Q_BLOCK, Q_BLOCK)
            copy = pltpu.make_async_copy(done_ref.at[:, part], out_ref.at[:, part], sem.at[h])
            copy.start()
            copies.append(copy)
        for copy in copies:
            copy.wait()
        return jnp.max(worst)

    @pl.when(finish(False) * EXPONENT > LIMIT)
    def _():
        finish(True)


def cost(rows, keys, exps):
    return pl.CostEstimate(
        flops=32 * rows * keys * Q_WIDTH, bytes_accessed=4 * rows * Q_WIDTH, transcendentals=exps
    )


def call_first(plan, facts, query, blocks, pieces):
    tokens, width = query.shape[0], plan.size
    rows = HEADS_PER_KV * tokens
    f32, bf16 = jnp.float32, jnp.bfloat16
    shapes = [
        jax.ShapeDtypeStruct((KEY_VALUE_HEADS, rows, 2 * HEAD_SIZE), f32),
        jax.ShapeDtypeStruct((KEY_VALUE_HEADS, rows, HEAD_SIZE), f32),
        jax.ShapeDtypeStruct((KEY_VALUE_HEADS, STACKED, 2 * HEAD_SIZE), f32),
        jax.ShapeDtypeStruct((KEY_VALUE_HEADS, STACKED, HEAD_SIZE), f32),
        jax.ShapeDtypeStruct((PADDED_ROWS, Q_WIDTH), bf16),
    ]
    every = (width - 1) * tokens
    return pl.pallas_call(
        lambda *refs: first_kernel(plan, len(blocks), *refs),
        in_specs=[SMEM, ANY] + [VMEM] * (len(blocks) + 2 * width - 3),
        out_specs=[VMEM] * len(shapes),
        out_shape=shapes,
        scratch_shapes=[
            pltpu.VMEM((tokens, Q_WIDTH), bf16),
            pltpu.VMEM((PADDED_ROWS, 2 * KV_WIDTH), bf16),
            pltpu.SemaphoreType.DMA((KEY_VALUE_HEADS,)),
        ],
        compiler_params=pltpu.CompilerParams(vmem_limit_bytes=(28 + width) * MIB),
        cost_estimate=cost(tokens, every, tokens * every * QUERY_HEADS),
        name="first_shards",
    )(facts, query, *pieces[0][:1], *[a for pair in pieces[1:] for a in pair], *blocks)


def call_decode(plan, pd_size, facts, state, piece):
    tokens = piece[0].shape[0] // 2
    return pl.pallas_call(
        lambda *refs: decode_kernel(plan, pd_size, *refs),
        in_specs=[SMEM] + [VMEM] * 5,
        out_specs=VMEM,
        out_shape=jax.ShapeDtypeStruct((PADDED_ROWS, Q_WIDTH), jnp.bfloat16),
        compiler_params=pltpu.CompilerParams(vmem_limit_bytes=32 * MIB),
        cost_estimate=cost(PADDED_ROWS, tokens, PADDED_ROWS * tokens * QUERY_HEADS),
        name="last_shard_decode",
    )(facts, *state[2:], *piece)


def call_prefill(plan, facts, query, state, piece):
    tokens = query.shape[0]
    return pl.pallas_call(
        lambda *refs: prefill_kernel(plan, *refs),
        in_specs=[SMEM] + [VMEM] * 5,
        out_specs=ANY,
        out_shape=jax.ShapeDtypeStruct((tokens, Q_WIDTH), jnp.bfloat16),
        scratch_shapes=[
            pltpu.VMEM((tokens, Q_WIDTH), jnp.bfloat16),
            pltpu.SemaphoreType.DMA((KEY_VALUE_HEADS,)),
        ],
        compiler_params=pltpu.CompilerParams(vmem_limit_bytes=32 * MIB),
        cost_estimate=cost(tokens, tokens, tokens * tokens * QUERY_HEADS),
        name="last_shard_prefill",
    )(facts, query, *state[:2], *piece)


def ring(size, step):
    return [(i, (i + step) % size) for i in range(size)]


def body(
    prompt_query,
    prompt_key,
    prompt_value,
    prompt_lengths,
    decode_slot,
    decoded_query,
    decoded_key,
    decoded_value,
):
    plan = Ring(lax.axis_size("tp"))
    pd_size = lax.axis_size("pd")
    my_group = lax.axis_index("pd")
    facts = facts_row(plan, prompt_lengths, decode_slot)
    kv, decoded_query = lax.optimization_barrier(
        (jnp.concatenate([prompt_key, prompt_value], axis=0), decoded_query)
    )
    own = jnp.concatenate([decoded_query, decoded_key, decoded_value], axis=2).reshape(
        DECODE_ROWS, Q_WIDTH + 2 * KV_WIDTH
    )
    later_kv, own, facts = lax.optimization_barrier((kv, own, facts))
    pieces, blocks = [[kv, later_kv]], None
    for s in range(1, plan.size):
        if s > 1:
            pieces[1:], own, blocks = lax.optimization_barrier((pieces[1:], own, blocks))
        pieces.append(plan.steps(pieces[-1]))
        if s == 2:
            blocks = [own] + [lax.ppermute(own, "pd", ring(pd_size, k)) for k in range(1, pd_size)]

    state = call_first(plan, facts, prompt_query, blocks, pieces[:-1])
    outgoing = call_decode(plan, pd_size, facts, state, pieces[-1])
    arrived = [outgoing[:DECODE_STEPS]]
    for k in range(1, pd_size):
        part = outgoing[k * DECODE_STEPS : (k + 1) * DECODE_STEPS]
        arrived.append(lax.ppermute(part, "pd", ring(pd_size, k)))
    pre_out = call_prefill(plan, facts, prompt_query, state, pieces[-1])

    numbers = jnp.arange(decode_slot.shape[0], dtype=jnp.int32)
    wanted = my_group * GROUP_REQUESTS + jnp.arange(GROUP_REQUESTS, dtype=jnp.int32)
    owner = jnp.sum(
        jnp.where(decode_slot[None, :] == wanted[:, None], numbers[None, :] // GROUP_REQUESTS, 0), axis=1
    )
    from_block = (my_group - owner) % pd_size
    dec_out = jnp.zeros((GROUP_REQUESTS, DECODE_STEPS, Q_WIDTH), jnp.bfloat16)
    for k in range(pd_size):
        dec_out = jnp.where((from_block == k)[:, None, None], arrived[k][None], dec_out)
    return (pre_out, dec_out)


def solution(mesh):
    placed = (
        P(("rep", "pd", "tp"), None),
        P(("rep", "pd", "tp"), None),
        P(("rep", "pd", "tp"), None),
        P("rep", None),
        P("rep"),
        P(("rep", "pd"), None, None),
        P(("rep", "pd"), None, None),
        P(("rep", "pd"), None, None),
    )
    return jax.shard_map(
        body,
        mesh=mesh,
        in_specs=placed,
        out_specs=(P(("rep", "pd", "tp"), None), P(("rep", "pd"), None, None)),
        check_vma=False,
    )
```

```python
import math

import jax
import jax.numpy as jnp
import numpy as np
from jax import lax
from jax.experimental import pallas as pl
from jax.experimental.pallas import tpu as pltpu
from jax.sharding import PartitionSpec as P

QUERY_HEADS = 32
KEY_VALUE_HEADS = 4
HEAD_SIZE = 128
PAGE = 16
GROUP_REQUESTS = 4
DECODE_STEPS = 2
HEADS_PER_KV = QUERY_HEADS // KEY_VALUE_HEADS
KV_WIDTH = KEY_VALUE_HEADS * HEAD_SIZE
Q_WIDTH = QUERY_HEADS * HEAD_SIZE
Q_BLOCK = HEADS_PER_KV * HEAD_SIZE
DECODE_ROWS = GROUP_REQUESTS * DECODE_STEPS
PADDED_ROWS = 16
STACKED = HEADS_PER_KV * PADDED_ROWS
MIB = 1024 * 1024

MASKED = -1e30
LIMIT = 60.0
EXPONENT = math.log2(math.e) / math.sqrt(HEAD_SIZE)

VMEM = pl.BlockSpec(memory_space=pltpu.VMEM)
SMEM = pl.BlockSpec(memory_space=pltpu.SMEM)
ANY = pl.BlockSpec(memory_space=pl.ANY)


class Ring:
    def __init__(self, size):
        self.size = size
        order = [0] + list(range(1, size, 2)) + [i for i in range(size - 1, 0, -1) if i % 2 == 0]
        self.pairs = [(order[i], order[(i + 1) % size]) for i in range(size)]
        place = {m: i for i, m in enumerate(order)}
        self.source = np.array(
            [[order[(place[m] - s) % size] for s in range(size)] for m in range(size)], np.int32
        )

    def step(self, array):
        return lax.ppermute(array, "tp", self.pairs)


def scores_of(queries, keys):
    return lax.dot_general(
        queries, keys, (((1,), (1,)), ((), ())), preferred_element_type=jnp.float32
    )


def product(left, right):
    return jnp.dot(left, right, preferred_element_type=jnp.float32)


def iota(shape, axis):
    return lax.broadcasted_iota(jnp.int32, shape, axis)


def span(start, size):
    if isinstance(start, int):
        return slice(start, start + size)
    return pl.ds(pl.multiple_of(start, size), size)


def with_ones(values):
    return jnp.concatenate([values, jnp.ones_like(values)], axis=1)


def page_position(offset, member, width):
    return (offset // PAGE * width + member) * PAGE + offset % PAGE


def key_positions(rows, sources, width):
    column = iota((1, len(sources) * rows), 1)
    part = column // rows
    source = jnp.zeros_like(column) + sources[0]
    for b in range(1, len(sources)):
        source = jnp.where(part == b, sources[b], source)
    return page_position(column - part * rows, source, width)


class Facts:
    def __init__(self, ref, width):
        self.width = width
        self.group, self.member = ref[0], ref[1]
        self.slots = [ref[2 + r] for r in range(GROUP_REQUESTS)]
        first = 2 + GROUP_REQUESTS
        self.ends = []
        total = jnp.int32(0)
        for r in range(GROUP_REQUESTS):
            total = total + ref[first + r] * PAGE
            self.ends.append(total)
        first += GROUP_REQUESTS
        self.source = [ref[first + s] for s in range(width)]


def facts_row(plan, lengths, slots):
    group, member = lax.axis_index("pd"), lax.axis_index("tp")
    return jnp.concatenate(
        [
            jnp.stack([group, member]).astype(jnp.int32),
            lax.dynamic_slice_in_dim(slots, group * GROUP_REQUESTS, GROUP_REQUESTS, 0),
            lax.dynamic_index_in_dim(lengths, group, 0, keepdims=False),
            lax.dynamic_index_in_dim(jnp.asarray(plan.source), member, 0, keepdims=False),
        ]
    )


def causal_bias(start, rows, keys, sources, ends, member, width):
    qpos = page_position(start + iota((rows, 1), 0), member, width)
    low = jnp.zeros_like(qpos)
    for end in ends:
        low = jnp.where(qpos >= end, end, low)
    kpos = key_positions(keys, sources, width)
    return jnp.where((kpos >= low) & (kpos <= qpos), 0.0, MASKED)


def request_mask(ends, keys, sources, width):
    request = iota((STACKED, 1), 0) % PADDED_ROWS // DECODE_STEPS
    low = jnp.zeros_like(request)
    high = jnp.zeros_like(request) + ends[0]
    for r in range(1, GROUP_REQUESTS):
        low = jnp.where(request == r, ends[r - 1], low)
        high = jnp.where(request == r, ends[r], high)
    kpos = key_positions(keys, sources, width)
    return (kpos >= low) & (kpos < high)


def stacked_heads(ref, rows, first, count):
    return jnp.concatenate(
        [ref[rows, span(first + i * HEAD_SIZE, HEAD_SIZE)] for i in range(count)], axis=0
    )


def each_kv_head(width, step):
    if width <= 8:
        for h in range(KEY_VALUE_HEADS):
            step(h)
    else:
        lax.fori_loop(0, KEY_VALUE_HEADS, lambda h, c: (step(h), c)[1], 0)


def first_kernel(plan, pd_size, facts_ref, q_hbm_ref, k_hbm_ref, v_hbm_ref, *refs):
    width = plan.size
    k_refs, v_refs, refs = refs[: width - 2], refs[width - 2 : 2 * width - 4], refs[2 * width - 4 :]
    block_refs, refs = refs[:pd_size], refs[pd_size:]
    acc_ref, top_ref, dec_acc_ref, dec_top_ref, queries_ref, q_ref, k_ref, v_ref, fresh_ref, sem = refs
    k_refs, v_refs = (k_ref,) + k_refs, (v_ref,) + v_refs
    copies = [
        pltpu.make_async_copy(k_hbm_ref, k_ref, sem.at[KEY_VALUE_HEADS]),
        pltpu.make_async_copy(v_hbm_ref, v_ref, sem.at[KEY_VALUE_HEADS + 1]),
    ]
    for h in range(KEY_VALUE_HEADS):
        part = pl.ds(h * Q_BLOCK, Q_BLOCK)
        copies.append(pltpu.make_async_copy(q_hbm_ref.at[:, part], q_ref.at[:, part], sem.at[h]))
    for copy in copies:
        copy.start()
    tokens = q_ref.shape[0]
    half = tokens // 2
    facts = Facts(facts_ref, width)
    group, member, ends = facts.group, facts.member, facts.ends
    sources = facts.source[:-1]

    row = iota((PADDED_ROWS, DECODE_ROWS), 0)
    column = iota((PADDED_ROWS, DECODE_ROWS), 1)
    total = None
    for k in range(pd_size):
        pick = column < 0
        for r in range(GROUP_REQUESTS):
            slot = facts.slots[r]
            back = group - slot // GROUP_REQUESTS
            back = jnp.where(back < 0, back + pd_size, back)
            first = jnp.where(back == k, slot % GROUP_REQUESTS * DECODE_STEPS, -DECODE_ROWS * 4)
            pick = pick | ((row // DECODE_STEPS == r) & (column == first + row - r * DECODE_STEPS))
        part = product(pick.astype(jnp.float32).astype(jnp.bfloat16), block_refs[k][...])
        total = part if total is None else total + part
    total = total.astype(jnp.bfloat16)
    queries_ref[...] = total[:, :Q_WIDTH]
    fresh_ref[...] = total[:, Q_WIDTH:]

    row = iota((STACKED, PADDED_ROWS), 0) % PADDED_ROWS
    column = iota((STACKED, PADDED_ROWS), 1)
    fresh_mask = (column // DECODE_STEPS == row // DECODE_STEPS) & (
        column % DECODE_STEPS <= row % DECODE_STEPS
    )
    mask = request_mask(ends, tokens, sources, width)
    spans = ((0, half), (half, tokens))
    biases = [causal_bias(s, half, keys, sources, ends, member, width) for s, keys in spans]
    together = max(1, min(HEADS_PER_KV, HEADS_PER_KV * 4 // width))

    def step(h):
        columns = span(h * HEAD_SIZE, HEAD_SIZE)
        first = h * Q_BLOCK
        queries = stacked_heads(queries_ref, slice(None), first, HEADS_PER_KV)
        fresh_scores = jnp.where(fresh_mask, scores_of(queries, fresh_ref[:, columns]), MASKED)
        k_all = jnp.concatenate([ref[:, columns] for ref in k_refs], axis=0)
        v_all = with_ones(jnp.concatenate([ref[:, columns] for ref in v_refs], axis=0))
        scores = jnp.where(mask, scores_of(queries, k_all), MASKED)
        top = jnp.maximum(
            jnp.max(scores, axis=1, keepdims=True), jnp.max(fresh_scores, axis=1, keepdims=True)
        )
        weights = jnp.exp2((scores - top) * EXPONENT).astype(jnp.bfloat16)
        fresh_weights = jnp.exp2((fresh_scores - top) * EXPONENT).astype(jnp.bfloat16)
        fresh_values = fresh_ref[:, span(KV_WIDTH + h * HEAD_SIZE, HEAD_SIZE)]
        dec_acc_ref[h] = product(weights, v_all) + product(fresh_weights, with_ones(fresh_values))
        dec_top_ref[h] = jnp.broadcast_to(top, (STACKED, HEAD_SIZE))
        for (start, keys), bias in zip(spans, biases):
            if keys < tokens:
                k_part = jnp.concatenate([ref[:keys, columns] for ref in k_refs], axis=0)
                v_part = with_ones(jnp.concatenate([ref[:keys, columns] for ref in v_refs], axis=0))
            else:
                k_part, v_part = k_all, v_all
            for g in range(0, HEADS_PER_KV, together):
                queries = stacked_heads(
                    q_ref, slice(start, start + half), first + g * HEAD_SIZE, together
                )
                scores = scores_of(queries, k_part).reshape(together, half, bias.shape[1]) + bias[None]
                top = jnp.max(scores, axis=2, keepdims=True)
                weights = jnp.exp2((scores - top) * EXPONENT).astype(jnp.bfloat16)
                rows = slice(
                    start * HEADS_PER_KV + g * half, start * HEADS_PER_KV + (g + together) * half
                )
                acc_ref[h, rows, :] = product(weights.reshape(together * half, bias.shape[1]), v_part)
                top_ref[h, rows, :] = jnp.broadcast_to(top, (together, half, HEAD_SIZE)).reshape(
                    together * half, HEAD_SIZE
                )

    for copy in copies:
        copy.wait()
    each_kv_head(width, step)


def divided(acc):
    return (acc[:, :HEAD_SIZE] / acc[:, HEAD_SIZE:]).astype(jnp.bfloat16)


def merge(acc, old_top, scores, values):
    top = jnp.maximum(old_top, jnp.max(scores, axis=1, keepdims=True))
    weights = jnp.exp2((scores - top) * EXPONENT).astype(jnp.bfloat16)
    factor = jnp.exp2((old_top - top) * EXPONENT)
    return acc * jnp.concatenate([factor, factor], axis=1) + product(weights, with_ones(values))


def decode_kernel(plan, pd_size, facts_ref, acc_ref, top_ref, queries_ref, k_ref, v_ref, out_ref):
    width = plan.size
    tokens = k_ref.shape[0]
    facts = Facts(facts_ref, width)
    mask = request_mask(facts.ends, tokens, facts.source[-1:], width)
    row = iota((PADDED_ROWS, PADDED_ROWS), 0)
    column = iota((PADDED_ROWS, PADDED_ROWS), 1)
    pick = column < 0
    for r in range(GROUP_REQUESTS):
        ahead = facts.slots[r] // GROUP_REQUESTS - facts.group
        ahead = jnp.where(ahead < 0, ahead + pd_size, ahead)
        pick = pick | (
            (column // DECODE_STEPS == r) & (row == ahead * DECODE_STEPS + column - r * DECODE_STEPS)
        )
    pick = pick.astype(jnp.float32).astype(jnp.bfloat16)
    heads = range(KEY_VALUE_HEADS)
    columns = [slice(h * HEAD_SIZE, (h + 1) * HEAD_SIZE) for h in heads]
    scores = [
        scores_of(stacked_heads(queries_ref, slice(None), h * Q_BLOCK, HEADS_PER_KV), k_ref[:, columns[h]])
        for h in heads
    ]
    scores = [jnp.where(mask, s, MASKED) for s in scores]
    out = [divided(merge(acc_ref[h], top_ref[h], scores[h], v_ref[:, columns[h]])) for h in heads]
    out = jnp.concatenate(
        [o[g * PADDED_ROWS : (g + 1) * PADDED_ROWS] for o in out for g in range(HEADS_PER_KV)], axis=1
    )
    out_ref[...] = product(pick, out).astype(jnp.bfloat16)


def prefill_kernel(plan, facts_ref, q_ref, acc_ref, top_ref, k_ref, v_ref, out_ref, done_ref, sem):
    width = plan.size
    tokens = q_ref.shape[0]
    half = tokens // 2
    facts = Facts(facts_ref, width)
    biases = [
        causal_bias(s, half, tokens, facts.source[-1:], facts.ends, facts.member, width)
        for s in (0, half)
    ]

    def finish(rescale):
        copies = []
        worst = jnp.full((half, tokens), MASKED, jnp.float32)
        for h in range(KEY_VALUE_HEADS):
            columns = slice(h * HEAD_SIZE, (h + 1) * HEAD_SIZE)
            keys, values = k_ref[:, columns], v_ref[:, columns]
            for start, bias in zip((0, half), biases):
                queries = stacked_heads(q_ref, slice(start, start + half), h * Q_BLOCK, HEADS_PER_KV)
                scores = scores_of(queries, keys).reshape(HEADS_PER_KV, half, tokens) + bias[None]
                rows = slice(start * HEADS_PER_KV, (start + half) * HEADS_PER_KV)
                if rescale:
                    scores = scores.reshape(HEADS_PER_KV * half, tokens)
                    acc = merge(acc_ref[h, rows, :], top_ref[h, rows, :], scores, values)
                else:
                    above = scores - top_ref[h, rows, :].reshape(HEADS_PER_KV, half, tokens)
                    worst = jnp.maximum(worst, jnp.max(above, axis=0))
                    weights = jnp.exp2(above * EXPONENT).astype(jnp.bfloat16)
                    weights = weights.reshape(HEADS_PER_KV * half, tokens)
                    acc = acc_ref[h, rows, :] + product(weights, with_ones(values))
                out = divided(acc)
                for g in range(HEADS_PER_KV):
                    done_ref[
                        start : start + half,
                        h * Q_BLOCK + g * HEAD_SIZE : h * Q_BLOCK + (g + 1) * HEAD_SIZE,
                    ] = out[g * half : (g + 1) * half]
            part = pl.ds(h * Q_BLOCK, Q_BLOCK)
            copy = pltpu.make_async_copy(done_ref.at[:, part], out_ref.at[:, part], sem.at[h])
            copy.start()
            copies.append(copy)
        for copy in copies:
            copy.wait()
        return jnp.max(worst)

    @pl.when(finish(False) * EXPONENT > LIMIT)
    def _():
        finish(True)


def cost(rows, keys, exps):
    return pl.CostEstimate(
        flops=32 * rows * keys * Q_WIDTH, bytes_accessed=4 * rows * Q_WIDTH, transcendentals=exps
    )


def call_first(plan, facts, query, blocks, keys, values):
    tokens, width = query.shape[0], plan.size
    rows = HEADS_PER_KV * tokens
    f32, bf16 = jnp.float32, jnp.bfloat16
    shapes = [
        jax.ShapeDtypeStruct((KEY_VALUE_HEADS, rows, 2 * HEAD_SIZE), f32),
        jax.ShapeDtypeStruct((KEY_VALUE_HEADS, rows, HEAD_SIZE), f32),
        jax.ShapeDtypeStruct((KEY_VALUE_HEADS, STACKED, 2 * HEAD_SIZE), f32),
        jax.ShapeDtypeStruct((KEY_VALUE_HEADS, STACKED, HEAD_SIZE), f32),
        jax.ShapeDtypeStruct((PADDED_ROWS, Q_WIDTH), bf16),
    ]
    every = (width - 1) * tokens
    return pl.pallas_call(
        lambda *refs: first_kernel(plan, len(blocks), *refs),
        in_specs=[SMEM] + [ANY] * 3 + [VMEM] * (len(blocks) + 2 * (width - 2)),
        out_specs=[VMEM] * len(shapes),
        out_shape=shapes,
        scratch_shapes=[
            pltpu.VMEM((tokens, Q_WIDTH), bf16),
            pltpu.VMEM((tokens, KV_WIDTH), bf16),
            pltpu.VMEM((tokens, KV_WIDTH), bf16),
            pltpu.VMEM((PADDED_ROWS, 2 * KV_WIDTH), bf16),
            pltpu.SemaphoreType.DMA((KEY_VALUE_HEADS + 2,)),
        ],
        compiler_params=pltpu.CompilerParams(vmem_limit_bytes=(28 + width) * MIB),
        cost_estimate=cost(tokens, every, tokens * every * QUERY_HEADS),
        name="first_shards",
    )(facts, query, keys[0], values[0], *keys[1:], *values[1:], *blocks)


def call_decode(plan, pd_size, facts, state, key, value):
    tokens = key.shape[0]
    return pl.pallas_call(
        lambda *refs: decode_kernel(plan, pd_size, *refs),
        in_specs=[SMEM] + [VMEM] * 5,
        out_specs=VMEM,
        out_shape=jax.ShapeDtypeStruct((PADDED_ROWS, Q_WIDTH), jnp.bfloat16),
        compiler_params=pltpu.CompilerParams(vmem_limit_bytes=32 * MIB),
        cost_estimate=cost(PADDED_ROWS, tokens, PADDED_ROWS * tokens * QUERY_HEADS),
        name="last_shard_decode",
    )(facts, *state[2:], key, value)


def call_prefill(plan, facts, query, state, key, value):
    tokens = query.shape[0]
    return pl.pallas_call(
        lambda *refs: prefill_kernel(plan, *refs),
        in_specs=[SMEM] + [VMEM] * 5,
        out_specs=ANY,
        out_shape=jax.ShapeDtypeStruct((tokens, Q_WIDTH), jnp.bfloat16),
        scratch_shapes=[
            pltpu.VMEM((tokens, Q_WIDTH), jnp.bfloat16),
            pltpu.SemaphoreType.DMA((KEY_VALUE_HEADS,)),
        ],
        compiler_params=pltpu.CompilerParams(vmem_limit_bytes=32 * MIB),
        cost_estimate=cost(tokens, tokens, tokens * tokens * QUERY_HEADS),
        name="last_shard_prefill",
    )(facts, query, *state[:2], key, value)


def after(row, *arrays):
    def kernel(row_ref, *refs):
        out_ref = refs[-1]
        for i in range(row.shape[0]):
            out_ref[i] = row_ref[i]

    return pl.pallas_call(
        kernel,
        in_specs=[SMEM] + [ANY] * len(arrays),
        out_specs=SMEM,
        out_shape=jax.ShapeDtypeStruct(row.shape, row.dtype),
        cost_estimate=pl.CostEstimate(flops=5 * 10**9, bytes_accessed=0, transcendentals=0),
        name="after",
    )(row, *arrays)


def ring(size, step):
    return [(i, (i + step) % size) for i in range(size)]


def body(
    prompt_query,
    prompt_key,
    prompt_value,
    prompt_lengths,
    decode_slot,
    decoded_query,
    decoded_key,
    decoded_value,
):
    plan = Ring(lax.axis_size("tp"))
    pd_size = lax.axis_size("pd")
    my_group = lax.axis_index("pd")
    own = jnp.concatenate([decoded_query, decoded_key, decoded_value], axis=2).reshape(
        DECODE_ROWS, Q_WIDTH + 2 * KV_WIDTH
    )
    facts = facts_row(plan, prompt_lengths, decode_slot)
    prompt_key, decoded_query = lax.optimization_barrier((prompt_key, decoded_query))
    prompt_value, own, facts = lax.optimization_barrier((prompt_value, own, facts))
    keys, values = [prompt_key], [prompt_value]
    for s in range(1, plan.size):
        if s == 2:
            keys[1], own = lax.optimization_barrier((keys[1], own))
        if s == plan.size - 1:
            facts = after(facts, keys[-1], values[-1])
            values[-1], blocks, facts = lax.optimization_barrier((values[-1], blocks, facts))
        keys.append(plan.step(keys[-1]))
        values.append(plan.step(values[-1]))
        if s == 2:
            blocks = [own] + [lax.ppermute(own, "pd", ring(pd_size, k)) for k in range(1, pd_size)]

    state = call_first(plan, facts, prompt_query, blocks, keys[:-1], values[:-1])
    outgoing = call_decode(plan, pd_size, facts, state, keys[-1], values[-1])
    arrived = [outgoing[:DECODE_STEPS]]
    for k in range(1, pd_size):
        part = outgoing[k * DECODE_STEPS : (k + 1) * DECODE_STEPS]
        arrived.append(lax.ppermute(part, "pd", ring(pd_size, k)))
    pre_out = call_prefill(plan, facts, prompt_query, state, keys[-1], values[-1])

    numbers = jnp.arange(decode_slot.shape[0], dtype=jnp.int32)
    wanted = my_group * GROUP_REQUESTS + jnp.arange(GROUP_REQUESTS, dtype=jnp.int32)
    owner = jnp.sum(
        jnp.where(decode_slot[None, :] == wanted[:, None], numbers[None, :] // GROUP_REQUESTS, 0), axis=1
    )
    from_block = (my_group - owner) % pd_size
    dec_out = jnp.zeros((GROUP_REQUESTS, DECODE_STEPS, Q_WIDTH), jnp.bfloat16)
    for k in range(pd_size):
        dec_out = jnp.where((from_block == k)[:, None, None], arrived[k][None], dec_out)
    return (pre_out, dec_out)


def solution(mesh):
    placed = (
        P(("rep", "pd", "tp"), None),
        P(("rep", "pd", "tp"), None),
        P(("rep", "pd", "tp"), None),
        P("rep", None),
        P("rep"),
        P(("rep", "pd"), None, None),
        P(("rep", "pd"), None, None),
        P(("rep", "pd"), None, None),
    )
    return jax.shard_map(
        body,
        mesh=mesh,
        in_specs=placed,
        out_specs=(P(("rep", "pd", "tp"), None), P(("rep", "pd"), None, None)),
        check_vma=False,
    )
```

```python
import math

import jax
import jax.numpy as jnp
from jax import lax
from jax.experimental import pallas as pl
from jax.experimental.pallas import tpu as pltpu
from jax.sharding import PartitionSpec as P

QUERY_HEADS = 32
KEY_VALUE_HEADS = 4
HEAD_SIZE = 128
PAGE = 16
GROUP_REQUESTS = 4
DECODE_STEPS = 2
HEADS_PER_KV = QUERY_HEADS // KEY_VALUE_HEADS
KV_WIDTH = KEY_VALUE_HEADS * HEAD_SIZE
Q_WIDTH = QUERY_HEADS * HEAD_SIZE
Q_BLOCK = HEADS_PER_KV * HEAD_SIZE
DECODE_ROWS = GROUP_REQUESTS * DECODE_STEPS
PADDED_ROWS = 16
STACKED = HEADS_PER_KV * PADDED_ROWS
MIB = 1024 * 1024

MASKED = -1e30
LIMIT = 60.0
EXPONENT = math.log2(math.e) / math.sqrt(HEAD_SIZE)

VMEM = pl.BlockSpec(memory_space=pltpu.VMEM)
SMEM = pl.BlockSpec(memory_space=pltpu.SMEM)
ANY = pl.BlockSpec(memory_space=pl.ANY)
HBM = pl.BlockSpec(memory_space=pltpu.HBM)


class Ring:
    def __init__(self, size):
        self.size = size
        order = [0] + list(range(1, size, 2)) + [i for i in range(size - 1, 0, -1) if i % 2 == 0]
        self.pairs = [(order[i], order[(i + 1) % size]) for i in range(size)]

    def step(self, array):
        return lax.ppermute(array, "tp", self.pairs)


def scores_of(queries, keys):
    return lax.dot_general(
        queries, keys, (((1,), (1,)), ((), ())), preferred_element_type=jnp.float32
    )


def product(left, right):
    return jnp.dot(left, right, preferred_element_type=jnp.float32)


def iota(shape, axis):
    return lax.broadcasted_iota(jnp.int32, shape, axis)


def span(start, size):
    if isinstance(start, int):
        return slice(start, start + size)
    return pl.ds(pl.multiple_of(start, size), size)


def with_ones(values):
    return jnp.concatenate([values, jnp.ones_like(values)], axis=1)


def page_position(offset, member, width):
    return (offset // PAGE * width + member) * PAGE + offset % PAGE


def key_positions(rows, sources, width):
    column = iota((1, len(sources) * rows), 1)
    part = column // rows
    source = jnp.zeros_like(column) + sources[0]
    for b in range(1, len(sources)):
        source = jnp.where(part == b, sources[b], source)
    return page_position(column - part * rows, source, width)


class Facts:
    def __init__(self, ref, width):
        self.width = width
        self.group, self.member = ref[0], ref[1]
        self.slots = [ref[2 + r] for r in range(GROUP_REQUESTS)]
        first = 2 + GROUP_REQUESTS
        self.ends = []
        total = jnp.int32(0)
        for r in range(GROUP_REQUESTS):
            total = total + ref[first + r] * PAGE
            self.ends.append(total)
        first += GROUP_REQUESTS
        self.source = [ref[first + s] for s in range(width)]


def facts_row(plan, lengths, slots):
    width, groups, requests = plan.size, lengths.shape[0], slots.shape[0]

    def kernel(lengths_ref, slots_ref, out_ref):
        group, member = lax.axis_index("pd"), lax.axis_index("tp")
        values = [group, member]
        values += [slots_ref[group * GROUP_REQUESTS + r] for r in range(GROUP_REQUESTS)]
        values += [lengths_ref[group, r] for r in range(GROUP_REQUESTS)]
        place = jnp.where(member % 2 == 1, (member + 1) // 2, width - member // 2)
        for s in range(width):
            before = (place + width - s) % width
            up = 2 * before - 1
            values.append(jnp.where(before == 0, 0, jnp.where(before <= width // 2, up, 2 * (width - before))))
        for i, value in enumerate(values):
            out_ref[i] = value.astype(jnp.int32)
        for q in range(requests):
            place = slots_ref[q] - group * GROUP_REQUESTS

            @pl.when((place >= 0) & (place < GROUP_REQUESTS))
            def _():
                back = group - q // GROUP_REQUESTS
                out_ref[len(values) + place] = jnp.where(back < 0, back + groups, back).astype(jnp.int32)

    length = 2 + 2 * GROUP_REQUESTS + width + GROUP_REQUESTS
    return pl.pallas_call(
        kernel,
        in_specs=[SMEM, SMEM],
        out_specs=SMEM,
        out_shape=jax.ShapeDtypeStruct((length,), jnp.int32),
        cost_estimate=pl.CostEstimate(flops=5 * 10**9, bytes_accessed=0, transcendentals=0),
        name="facts",
    )(lengths, slots)


def causal_bias(start, rows, keys, sources, ends, member, width):
    qpos = page_position(start + iota((rows, 1), 0), member, width)
    low = jnp.zeros_like(qpos)
    for end in ends:
        low = jnp.where(qpos >= end, end, low)
    kpos = key_positions(keys, sources, width)
    return jnp.where((kpos >= low) & (kpos <= qpos), 0.0, MASKED)


def request_mask(ends, keys, sources, width):
    request = iota((STACKED, 1), 0) % PADDED_ROWS // DECODE_STEPS
    low = jnp.zeros_like(request)
    high = jnp.zeros_like(request) + ends[0]
    for r in range(1, GROUP_REQUESTS):
        low = jnp.where(request == r, ends[r - 1], low)
        high = jnp.where(request == r, ends[r], high)
    kpos = key_positions(keys, sources, width)
    return (kpos >= low) & (kpos < high)


def stacked_heads(ref, rows, first, count):
    return jnp.concatenate(
        [ref[rows, span(first + i * HEAD_SIZE, HEAD_SIZE)] for i in range(count)], axis=0
    )


def each_kv_head(width, step):
    if width <= 8:
        for h in range(KEY_VALUE_HEADS):
            step(h)
    else:
        lax.fori_loop(0, KEY_VALUE_HEADS, lambda h, c: (step(h), c)[1], 0)


def peak(exponents):
    return jnp.max(exponents.reshape(-1, 8, exponents.shape[-1]), axis=0)


def picked_rows(facts, pd_size, block_refs):
    row = iota((PADDED_ROWS, DECODE_ROWS), 0)
    column = iota((PADDED_ROWS, DECODE_ROWS), 1)
    total = None
    for k in range(pd_size):
        pick = column < 0
        for r in range(GROUP_REQUESTS):
            slot = facts.slots[r]
            back = facts.group - slot // GROUP_REQUESTS
            back = jnp.where(back < 0, back + pd_size, back)
            first = jnp.where(back == k, slot % GROUP_REQUESTS * DECODE_STEPS, -DECODE_ROWS * 4)
            pick = pick | ((row // DECODE_STEPS == r) & (column == first + row - r * DECODE_STEPS))
        part = product(pick.astype(jnp.float32).astype(jnp.bfloat16), block_refs[k][...])
        total = part if total is None else total + part
    return total.astype(jnp.bfloat16)


def fresh_mask():
    row = iota((STACKED, PADDED_ROWS), 0) % PADDED_ROWS
    column = iota((STACKED, PADDED_ROWS), 1)
    return (column // DECODE_STEPS == row // DECODE_STEPS) & (
        column % DECODE_STEPS <= row % DECODE_STEPS
    )


def first_kernel(plan, pd_size, facts_ref, q_hbm_ref, k_hbm_ref, v_hbm_ref, *refs):
    width = plan.size
    k_refs, v_refs, refs = refs[: width - 2], refs[width - 2 : 2 * width - 4], refs[2 * width - 4 :]
    block_refs, refs = refs[:pd_size], refs[pd_size:]
    acc_ref, dec_acc_ref, worst_ref, queries_ref, fresh_ref, q_ref, k_ref, v_ref, sem = refs
    k_refs, v_refs = (k_ref,) + k_refs, (v_ref,) + v_refs
    copies = [
        pltpu.make_async_copy(k_hbm_ref, k_ref, sem.at[KEY_VALUE_HEADS]),
        pltpu.make_async_copy(v_hbm_ref, v_ref, sem.at[KEY_VALUE_HEADS + 1]),
    ]
    for h in range(KEY_VALUE_HEADS):
        part = pl.ds(h * Q_BLOCK, Q_BLOCK)
        copies.append(pltpu.make_async_copy(q_hbm_ref.at[:, part], q_ref.at[:, part], sem.at[h]))
    for copy in copies:
        copy.start()
    tokens = q_ref.shape[0]
    half = tokens // 2
    facts = Facts(facts_ref, width)
    sources = facts.source[:-1]
    rows = picked_rows(facts, pd_size, block_refs)
    queries_ref[...] = rows[:, :Q_WIDTH]
    fresh_ref[...] = rows[:, Q_WIDTH:]
    worst_ref[...] = jnp.full(worst_ref.shape, MASKED, jnp.float32)
    new_mask = fresh_mask()
    mask = request_mask(facts.ends, tokens, sources, width)
    spans = ((0, half), (half, tokens))
    biases = [
        causal_bias(s, half, keys, sources, facts.ends, facts.member, width) for s, keys in spans
    ]
    together = max(1, min(HEADS_PER_KV, HEADS_PER_KV * 4 // width))

    def weigh(exponents):
        top = jnp.max(peak(exponents), axis=1, keepdims=True)
        worst_ref[...] = jnp.maximum(worst_ref[...], top)
        return jnp.exp2(exponents).astype(jnp.bfloat16)

    def step(h):
        columns = span(h * HEAD_SIZE, HEAD_SIZE)
        first = h * Q_BLOCK
        queries = stacked_heads(queries_ref, slice(None), first, HEADS_PER_KV)
        k_all = jnp.concatenate([ref[:, columns] for ref in k_refs], axis=0)
        v_all = with_ones(jnp.concatenate([ref[:, columns] for ref in v_refs], axis=0))
        new_scores = scores_of(queries, fresh_ref[:, columns]) * EXPONENT
        new_weights = weigh(jnp.where(new_mask, new_scores, MASKED))
        new_values = fresh_ref[:, span(KV_WIDTH + h * HEAD_SIZE, HEAD_SIZE)]
        weights = weigh(jnp.where(mask, scores_of(queries, k_all) * EXPONENT, MASKED))
        dec_acc_ref[h] = product(weights, v_all) + product(new_weights, with_ones(new_values))
        for (start, keys), bias in zip(spans, biases):
            if keys < tokens:
                k_part = jnp.concatenate([ref[:keys, columns] for ref in k_refs], axis=0)
                v_part = with_ones(jnp.concatenate([ref[:keys, columns] for ref in v_refs], axis=0))
            else:
                k_part, v_part = k_all, v_all
            for g in range(0, HEADS_PER_KV, together):
                queries = stacked_heads(
                    q_ref, slice(start, start + half), first + g * HEAD_SIZE, together
                )
                scores = scores_of(queries, k_part).reshape(together, half, bias.shape[1])
                exponents = (scores * EXPONENT + bias[None]).reshape(together * half, bias.shape[1])
                rows = slice(
                    start * HEADS_PER_KV + g * half, start * HEADS_PER_KV + (g + together) * half
                )
                acc_ref[h, rows, :] = product(weigh(exponents), v_part)

    for copy in copies:
        copy.wait()
    each_kv_head(width, step)


def divided(acc):
    return (acc[:, :HEAD_SIZE] * pl.reciprocal(acc[:, HEAD_SIZE:], approx=True)).astype(jnp.bfloat16)


def fold(state, scores_list, values_list):
    top = None if state is None else state[0]
    for scores in scores_list:
        part = jnp.max(scores, axis=1, keepdims=True)
        top = part if top is None else jnp.maximum(top, part)
    acc = None
    for scores, values in zip(scores_list, values_list):
        weights = jnp.exp2((scores - top) * EXPONENT).astype(jnp.bfloat16)
        part = product(weights, with_ones(values))
        acc = part if acc is None else acc + part
    if state is not None:
        acc = acc + state[1] * jnp.exp2((state[0] - top) * EXPONENT)
    return top, acc


def parts_in(width):
    return [range(c, min(c + 4, width)) for c in range(0, width, 4)]


def out_of_range(worst, least):
    return (jnp.max(worst) > LIMIT) | (jnp.min(least) < 2.0**-LIMIT)


def decode_kernel(plan, pd_size, facts_ref, acc_ref, worst_ref, queries_ref, fresh_ref, *refs):
    width = plan.size
    k_refs, v_refs, (out_ref,) = refs[:width], refs[width : 2 * width], refs[2 * width :]
    tokens = k_refs[0].shape[0]
    facts = Facts(facts_ref, width)
    mask = request_mask(facts.ends, tokens, facts.source[-1:], width)
    row = iota((PADDED_ROWS, PADDED_ROWS), 0)
    column = iota((PADDED_ROWS, PADDED_ROWS), 1)
    pick = column < 0
    for r in range(GROUP_REQUESTS):
        ahead = facts.slots[r] // GROUP_REQUESTS - facts.group
        ahead = jnp.where(ahead < 0, ahead + pd_size, ahead)
        pick = pick | (
            (column // DECODE_STEPS == r) & (row == ahead * DECODE_STEPS + column - r * DECODE_STEPS)
        )
    pick = pick.astype(jnp.float32).astype(jnp.bfloat16)
    heads = range(KEY_VALUE_HEADS)
    columns = [slice(h * HEAD_SIZE, (h + 1) * HEAD_SIZE) for h in heads]

    def queries_of(h):
        return stacked_heads(queries_ref, slice(None), h * Q_BLOCK, HEADS_PER_KV)

    def send(acc):
        out = [divided(a) for a in acc]
        out = jnp.concatenate(
            [o[g * PADDED_ROWS : (g + 1) * PADDED_ROWS] for o in out for g in range(HEADS_PER_KV)], axis=1
        )
        out_ref[...] = product(pick, out).astype(jnp.bfloat16)

    exponents = [
        jnp.where(mask, scores_of(queries_of(h), k_refs[-1][:, columns[h]]) * EXPONENT, MASKED)
        for h in heads
    ]
    acc = [
        acc_ref[h] + product(jnp.exp2(exponents[h]).astype(jnp.bfloat16), with_ones(v_refs[-1][:, columns[h]]))
        for h in heads
    ]
    send(acc)
    worst, least = worst_ref[...], None
    for h in heads:
        worst = jnp.maximum(worst, peak(exponents[h]))
        part = jnp.min(acc[h][:, HEAD_SIZE:].reshape(-1, 8, HEAD_SIZE), axis=0)
        least = part if least is None else jnp.minimum(least, part)

    @pl.when(out_of_range(worst, least))
    def _():
        new_mask = fresh_mask()
        again = []
        for h in heads:
            queries = queries_of(h)
            scores = jnp.where(new_mask, scores_of(queries, fresh_ref[:, columns[h]]), MASKED)
            new_columns = slice(KV_WIDTH + h * HEAD_SIZE, KV_WIDTH + (h + 1) * HEAD_SIZE)
            state = fold(None, [scores], [fresh_ref[:, new_columns]])
            for parts in parts_in(width):
                k_part = jnp.concatenate([k_refs[s][:, columns[h]] for s in parts], axis=0)
                v_part = jnp.concatenate([v_refs[s][:, columns[h]] for s in parts], axis=0)
                here = request_mask(facts.ends, tokens, [facts.source[s] for s in parts], width)
                state = fold(state, [jnp.where(here, scores_of(queries, k_part), MASKED)], [v_part])
            again.append(state[1])
        send(again)


def prefill_kernel(plan, facts_ref, acc_ref, worst_ref, q_ref, *refs):
    width = plan.size
    k_refs, v_refs, refs = refs[:width], refs[width : 2 * width], refs[2 * width :]
    out_ref, done_ref, sem = refs
    tokens = q_ref.shape[0]
    half = tokens // 2
    facts = Facts(facts_ref, width)

    def bias_of(start, sources):
        return causal_bias(start, half, tokens, sources, facts.ends, facts.member, width)

    def write(h, start, acc):
        out = divided(acc)
        for g in range(HEADS_PER_KV):
            done_ref[start : start + half, span(h * Q_BLOCK + g * HEAD_SIZE, HEAD_SIZE)] = out[
                g * half : (g + 1) * half
            ]

    def copy_out(h):
        part = pl.ds(h * Q_BLOCK, Q_BLOCK)
        return pltpu.make_async_copy(done_ref.at[:, part], out_ref.at[:, part], sem.at[h])

    biases = [bias_of(start, facts.source[-1:]) for start in (0, half)]
    worst, least = worst_ref[...], None
    for h in range(KEY_VALUE_HEADS):
        columns = slice(h * HEAD_SIZE, (h + 1) * HEAD_SIZE)
        keys, values = k_refs[-1][:, columns], with_ones(v_refs[-1][:, columns])
        for start, bias in zip((0, half), biases):
            queries = stacked_heads(q_ref, slice(start, start + half), h * Q_BLOCK, HEADS_PER_KV)
            scores = scores_of(queries, keys).reshape(HEADS_PER_KV, half, tokens)
            exponents = (scores * EXPONENT + bias[None]).reshape(HEADS_PER_KV * half, tokens)
            worst = jnp.maximum(worst, peak(exponents))
            rows = slice(start * HEADS_PER_KV, (start + half) * HEADS_PER_KV)
            acc = acc_ref[h, rows, :] + product(jnp.exp2(exponents).astype(jnp.bfloat16), values)
            part = jnp.min(acc[:, HEAD_SIZE:].reshape(-1, 8, HEAD_SIZE), axis=0)
            least = part if least is None else jnp.minimum(least, part)
            write(h, start, acc)
        copy_out(h).start()
    redo = out_of_range(worst, least)
    for h in range(KEY_VALUE_HEADS):
        copy_out(h).wait()

    @pl.when(redo)
    def _():
        def step(h, carry):
            columns = span(h * HEAD_SIZE, HEAD_SIZE)
            for start in (0, half):
                queries = stacked_heads(q_ref, slice(start, start + half), h * Q_BLOCK, HEADS_PER_KV)
                state = None
                for parts in parts_in(width):
                    k_part = jnp.concatenate([k_refs[s][:, columns] for s in parts], axis=0)
                    v_part = jnp.concatenate([v_refs[s][:, columns] for s in parts], axis=0)
                    bias = bias_of(start, [facts.source[s] for s in parts])
                    scores = scores_of(queries, k_part).reshape(HEADS_PER_KV, half, bias.shape[1])
                    scores = (scores + bias[None]).reshape(HEADS_PER_KV * half, bias.shape[1])
                    state = fold(state, [scores], [v_part])
                write(h, start, state[1])
            return carry

        lax.fori_loop(0, KEY_VALUE_HEADS, step, 0)
        for h in range(KEY_VALUE_HEADS):
            copy_out(h).start()
        for h in range(KEY_VALUE_HEADS):
            copy_out(h).wait()


def cost(rows, keys, exps):
    return pl.CostEstimate(
        flops=32 * rows * keys * Q_WIDTH, bytes_accessed=4 * rows * Q_WIDTH, transcendentals=exps
    )


def call_first(plan, facts, query, blocks, keys, values):
    tokens, width = query.shape[0], plan.size
    rows = HEADS_PER_KV * tokens
    f32, bf16 = jnp.float32, jnp.bfloat16
    every = (width - 1) * tokens
    shapes = [
        jax.ShapeDtypeStruct((KEY_VALUE_HEADS, rows, 2 * HEAD_SIZE), f32),
        jax.ShapeDtypeStruct((KEY_VALUE_HEADS, STACKED, 2 * HEAD_SIZE), f32),
        jax.ShapeDtypeStruct((8, HEAD_SIZE), f32),
        jax.ShapeDtypeStruct((PADDED_ROWS, Q_WIDTH), bf16),
        jax.ShapeDtypeStruct((PADDED_ROWS, 2 * KV_WIDTH), bf16),
        jax.ShapeDtypeStruct((tokens, Q_WIDTH), bf16),
        jax.ShapeDtypeStruct((tokens, KV_WIDTH), bf16),
        jax.ShapeDtypeStruct((tokens, KV_WIDTH), bf16),
    ]
    return pl.pallas_call(
        lambda *refs: first_kernel(plan, len(blocks), *refs),
        in_specs=[SMEM] + [HBM] * 3 + [VMEM] * (len(blocks) + 2 * (width - 2)),
        out_specs=[VMEM] * len(shapes),
        out_shape=shapes,
        scratch_shapes=[pltpu.SemaphoreType.DMA((KEY_VALUE_HEADS + 2,))],
        compiler_params=pltpu.CompilerParams(vmem_limit_bytes=(28 + width) * MIB),
        cost_estimate=cost(tokens, every, tokens * every * QUERY_HEADS),
        name="first_shards",
    )(facts, query, keys[0], values[0], *keys[1:], *values[1:], *blocks)


def call_decode(plan, pd_size, facts, dec_acc, worst, rows, fresh, keys, values):
    tokens, width = keys[0].shape[0], plan.size
    return pl.pallas_call(
        lambda *refs: decode_kernel(plan, pd_size, *refs),
        in_specs=[SMEM] + [VMEM] * (4 + 2 * width),
        out_specs=VMEM,
        out_shape=jax.ShapeDtypeStruct((PADDED_ROWS, Q_WIDTH), jnp.bfloat16),
        compiler_params=pltpu.CompilerParams(vmem_limit_bytes=(28 + width) * MIB),
        cost_estimate=cost(PADDED_ROWS, tokens, PADDED_ROWS * tokens * QUERY_HEADS),
        name="last_shard_decode",
    )(facts, dec_acc, worst, rows, fresh, *keys, *values)


def call_prefill(plan, facts, acc, worst, query, keys, values):
    tokens, width = query.shape[0], plan.size
    return pl.pallas_call(
        lambda *refs: prefill_kernel(plan, *refs),
        in_specs=[SMEM] + [VMEM] * (3 + 2 * width),
        out_specs=ANY,
        out_shape=jax.ShapeDtypeStruct((tokens, Q_WIDTH), jnp.bfloat16),
        scratch_shapes=[
            pltpu.VMEM((tokens, Q_WIDTH), jnp.bfloat16),
            pltpu.SemaphoreType.DMA((KEY_VALUE_HEADS,)),
        ],
        compiler_params=pltpu.CompilerParams(vmem_limit_bytes=(28 + width) * MIB),
        cost_estimate=cost(tokens, tokens, tokens * tokens * QUERY_HEADS),
        name="last_shard_prefill",
    )(facts, acc, worst, query, *keys, *values)


def after(row, *arrays):
    for array in arrays:
        row = jnp.where(array[0, 0] == array[0, 0], row, 0)
    return row


def ring(size, step):
    return [(i, (i + step) % size) for i in range(size)]


def body(
    prompt_query,
    prompt_key,
    prompt_value,
    prompt_lengths,
    decode_slot,
    decoded_query,
    decoded_key,
    decoded_value,
):
    plan = Ring(lax.axis_size("tp"))
    pd_size = lax.axis_size("pd")
    own = jnp.concatenate([decoded_query, decoded_key, decoded_value], axis=2).reshape(
        DECODE_ROWS, Q_WIDTH + 2 * KV_WIDTH
    )
    facts = facts_row(plan, prompt_lengths, decode_slot)
    prompt_key, decoded_query = lax.optimization_barrier((prompt_key, decoded_query))
    prompt_value, own, facts = lax.optimization_barrier((prompt_value, own, facts))
    keys, values = [prompt_key], [prompt_value]
    for s in range(1, plan.size):
        if s == 2:
            keys[1], own = lax.optimization_barrier((keys[1], own))
        if s == plan.size - 1:
            facts = after(facts, keys[-1], values[-1])
            values[-1], facts = lax.optimization_barrier((values[-1], facts))
        keys.append(plan.step(keys[-1]))
        values.append(plan.step(values[-1]))
        if s == 2:
            blocks = [own] + [lax.ppermute(own, "pd", ring(pd_size, k)) for k in range(1, pd_size)]

    acc, dec_acc, worst, rows, fresh, query, key, value = call_first(
        plan, facts, prompt_query, blocks, keys[:-1], values[:-1]
    )
    keys[0], values[0] = key, value
    outgoing = call_decode(plan, pd_size, facts, dec_acc, worst, rows, fresh, keys, values)
    arrived = [outgoing[:DECODE_STEPS]]
    for k in range(1, pd_size):
        part = outgoing[k * DECODE_STEPS : (k + 1) * DECODE_STEPS]
        arrived.append(lax.ppermute(part, "pd", ring(pd_size, k)))
    pre_out = call_prefill(plan, facts, acc, worst, query, keys, values)

    from_block = facts[-GROUP_REQUESTS:]
    dec_out = jnp.zeros((GROUP_REQUESTS, DECODE_STEPS, Q_WIDTH), jnp.bfloat16)
    for k in range(pd_size):
        dec_out = jnp.where((from_block == k)[:, None, None], arrived[k][None], dec_out)
    return (pre_out, dec_out)


def solution(mesh):
    placed = (
        P(("rep", "pd", "tp"), None),
        P(("rep", "pd", "tp"), None),
        P(("rep", "pd", "tp"), None),
        P("rep", None),
        P("rep"),
        P(("rep", "pd"), None, None),
        P(("rep", "pd"), None, None),
        P(("rep", "pd"), None, None),
    )
    return jax.shard_map(
        body,
        mesh=mesh,
        in_specs=placed,
        out_specs=(P(("rep", "pd", "tp"), None), P(("rep", "pd"), None, None)),
        check_vma=False,
    )
```

```python
import math

import jax
import jax.numpy as jnp
from jax import lax
from jax.experimental import pallas as pl
from jax.experimental.pallas import tpu as pltpu
from jax.sharding import PartitionSpec as P

QUERY_HEADS = 32
KEY_VALUE_HEADS = 4
HEAD_SIZE = 128
PAGE = 16
GROUP_REQUESTS = 4
DECODE_STEPS = 2
HEADS_PER_KV = QUERY_HEADS // KEY_VALUE_HEADS
KV_WIDTH = KEY_VALUE_HEADS * HEAD_SIZE
Q_WIDTH = QUERY_HEADS * HEAD_SIZE
Q_BLOCK = HEADS_PER_KV * HEAD_SIZE
DECODE_ROWS = GROUP_REQUESTS * DECODE_STEPS
PADDED_ROWS = 16
STACKED = HEADS_PER_KV * PADDED_ROWS
MIB = 1024 * 1024

MASKED = -1e30
LIMIT = 60.0
EXPONENT = math.log2(math.e) / math.sqrt(HEAD_SIZE)

VMEM = pl.BlockSpec(memory_space=pltpu.VMEM)
SMEM = pl.BlockSpec(memory_space=pltpu.SMEM)
ANY = pl.BlockSpec(memory_space=pl.ANY)
HBM = pl.BlockSpec(memory_space=pltpu.HBM)


class Ring:
    def __init__(self, size):
        self.size = size
        order = [0] + list(range(1, size, 2)) + [i for i in range(size - 1, 0, -1) if i % 2 == 0]
        self.pairs = [(order[i], order[(i + 1) % size]) for i in range(size)]

    def step(self, array):
        return lax.ppermute(array, "tp", self.pairs)


def scores_of(queries, keys):
    return lax.dot_general(
        queries, keys, (((1,), (1,)), ((), ())), preferred_element_type=jnp.float32
    )


def product(left, right):
    return jnp.dot(left, right, preferred_element_type=jnp.float32)


def iota(shape, axis):
    return lax.broadcasted_iota(jnp.int32, shape, axis)


def span(start, size):
    if isinstance(start, int):
        return slice(start, start + size)
    return pl.ds(pl.multiple_of(start, size), size)


def with_ones(values):
    return jnp.concatenate([values, jnp.ones_like(values)], axis=1)


def page_position(offset, member, width):
    return (offset // PAGE * width + member) * PAGE + offset % PAGE


def key_positions(rows, sources, width):
    column = iota((1, len(sources) * rows), 1)
    part = column // rows
    source = jnp.zeros_like(column) + sources[0]
    for b in range(1, len(sources)):
        source = jnp.where(part == b, sources[b], source)
    return page_position(column - part * rows, source, width)


class Facts:
    def __init__(self, ref, width):
        self.width = width
        self.group, self.member = ref[0], ref[1]
        self.slots = [ref[2 + r] for r in range(GROUP_REQUESTS)]
        first = 2 + GROUP_REQUESTS
        self.ends = []
        total = jnp.int32(0)
        for r in range(GROUP_REQUESTS):
            total = total + ref[first + r] * PAGE
            self.ends.append(total)
        first += GROUP_REQUESTS
        self.source = [ref[first + s] for s in range(width)]


def facts_row(plan, lengths, slots):
    width, requests = plan.size, slots.shape[0]

    def kernel(lengths_ref, slots_ref, out_ref):
        group, member = lax.axis_index("pd"), lax.axis_index("tp")
        values = [group, member]
        values += [slots_ref[group * GROUP_REQUESTS + r] for r in range(GROUP_REQUESTS)]
        values += [lengths_ref[group, r] for r in range(GROUP_REQUESTS)]
        place = jnp.where(member % 2 == 1, (member + 1) // 2, width - member // 2)
        for s in range(width):
            before = (place + width - s) % width
            up = 2 * before - 1
            values.append(jnp.where(before == 0, 0, jnp.where(before <= width // 2, up, 2 * (width - before))))
        for i, value in enumerate(values):
            out_ref[i] = value.astype(jnp.int32)
        for q in range(requests):
            place = slots_ref[q] - group * GROUP_REQUESTS

            @pl.when((place >= 0) & (place < GROUP_REQUESTS))
            def _():
                out_ref[len(values) + place] = group ^ (q // GROUP_REQUESTS)

    length = 2 + 2 * GROUP_REQUESTS + width + GROUP_REQUESTS
    return pl.pallas_call(
        kernel,
        in_specs=[SMEM, SMEM],
        out_specs=SMEM,
        out_shape=jax.ShapeDtypeStruct((length,), jnp.int32),
        cost_estimate=pl.CostEstimate(flops=5 * 10**9, bytes_accessed=0, transcendentals=0),
        name="facts",
    )(lengths, slots)


def causal_bias(start, rows, keys, sources, ends, member, width):
    qpos = page_position(start + iota((rows, 1), 0), member, width)
    low = jnp.zeros_like(qpos)
    for end in ends:
        low = jnp.where(qpos >= end, end, low)
    kpos = key_positions(keys, sources, width)
    return jnp.where((kpos >= low) & (kpos <= qpos), 0.0, MASKED)


def request_mask(ends, keys, sources, width):
    request = iota((STACKED, 1), 0) % PADDED_ROWS // DECODE_STEPS
    low = jnp.zeros_like(request)
    high = jnp.zeros_like(request) + ends[0]
    for r in range(1, GROUP_REQUESTS):
        low = jnp.where(request == r, ends[r - 1], low)
        high = jnp.where(request == r, ends[r], high)
    kpos = key_positions(keys, sources, width)
    return (kpos >= low) & (kpos < high)


def stacked_heads(ref, rows, first, count):
    return jnp.concatenate(
        [ref[rows, span(first + i * HEAD_SIZE, HEAD_SIZE)] for i in range(count)], axis=0
    )


def each_kv_head(width, step):
    if width <= 8:
        for h in range(KEY_VALUE_HEADS):
            step(h)
    else:
        lax.fori_loop(0, KEY_VALUE_HEADS, lambda h, c: (step(h), c)[1], 0)


def peak(exponents):
    return jnp.max(exponents.reshape(-1, 8, exponents.shape[-1]), axis=0)


def picked_rows(facts, pd_size, block_refs):
    row = iota((PADDED_ROWS, DECODE_ROWS), 0)
    column = iota((PADDED_ROWS, DECODE_ROWS), 1)
    total = None
    for k in range(pd_size):
        pick = column < 0
        for r in range(GROUP_REQUESTS):
            slot = facts.slots[r]
            first = jnp.where(facts.group ^ (slot // GROUP_REQUESTS) == k, slot % GROUP_REQUESTS * DECODE_STEPS, -DECODE_ROWS * 4)
            pick = pick | ((row // DECODE_STEPS == r) & (column == first + row - r * DECODE_STEPS))
        part = product(pick.astype(jnp.float32).astype(jnp.bfloat16), block_refs[k][...])
        total = part if total is None else total + part
    return total.astype(jnp.bfloat16)


def pick_matrix(facts):
    row = iota((PADDED_ROWS, PADDED_ROWS), 0)
    column = iota((PADDED_ROWS, PADDED_ROWS), 1)
    pick = column < 0
    for r in range(GROUP_REQUESTS):
        ahead = facts.group ^ (facts.slots[r] // GROUP_REQUESTS)
        pick = pick | (
            (column // DECODE_STEPS == r) & (row == ahead * DECODE_STEPS + column - r * DECODE_STEPS)
        )
    return pick.astype(jnp.float32).astype(jnp.bfloat16)


def fresh_mask():
    row = iota((STACKED, PADDED_ROWS), 0) % PADDED_ROWS
    column = iota((STACKED, PADDED_ROWS), 1)
    return (column // DECODE_STEPS == row // DECODE_STEPS) & (
        column % DECODE_STEPS <= row % DECODE_STEPS
    )


def first_kernel(plan, pd_size, facts_ref, maxima_ref, q_ref, *refs):
    width = plan.size
    k_refs, v_refs, refs = refs[: width - 1], refs[width - 1 : 2 * width - 2], refs[2 * width - 2 :]
    block_refs, refs = refs[:pd_size], refs[pd_size:]
    acc_ref, bias_ref, dec_acc_ref, dec_bias_ref, worst_ref, queries_ref, fresh_ref, pick_ref = refs
    tokens = q_ref.shape[0]
    half = tokens // 2
    facts = Facts(facts_ref, width)
    sources = facts.source[:-1]
    pick_ref[...] = pick_matrix(facts)
    for s in range(width):
        bias_ref[s] = causal_bias(0, tokens, tokens, facts.source[s : s + 1], facts.ends, facts.member, width)
        dec_bias_ref[s] = jnp.where(
            request_mask(facts.ends, tokens, facts.source[s : s + 1], width), 0.0, MASKED
        )
    rows = picked_rows(facts, pd_size, block_refs)
    queries_ref[...] = rows[:, :Q_WIDTH]
    fresh_ref[...] = rows[:, Q_WIDTH:]
    worst_ref[...] = maxima_ref[...]
    new_mask = fresh_mask()
    mask = request_mask(facts.ends, tokens, sources, width)
    spans = ((0, half), (half, tokens))
    biases = [
        causal_bias(s, half, keys, sources, facts.ends, facts.member, width) for s, keys in spans
    ]
    together = max(1, min(HEADS_PER_KV, HEADS_PER_KV * 4 // width))

    def weigh(exponents):
        top = jnp.max(peak(exponents), axis=1, keepdims=True)
        worst_ref[...] = jnp.maximum(worst_ref[...], top)
        return jnp.exp2(exponents).astype(jnp.bfloat16)

    def step(h):
        columns = span(h * HEAD_SIZE, HEAD_SIZE)
        first = h * Q_BLOCK
        queries = stacked_heads(queries_ref, slice(None), first, HEADS_PER_KV)
        k_all = jnp.concatenate([ref[:, columns] for ref in k_refs], axis=0)
        v_all = with_ones(jnp.concatenate([ref[:, columns] for ref in v_refs], axis=0))
        new_scores = scores_of(queries, fresh_ref[:, columns]) * EXPONENT
        new_weights = weigh(jnp.where(new_mask, new_scores, MASKED))
        new_values = fresh_ref[:, span(KV_WIDTH + h * HEAD_SIZE, HEAD_SIZE)]
        weights = weigh(jnp.where(mask, scores_of(queries, k_all) * EXPONENT, MASKED))
        dec_acc_ref[h] = product(weights, v_all) + product(new_weights, with_ones(new_values))
        for (start, keys), bias in zip(spans, biases):
            if keys < tokens:
                k_part = jnp.concatenate([ref[:keys, columns] for ref in k_refs], axis=0)
                v_part = with_ones(jnp.concatenate([ref[:keys, columns] for ref in v_refs], axis=0))
            else:
                k_part, v_part = k_all, v_all
            for g in range(0, HEADS_PER_KV, together):
                queries = stacked_heads(
                    q_ref, slice(start, start + half), first + g * HEAD_SIZE, together
                )
                scores = scores_of(queries, k_part).reshape(together, half, bias.shape[1])
                exponents = (scores * EXPONENT + bias[None]).reshape(together * half, bias.shape[1])
                rows = slice(
                    start * HEADS_PER_KV + g * half, start * HEADS_PER_KV + (g + together) * half
                )
                acc_ref[h, rows, :] = product(weigh(exponents), v_part)

    each_kv_head(width, step)


def divided(acc):
    return (acc[:, :HEAD_SIZE] * pl.reciprocal(acc[:, HEAD_SIZE:], approx=True)).astype(jnp.bfloat16)


def fold(state, scores_list, values_list):
    top = None if state is None else state[0]
    for scores in scores_list:
        part = jnp.max(scores, axis=1, keepdims=True)
        top = part if top is None else jnp.maximum(top, part)
    acc = None
    for scores, values in zip(scores_list, values_list):
        weights = jnp.exp2((scores - top) * EXPONENT).astype(jnp.bfloat16)
        part = product(weights, with_ones(values))
        acc = part if acc is None else acc + part
    if state is not None:
        acc = acc + state[1] * jnp.exp2((state[0] - top) * EXPONENT)
    return top, acc


def parts_in(width):
    return [range(c, min(c + 4, width)) for c in range(0, width, 4)]


def out_of_range(worst, least):
    return (jnp.max(worst) > LIMIT) | (jnp.min(least) < 2.0**-LIMIT)


def decode_kernel(plan, acc_ref, bias_ref, worst_ref, queries_ref, fresh_ref, pick_ref, *refs):
    width = plan.size
    k_refs, v_refs, (out_ref,) = refs[:width], refs[width : 2 * width], refs[2 * width :]
    heads = range(KEY_VALUE_HEADS)
    columns = [slice(h * HEAD_SIZE, (h + 1) * HEAD_SIZE) for h in heads]

    def queries_of(h):
        return stacked_heads(queries_ref, slice(None), h * Q_BLOCK, HEADS_PER_KV)

    def send(acc):
        out = [divided(a) for a in acc]
        out = jnp.concatenate(
            [o[g * PADDED_ROWS : (g + 1) * PADDED_ROWS] for o in out for g in range(HEADS_PER_KV)], axis=1
        )
        out_ref[...] = product(pick_ref[...], out).astype(jnp.bfloat16)

    exponents = [
        scores_of(queries_of(h), k_refs[-1][:, columns[h]]) * EXPONENT + bias_ref[width - 1]
        for h in heads
    ]
    acc = [
        acc_ref[h] + product(jnp.exp2(exponents[h]).astype(jnp.bfloat16), with_ones(v_refs[-1][:, columns[h]]))
        for h in heads
    ]
    send(acc)
    worst, least = worst_ref[...], None
    for h in heads:
        worst = jnp.maximum(worst, peak(exponents[h]))
        part = jnp.min(acc[h][:, HEAD_SIZE:].reshape(-1, 8, HEAD_SIZE), axis=0)
        least = part if least is None else jnp.minimum(least, part)

    @pl.when(out_of_range(worst, least))
    def _():
        new_mask = fresh_mask()
        again = []
        for h in heads:
            queries = queries_of(h)
            scores = jnp.where(new_mask, scores_of(queries, fresh_ref[:, columns[h]]), MASKED)
            new_columns = slice(KV_WIDTH + h * HEAD_SIZE, KV_WIDTH + (h + 1) * HEAD_SIZE)
            state = fold(None, [scores], [fresh_ref[:, new_columns]])
            for parts in parts_in(width):
                k_part = jnp.concatenate([k_refs[s][:, columns[h]] for s in parts], axis=0)
                v_part = jnp.concatenate([v_refs[s][:, columns[h]] for s in parts], axis=0)
                bias = jnp.concatenate([bias_ref[s] for s in parts], axis=1)
                state = fold(state, [scores_of(queries, k_part) + bias], [v_part])
            again.append(state[1])
        send(again)


def prefill_kernel(plan, acc_ref, bias_ref, worst_ref, q_ref, *refs):
    width = plan.size
    k_refs, v_refs, refs = refs[:width], refs[width : 2 * width], refs[2 * width :]
    out_ref, done_ref, sem = refs
    tokens = q_ref.shape[0]
    half = tokens // 2
    def write(h, start, acc):
        out = divided(acc)
        for g in range(HEADS_PER_KV):
            done_ref[start : start + half, span(h * Q_BLOCK + g * HEAD_SIZE, HEAD_SIZE)] = out[
                g * half : (g + 1) * half
            ]

    def copy_out(h):
        part = pl.ds(h * Q_BLOCK, Q_BLOCK)
        return pltpu.make_async_copy(done_ref.at[:, part], out_ref.at[:, part], sem.at[h])

    biases = [bias_ref[width - 1, start : start + half, :] for start in (0, half)]
    worst, least = worst_ref[...], None
    for h in range(KEY_VALUE_HEADS):
        columns = slice(h * HEAD_SIZE, (h + 1) * HEAD_SIZE)
        keys, values = k_refs[-1][:, columns], with_ones(v_refs[-1][:, columns])
        for start, bias in zip((0, half), biases):
            queries = stacked_heads(q_ref, slice(start, start + half), h * Q_BLOCK, HEADS_PER_KV)
            scores = scores_of(queries, keys).reshape(HEADS_PER_KV, half, tokens)
            exponents = (scores * EXPONENT + bias[None]).reshape(HEADS_PER_KV * half, tokens)
            worst = jnp.maximum(worst, peak(exponents))
            rows = slice(start * HEADS_PER_KV, (start + half) * HEADS_PER_KV)
            acc = acc_ref[h, rows, :] + product(jnp.exp2(exponents).astype(jnp.bfloat16), values)
            part = jnp.min(acc[:, HEAD_SIZE:].reshape(-1, 8, HEAD_SIZE), axis=0)
            least = part if least is None else jnp.minimum(least, part)
            write(h, start, acc)
        copy_out(h).start()
    redo = out_of_range(worst, least)
    for h in range(KEY_VALUE_HEADS):
        copy_out(h).wait()

    @pl.when(redo)
    def _():
        def step(h, carry):
            columns = span(h * HEAD_SIZE, HEAD_SIZE)
            for start in (0, half):
                queries = stacked_heads(q_ref, slice(start, start + half), h * Q_BLOCK, HEADS_PER_KV)
                state = None
                for parts in parts_in(width):
                    k_part = jnp.concatenate([k_refs[s][:, columns] for s in parts], axis=0)
                    v_part = jnp.concatenate([v_refs[s][:, columns] for s in parts], axis=0)
                    bias = jnp.concatenate([bias_ref[s, start : start + half, :] for s in parts], axis=1)
                    scores = scores_of(queries, k_part).reshape(HEADS_PER_KV, half, bias.shape[1])
                    scores = (scores + bias[None]).reshape(HEADS_PER_KV * half, bias.shape[1])
                    state = fold(state, [scores], [v_part])
                write(h, start, state[1])
            return carry

        lax.fori_loop(0, KEY_VALUE_HEADS, step, 0)
        for h in range(KEY_VALUE_HEADS):
            copy_out(h).start()
        for h in range(KEY_VALUE_HEADS):
            copy_out(h).wait()


def cost(rows, keys, exps):
    return pl.CostEstimate(
        flops=32 * rows * keys * Q_WIDTH, bytes_accessed=4 * rows * Q_WIDTH, transcendentals=exps
    )


def call_first(plan, facts, maxima, query, blocks, keys, values):
    tokens, width = query.shape[0], plan.size
    rows = HEADS_PER_KV * tokens
    f32, bf16 = jnp.float32, jnp.bfloat16
    every = (width - 1) * tokens
    shapes = [
        jax.ShapeDtypeStruct((KEY_VALUE_HEADS, rows, 2 * HEAD_SIZE), f32),
        jax.ShapeDtypeStruct((width, tokens, tokens), f32),
        jax.ShapeDtypeStruct((KEY_VALUE_HEADS, STACKED, 2 * HEAD_SIZE), f32),
        jax.ShapeDtypeStruct((width, STACKED, tokens), f32),
        jax.ShapeDtypeStruct((8, HEAD_SIZE), f32),
        jax.ShapeDtypeStruct((PADDED_ROWS, Q_WIDTH), bf16),
        jax.ShapeDtypeStruct((PADDED_ROWS, 2 * KV_WIDTH), bf16),
        jax.ShapeDtypeStruct((PADDED_ROWS, PADDED_ROWS), bf16),
    ]
    return pl.pallas_call(
        lambda *refs: first_kernel(plan, len(blocks), *refs),
        in_specs=[SMEM] + [VMEM] * (2 + len(blocks) + 2 * (width - 1)),
        out_specs=[VMEM] * len(shapes),
        out_shape=shapes,
        compiler_params=pltpu.CompilerParams(vmem_limit_bytes=(28 + width) * MIB),
        cost_estimate=cost(tokens, every, tokens * every * QUERY_HEADS),
        name="first_shards",
    )(facts, maxima, query, *keys, *values, *blocks)


def call_decode(plan, state, keys, values):
    tokens, width = keys[0].shape[0], plan.size
    return pl.pallas_call(
        lambda *refs: decode_kernel(plan, *refs),
        in_specs=[VMEM] * (6 + 2 * width),
        out_specs=VMEM,
        out_shape=jax.ShapeDtypeStruct((PADDED_ROWS, Q_WIDTH), jnp.bfloat16),
        compiler_params=pltpu.CompilerParams(vmem_limit_bytes=(28 + width) * MIB),
        cost_estimate=cost(PADDED_ROWS, tokens, PADDED_ROWS * tokens * QUERY_HEADS),
        name="last_shard_decode",
    )(*state[2:], *keys, *values)


def call_prefill(plan, state, query, keys, values):
    tokens, width = query.shape[0], plan.size
    return pl.pallas_call(
        lambda *refs: prefill_kernel(plan, *refs),
        in_specs=[VMEM] * (4 + 2 * width),
        out_specs=ANY,
        out_shape=jax.ShapeDtypeStruct((tokens, Q_WIDTH), jnp.bfloat16),
        scratch_shapes=[
            pltpu.VMEM((tokens, Q_WIDTH), jnp.bfloat16),
            pltpu.SemaphoreType.DMA((KEY_VALUE_HEADS,)),
        ],
        compiler_params=pltpu.CompilerParams(vmem_limit_bytes=(28 + width) * MIB),
        cost_estimate=cost(tokens, tokens, tokens * tokens * QUERY_HEADS),
        name="last_shard_prefill",
    )(*state[:2], state[4], query, *keys, *values)


def start_maxima(*arrays):
    def kernel(*refs):
        refs[-1][...] = jnp.full((8, HEAD_SIZE), MASKED, jnp.float32)

    return pl.pallas_call(
        kernel,
        in_specs=[VMEM] * len(arrays),
        out_specs=VMEM,
        out_shape=jax.ShapeDtypeStruct((8, HEAD_SIZE), jnp.float32),
        cost_estimate=pl.CostEstimate(flops=5 * 10**9, bytes_accessed=0, transcendentals=0),
        name="start_maxima",
    )(*arrays)


def paired(array, k):
    return lax.ppermute(array, "pd", [(g, g ^ k) for g in range(lax.axis_size("pd"))])


def body(
    prompt_query,
    prompt_key,
    prompt_value,
    prompt_lengths,
    decode_slot,
    decoded_query,
    decoded_key,
    decoded_value,
):
    plan = Ring(lax.axis_size("tp"))
    pd_size = lax.axis_size("pd")
    own = jnp.concatenate([decoded_query, decoded_key, decoded_value], axis=2).reshape(
        DECODE_ROWS, Q_WIDTH + 2 * KV_WIDTH
    )
    facts = facts_row(plan, prompt_lengths, decode_slot)
    prompt_key, decoded_query = lax.optimization_barrier((prompt_key, decoded_query))
    prompt_value, own, facts = lax.optimization_barrier((prompt_value, own, facts))
    keys, values, maxima = [prompt_key], [prompt_value], None
    for s in range(1, plan.size):
        if s == 2:
            keys[1], own = lax.optimization_barrier((keys[1], own))
        if s == plan.size - 1:
            maxima = start_maxima(keys[-1], values[-1])
            values[-1], maxima = lax.optimization_barrier((values[-1], maxima))
        keys.append(plan.step(keys[-1]))
        values.append(plan.step(values[-1]))
        if s == 2:
            blocks = [own] + [paired(own, k) for k in range(1, pd_size)]

    state = call_first(plan, facts, maxima, prompt_query, blocks, keys[:-1], values[:-1])
    outgoing = call_decode(plan, state, keys, values)
    arrived = [outgoing[:DECODE_STEPS]]
    for k in range(1, pd_size):
        arrived.append(paired(outgoing[k * DECODE_STEPS : (k + 1) * DECODE_STEPS], k))
    pre_out = call_prefill(plan, state, prompt_query, keys, values)

    from_block = facts[-GROUP_REQUESTS:]
    dec_out = jnp.zeros((GROUP_REQUESTS, DECODE_STEPS, Q_WIDTH), jnp.bfloat16)
    for k in range(pd_size):
        dec_out = jnp.where((from_block == k)[:, None, None], arrived[k][None], dec_out)
    return (pre_out, dec_out)


def solution(mesh):
    placed = (
        P(("rep", "pd", "tp"), None),
        P(("rep", "pd", "tp"), None),
        P(("rep", "pd", "tp"), None),
        P("rep", None),
        P("rep"),
        P(("rep", "pd"), None, None),
        P(("rep", "pd"), None, None),
        P(("rep", "pd"), None, None),
    )
    return jax.shard_map(
        body,
        mesh=mesh,
        in_specs=placed,
        out_specs=(P(("rep", "pd", "tp"), None), P(("rep", "pd"), None, None)),
        check_vma=False,
    )
```

```python
import math

import jax
import jax.numpy as jnp
from jax import lax
from jax.experimental import pallas as pl
from jax.experimental.pallas import tpu as pltpu
from jax.sharding import PartitionSpec as P

QUERY_HEADS = 32
KEY_VALUE_HEADS = 4
HEAD_SIZE = 128
PAGE = 16
GROUP_REQUESTS = 4
DECODE_STEPS = 2
HEADS_PER_KV = QUERY_HEADS // KEY_VALUE_HEADS
KV_WIDTH = KEY_VALUE_HEADS * HEAD_SIZE
Q_WIDTH = QUERY_HEADS * HEAD_SIZE
Q_BLOCK = HEADS_PER_KV * HEAD_SIZE
DECODE_ROWS = GROUP_REQUESTS * DECODE_STEPS
PADDED_ROWS = 16
STACKED = HEADS_PER_KV * PADDED_ROWS
MIB = 1024 * 1024

MASKED = -1e30
LIMIT = 60.0
EXPONENT = math.log2(math.e) / math.sqrt(HEAD_SIZE)

VMEM = pl.BlockSpec(memory_space=pltpu.VMEM)
SMEM = pl.BlockSpec(memory_space=pltpu.SMEM)
ANY = pl.BlockSpec(memory_space=pl.ANY)
HBM = pl.BlockSpec(memory_space=pltpu.HBM)


class Ring:
    def __init__(self, size):
        self.size = size
        order = [0] + list(range(1, size, 2)) + [i for i in range(size - 1, 0, -1) if i % 2 == 0]
        self.pairs = [(order[i], order[(i + 1) % size]) for i in range(size)]

    def step(self, array):
        return lax.ppermute(array, "tp", self.pairs)


def scores_of(queries, keys):
    return lax.dot_general(
        queries, keys, (((1,), (1,)), ((), ())), preferred_element_type=jnp.float32
    )


def product(left, right):
    return jnp.dot(left, right, preferred_element_type=jnp.float32)


def iota(shape, axis):
    return lax.broadcasted_iota(jnp.int32, shape, axis)


def span(start, size):
    if isinstance(start, int):
        return slice(start, start + size)
    return pl.ds(pl.multiple_of(start, size), size)


def with_ones(values):
    return jnp.concatenate([values, jnp.ones_like(values)], axis=1)


def page_position(offset, member, width):
    return (offset // PAGE * width + member) * PAGE + offset % PAGE


def key_positions(rows, sources, width):
    column = iota((1, len(sources) * rows), 1)
    part = column // rows
    source = jnp.zeros_like(column) + sources[0]
    for b in range(1, len(sources)):
        source = jnp.where(part == b, sources[b], source)
    return page_position(column - part * rows, source, width)


class Facts:
    def __init__(self, ref, width):
        self.width = width
        self.group, self.member = ref[0], ref[1]
        self.slots = [ref[2 + r] for r in range(GROUP_REQUESTS)]
        first = 2 + GROUP_REQUESTS
        self.ends = []
        total = jnp.int32(0)
        for r in range(GROUP_REQUESTS):
            total = total + ref[first + r] * PAGE
            self.ends.append(total)
        first += GROUP_REQUESTS
        self.source = [ref[first + s] for s in range(width)]


def facts_row(plan, lengths, slots):
    width, requests = plan.size, slots.shape[0]

    def kernel(lengths_ref, slots_ref, out_ref):
        group, member = lax.axis_index("pd"), lax.axis_index("tp")
        values = [group, member]
        values += [slots_ref[group * GROUP_REQUESTS + r] for r in range(GROUP_REQUESTS)]
        values += [lengths_ref[group, r] for r in range(GROUP_REQUESTS)]
        place = jnp.where(member % 2 == 1, (member + 1) // 2, width - member // 2)
        for s in range(width):
            before = (place + width - s) % width
            up = 2 * before - 1
            values.append(jnp.where(before == 0, 0, jnp.where(before <= width // 2, up, 2 * (width - before))))
        for i, value in enumerate(values):
            out_ref[i] = value.astype(jnp.int32)
        for q in range(requests):
            place = slots_ref[q] - group * GROUP_REQUESTS

            @pl.when((place >= 0) & (place < GROUP_REQUESTS))
            def _():
                out_ref[len(values) + place] = group ^ (q // GROUP_REQUESTS)

    length = 2 + 2 * GROUP_REQUESTS + width + GROUP_REQUESTS
    return pl.pallas_call(
        kernel,
        in_specs=[SMEM, SMEM],
        out_specs=SMEM,
        out_shape=jax.ShapeDtypeStruct((length,), jnp.int32),
        cost_estimate=pl.CostEstimate(flops=5 * 10**9, bytes_accessed=0, transcendentals=0),
        compiler_params=pltpu.CompilerParams(vmem_limit_bytes=MIB),
        name="facts",
    )(lengths, slots)


def causal_bias(start, rows, keys, sources, ends, member, width):
    qpos = page_position(start + iota((rows, 1), 0), member, width)
    low = jnp.zeros_like(qpos)
    for end in ends:
        low = jnp.where(qpos >= end, end, low)
    kpos = key_positions(keys, sources, width)
    return jnp.where((kpos >= low) & (kpos <= qpos), 0.0, MASKED)


def request_mask(ends, keys, sources, width):
    request = iota((STACKED, 1), 0) % PADDED_ROWS // DECODE_STEPS
    low = jnp.zeros_like(request)
    high = jnp.zeros_like(request) + ends[0]
    for r in range(1, GROUP_REQUESTS):
        low = jnp.where(request == r, ends[r - 1], low)
        high = jnp.where(request == r, ends[r], high)
    kpos = key_positions(keys, sources, width)
    return (kpos >= low) & (kpos < high)


def stacked_heads(ref, rows, first, count):
    return jnp.concatenate(
        [ref[rows, span(first + i * HEAD_SIZE, HEAD_SIZE)] for i in range(count)], axis=0
    )


def each_kv_head(width, step):
    if width <= 8:
        for h in range(KEY_VALUE_HEADS):
            step(h)
    else:
        lax.fori_loop(0, KEY_VALUE_HEADS, lambda h, c: (step(h), c)[1], 0)


def peak(exponents):
    return jnp.max(exponents.reshape(-1, 8, exponents.shape[-1]), axis=0)


def picked_rows(facts, pd_size, block_refs):
    row = iota((PADDED_ROWS, DECODE_ROWS), 0)
    column = iota((PADDED_ROWS, DECODE_ROWS), 1)
    total = None
    for k in range(pd_size):
        pick = column < 0
        for r in range(GROUP_REQUESTS):
            slot = facts.slots[r]
            first = jnp.where(facts.group ^ (slot // GROUP_REQUESTS) == k, slot % GROUP_REQUESTS * DECODE_STEPS, -DECODE_ROWS * 4)
            pick = pick | ((row // DECODE_STEPS == r) & (column == first + row - r * DECODE_STEPS))
        part = product(pick.astype(jnp.float32).astype(jnp.bfloat16), block_refs[k][...])
        total = part if total is None else total + part
    return total.astype(jnp.bfloat16)


def pick_matrix(facts):
    row = iota((PADDED_ROWS, PADDED_ROWS), 0)
    column = iota((PADDED_ROWS, PADDED_ROWS), 1)
    pick = column < 0
    for r in range(GROUP_REQUESTS):
        ahead = facts.group ^ (facts.slots[r] // GROUP_REQUESTS)
        pick = pick | (
            (column // DECODE_STEPS == r) & (row == ahead * DECODE_STEPS + column - r * DECODE_STEPS)
        )
    return pick.astype(jnp.float32).astype(jnp.bfloat16)


def fresh_mask():
    row = iota((STACKED, PADDED_ROWS), 0) % PADDED_ROWS
    column = iota((STACKED, PADDED_ROWS), 1)
    return (column // DECODE_STEPS == row // DECODE_STEPS) & (
        column % DECODE_STEPS <= row % DECODE_STEPS
    )


def first_kernel(plan, pd_size, facts_ref, maxima_ref, q_ref, *refs):
    width = plan.size
    k_refs, v_refs, refs = refs[: width - 1], refs[width - 1 : 2 * width - 2], refs[2 * width - 2 :]
    block_refs, refs = refs[:pd_size], refs[pd_size:]
    acc_ref, bias_ref, dec_acc_ref, dec_bias_ref, worst_ref, queries_ref, fresh_ref, pick_ref = refs
    tokens = q_ref.shape[0]
    half = tokens // 2
    facts = Facts(facts_ref, width)
    sources = facts.source[:-1]
    pick_ref[...] = pick_matrix(facts)
    for s in range(width):
        bias_ref[s] = causal_bias(0, tokens, tokens, facts.source[s : s + 1], facts.ends, facts.member, width)
        dec_bias_ref[s] = jnp.where(
            request_mask(facts.ends, tokens, facts.source[s : s + 1], width), 0.0, MASKED
        )
    rows = picked_rows(facts, pd_size, block_refs)
    queries_ref[...] = rows[:, :Q_WIDTH]
    fresh_ref[...] = rows[:, Q_WIDTH:]
    worst_ref[...] = maxima_ref[...]
    new_mask = fresh_mask()
    mask = request_mask(facts.ends, tokens, sources, width)
    spans = ((0, half), (half, tokens))
    biases = [
        causal_bias(s, half, keys, sources, facts.ends, facts.member, width) for s, keys in spans
    ]
    together = max(1, min(HEADS_PER_KV, HEADS_PER_KV * 4 // width))

    def weigh(exponents):
        top = jnp.max(peak(exponents), axis=1, keepdims=True)
        worst_ref[...] = jnp.maximum(worst_ref[...], top)
        return jnp.exp2(exponents).astype(jnp.bfloat16)

    def step(h):
        columns = span(h * HEAD_SIZE, HEAD_SIZE)
        first = h * Q_BLOCK
        queries = stacked_heads(queries_ref, slice(None), first, HEADS_PER_KV)
        k_all = jnp.concatenate([ref[:, columns] for ref in k_refs], axis=0)
        v_all = with_ones(jnp.concatenate([ref[:, columns] for ref in v_refs], axis=0))
        new_scores = scores_of(queries, fresh_ref[:, columns]) * EXPONENT
        new_weights = weigh(jnp.where(new_mask, new_scores, MASKED))
        new_values = fresh_ref[:, span(KV_WIDTH + h * HEAD_SIZE, HEAD_SIZE)]
        weights = weigh(jnp.where(mask, scores_of(queries, k_all) * EXPONENT, MASKED))
        dec_acc_ref[h] = product(weights, v_all) + product(new_weights, with_ones(new_values))
        for (start, keys), bias in zip(spans, biases):
            if keys < tokens:
                k_part = jnp.concatenate([ref[:keys, columns] for ref in k_refs], axis=0)
                v_part = with_ones(jnp.concatenate([ref[:keys, columns] for ref in v_refs], axis=0))
            else:
                k_part, v_part = k_all, v_all
            for g in range(0, HEADS_PER_KV, together):
                queries = stacked_heads(
                    q_ref, slice(start, start + half), first + g * HEAD_SIZE, together
                )
                scores = scores_of(queries, k_part).reshape(together, half, bias.shape[1])
                exponents = (scores * EXPONENT + bias[None]).reshape(together * half, bias.shape[1])
                rows = slice(
                    start * HEADS_PER_KV + g * half, start * HEADS_PER_KV + (g + together) * half
                )
                acc_ref[h, rows, :] = product(weigh(exponents), v_part)

    each_kv_head(width, step)


def divided(acc):
    return (acc[:, :HEAD_SIZE] * pl.reciprocal(acc[:, HEAD_SIZE:], approx=True)).astype(jnp.bfloat16)


def fold(state, scores_list, values_list):
    top = None if state is None else state[0]
    for scores in scores_list:
        part = jnp.max(scores, axis=1, keepdims=True)
        top = part if top is None else jnp.maximum(top, part)
    acc = None
    for scores, values in zip(scores_list, values_list):
        weights = jnp.exp2((scores - top) * EXPONENT).astype(jnp.bfloat16)
        part = product(weights, with_ones(values))
        acc = part if acc is None else acc + part
    if state is not None:
        acc = acc + state[1] * jnp.exp2((state[0] - top) * EXPONENT)
    return top, acc


def parts_in(width):
    return [range(c, min(c + 4, width)) for c in range(0, width, 4)]


def out_of_range(worst, least):
    return (jnp.max(worst) > LIMIT) | (jnp.min(least) < 2.0**-LIMIT)


def decode_kernel(plan, acc_ref, bias_ref, worst_ref, queries_ref, fresh_ref, pick_ref, *refs):
    width = plan.size
    k_refs, v_refs, (out_ref,) = refs[:width], refs[width : 2 * width], refs[2 * width :]
    heads = range(KEY_VALUE_HEADS)
    columns = [slice(h * HEAD_SIZE, (h + 1) * HEAD_SIZE) for h in heads]

    def queries_of(h):
        return stacked_heads(queries_ref, slice(None), h * Q_BLOCK, HEADS_PER_KV)

    def send(acc):
        out = [divided(a) for a in acc]
        out = jnp.concatenate(
            [o[g * PADDED_ROWS : (g + 1) * PADDED_ROWS] for o in out for g in range(HEADS_PER_KV)], axis=1
        )
        out_ref[...] = product(pick_ref[...], out).astype(jnp.bfloat16)

    exponents = [
        scores_of(queries_of(h), k_refs[-1][:, columns[h]]) * EXPONENT + bias_ref[width - 1]
        for h in heads
    ]
    acc = [
        acc_ref[h] + product(jnp.exp2(exponents[h]).astype(jnp.bfloat16), with_ones(v_refs[-1][:, columns[h]]))
        for h in heads
    ]
    send(acc)
    worst, least = worst_ref[...], None
    for h in heads:
        worst = jnp.maximum(worst, peak(exponents[h]))
        part = jnp.min(acc[h][:, HEAD_SIZE:].reshape(-1, 8, HEAD_SIZE), axis=0)
        least = part if least is None else jnp.minimum(least, part)

    @pl.when(out_of_range(worst, least))
    def _():
        new_mask = fresh_mask()
        again = []
        for h in heads:
            queries = queries_of(h)
            scores = jnp.where(new_mask, scores_of(queries, fresh_ref[:, columns[h]]), MASKED)
            new_columns = slice(KV_WIDTH + h * HEAD_SIZE, KV_WIDTH + (h + 1) * HEAD_SIZE)
            state = fold(None, [scores], [fresh_ref[:, new_columns]])
            for parts in parts_in(width):
                k_part = jnp.concatenate([k_refs[s][:, columns[h]] for s in parts], axis=0)
                v_part = jnp.concatenate([v_refs[s][:, columns[h]] for s in parts], axis=0)
                bias = jnp.concatenate([bias_ref[s] for s in parts], axis=1)
                state = fold(state, [scores_of(queries, k_part) + bias], [v_part])
            again.append(state[1])
        send(again)


def prefill_kernel(plan, acc_ref, bias_ref, worst_ref, q_ref, *refs):
    width = plan.size
    k_refs, v_refs, refs = refs[:width], refs[width : 2 * width], refs[2 * width :]
    out_ref, done_ref, sem = refs
    tokens = q_ref.shape[0]
    half = tokens // 2
    def write(h, start, acc):
        out = divided(acc)
        for g in range(HEADS_PER_KV):
            done_ref[start : start + half, span(h * Q_BLOCK + g * HEAD_SIZE, HEAD_SIZE)] = out[
                g * half : (g + 1) * half
            ]

    def copy_out(h):
        part = pl.ds(h * Q_BLOCK, Q_BLOCK)
        return pltpu.make_async_copy(done_ref.at[:, part], out_ref.at[:, part], sem.at[h])

    biases = [bias_ref[width - 1, start : start + half, :] for start in (0, half)]
    worst, least = worst_ref[...], None
    for h in range(KEY_VALUE_HEADS):
        columns = slice(h * HEAD_SIZE, (h + 1) * HEAD_SIZE)
        keys, values = k_refs[-1][:, columns], with_ones(v_refs[-1][:, columns])
        for start, bias in zip((0, half), biases):
            queries = stacked_heads(q_ref, slice(start, start + half), h * Q_BLOCK, HEADS_PER_KV)
            scores = scores_of(queries, keys).reshape(HEADS_PER_KV, half, tokens)
            exponents = (scores * EXPONENT + bias[None]).reshape(HEADS_PER_KV * half, tokens)
            worst = jnp.maximum(worst, peak(exponents))
            rows = slice(start * HEADS_PER_KV, (start + half) * HEADS_PER_KV)
            acc = acc_ref[h, rows, :] + product(jnp.exp2(exponents).astype(jnp.bfloat16), values)
            part = jnp.min(acc[:, HEAD_SIZE:].reshape(-1, 8, HEAD_SIZE), axis=0)
            least = part if least is None else jnp.minimum(least, part)
            write(h, start, acc)
        copy_out(h).start()
    redo = out_of_range(worst, least)
    for h in range(KEY_VALUE_HEADS):
        copy_out(h).wait()

    @pl.when(redo)
    def _():
        def step(h, carry):
            columns = span(h * HEAD_SIZE, HEAD_SIZE)
            for start in (0, half):
                queries = stacked_heads(q_ref, slice(start, start + half), h * Q_BLOCK, HEADS_PER_KV)
                state = None
                for parts in parts_in(width):
                    k_part = jnp.concatenate([k_refs[s][:, columns] for s in parts], axis=0)
                    v_part = jnp.concatenate([v_refs[s][:, columns] for s in parts], axis=0)
                    bias = jnp.concatenate([bias_ref[s, start : start + half, :] for s in parts], axis=1)
                    scores = scores_of(queries, k_part).reshape(HEADS_PER_KV, half, bias.shape[1])
                    scores = (scores + bias[None]).reshape(HEADS_PER_KV * half, bias.shape[1])
                    state = fold(state, [scores], [v_part])
                write(h, start, state[1])
            return carry

        lax.fori_loop(0, KEY_VALUE_HEADS, step, 0)
        for h in range(KEY_VALUE_HEADS):
            copy_out(h).start()
        for h in range(KEY_VALUE_HEADS):
            copy_out(h).wait()


def cost(rows, keys, exps):
    return pl.CostEstimate(
        flops=32 * rows * keys * Q_WIDTH, bytes_accessed=4 * rows * Q_WIDTH, transcendentals=exps
    )


def call_first(plan, facts, maxima, query, blocks, keys, values):
    tokens, width = query.shape[0], plan.size
    rows = HEADS_PER_KV * tokens
    f32, bf16 = jnp.float32, jnp.bfloat16
    every = (width - 1) * tokens
    shapes = [
        jax.ShapeDtypeStruct((KEY_VALUE_HEADS, rows, 2 * HEAD_SIZE), f32),
        jax.ShapeDtypeStruct((width, tokens, tokens), f32),
        jax.ShapeDtypeStruct((KEY_VALUE_HEADS, STACKED, 2 * HEAD_SIZE), f32),
        jax.ShapeDtypeStruct((width, STACKED, tokens), f32),
        jax.ShapeDtypeStruct((8, HEAD_SIZE), f32),
        jax.ShapeDtypeStruct((PADDED_ROWS, Q_WIDTH), bf16),
        jax.ShapeDtypeStruct((PADDED_ROWS, 2 * KV_WIDTH), bf16),
        jax.ShapeDtypeStruct((PADDED_ROWS, PADDED_ROWS), bf16),
    ]
    return pl.pallas_call(
        lambda *refs: first_kernel(plan, len(blocks), *refs),
        in_specs=[SMEM] + [VMEM] * (2 + len(blocks) + 2 * (width - 1)),
        out_specs=[VMEM] * len(shapes),
        out_shape=shapes,
        compiler_params=pltpu.CompilerParams(vmem_limit_bytes=(28 + width) * MIB),
        cost_estimate=cost(tokens, every, tokens * every * QUERY_HEADS),
        name="first_shards",
    )(facts, maxima, query, *keys, *values, *blocks)


def call_decode(plan, state, keys, values):
    tokens, width = keys[0].shape[0], plan.size
    return pl.pallas_call(
        lambda *refs: decode_kernel(plan, *refs),
        in_specs=[VMEM] * (6 + 2 * width),
        out_specs=VMEM,
        out_shape=jax.ShapeDtypeStruct((PADDED_ROWS, Q_WIDTH), jnp.bfloat16),
        compiler_params=pltpu.CompilerParams(vmem_limit_bytes=(28 + width) * MIB),
        cost_estimate=cost(PADDED_ROWS, tokens, PADDED_ROWS * tokens * QUERY_HEADS),
        name="last_shard_decode",
    )(*state[2:], *keys, *values)


def call_prefill(plan, state, query, keys, values):
    tokens, width = query.shape[0], plan.size
    return pl.pallas_call(
        lambda *refs: prefill_kernel(plan, *refs),
        in_specs=[VMEM] * (4 + 2 * width),
        out_specs=ANY,
        out_shape=jax.ShapeDtypeStruct((tokens, Q_WIDTH), jnp.bfloat16),
        scratch_shapes=[
            pltpu.VMEM((tokens, Q_WIDTH), jnp.bfloat16),
            pltpu.SemaphoreType.DMA((KEY_VALUE_HEADS,)),
        ],
        compiler_params=pltpu.CompilerParams(vmem_limit_bytes=(28 + width) * MIB),
        cost_estimate=cost(tokens, tokens, tokens * tokens * QUERY_HEADS),
        name="last_shard_prefill",
    )(*state[:2], state[4], query, *keys, *values)


def start_maxima(*arrays):
    def kernel(*refs):
        refs[-1][...] = jnp.full((8, HEAD_SIZE), MASKED, jnp.float32)

    return pl.pallas_call(
        kernel,
        in_specs=[VMEM] * len(arrays),
        out_specs=VMEM,
        out_shape=jax.ShapeDtypeStruct((8, HEAD_SIZE), jnp.float32),
        cost_estimate=pl.CostEstimate(flops=5 * 10**9, bytes_accessed=0, transcendentals=0),
        compiler_params=pltpu.CompilerParams(vmem_limit_bytes=MIB),
        name="start_maxima",
    )(*arrays)


def paired(array, k):
    return lax.ppermute(array, "pd", [(g, g ^ k) for g in range(lax.axis_size("pd"))])


def body(
    prompt_query,
    prompt_key,
    prompt_value,
    prompt_lengths,
    decode_slot,
    decoded_query,
    decoded_key,
    decoded_value,
):
    plan = Ring(lax.axis_size("tp"))
    pd_size = lax.axis_size("pd")
    own = jnp.concatenate([decoded_query, decoded_key, decoded_value], axis=2).reshape(
        DECODE_ROWS, Q_WIDTH + 2 * KV_WIDTH
    )
    facts = facts_row(plan, prompt_lengths, decode_slot)
    prompt_key, decoded_query = lax.optimization_barrier((prompt_key, decoded_query))
    prompt_value, own, facts = lax.optimization_barrier((prompt_value, own, facts))
    keys, values, maxima = [prompt_key], [prompt_value], None
    for s in range(1, plan.size):
        if s == 2:
            keys[1], own = lax.optimization_barrier((keys[1], own))
        if s == plan.size - 1:
            maxima = start_maxima(keys[-1], values[-1])
            values[-1], maxima = lax.optimization_barrier((values[-1], maxima))
        keys.append(plan.step(keys[-1]))
        values.append(plan.step(values[-1]))
        if s == 2:
            blocks = [own] + [paired(own, k) for k in range(1, pd_size)]

    state = call_first(plan, facts, maxima, prompt_query, blocks, keys[:-1], values[:-1])
    outgoing = call_decode(plan, state, keys, values)
    arrived = [outgoing[:DECODE_STEPS]]
    for k in range(1, pd_size):
        arrived.append(paired(outgoing[k * DECODE_STEPS : (k + 1) * DECODE_STEPS], k))
    pre_out = call_prefill(plan, state, prompt_query, keys, values)

    from_block = facts[-GROUP_REQUESTS:]
    dec_out = jnp.zeros((GROUP_REQUESTS, DECODE_STEPS, Q_WIDTH), jnp.bfloat16)
    for k in range(pd_size):
        dec_out = jnp.where((from_block == k)[:, None, None], arrived[k][None], dec_out)
    return (pre_out, dec_out)


def solution(mesh):
    placed = (
        P(("rep", "pd", "tp"), None),
        P(("rep", "pd", "tp"), None),
        P(("rep", "pd", "tp"), None),
        P("rep", None),
        P("rep"),
        P(("rep", "pd"), None, None),
        P(("rep", "pd"), None, None),
        P(("rep", "pd"), None, None),
    )
    return jax.shard_map(
        body,
        mesh=mesh,
        in_specs=placed,
        out_specs=(P(("rep", "pd", "tp"), None), P(("rep", "pd"), None, None)),
        check_vma=False,
    )
```

```python
import math

import jax
import jax.numpy as jnp
from jax import lax
from jax.experimental import pallas as pl
from jax.experimental.pallas import tpu as pltpu
from jax.sharding import PartitionSpec as P

QUERY_HEADS = 32
KEY_VALUE_HEADS = 4
HEAD_SIZE = 128
PAGE = 16
GROUP_REQUESTS = 4
DECODE_STEPS = 2
HEADS_PER_KV = QUERY_HEADS // KEY_VALUE_HEADS
KV_WIDTH = KEY_VALUE_HEADS * HEAD_SIZE
Q_WIDTH = QUERY_HEADS * HEAD_SIZE
Q_BLOCK = HEADS_PER_KV * HEAD_SIZE
DECODE_ROWS = GROUP_REQUESTS * DECODE_STEPS
PADDED_ROWS = 16
STACKED = HEADS_PER_KV * PADDED_ROWS
MIB = 1024 * 1024

MASKED = -1e30
LIMIT = 60.0
EXPONENT = math.log2(math.e) / math.sqrt(HEAD_SIZE)

VMEM = pl.BlockSpec(memory_space=pltpu.VMEM)
SMEM = pl.BlockSpec(memory_space=pltpu.SMEM)
ANY = pl.BlockSpec(memory_space=pl.ANY)
HBM = pl.BlockSpec(memory_space=pltpu.HBM)


class Ring:
    def __init__(self, size):
        self.size = size
        order = [0] + list(range(1, size, 2)) + [i for i in range(size - 1, 0, -1) if i % 2 == 0]
        self.pairs = [(order[i], order[(i + 1) % size]) for i in range(size)]

    def step(self, array):
        return lax.ppermute(array, "tp", self.pairs)


def scores_of(queries, keys):
    return lax.dot_general(
        queries, keys, (((1,), (1,)), ((), ())), preferred_element_type=jnp.float32
    )


def product(left, right):
    return jnp.dot(left, right, preferred_element_type=jnp.float32)


def iota(shape, axis):
    return lax.broadcasted_iota(jnp.int32, shape, axis)


def span(start, size):
    if isinstance(start, int):
        return slice(start, start + size)
    return pl.ds(pl.multiple_of(start, size), size)


def with_ones(values):
    return jnp.concatenate([values, jnp.ones_like(values)], axis=1)


def page_position(offset, member, width):
    return (offset // PAGE * width + member) * PAGE + offset % PAGE


def key_positions(rows, sources, width):
    column = iota((1, len(sources) * rows), 1)
    part = column // rows
    source = jnp.zeros_like(column) + sources[0]
    for b in range(1, len(sources)):
        source = jnp.where(part == b, sources[b], source)
    return page_position(column - part * rows, source, width)


class Facts:
    def __init__(self, ref, width):
        self.width = width
        self.group, self.member = ref[0], ref[1]
        self.slots = [ref[2 + r] for r in range(GROUP_REQUESTS)]
        first = 2 + GROUP_REQUESTS
        self.ends = []
        total = jnp.int32(0)
        for r in range(GROUP_REQUESTS):
            total = total + ref[first + r] * PAGE
            self.ends.append(total)
        first += GROUP_REQUESTS
        self.source = [ref[first + s] for s in range(width)]


def facts_row(plan, lengths, slots):
    width, requests = plan.size, slots.shape[0]

    def kernel(lengths_ref, slots_ref, out_ref):
        group, member = lax.axis_index("pd"), lax.axis_index("tp")
        values = [group, member]
        values += [slots_ref[group * GROUP_REQUESTS + r] for r in range(GROUP_REQUESTS)]
        values += [lengths_ref[group, r] for r in range(GROUP_REQUESTS)]
        place = jnp.where(member % 2 == 1, (member + 1) // 2, width - member // 2)
        for s in range(width):
            before = (place + width - s) % width
            up = 2 * before - 1
            values.append(jnp.where(before == 0, 0, jnp.where(before <= width // 2, up, 2 * (width - before))))
        for i, value in enumerate(values):
            out_ref[i] = value.astype(jnp.int32)
        for q in range(requests):
            place = slots_ref[q] - group * GROUP_REQUESTS

            @pl.when((place >= 0) & (place < GROUP_REQUESTS))
            def _():
                out_ref[len(values) + place] = group ^ (q // GROUP_REQUESTS)

    length = 2 + 2 * GROUP_REQUESTS + width + GROUP_REQUESTS
    return pl.pallas_call(
        kernel,
        in_specs=[SMEM, SMEM],
        out_specs=SMEM,
        out_shape=jax.ShapeDtypeStruct((length,), jnp.int32),
        cost_estimate=pl.CostEstimate(flops=5 * 10**9, bytes_accessed=0, transcendentals=0),
        name="facts",
    )(lengths, slots)


def causal_bias(start, rows, keys, sources, ends, member, width):
    qpos = page_position(start + iota((rows, 1), 0), member, width)
    low = jnp.zeros_like(qpos)
    for end in ends:
        low = jnp.where(qpos >= end, end, low)
    kpos = key_positions(keys, sources, width)
    return jnp.where((kpos >= low) & (kpos <= qpos), 0.0, MASKED)


def request_mask(ends, keys, sources, width):
    request = iota((STACKED, 1), 0) % PADDED_ROWS // DECODE_STEPS
    low = jnp.zeros_like(request)
    high = jnp.zeros_like(request) + ends[0]
    for r in range(1, GROUP_REQUESTS):
        low = jnp.where(request == r, ends[r - 1], low)
        high = jnp.where(request == r, ends[r], high)
    kpos = key_positions(keys, sources, width)
    return (kpos >= low) & (kpos < high)


def stacked_heads(ref, rows, first, count):
    return jnp.concatenate(
        [ref[rows, span(first + i * HEAD_SIZE, HEAD_SIZE)] for i in range(count)], axis=0
    )


def each_kv_head(width, step):
    if width <= 8:
        for h in range(KEY_VALUE_HEADS):
            step(h)
    else:
        lax.fori_loop(0, KEY_VALUE_HEADS, lambda h, c: (step(h), c)[1], 0)


def peak(exponents):
    return jnp.max(exponents.reshape(-1, 8, exponents.shape[-1]), axis=0)


def picked_rows(facts, pd_size, block_refs):
    row = iota((PADDED_ROWS, DECODE_ROWS), 0)
    column = iota((PADDED_ROWS, DECODE_ROWS), 1)
    total = None
    for k in range(pd_size):
        pick = column < 0
        for r in range(GROUP_REQUESTS):
            slot = facts.slots[r]
            first = jnp.where(facts.group ^ (slot // GROUP_REQUESTS) == k, slot % GROUP_REQUESTS * DECODE_STEPS, -DECODE_ROWS * 4)
            pick = pick | ((row // DECODE_STEPS == r) & (column == first + row - r * DECODE_STEPS))
        part = product(pick.astype(jnp.float32).astype(jnp.bfloat16), block_refs[k][...])
        total = part if total is None else total + part
    return total.astype(jnp.bfloat16)


def pick_matrix(facts):
    row = iota((PADDED_ROWS, PADDED_ROWS), 0)
    column = iota((PADDED_ROWS, PADDED_ROWS), 1)
    pick = column < 0
    for r in range(GROUP_REQUESTS):
        ahead = facts.group ^ (facts.slots[r] // GROUP_REQUESTS)
        pick = pick | (
            (column // DECODE_STEPS == r) & (row == ahead * DECODE_STEPS + column - r * DECODE_STEPS)
        )
    return pick.astype(jnp.float32).astype(jnp.bfloat16)


def fresh_mask():
    row = iota((STACKED, PADDED_ROWS), 0) % PADDED_ROWS
    column = iota((STACKED, PADDED_ROWS), 1)
    return (column // DECODE_STEPS == row // DECODE_STEPS) & (
        column % DECODE_STEPS <= row % DECODE_STEPS
    )


def first_kernel(plan, pd_size, facts_ref, maxima_ref, q_ref, *refs):
    width = plan.size
    k_refs, v_refs, refs = refs[: width - 1], refs[width - 1 : 2 * width - 2], refs[2 * width - 2 :]
    block_refs, refs = refs[:pd_size], refs[pd_size:]
    acc_ref, bias_ref, dec_acc_ref, dec_bias_ref, worst_ref, queries_ref, fresh_ref, pick_ref = refs
    tokens = q_ref.shape[0]
    half = tokens // 2
    facts = Facts(facts_ref, width)
    sources = facts.source[:-1]
    pick_ref[...] = pick_matrix(facts)
    for s in range(width):
        bias_ref[s] = causal_bias(0, tokens, tokens, facts.source[s : s + 1], facts.ends, facts.member, width)
        dec_bias_ref[s] = jnp.where(
            request_mask(facts.ends, tokens, facts.source[s : s + 1], width), 0.0, MASKED
        )
    rows = picked_rows(facts, pd_size, block_refs)
    queries_ref[...] = rows[:, :Q_WIDTH]
    fresh_ref[...] = rows[:, Q_WIDTH:]
    worst_ref[...] = maxima_ref[...]
    new_mask = fresh_mask()
    mask = request_mask(facts.ends, tokens, sources, width)
    spans = ((0, half), (half, tokens))
    biases = [
        causal_bias(s, half, keys, sources, facts.ends, facts.member, width) for s, keys in spans
    ]
    together = max(1, min(HEADS_PER_KV, HEADS_PER_KV * 4 // width))

    def weigh(exponents):
        top = jnp.max(peak(exponents), axis=1, keepdims=True)
        worst_ref[...] = jnp.maximum(worst_ref[...], top)
        return jnp.exp2(exponents).astype(jnp.bfloat16)

    def step(h):
        columns = span(h * HEAD_SIZE, HEAD_SIZE)
        first = h * Q_BLOCK
        queries = stacked_heads(queries_ref, slice(None), first, HEADS_PER_KV)
        k_all = jnp.concatenate([ref[:, columns] for ref in k_refs], axis=0)
        v_all = with_ones(jnp.concatenate([ref[:, columns] for ref in v_refs], axis=0))
        new_scores = scores_of(queries, fresh_ref[:, columns]) * EXPONENT
        new_weights = weigh(jnp.where(new_mask, new_scores, MASKED))
        new_values = fresh_ref[:, span(KV_WIDTH + h * HEAD_SIZE, HEAD_SIZE)]
        weights = weigh(jnp.where(mask, scores_of(queries, k_all) * EXPONENT, MASKED))
        dec_acc_ref[h] = product(weights, v_all) + product(new_weights, with_ones(new_values))
        for (start, keys), bias in zip(spans, biases):
            if keys < tokens:
                k_part = jnp.concatenate([ref[:keys, columns] for ref in k_refs], axis=0)
                v_part = with_ones(jnp.concatenate([ref[:keys, columns] for ref in v_refs], axis=0))
            else:
                k_part, v_part = k_all, v_all
            for g in range(0, HEADS_PER_KV, together):
                queries = stacked_heads(
                    q_ref, slice(start, start + half), first + g * HEAD_SIZE, together
                )
                scores = scores_of(queries, k_part).reshape(together, half, bias.shape[1])
                exponents = (scores * EXPONENT + bias[None]).reshape(together * half, bias.shape[1])
                rows = slice(
                    start * HEADS_PER_KV + g * half, start * HEADS_PER_KV + (g + together) * half
                )
                acc_ref[h, rows, :] = product(weigh(exponents), v_part)

    each_kv_head(width, step)


def divided(acc):
    return (acc[:, :HEAD_SIZE] * pl.reciprocal(acc[:, HEAD_SIZE:], approx=True)).astype(jnp.bfloat16)


def fold(state, scores_list, values_list):
    top = None if state is None else state[0]
    for scores in scores_list:
        part = jnp.max(scores, axis=1, keepdims=True)
        top = part if top is None else jnp.maximum(top, part)
    acc = None
    for scores, values in zip(scores_list, values_list):
        weights = jnp.exp2((scores - top) * EXPONENT).astype(jnp.bfloat16)
        part = product(weights, with_ones(values))
        acc = part if acc is None else acc + part
    if state is not None:
        acc = acc + state[1] * jnp.exp2((state[0] - top) * EXPONENT)
    return top, acc


def parts_in(width):
    return [range(c, min(c + 4, width)) for c in range(0, width, 4)]


def out_of_range(worst, least):
    return (jnp.max(worst) > LIMIT) | (jnp.min(least) < 2.0**-LIMIT)


def decode_kernel(plan, acc_ref, bias_ref, worst_ref, queries_ref, fresh_ref, pick_ref, *refs):
    width = plan.size
    k_refs, v_refs, (out_ref,) = refs[:width], refs[width : 2 * width], refs[2 * width :]
    heads = range(KEY_VALUE_HEADS)
    columns = [slice(h * HEAD_SIZE, (h + 1) * HEAD_SIZE) for h in heads]

    def queries_of(h):
        return stacked_heads(queries_ref, slice(None), h * Q_BLOCK, HEADS_PER_KV)

    def send(acc):
        out = [divided(a) for a in acc]
        out = jnp.concatenate(
            [o[g * PADDED_ROWS : (g + 1) * PADDED_ROWS] for o in out for g in range(HEADS_PER_KV)], axis=1
        )
        out_ref[...] = product(pick_ref[...], out).astype(jnp.bfloat16)

    exponents = [
        scores_of(queries_of(h), k_refs[-1][:, columns[h]]) * EXPONENT + bias_ref[width - 1]
        for h in heads
    ]
    acc = [
        acc_ref[h] + product(jnp.exp2(exponents[h]).astype(jnp.bfloat16), with_ones(v_refs[-1][:, columns[h]]))
        for h in heads
    ]
    send(acc)
    worst, least = worst_ref[...], None
    for h in heads:
        worst = jnp.maximum(worst, peak(exponents[h]))
        part = jnp.min(acc[h][:, HEAD_SIZE:].reshape(-1, 8, HEAD_SIZE), axis=0)
        least = part if least is None else jnp.minimum(least, part)

    @pl.when(out_of_range(worst, least))
    def _():
        new_mask = fresh_mask()
        again = []
        for h in heads:
            queries = queries_of(h)
            scores = jnp.where(new_mask, scores_of(queries, fresh_ref[:, columns[h]]), MASKED)
            new_columns = slice(KV_WIDTH + h * HEAD_SIZE, KV_WIDTH + (h + 1) * HEAD_SIZE)
            state = fold(None, [scores], [fresh_ref[:, new_columns]])
            for parts in parts_in(width):
                k_part = jnp.concatenate([k_refs[s][:, columns[h]] for s in parts], axis=0)
                v_part = jnp.concatenate([v_refs[s][:, columns[h]] for s in parts], axis=0)
                bias = jnp.concatenate([bias_ref[s] for s in parts], axis=1)
                state = fold(state, [scores_of(queries, k_part) + bias], [v_part])
            again.append(state[1])
        send(again)


def prefill_kernel(plan, acc_ref, bias_ref, worst_ref, q_ref, *refs):
    width = plan.size
    k_refs, v_refs, refs = refs[:width], refs[width : 2 * width], refs[2 * width :]
    out_ref, done_ref, sem = refs
    tokens = q_ref.shape[0]
    half = tokens // 2
    def write(h, start, acc):
        out = divided(acc)
        for g in range(HEADS_PER_KV):
            done_ref[start : start + half, span(h * Q_BLOCK + g * HEAD_SIZE, HEAD_SIZE)] = out[
                g * half : (g + 1) * half
            ]

    def copy_out(h):
        part = pl.ds(h * Q_BLOCK, Q_BLOCK)
        return pltpu.make_async_copy(done_ref.at[:, part], out_ref.at[:, part], sem.at[h])

    biases = [bias_ref[width - 1, start : start + half, :] for start in (0, half)]
    worst, least = worst_ref[...], None
    for h in range(KEY_VALUE_HEADS):
        columns = slice(h * HEAD_SIZE, (h + 1) * HEAD_SIZE)
        keys, values = k_refs[-1][:, columns], with_ones(v_refs[-1][:, columns])
        for start, bias in zip((0, half), biases):
            queries = stacked_heads(q_ref, slice(start, start + half), h * Q_BLOCK, HEADS_PER_KV)
            scores = scores_of(queries, keys).reshape(HEADS_PER_KV, half, tokens)
            exponents = (scores * EXPONENT + bias[None]).reshape(HEADS_PER_KV * half, tokens)
            worst = jnp.maximum(worst, peak(exponents))
            rows = slice(start * HEADS_PER_KV, (start + half) * HEADS_PER_KV)
            acc = acc_ref[h, rows, :] + product(jnp.exp2(exponents).astype(jnp.bfloat16), values)
            part = jnp.min(acc[:, HEAD_SIZE:].reshape(-1, 8, HEAD_SIZE), axis=0)
            least = part if least is None else jnp.minimum(least, part)
            write(h, start, acc)
        copy_out(h).start()
    redo = out_of_range(worst, least)
    for h in range(KEY_VALUE_HEADS):
        copy_out(h).wait()

    @pl.when(redo)
    def _():
        def step(h, carry):
            columns = span(h * HEAD_SIZE, HEAD_SIZE)
            for start in (0, half):
                queries = stacked_heads(q_ref, slice(start, start + half), h * Q_BLOCK, HEADS_PER_KV)
                state = None
                for parts in parts_in(width):
                    k_part = jnp.concatenate([k_refs[s][:, columns] for s in parts], axis=0)
                    v_part = jnp.concatenate([v_refs[s][:, columns] for s in parts], axis=0)
                    bias = jnp.concatenate([bias_ref[s, start : start + half, :] for s in parts], axis=1)
                    scores = scores_of(queries, k_part).reshape(HEADS_PER_KV, half, bias.shape[1])
                    scores = (scores + bias[None]).reshape(HEADS_PER_KV * half, bias.shape[1])
                    state = fold(state, [scores], [v_part])
                write(h, start, state[1])
            return carry

        lax.fori_loop(0, KEY_VALUE_HEADS, step, 0)
        for h in range(KEY_VALUE_HEADS):
            copy_out(h).start()
        for h in range(KEY_VALUE_HEADS):
            copy_out(h).wait()


def cost(rows, keys, exps):
    return pl.CostEstimate(
        flops=32 * rows * keys * Q_WIDTH, bytes_accessed=4 * rows * Q_WIDTH, transcendentals=exps
    )


def call_first(plan, facts, maxima, query, blocks, keys, values):
    tokens, width = query.shape[0], plan.size
    rows = HEADS_PER_KV * tokens
    f32, bf16 = jnp.float32, jnp.bfloat16
    every = (width - 1) * tokens
    shapes = [
        jax.ShapeDtypeStruct((KEY_VALUE_HEADS, rows, 2 * HEAD_SIZE), f32),
        jax.ShapeDtypeStruct((width, tokens, tokens), f32),
        jax.ShapeDtypeStruct((KEY_VALUE_HEADS, STACKED, 2 * HEAD_SIZE), f32),
        jax.ShapeDtypeStruct((width, STACKED, tokens), f32),
        jax.ShapeDtypeStruct((8, HEAD_SIZE), f32),
        jax.ShapeDtypeStruct((PADDED_ROWS, Q_WIDTH), bf16),
        jax.ShapeDtypeStruct((PADDED_ROWS, 2 * KV_WIDTH), bf16),
        jax.ShapeDtypeStruct((PADDED_ROWS, PADDED_ROWS), bf16),
    ]
    return pl.pallas_call(
        lambda *refs: first_kernel(plan, len(blocks), *refs),
        in_specs=[SMEM] + [VMEM] * (2 + len(blocks) + 2 * (width - 1)),
        out_specs=[VMEM] * len(shapes),
        out_shape=shapes,
        compiler_params=pltpu.CompilerParams(vmem_limit_bytes=(28 + width) * MIB),
        cost_estimate=cost(tokens, every, tokens * every * QUERY_HEADS),
        name="first_shards",
    )(facts, maxima, query, *keys, *values, *blocks)


def call_decode(plan, state, keys, values):
    tokens, width = keys[0].shape[0], plan.size
    return pl.pallas_call(
        lambda *refs: decode_kernel(plan, *refs),
        in_specs=[VMEM] * (6 + 2 * width),
        out_specs=VMEM,
        out_shape=jax.ShapeDtypeStruct((PADDED_ROWS, Q_WIDTH), jnp.bfloat16),
        compiler_params=pltpu.CompilerParams(vmem_limit_bytes=(28 + width) * MIB),
        cost_estimate=cost(PADDED_ROWS, tokens, PADDED_ROWS * tokens * QUERY_HEADS),
        name="last_shard_decode",
    )(*state[2:], *keys, *values)


def call_prefill(plan, state, query, keys, values):
    tokens, width = query.shape[0], plan.size
    return pl.pallas_call(
        lambda *refs: prefill_kernel(plan, *refs),
        in_specs=[VMEM] * (4 + 2 * width),
        out_specs=ANY,
        out_shape=jax.ShapeDtypeStruct((tokens, Q_WIDTH), jnp.bfloat16),
        scratch_shapes=[
            pltpu.VMEM((tokens, Q_WIDTH), jnp.bfloat16),
            pltpu.SemaphoreType.DMA((KEY_VALUE_HEADS,)),
        ],
        compiler_params=pltpu.CompilerParams(vmem_limit_bytes=(28 + width) * MIB),
        cost_estimate=cost(tokens, tokens, tokens * tokens * QUERY_HEADS),
        name="last_shard_prefill",
    )(*state[:2], state[4], query, *keys, *values)


def start_maxima(*arrays, flops=5 * 10**9):
    def kernel(*refs):
        refs[-1][...] = jnp.full((8, HEAD_SIZE), MASKED, jnp.float32)

    return pl.pallas_call(
        kernel,
        in_specs=[VMEM] * len(arrays),
        out_specs=VMEM,
        out_shape=jax.ShapeDtypeStruct((8, HEAD_SIZE), jnp.float32),
        cost_estimate=pl.CostEstimate(flops=flops, bytes_accessed=0, transcendentals=0),
        compiler_params=pltpu.CompilerParams(vmem_limit_bytes=MIB),
        name="start_maxima",
    )(*arrays)


def paired(array, k):
    return lax.ppermute(array, "pd", [(g, g ^ k) for g in range(lax.axis_size("pd"))])


def body(
    prompt_query,
    prompt_key,
    prompt_value,
    prompt_lengths,
    decode_slot,
    decoded_query,
    decoded_key,
    decoded_value,
):
    plan = Ring(lax.axis_size("tp"))
    pd_size = lax.axis_size("pd")
    own = jnp.concatenate([decoded_query, decoded_key, decoded_value], axis=2).reshape(
        DECODE_ROWS, Q_WIDTH + 2 * KV_WIDTH
    )
    facts = facts_row(plan, prompt_lengths, decode_slot)
    prompt_key, decoded_query = lax.optimization_barrier((prompt_key, decoded_query))
    prompt_value, own, facts = lax.optimization_barrier((prompt_value, own, facts))
    keys, values, maxima = [prompt_key], [prompt_value], None
    for s in range(1, plan.size):
        if s == 2:
            keys[1], own = lax.optimization_barrier((keys[1], own))
        if s == plan.size - 1:
            maxima = start_maxima(keys[-1])
            keys[-1], maxima = lax.optimization_barrier((keys[-1], maxima))
        keys.append(plan.step(keys[-1]))
        values.append(plan.step(values[-1]))
        if s == 2:
            blocks = [own] + [paired(own, k) for k in range(1, pd_size)]

    state = call_first(plan, facts, maxima, prompt_query, blocks, keys[:-1], values[:-1])
    outgoing = call_decode(plan, state, keys, values)
    arrived = [outgoing[:DECODE_STEPS]]
    for k in range(1, pd_size):
        arrived.append(paired(outgoing[k * DECODE_STEPS : (k + 1) * DECODE_STEPS], k))
    pre_out = call_prefill(plan, state, prompt_query, keys, values)

    from_block = facts[-GROUP_REQUESTS:]
    dec_out = jnp.zeros((GROUP_REQUESTS, DECODE_STEPS, Q_WIDTH), jnp.bfloat16)
    for k in range(pd_size):
        dec_out = jnp.where((from_block == k)[:, None, None], arrived[k][None], dec_out)
    return (pre_out, dec_out)


def solution(mesh):
    placed = (
        P(("rep", "pd", "tp"), None),
        P(("rep", "pd", "tp"), None),
        P(("rep", "pd", "tp"), None),
        P("rep", None),
        P("rep"),
        P(("rep", "pd"), None, None),
        P(("rep", "pd"), None, None),
        P(("rep", "pd"), None, None),
    )
    return jax.shard_map(
        body,
        mesh=mesh,
        in_specs=placed,
        out_specs=(P(("rep", "pd", "tp"), None), P(("rep", "pd"), None, None)),
        check_vma=False,
    )
```

```python
import math

import jax
import jax.numpy as jnp
from jax import lax
from jax.experimental import pallas as pl
from jax.experimental.pallas import tpu as pltpu
from jax.sharding import PartitionSpec as P

QUERY_HEADS = 32
KEY_VALUE_HEADS = 4
HEAD_SIZE = 128
PAGE = 16
GROUP_REQUESTS = 4
DECODE_STEPS = 2
HEADS_PER_KV = QUERY_HEADS // KEY_VALUE_HEADS
KV_WIDTH = KEY_VALUE_HEADS * HEAD_SIZE
Q_WIDTH = QUERY_HEADS * HEAD_SIZE
Q_BLOCK = HEADS_PER_KV * HEAD_SIZE
DECODE_ROWS = GROUP_REQUESTS * DECODE_STEPS
PADDED_ROWS = 16
STACKED = HEADS_PER_KV * PADDED_ROWS
MIB = 1024 * 1024

MASKED = -1e30
LIMIT = 60.0
EXPONENT = math.log2(math.e) / math.sqrt(HEAD_SIZE)

VMEM = pl.BlockSpec(memory_space=pltpu.VMEM)
SMEM = pl.BlockSpec(memory_space=pltpu.SMEM)
ANY = pl.BlockSpec(memory_space=pl.ANY)
HBM = pl.BlockSpec(memory_space=pltpu.HBM)


class Ring:
    def __init__(self, size):
        self.size = size
        order = [0] + list(range(1, size, 2)) + [i for i in range(size - 1, 0, -1) if i % 2 == 0]
        self.pairs = [(order[i], order[(i + 1) % size]) for i in range(size)]

    def step(self, array):
        return lax.ppermute(array, "tp", self.pairs)


def scores_of(queries, keys):
    return lax.dot_general(
        queries, keys, (((1,), (1,)), ((), ())), preferred_element_type=jnp.float32
    )


def product(left, right):
    return jnp.dot(left, right, preferred_element_type=jnp.float32)


def iota(shape, axis):
    return lax.broadcasted_iota(jnp.int32, shape, axis)


def span(start, size):
    if isinstance(start, int):
        return slice(start, start + size)
    return pl.ds(pl.multiple_of(start, size), size)


def with_ones(values):
    return jnp.concatenate([values, jnp.ones_like(values)], axis=1)


def page_position(offset, member, width):
    return (offset // PAGE * width + member) * PAGE + offset % PAGE


def key_positions(rows, sources, width):
    column = iota((1, len(sources) * rows), 1)
    part = column // rows
    source = jnp.zeros_like(column) + sources[0]
    for b in range(1, len(sources)):
        source = jnp.where(part == b, sources[b], source)
    return page_position(column - part * rows, source, width)


class Facts:
    def __init__(self, ref, width):
        self.width = width
        self.group, self.member = ref[0], ref[1]
        self.slots = [ref[2 + r] for r in range(GROUP_REQUESTS)]
        first = 2 + GROUP_REQUESTS
        self.ends = []
        total = jnp.int32(0)
        for r in range(GROUP_REQUESTS):
            total = total + ref[first + r] * PAGE
            self.ends.append(total)
        first += GROUP_REQUESTS
        self.source = [ref[first + s] for s in range(width)]
        first += width
        self.owner = [ref[first + p] for p in range(GROUP_REQUESTS)]


def facts_row(plan, lengths, slots):
    width, requests = plan.size, slots.shape[0]

    def kernel(lengths_ref, slots_ref, out_ref):
        group, member = lax.axis_index("pd"), lax.axis_index("tp")
        values = [group, member]
        values += [slots_ref[group * GROUP_REQUESTS + r] for r in range(GROUP_REQUESTS)]
        values += [lengths_ref[group, r] for r in range(GROUP_REQUESTS)]
        place = jnp.where(member % 2 == 1, (member + 1) // 2, width - member // 2)
        for s in range(width):
            before = (place + width - s) % width
            up = 2 * before - 1
            values.append(jnp.where(before == 0, 0, jnp.where(before <= width // 2, up, 2 * (width - before))))
        for i, value in enumerate(values):
            out_ref[i] = value.astype(jnp.int32)
        for q in range(requests):
            place = slots_ref[q] - group * GROUP_REQUESTS

            @pl.when((place >= 0) & (place < GROUP_REQUESTS))
            def _():
                out_ref[len(values) + place] = group ^ (q // GROUP_REQUESTS)

    length = 2 + 2 * GROUP_REQUESTS + width + GROUP_REQUESTS
    return pl.pallas_call(
        kernel,
        in_specs=[SMEM, SMEM],
        out_specs=SMEM,
        out_shape=jax.ShapeDtypeStruct((length,), jnp.int32),
        cost_estimate=pl.CostEstimate(flops=5 * 10**9, bytes_accessed=0, transcendentals=0),
        name="facts",
    )(lengths, slots)


def causal_bias(start, rows, keys, sources, ends, member, width):
    qpos = page_position(start + iota((rows, 1), 0), member, width)
    low = jnp.zeros_like(qpos)
    for end in ends:
        low = jnp.where(qpos >= end, end, low)
    kpos = key_positions(keys, sources, width)
    return jnp.where((kpos >= low) & (kpos <= qpos), 0.0, MASKED)


def request_mask(ends, keys, sources, width):
    request = iota((STACKED, 1), 0) % PADDED_ROWS // DECODE_STEPS
    low = jnp.zeros_like(request)
    high = jnp.zeros_like(request) + ends[0]
    for r in range(1, GROUP_REQUESTS):
        low = jnp.where(request == r, ends[r - 1], low)
        high = jnp.where(request == r, ends[r], high)
    kpos = key_positions(keys, sources, width)
    return (kpos >= low) & (kpos < high)


def stacked_heads(ref, rows, first, count):
    return jnp.concatenate(
        [ref[rows, span(first + i * HEAD_SIZE, HEAD_SIZE)] for i in range(count)], axis=0
    )


def each_kv_head(width, step):
    if width <= 8:
        for h in range(KEY_VALUE_HEADS):
            step(h)
    else:
        lax.fori_loop(0, KEY_VALUE_HEADS, lambda h, c: (step(h), c)[1], 0)


def peak(exponents):
    return jnp.max(exponents.reshape(-1, 8, exponents.shape[-1]), axis=0)


def picked_rows(facts, pd_size, block_refs):
    row = iota((PADDED_ROWS, DECODE_ROWS), 0)
    column = iota((PADDED_ROWS, DECODE_ROWS), 1)
    total = None
    for k in range(pd_size):
        pick = column < 0
        for r in range(GROUP_REQUESTS):
            slot = facts.slots[r]
            first = jnp.where(facts.group ^ (slot // GROUP_REQUESTS) == k, slot % GROUP_REQUESTS * DECODE_STEPS, -DECODE_ROWS * 4)
            pick = pick | ((row // DECODE_STEPS == r) & (column == first + row - r * DECODE_STEPS))
        part = product(pick.astype(jnp.float32).astype(jnp.bfloat16), block_refs[k][...])
        total = part if total is None else total + part
    return total.astype(jnp.bfloat16)


def pick_matrix(facts):
    row = iota((PADDED_ROWS, PADDED_ROWS), 0)
    column = iota((PADDED_ROWS, PADDED_ROWS), 1)
    pick = column < 0
    for r in range(GROUP_REQUESTS):
        ahead = facts.group ^ (facts.slots[r] // GROUP_REQUESTS)
        pick = pick | (
            (column // DECODE_STEPS == r) & (row == ahead * DECODE_STEPS + column - r * DECODE_STEPS)
        )
    return pick.astype(jnp.float32).astype(jnp.bfloat16)


def fresh_mask():
    row = iota((STACKED, PADDED_ROWS), 0) % PADDED_ROWS
    column = iota((STACKED, PADDED_ROWS), 1)
    return (column // DECODE_STEPS == row // DECODE_STEPS) & (
        column % DECODE_STEPS <= row % DECODE_STEPS
    )


def first_kernel(plan, pd_size, facts_ref, maxima_ref, q_ref, *refs):
    width = plan.size
    k_refs, v_refs, refs = refs[: width - 1], refs[width - 1 : 2 * width - 2], refs[2 * width - 2 :]
    block_refs, refs = refs[:pd_size], refs[pd_size:]
    acc_ref, bias_ref, dec_acc_ref, dec_bias_ref, worst_ref, queries_ref, fresh_ref, pick_ref, owner_ref = refs
    tokens = q_ref.shape[0]
    half = tokens // 2
    facts = Facts(facts_ref, width)
    sources = facts.source[:-1]
    pick_ref[...] = pick_matrix(facts)
    slot = iota((8, HEAD_SIZE), 0)
    owner = jnp.zeros_like(slot)
    for p in range(GROUP_REQUESTS):
        owner = jnp.where(slot == p, facts.owner[p], owner)
    owner_ref[...] = owner
    for s in range(width):
        bias_ref[s] = causal_bias(0, tokens, tokens, facts.source[s : s + 1], facts.ends, facts.member, width)
        dec_bias_ref[s] = jnp.where(
            request_mask(facts.ends, tokens, facts.source[s : s + 1], width), 0.0, MASKED
        )
    rows = picked_rows(facts, pd_size, block_refs)
    queries_ref[...] = rows[:, :Q_WIDTH]
    fresh_ref[...] = rows[:, Q_WIDTH:]
    worst_ref[...] = maxima_ref[...]
    new_mask = fresh_mask()
    mask = request_mask(facts.ends, tokens, sources, width)
    spans = ((0, half), (half, tokens))
    biases = [
        causal_bias(s, half, keys, sources, facts.ends, facts.member, width) for s, keys in spans
    ]
    together = max(1, min(HEADS_PER_KV, HEADS_PER_KV * 4 // width))

    def weigh(exponents):
        top = jnp.max(peak(exponents), axis=1, keepdims=True)
        worst_ref[...] = jnp.maximum(worst_ref[...], top)
        return jnp.exp2(exponents).astype(jnp.bfloat16)

    def step(h):
        columns = span(h * HEAD_SIZE, HEAD_SIZE)
        first = h * Q_BLOCK
        queries = stacked_heads(queries_ref, slice(None), first, HEADS_PER_KV)
        k_all = jnp.concatenate([ref[:, columns] for ref in k_refs], axis=0)
        v_all = with_ones(jnp.concatenate([ref[:, columns] for ref in v_refs], axis=0))
        new_scores = scores_of(queries, fresh_ref[:, columns]) * EXPONENT
        new_weights = weigh(jnp.where(new_mask, new_scores, MASKED))
        new_values = fresh_ref[:, span(KV_WIDTH + h * HEAD_SIZE, HEAD_SIZE)]
        weights = weigh(jnp.where(mask, scores_of(queries, k_all) * EXPONENT, MASKED))
        dec_acc_ref[h] = product(weights, v_all) + product(new_weights, with_ones(new_values))
        for (start, keys), bias in zip(spans, biases):
            if keys < tokens:
                k_part = jnp.concatenate([ref[:keys, columns] for ref in k_refs], axis=0)
                v_part = with_ones(jnp.concatenate([ref[:keys, columns] for ref in v_refs], axis=0))
            else:
                k_part, v_part = k_all, v_all
            for g in range(0, HEADS_PER_KV, together):
                queries = stacked_heads(
                    q_ref, slice(start, start + half), first + g * HEAD_SIZE, together
                )
                scores = scores_of(queries, k_part).reshape(together, half, bias.shape[1])
                exponents = (scores * EXPONENT + bias[None]).reshape(together * half, bias.shape[1])
                rows = slice(
                    start * HEADS_PER_KV + g * half, start * HEADS_PER_KV + (g + together) * half
                )
                acc_ref[h, rows, :] = product(weigh(exponents), v_part)

    each_kv_head(width, step)


def divided(acc):
    return (acc[:, :HEAD_SIZE] * pl.reciprocal(acc[:, HEAD_SIZE:], approx=True)).astype(jnp.bfloat16)


def fold(state, scores_list, values_list):
    top = None if state is None else state[0]
    for scores in scores_list:
        part = jnp.max(scores, axis=1, keepdims=True)
        top = part if top is None else jnp.maximum(top, part)
    acc = None
    for scores, values in zip(scores_list, values_list):
        weights = jnp.exp2((scores - top) * EXPONENT).astype(jnp.bfloat16)
        part = product(weights, with_ones(values))
        acc = part if acc is None else acc + part
    if state is not None:
        acc = acc + state[1] * jnp.exp2((state[0] - top) * EXPONENT)
    return top, acc


def parts_in(width):
    return [range(c, min(c + 4, width)) for c in range(0, width, 4)]


def out_of_range(worst, least):
    return (jnp.max(worst) > LIMIT) | (jnp.min(least) < 2.0**-LIMIT)


def decode_kernel(plan, acc_ref, bias_ref, worst_ref, queries_ref, fresh_ref, pick_ref, *refs):
    width = plan.size
    k_refs, v_refs, (out_ref,) = refs[:width], refs[width : 2 * width], refs[2 * width :]
    heads = range(KEY_VALUE_HEADS)
    columns = [slice(h * HEAD_SIZE, (h + 1) * HEAD_SIZE) for h in heads]

    def queries_of(h):
        return stacked_heads(queries_ref, slice(None), h * Q_BLOCK, HEADS_PER_KV)

    def send(acc):
        out = [divided(a) for a in acc]
        out = jnp.concatenate(
            [o[g * PADDED_ROWS : (g + 1) * PADDED_ROWS] for o in out for g in range(HEADS_PER_KV)], axis=1
        )
        out_ref[...] = product(pick_ref[...], out).astype(jnp.bfloat16)

    exponents = [
        scores_of(queries_of(h), k_refs[-1][:, columns[h]]) * EXPONENT + bias_ref[width - 1]
        for h in heads
    ]
    acc = [
        acc_ref[h] + product(jnp.exp2(exponents[h]).astype(jnp.bfloat16), with_ones(v_refs[-1][:, columns[h]]))
        for h in heads
    ]
    send(acc)
    worst, least = worst_ref[...], None
    for h in heads:
        worst = jnp.maximum(worst, peak(exponents[h]))
        part = jnp.min(acc[h][:, HEAD_SIZE:].reshape(-1, 8, HEAD_SIZE), axis=0)
        least = part if least is None else jnp.minimum(least, part)

    @pl.when(out_of_range(worst, least))
    def _():
        new_mask = fresh_mask()
        again = []
        for h in heads:
            queries = queries_of(h)
            scores = jnp.where(new_mask, scores_of(queries, fresh_ref[:, columns[h]]), MASKED)
            new_columns = slice(KV_WIDTH + h * HEAD_SIZE, KV_WIDTH + (h + 1) * HEAD_SIZE)
            state = fold(None, [scores], [fresh_ref[:, new_columns]])
            for parts in parts_in(width):
                k_part = jnp.concatenate([k_refs[s][:, columns[h]] for s in parts], axis=0)
                v_part = jnp.concatenate([v_refs[s][:, columns[h]] for s in parts], axis=0)
                bias = jnp.concatenate([bias_ref[s] for s in parts], axis=1)
                state = fold(state, [scores_of(queries, k_part) + bias], [v_part])
            again.append(state[1])
        send(again)


def prefill_kernel(plan, acc_ref, bias_ref, worst_ref, q_ref, *refs):
    width = plan.size
    k_refs, v_refs, refs = refs[:width], refs[width : 2 * width], refs[2 * width :]
    out_ref, done_ref, sem = refs
    tokens = q_ref.shape[0]
    half = tokens // 2
    def write(h, start, acc):
        out = divided(acc)
        for g in range(HEADS_PER_KV):
            done_ref[start : start + half, span(h * Q_BLOCK + g * HEAD_SIZE, HEAD_SIZE)] = out[
                g * half : (g + 1) * half
            ]

    def copy_out(h):
        part = pl.ds(h * Q_BLOCK, Q_BLOCK)
        return pltpu.make_async_copy(done_ref.at[:, part], out_ref.at[:, part], sem.at[h])

    biases = [bias_ref[width - 1, start : start + half, :] for start in (0, half)]
    worst, least = worst_ref[...], None
    for h in range(KEY_VALUE_HEADS):
        columns = slice(h * HEAD_SIZE, (h + 1) * HEAD_SIZE)
        keys, values = k_refs[-1][:, columns], with_ones(v_refs[-1][:, columns])
        for start, bias in zip((0, half), biases):
            queries = stacked_heads(q_ref, slice(start, start + half), h * Q_BLOCK, HEADS_PER_KV)
            scores = scores_of(queries, keys).reshape(HEADS_PER_KV, half, tokens)
            exponents = (scores * EXPONENT + bias[None]).reshape(HEADS_PER_KV * half, tokens)
            worst = jnp.maximum(worst, peak(exponents))
            rows = slice(start * HEADS_PER_KV, (start + half) * HEADS_PER_KV)
            acc = acc_ref[h, rows, :] + product(jnp.exp2(exponents).astype(jnp.bfloat16), values)
            part = jnp.min(acc[:, HEAD_SIZE:].reshape(-1, 8, HEAD_SIZE), axis=0)
            least = part if least is None else jnp.minimum(least, part)
            write(h, start, acc)
        copy_out(h).start()
    redo = out_of_range(worst, least)
    for h in range(KEY_VALUE_HEADS):
        copy_out(h).wait()

    @pl.when(redo)
    def _():
        def step(h, carry):
            columns = span(h * HEAD_SIZE, HEAD_SIZE)
            for start in (0, half):
                queries = stacked_heads(q_ref, slice(start, start + half), h * Q_BLOCK, HEADS_PER_KV)
                state = None
                for parts in parts_in(width):
                    k_part = jnp.concatenate([k_refs[s][:, columns] for s in parts], axis=0)
                    v_part = jnp.concatenate([v_refs[s][:, columns] for s in parts], axis=0)
                    bias = jnp.concatenate([bias_ref[s, start : start + half, :] for s in parts], axis=1)
                    scores = scores_of(queries, k_part).reshape(HEADS_PER_KV, half, bias.shape[1])
                    scores = (scores + bias[None]).reshape(HEADS_PER_KV * half, bias.shape[1])
                    state = fold(state, [scores], [v_part])
                write(h, start, state[1])
            return carry

        lax.fori_loop(0, KEY_VALUE_HEADS, step, 0)
        for h in range(KEY_VALUE_HEADS):
            copy_out(h).start()
        for h in range(KEY_VALUE_HEADS):
            copy_out(h).wait()


def cost(rows, keys, exps):
    return pl.CostEstimate(
        flops=32 * rows * keys * Q_WIDTH, bytes_accessed=4 * rows * Q_WIDTH, transcendentals=exps
    )


def call_first(plan, facts, maxima, query, blocks, keys, values):
    tokens, width = query.shape[0], plan.size
    rows = HEADS_PER_KV * tokens
    f32, bf16 = jnp.float32, jnp.bfloat16
    every = (width - 1) * tokens
    shapes = [
        jax.ShapeDtypeStruct((KEY_VALUE_HEADS, rows, 2 * HEAD_SIZE), f32),
        jax.ShapeDtypeStruct((width, tokens, tokens), f32),
        jax.ShapeDtypeStruct((KEY_VALUE_HEADS, STACKED, 2 * HEAD_SIZE), f32),
        jax.ShapeDtypeStruct((width, STACKED, tokens), f32),
        jax.ShapeDtypeStruct((8, HEAD_SIZE), f32),
        jax.ShapeDtypeStruct((PADDED_ROWS, Q_WIDTH), bf16),
        jax.ShapeDtypeStruct((PADDED_ROWS, 2 * KV_WIDTH), bf16),
        jax.ShapeDtypeStruct((PADDED_ROWS, PADDED_ROWS), bf16),
        jax.ShapeDtypeStruct((8, HEAD_SIZE), jnp.int32),
    ]
    return pl.pallas_call(
        lambda *refs: first_kernel(plan, len(blocks), *refs),
        in_specs=[SMEM] + [VMEM] * (2 + len(blocks) + 2 * (width - 1)),
        out_specs=[VMEM] * len(shapes),
        out_shape=shapes,
        compiler_params=pltpu.CompilerParams(vmem_limit_bytes=(28 + width) * MIB),
        cost_estimate=cost(tokens, every, tokens * every * QUERY_HEADS),
        name="first_shards",
    )(facts, maxima, query, *keys, *values, *blocks)


def call_decode(plan, state, keys, values):
    tokens, width = keys[0].shape[0], plan.size
    return pl.pallas_call(
        lambda *refs: decode_kernel(plan, *refs),
        in_specs=[VMEM] * (6 + 2 * width),
        out_specs=VMEM,
        out_shape=jax.ShapeDtypeStruct((PADDED_ROWS, Q_WIDTH), jnp.bfloat16),
        compiler_params=pltpu.CompilerParams(vmem_limit_bytes=(28 + width) * MIB),
        cost_estimate=cost(PADDED_ROWS, tokens, PADDED_ROWS * tokens * QUERY_HEADS),
        name="last_shard_decode",
    )(*state[2:8], *keys, *values)


def call_prefill(plan, state, query, keys, values):
    tokens, width = query.shape[0], plan.size
    return pl.pallas_call(
        lambda *refs: prefill_kernel(plan, *refs),
        in_specs=[VMEM] * (4 + 2 * width),
        out_specs=ANY,
        out_shape=jax.ShapeDtypeStruct((tokens, Q_WIDTH), jnp.bfloat16),
        scratch_shapes=[
            pltpu.VMEM((tokens, Q_WIDTH), jnp.bfloat16),
            pltpu.SemaphoreType.DMA((KEY_VALUE_HEADS,)),
        ],
        compiler_params=pltpu.CompilerParams(vmem_limit_bytes=(28 + width) * MIB),
        cost_estimate=cost(tokens, tokens, tokens * tokens * QUERY_HEADS),
        name="last_shard_prefill",
    )(*state[:2], state[4], query, *keys, *values)


def start_maxima(*arrays, flops=5 * 10**9):
    def kernel(*refs):
        refs[-1][...] = jnp.full((8, HEAD_SIZE), MASKED, jnp.float32)

    return pl.pallas_call(
        kernel,
        in_specs=[VMEM] * len(arrays),
        out_specs=VMEM,
        out_shape=jax.ShapeDtypeStruct((8, HEAD_SIZE), jnp.float32),
        cost_estimate=pl.CostEstimate(flops=flops, bytes_accessed=0, transcendentals=0),
        compiler_params=pltpu.CompilerParams(vmem_limit_bytes=MIB),
        name="start_maxima",
    )(*arrays)


def paired(array, k):
    return lax.ppermute(array, "pd", [(g, g ^ k) for g in range(lax.axis_size("pd"))])


def body(
    prompt_query,
    prompt_key,
    prompt_value,
    prompt_lengths,
    decode_slot,
    decoded_query,
    decoded_key,
    decoded_value,
):
    plan = Ring(lax.axis_size("tp"))
    pd_size = lax.axis_size("pd")
    own = jnp.concatenate([decoded_query, decoded_key, decoded_value], axis=2).reshape(
        DECODE_ROWS, Q_WIDTH + 2 * KV_WIDTH
    )
    facts = facts_row(plan, prompt_lengths, decode_slot)
    prompt_key, decoded_query = lax.optimization_barrier((prompt_key, decoded_query))
    prompt_value, own = lax.optimization_barrier((prompt_value, own))
    keys, values, maxima = [prompt_key], [prompt_value], None
    for s in range(1, plan.size):
        if s == 2:
            keys[1], own, facts = lax.optimization_barrier((keys[1], own, facts))
        if s == plan.size - 1:
            maxima = start_maxima(keys[-1])
            keys[-1], maxima = lax.optimization_barrier((keys[-1], maxima))
        keys.append(plan.step(keys[-1]))
        values.append(plan.step(values[-1]))
        if s == 2:
            blocks = [own] + [paired(own, k) for k in range(1, pd_size)]

    state = call_first(plan, facts, maxima, prompt_query, blocks, keys[:-1], values[:-1])
    outgoing = call_decode(plan, state, keys, values)
    arrived = [outgoing[:DECODE_STEPS]]
    for k in range(1, pd_size):
        arrived.append(paired(outgoing[k * DECODE_STEPS : (k + 1) * DECODE_STEPS], k))
    pre_out = call_prefill(plan, state, prompt_query, keys, values)

    from_block = state[8][:GROUP_REQUESTS, 0]
    dec_out = jnp.zeros((GROUP_REQUESTS, DECODE_STEPS, Q_WIDTH), jnp.bfloat16)
    for k in range(pd_size):
        dec_out = jnp.where((from_block == k)[:, None, None], arrived[k][None], dec_out)
    return (pre_out, dec_out)


def solution(mesh):
    placed = (
        P(("rep", "pd", "tp"), None),
        P(("rep", "pd", "tp"), None),
        P(("rep", "pd", "tp"), None),
        P("rep", None),
        P("rep"),
        P(("rep", "pd"), None, None),
        P(("rep", "pd"), None, None),
        P(("rep", "pd"), None, None),
    )
    return jax.shard_map(
        body,
        mesh=mesh,
        in_specs=placed,
        out_specs=(P(("rep", "pd", "tp"), None), P(("rep", "pd"), None, None)),
        check_vma=False,
    )
```

```python
import math

import jax
import jax.numpy as jnp
from jax import lax
from jax.experimental import pallas as pl
from jax.experimental.pallas import tpu as pltpu
from jax.sharding import PartitionSpec as P

QUERY_HEADS = 32
KEY_VALUE_HEADS = 4
HEAD_SIZE = 128
PAGE = 16
GROUP_REQUESTS = 4
DECODE_STEPS = 2
HEADS_PER_KV = QUERY_HEADS // KEY_VALUE_HEADS
KV_WIDTH = KEY_VALUE_HEADS * HEAD_SIZE
Q_WIDTH = QUERY_HEADS * HEAD_SIZE
Q_BLOCK = HEADS_PER_KV * HEAD_SIZE
DECODE_ROWS = GROUP_REQUESTS * DECODE_STEPS
PADDED_ROWS = 16
STACKED = HEADS_PER_KV * PADDED_ROWS
MIB = 1024 * 1024

MASKED = -1e30
LIMIT = 60.0
EXPONENT = math.log2(math.e) / math.sqrt(HEAD_SIZE)

VMEM = pl.BlockSpec(memory_space=pltpu.VMEM)
SMEM = pl.BlockSpec(memory_space=pltpu.SMEM)
ANY = pl.BlockSpec(memory_space=pl.ANY)
HBM = pl.BlockSpec(memory_space=pltpu.HBM)


class Ring:
    def __init__(self, size):
        self.size = size
        order = [0] + list(range(1, size, 2)) + [i for i in range(size - 1, 0, -1) if i % 2 == 0]
        self.pairs = [(order[i], order[(i + 1) % size]) for i in range(size)]
        self.offsets = [0]
        for d in range(1, size // 2 + 1):
            self.offsets += [-d, d]
        self.offsets = self.offsets[:size]

    def step(self, array, up):
        return lax.ppermute(array, "tp", self.pairs if up else [(b, a) for a, b in self.pairs])


def scores_of(queries, keys):
    return lax.dot_general(
        queries, keys, (((1,), (1,)), ((), ())), preferred_element_type=jnp.float32
    )


def product(left, right):
    return jnp.dot(left, right, preferred_element_type=jnp.float32)


def iota(shape, axis):
    return lax.broadcasted_iota(jnp.int32, shape, axis)


def span(start, size):
    if isinstance(start, int):
        return slice(start, start + size)
    return pl.ds(pl.multiple_of(start, size), size)


def with_ones(values):
    return jnp.concatenate([values, jnp.ones_like(values)], axis=1)


def page_position(offset, member, width):
    return (offset // PAGE * width + member) * PAGE + offset % PAGE


def key_positions(rows, sources, width):
    column = iota((1, len(sources) * rows), 1)
    part = column // rows
    source = jnp.zeros_like(column) + sources[0]
    for b in range(1, len(sources)):
        source = jnp.where(part == b, sources[b], source)
    return page_position(column - part * rows, source, width)


class Facts:
    def __init__(self, ref, width):
        self.width = width
        self.group, self.member = ref[0], ref[1]
        self.slots = [ref[2 + r] for r in range(GROUP_REQUESTS)]
        first = 2 + GROUP_REQUESTS
        self.ends = []
        total = jnp.int32(0)
        for r in range(GROUP_REQUESTS):
            total = total + ref[first + r] * PAGE
            self.ends.append(total)
        first += GROUP_REQUESTS
        self.source = [ref[first + s] for s in range(width)]
        first += width
        self.owner = [ref[first + p] for p in range(GROUP_REQUESTS)]


def facts_row(plan, lengths, slots):
    width, requests = plan.size, slots.shape[0]

    def kernel(lengths_ref, slots_ref, out_ref):
        group, member = lax.axis_index("pd"), lax.axis_index("tp")
        values = [group, member]
        values += [slots_ref[group * GROUP_REQUESTS + r] for r in range(GROUP_REQUESTS)]
        values += [lengths_ref[group, r] for r in range(GROUP_REQUESTS)]
        place = jnp.where(member % 2 == 1, (member + 1) // 2, width - member // 2)
        for offset in plan.offsets:
            before = (place + width + offset) % width
            up = 2 * before - 1
            values.append(jnp.where(before == 0, 0, jnp.where(before <= width // 2, up, 2 * (width - before))))
        for i, value in enumerate(values):
            out_ref[i] = value.astype(jnp.int32)
        for q in range(requests):
            place = slots_ref[q] - group * GROUP_REQUESTS

            @pl.when((place >= 0) & (place < GROUP_REQUESTS))
            def _():
                out_ref[len(values) + place] = group ^ (q // GROUP_REQUESTS)

    length = 2 + 2 * GROUP_REQUESTS + width + GROUP_REQUESTS
    return pl.pallas_call(
        kernel,
        in_specs=[SMEM, SMEM],
        out_specs=SMEM,
        out_shape=jax.ShapeDtypeStruct((length,), jnp.int32),
        cost_estimate=pl.CostEstimate(flops=5 * 10**9, bytes_accessed=0, transcendentals=0),
        name="facts",
    )(lengths, slots)


def causal_bias(start, rows, keys, sources, ends, member, width):
    qpos = page_position(start + iota((rows, 1), 0), member, width)
    low = jnp.zeros_like(qpos)
    for end in ends:
        low = jnp.where(qpos >= end, end, low)
    kpos = key_positions(keys, sources, width)
    return jnp.where((kpos >= low) & (kpos <= qpos), 0.0, MASKED)


def request_mask(ends, keys, sources, width):
    request = iota((STACKED, 1), 0) % PADDED_ROWS // DECODE_STEPS
    low = jnp.zeros_like(request)
    high = jnp.zeros_like(request) + ends[0]
    for r in range(1, GROUP_REQUESTS):
        low = jnp.where(request == r, ends[r - 1], low)
        high = jnp.where(request == r, ends[r], high)
    kpos = key_positions(keys, sources, width)
    return (kpos >= low) & (kpos < high)


def stacked_heads(ref, rows, first, count):
    return jnp.concatenate(
        [ref[rows, span(first + i * HEAD_SIZE, HEAD_SIZE)] for i in range(count)], axis=0
    )


def each_kv_head(width, step):
    if width <= 8:
        for h in range(KEY_VALUE_HEADS):
            step(h)
    else:
        lax.fori_loop(0, KEY_VALUE_HEADS, lambda h, c: (step(h), c)[1], 0)


def peak(exponents):
    return jnp.max(exponents.reshape(-1, 8, exponents.shape[-1]), axis=0)


def picked_rows(facts, pd_size, block_refs):
    row = iota((PADDED_ROWS, DECODE_ROWS), 0)
    column = iota((PADDED_ROWS, DECODE_ROWS), 1)
    total = None
    for k in range(pd_size):
        pick = column < 0
        for r in range(GROUP_REQUESTS):
            slot = facts.slots[r]
            first = jnp.where(facts.group ^ (slot // GROUP_REQUESTS) == k, slot % GROUP_REQUESTS * DECODE_STEPS, -DECODE_ROWS * 4)
            pick = pick | ((row // DECODE_STEPS == r) & (column == first + row - r * DECODE_STEPS))
        part = product(pick.astype(jnp.float32).astype(jnp.bfloat16), block_refs[k][...])
        total = part if total is None else total + part
    return total.astype(jnp.bfloat16)


def pick_matrix(facts):
    row = iota((PADDED_ROWS, PADDED_ROWS), 0)
    column = iota((PADDED_ROWS, PADDED_ROWS), 1)
    pick = column < 0
    for r in range(GROUP_REQUESTS):
        ahead = facts.group ^ (facts.slots[r] // GROUP_REQUESTS)
        pick = pick | (
            (column // DECODE_STEPS == r) & (row == ahead * DECODE_STEPS + column - r * DECODE_STEPS)
        )
    return pick.astype(jnp.float32).astype(jnp.bfloat16)


def fresh_mask():
    row = iota((STACKED, PADDED_ROWS), 0) % PADDED_ROWS
    column = iota((STACKED, PADDED_ROWS), 1)
    return (column // DECODE_STEPS == row // DECODE_STEPS) & (
        column % DECODE_STEPS <= row % DECODE_STEPS
    )


def first_kernel(plan, pd_size, facts_ref, maxima_ref, q_ref, *refs):
    width = plan.size
    kv_refs, refs = refs[: width - 1], refs[width - 1 :]
    block_refs, refs = refs[:pd_size], refs[pd_size:]
    acc_ref, bias_ref, dec_acc_ref, dec_bias_ref, worst_ref, queries_ref, fresh_ref, pick_ref, owner_ref = refs
    tokens = q_ref.shape[0]
    half = tokens // 2
    facts = Facts(facts_ref, width)
    sources = facts.source[:-1]
    pick_ref[...] = pick_matrix(facts)
    slot = iota((8, HEAD_SIZE), 0)
    owner = jnp.zeros_like(slot)
    for p in range(GROUP_REQUESTS):
        owner = jnp.where(slot == p, facts.owner[p], owner)
    owner_ref[...] = owner
    for s in range(width):
        bias_ref[s] = causal_bias(0, tokens, tokens, facts.source[s : s + 1], facts.ends, facts.member, width)
        dec_bias_ref[s] = jnp.where(
            request_mask(facts.ends, tokens, facts.source[s : s + 1], width), 0.0, MASKED
        )
    rows = picked_rows(facts, pd_size, block_refs)
    queries_ref[...] = rows[:, :Q_WIDTH]
    fresh_ref[...] = rows[:, Q_WIDTH:]
    worst_ref[...] = maxima_ref[...]
    new_mask = fresh_mask()
    mask = request_mask(facts.ends, tokens, sources, width)
    spans = ((0, half), (half, tokens))
    biases = [
        causal_bias(s, half, keys, sources, facts.ends, facts.member, width) for s, keys in spans
    ]
    together = max(1, min(HEADS_PER_KV, HEADS_PER_KV * 4 // width))

    def weigh(exponents):
        top = jnp.max(peak(exponents), axis=1, keepdims=True)
        worst_ref[...] = jnp.maximum(worst_ref[...], top)
        return jnp.exp2(exponents).astype(jnp.bfloat16)

    def step(h):
        columns = span(h * HEAD_SIZE, HEAD_SIZE)
        first = h * Q_BLOCK
        queries = stacked_heads(queries_ref, slice(None), first, HEADS_PER_KV)
        k_all = jnp.concatenate([ref[:tokens, columns] for ref in kv_refs], axis=0)
        v_all = with_ones(jnp.concatenate([ref[tokens:, columns] for ref in kv_refs], axis=0))
        new_scores = scores_of(queries, fresh_ref[:, columns]) * EXPONENT
        new_weights = weigh(jnp.where(new_mask, new_scores, MASKED))
        new_values = fresh_ref[:, span(KV_WIDTH + h * HEAD_SIZE, HEAD_SIZE)]
        weights = weigh(jnp.where(mask, scores_of(queries, k_all) * EXPONENT, MASKED))
        dec_acc_ref[h] = product(weights, v_all) + product(new_weights, with_ones(new_values))
        for (start, keys), bias in zip(spans, biases):
            if keys < tokens:
                k_part = jnp.concatenate([ref[:keys, columns] for ref in kv_refs], axis=0)
                v_part = with_ones(
                    jnp.concatenate([ref[tokens : tokens + keys, columns] for ref in kv_refs], axis=0)
                )
            else:
                k_part, v_part = k_all, v_all
            for g in range(0, HEADS_PER_KV, together):
                queries = stacked_heads(
                    q_ref, slice(start, start + half), first + g * HEAD_SIZE, together
                )
                scores = scores_of(queries, k_part).reshape(together, half, bias.shape[1])
                exponents = (scores * EXPONENT + bias[None]).reshape(together * half, bias.shape[1])
                rows = slice(
                    start * HEADS_PER_KV + g * half, start * HEADS_PER_KV + (g + together) * half
                )
                acc_ref[h, rows, :] = product(weigh(exponents), v_part)

    each_kv_head(width, step)


def divided(acc):
    return (acc[:, :HEAD_SIZE] * pl.reciprocal(acc[:, HEAD_SIZE:], approx=True)).astype(jnp.bfloat16)


def fold(state, scores_list, values_list):
    top = None if state is None else state[0]
    for scores in scores_list:
        part = jnp.max(scores, axis=1, keepdims=True)
        top = part if top is None else jnp.maximum(top, part)
    acc = None
    for scores, values in zip(scores_list, values_list):
        weights = jnp.exp2((scores - top) * EXPONENT).astype(jnp.bfloat16)
        part = product(weights, with_ones(values))
        acc = part if acc is None else acc + part
    if state is not None:
        acc = acc + state[1] * jnp.exp2((state[0] - top) * EXPONENT)
    return top, acc


def parts_in(width):
    return [range(c, min(c + 4, width)) for c in range(0, width, 4)]


def out_of_range(worst, least):
    return (jnp.max(worst) > LIMIT) | (jnp.min(least) < 2.0**-LIMIT)


def decode_kernel(plan, acc_ref, bias_ref, worst_ref, queries_ref, fresh_ref, pick_ref, *refs):
    width = plan.size
    kv_refs, (out_ref,) = refs[:width], refs[width:]
    tokens = kv_refs[0].shape[0] // 2
    heads = range(KEY_VALUE_HEADS)
    columns = [slice(h * HEAD_SIZE, (h + 1) * HEAD_SIZE) for h in heads]

    def queries_of(h):
        return stacked_heads(queries_ref, slice(None), h * Q_BLOCK, HEADS_PER_KV)

    def send(acc):
        out = [divided(a) for a in acc]
        out = jnp.concatenate(
            [o[g * PADDED_ROWS : (g + 1) * PADDED_ROWS] for o in out for g in range(HEADS_PER_KV)], axis=1
        )
        out_ref[...] = product(pick_ref[...], out).astype(jnp.bfloat16)

    exponents = [
        scores_of(queries_of(h), kv_refs[-1][:tokens, columns[h]]) * EXPONENT + bias_ref[width - 1]
        for h in heads
    ]
    acc = [
        acc_ref[h] + product(jnp.exp2(exponents[h]).astype(jnp.bfloat16), with_ones(kv_refs[-1][tokens:, columns[h]]))
        for h in heads
    ]
    send(acc)
    worst, least = worst_ref[...], None
    for h in heads:
        worst = jnp.maximum(worst, peak(exponents[h]))
        part = jnp.min(acc[h][:, HEAD_SIZE:].reshape(-1, 8, HEAD_SIZE), axis=0)
        least = part if least is None else jnp.minimum(least, part)

    @pl.when(out_of_range(worst, least))
    def _():
        new_mask = fresh_mask()
        again = []
        for h in heads:
            queries = queries_of(h)
            scores = jnp.where(new_mask, scores_of(queries, fresh_ref[:, columns[h]]), MASKED)
            new_columns = slice(KV_WIDTH + h * HEAD_SIZE, KV_WIDTH + (h + 1) * HEAD_SIZE)
            state = fold(None, [scores], [fresh_ref[:, new_columns]])
            for parts in parts_in(width):
                k_part = jnp.concatenate([kv_refs[s][:tokens, columns[h]] for s in parts], axis=0)
                v_part = jnp.concatenate([kv_refs[s][tokens:, columns[h]] for s in parts], axis=0)
                bias = jnp.concatenate([bias_ref[s] for s in parts], axis=1)
                state = fold(state, [scores_of(queries, k_part) + bias], [v_part])
            again.append(state[1])
        send(again)


def prefill_kernel(plan, acc_ref, bias_ref, worst_ref, q_ref, *refs):
    width = plan.size
    kv_refs, refs = refs[:width], refs[width:]
    out_ref, done_ref, sem = refs
    tokens = q_ref.shape[0]
    half = tokens // 2
    def write(h, start, acc):
        out = divided(acc)
        for g in range(HEADS_PER_KV):
            done_ref[start : start + half, span(h * Q_BLOCK + g * HEAD_SIZE, HEAD_SIZE)] = out[
                g * half : (g + 1) * half
            ]

    def copy_out(h):
        part = pl.ds(h * Q_BLOCK, Q_BLOCK)
        return pltpu.make_async_copy(done_ref.at[:, part], out_ref.at[:, part], sem.at[h])

    biases = [bias_ref[width - 1, start : start + half, :] for start in (0, half)]
    worst, least = worst_ref[...], None
    for h in range(KEY_VALUE_HEADS):
        columns = slice(h * HEAD_SIZE, (h + 1) * HEAD_SIZE)
        keys, values = kv_refs[-1][:tokens, columns], with_ones(kv_refs[-1][tokens:, columns])
        for start, bias in zip((0, half), biases):
            queries = stacked_heads(q_ref, slice(start, start + half), h * Q_BLOCK, HEADS_PER_KV)
            scores = scores_of(queries, keys).reshape(HEADS_PER_KV, half, tokens)
            exponents = (scores * EXPONENT + bias[None]).reshape(HEADS_PER_KV * half, tokens)
            worst = jnp.maximum(worst, peak(exponents))
            rows = slice(start * HEADS_PER_KV, (start + half) * HEADS_PER_KV)
            acc = acc_ref[h, rows, :] + product(jnp.exp2(exponents).astype(jnp.bfloat16), values)
            part = jnp.min(acc[:, HEAD_SIZE:].reshape(-1, 8, HEAD_SIZE), axis=0)
            least = part if least is None else jnp.minimum(least, part)
            write(h, start, acc)
        copy_out(h).start()
    redo = out_of_range(worst, least)
    for h in range(KEY_VALUE_HEADS):
        copy_out(h).wait()

    @pl.when(redo)
    def _():
        def step(h, carry):
            columns = span(h * HEAD_SIZE, HEAD_SIZE)
            for start in (0, half):
                queries = stacked_heads(q_ref, slice(start, start + half), h * Q_BLOCK, HEADS_PER_KV)
                state = None
                for parts in parts_in(width):
                    k_part = jnp.concatenate([kv_refs[s][:tokens, columns] for s in parts], axis=0)
                    v_part = jnp.concatenate([kv_refs[s][tokens:, columns] for s in parts], axis=0)
                    bias = jnp.concatenate([bias_ref[s, start : start + half, :] for s in parts], axis=1)
                    scores = scores_of(queries, k_part).reshape(HEADS_PER_KV, half, bias.shape[1])
                    scores = (scores + bias[None]).reshape(HEADS_PER_KV * half, bias.shape[1])
                    state = fold(state, [scores], [v_part])
                write(h, start, state[1])
            return carry

        lax.fori_loop(0, KEY_VALUE_HEADS, step, 0)
        for h in range(KEY_VALUE_HEADS):
            copy_out(h).start()
        for h in range(KEY_VALUE_HEADS):
            copy_out(h).wait()


def cost(rows, keys, exps):
    return pl.CostEstimate(
        flops=32 * rows * keys * Q_WIDTH, bytes_accessed=4 * rows * Q_WIDTH, transcendentals=exps
    )


def call_first(plan, facts, maxima, query, blocks, pieces):
    tokens, width = query.shape[0], plan.size
    rows = HEADS_PER_KV * tokens
    f32, bf16 = jnp.float32, jnp.bfloat16
    every = (width - 1) * tokens
    shapes = [
        jax.ShapeDtypeStruct((KEY_VALUE_HEADS, rows, 2 * HEAD_SIZE), f32),
        jax.ShapeDtypeStruct((width, tokens, tokens), f32),
        jax.ShapeDtypeStruct((KEY_VALUE_HEADS, STACKED, 2 * HEAD_SIZE), f32),
        jax.ShapeDtypeStruct((width, STACKED, tokens), f32),
        jax.ShapeDtypeStruct((8, HEAD_SIZE), f32),
        jax.ShapeDtypeStruct((PADDED_ROWS, Q_WIDTH), bf16),
        jax.ShapeDtypeStruct((PADDED_ROWS, 2 * KV_WIDTH), bf16),
        jax.ShapeDtypeStruct((PADDED_ROWS, PADDED_ROWS), bf16),
        jax.ShapeDtypeStruct((8, HEAD_SIZE), jnp.int32),
    ]
    return pl.pallas_call(
        lambda *refs: first_kernel(plan, len(blocks), *refs),
        in_specs=[SMEM] + [VMEM] * (2 + len(blocks) + width - 1),
        out_specs=[VMEM] * len(shapes),
        out_shape=shapes,
        compiler_params=pltpu.CompilerParams(vmem_limit_bytes=(28 + width) * MIB),
        cost_estimate=cost(tokens, every, tokens * every * QUERY_HEADS),
        name="first_shards",
    )(facts, maxima, query, *pieces, *blocks)


def call_decode(plan, state, pieces):
    tokens, width = pieces[0].shape[0] // 2, plan.size
    return pl.pallas_call(
        lambda *refs: decode_kernel(plan, *refs),
        in_specs=[VMEM] * (6 + width),
        out_specs=VMEM,
        out_shape=jax.ShapeDtypeStruct((PADDED_ROWS, Q_WIDTH), jnp.bfloat16),
        compiler_params=pltpu.CompilerParams(vmem_limit_bytes=(28 + width) * MIB),
        cost_estimate=cost(PADDED_ROWS, tokens, PADDED_ROWS * tokens * QUERY_HEADS),
        name="last_shard_decode",
    )(*state[2:8], *pieces)


def call_prefill(plan, state, query, pieces):
    tokens, width = query.shape[0], plan.size
    return pl.pallas_call(
        lambda *refs: prefill_kernel(plan, *refs),
        in_specs=[VMEM] * (4 + width),
        out_specs=ANY,
        out_shape=jax.ShapeDtypeStruct((tokens, Q_WIDTH), jnp.bfloat16),
        scratch_shapes=[
            pltpu.VMEM((tokens, Q_WIDTH), jnp.bfloat16),
            pltpu.SemaphoreType.DMA((KEY_VALUE_HEADS,)),
        ],
        compiler_params=pltpu.CompilerParams(vmem_limit_bytes=(28 + width) * MIB),
        cost_estimate=cost(tokens, tokens, tokens * tokens * QUERY_HEADS),
        name="last_shard_prefill",
    )(*state[:2], state[4], query, *pieces)


def start_maxima(*arrays, flops=5 * 10**9):
    def kernel(*refs):
        refs[-1][...] = jnp.full((8, HEAD_SIZE), MASKED, jnp.float32)

    return pl.pallas_call(
        kernel,
        in_specs=[VMEM] * len(arrays),
        out_specs=VMEM,
        out_shape=jax.ShapeDtypeStruct((8, HEAD_SIZE), jnp.float32),
        cost_estimate=pl.CostEstimate(flops=flops, bytes_accessed=0, transcendentals=0),
        compiler_params=pltpu.CompilerParams(vmem_limit_bytes=MIB),
        name="start_maxima",
    )(*arrays)


def paired(array, k):
    return lax.ppermute(array, "pd", [(g, g ^ k) for g in range(lax.axis_size("pd"))])


def body(
    prompt_query,
    prompt_key,
    prompt_value,
    prompt_lengths,
    decode_slot,
    decoded_query,
    decoded_key,
    decoded_value,
):
    plan = Ring(lax.axis_size("tp"))
    pd_size = lax.axis_size("pd")
    own = jnp.concatenate([decoded_query, decoded_key, decoded_value], axis=2).reshape(
        DECODE_ROWS, Q_WIDTH + 2 * KV_WIDTH
    )
    facts = facts_row(plan, prompt_lengths, decode_slot)
    kv, decoded_query = lax.optimization_barrier(
        (jnp.concatenate([prompt_key, prompt_value], axis=0), decoded_query)
    )
    later_kv, own = lax.optimization_barrier((kv, own))
    pieces, maxima, up, down = [kv], None, kv, later_kv
    for d in range(1, plan.size // 2 + 1):
        if d == 2:
            up, facts = lax.optimization_barrier((up, facts))
        up = plan.step(up, True)
        down = plan.step(down, False) if 2 * d < plan.size else None
        pieces += [up, down]
    pieces = pieces[: plan.size]
    blocks = [own] + [paired(own, k) for k in range(1, pd_size)]
    maxima = start_maxima(pieces[1])

    state = call_first(plan, facts, maxima, prompt_query, blocks, pieces[:-1])
    outgoing = call_decode(plan, state, pieces)
    arrived = [outgoing[:DECODE_STEPS]]
    for k in range(1, pd_size):
        arrived.append(paired(outgoing[k * DECODE_STEPS : (k + 1) * DECODE_STEPS], k))
    pre_out = call_prefill(plan, state, prompt_query, pieces)

    from_block = state[8][:GROUP_REQUESTS, 0]
    dec_out = jnp.zeros((GROUP_REQUESTS, DECODE_STEPS, Q_WIDTH), jnp.bfloat16)
    for k in range(pd_size):
        dec_out = jnp.where((from_block == k)[:, None, None], arrived[k][None], dec_out)
    return (pre_out, dec_out)


def solution(mesh):
    placed = (
        P(("rep", "pd", "tp"), None),
        P(("rep", "pd", "tp"), None),
        P(("rep", "pd", "tp"), None),
        P("rep", None),
        P("rep"),
        P(("rep", "pd"), None, None),
        P(("rep", "pd"), None, None),
        P(("rep", "pd"), None, None),
    )
    return jax.shard_map(
        body,
        mesh=mesh,
        in_specs=placed,
        out_specs=(P(("rep", "pd", "tp"), None), P(("rep", "pd"), None, None)),
        check_vma=False,
    )
```

```python
import math

import jax
import jax.numpy as jnp
from jax import lax
from jax.experimental import pallas as pl
from jax.experimental.pallas import tpu as pltpu
from jax.sharding import PartitionSpec as P

QUERY_HEADS = 32
KEY_VALUE_HEADS = 4
HEAD_SIZE = 128
PAGE = 16
GROUP_REQUESTS = 4
DECODE_STEPS = 2
HEADS_PER_KV = QUERY_HEADS // KEY_VALUE_HEADS
KV_WIDTH = KEY_VALUE_HEADS * HEAD_SIZE
Q_WIDTH = QUERY_HEADS * HEAD_SIZE
Q_BLOCK = HEADS_PER_KV * HEAD_SIZE
DECODE_ROWS = GROUP_REQUESTS * DECODE_STEPS
PADDED_ROWS = 16
STACKED = HEADS_PER_KV * PADDED_ROWS
MIB = 1024 * 1024

MASKED = -1e30
LIMIT = 60.0
EXPONENT = math.log2(math.e) / math.sqrt(HEAD_SIZE)

VMEM = pl.BlockSpec(memory_space=pltpu.VMEM)
SMEM = pl.BlockSpec(memory_space=pltpu.SMEM)
ANY = pl.BlockSpec(memory_space=pl.ANY)
HBM = pl.BlockSpec(memory_space=pltpu.HBM)


class Ring:
    def __init__(self, size):
        self.size = size
        order = [0] + list(range(1, size, 2)) + [i for i in range(size - 1, 0, -1) if i % 2 == 0]
        self.pairs = [(order[i], order[(i + 1) % size]) for i in range(size)]
        self.offsets = [0]
        for d in range(1, size // 2 + 1):
            self.offsets += [-d, d]
        self.offsets = self.offsets[:size]

    def step(self, array, up):
        return lax.ppermute(array, "tp", self.pairs if up else [(b, a) for a, b in self.pairs])


def scores_of(queries, keys):
    return lax.dot_general(
        queries, keys, (((1,), (1,)), ((), ())), preferred_element_type=jnp.float32
    )


def product(left, right):
    return jnp.dot(left, right, preferred_element_type=jnp.float32)


def iota(shape, axis):
    return lax.broadcasted_iota(jnp.int32, shape, axis)


def span(start, size):
    if isinstance(start, int):
        return slice(start, start + size)
    return pl.ds(pl.multiple_of(start, size), size)


def with_ones(values):
    return jnp.concatenate([values, jnp.ones_like(values)], axis=1)


def page_position(offset, member, width):
    return (offset // PAGE * width + member) * PAGE + offset % PAGE


def key_positions(rows, sources, width):
    column = iota((1, len(sources) * rows), 1)
    part = column // rows
    source = jnp.zeros_like(column) + sources[0]
    for b in range(1, len(sources)):
        source = jnp.where(part == b, sources[b], source)
    return page_position(column - part * rows, source, width)


class Facts:
    def __init__(self, ref, width):
        self.width = width
        self.group, self.member = ref[0], ref[1]
        self.slots = [ref[2 + r] for r in range(GROUP_REQUESTS)]
        first = 2 + GROUP_REQUESTS
        self.ends = []
        total = jnp.int32(0)
        for r in range(GROUP_REQUESTS):
            total = total + ref[first + r] * PAGE
            self.ends.append(total)
        first += GROUP_REQUESTS
        self.source = [ref[first + s] for s in range(width)]
        first += width
        self.owner = [ref[first + p] for p in range(GROUP_REQUESTS)]


def facts_row(plan, lengths, slots):
    width, requests = plan.size, slots.shape[0]

    def kernel(lengths_ref, slots_ref, out_ref):
        group, member = lax.axis_index("pd"), lax.axis_index("tp")
        values = [group, member]
        values += [slots_ref[group * GROUP_REQUESTS + r] for r in range(GROUP_REQUESTS)]
        values += [lengths_ref[group, r] for r in range(GROUP_REQUESTS)]
        place = jnp.where(member % 2 == 1, (member + 1) // 2, width - member // 2)
        for offset in plan.offsets:
            before = (place + width + offset) % width
            up = 2 * before - 1
            values.append(jnp.where(before == 0, 0, jnp.where(before <= width // 2, up, 2 * (width - before))))
        for i, value in enumerate(values):
            out_ref[i] = value.astype(jnp.int32)
        for q in range(requests):
            place = slots_ref[q] - group * GROUP_REQUESTS

            @pl.when((place >= 0) & (place < GROUP_REQUESTS))
            def _():
                out_ref[len(values) + place] = group ^ (q // GROUP_REQUESTS)

    length = 2 + 2 * GROUP_REQUESTS + width + GROUP_REQUESTS
    return pl.pallas_call(
        kernel,
        in_specs=[SMEM, SMEM],
        out_specs=SMEM,
        out_shape=jax.ShapeDtypeStruct((length,), jnp.int32),
        cost_estimate=pl.CostEstimate(flops=5 * 10**9, bytes_accessed=0, transcendentals=0),
        name="facts",
    )(lengths, slots)


def causal_bias(start, rows, keys, sources, ends, member, width):
    qpos = page_position(start + iota((rows, 1), 0), member, width)
    low = jnp.zeros_like(qpos)
    for end in ends:
        low = jnp.where(qpos >= end, end, low)
    kpos = key_positions(keys, sources, width)
    return jnp.where((kpos >= low) & (kpos <= qpos), 0.0, MASKED)


def request_mask(ends, keys, sources, width):
    request = iota((STACKED, 1), 0) % PADDED_ROWS // DECODE_STEPS
    low = jnp.zeros_like(request)
    high = jnp.zeros_like(request) + ends[0]
    for r in range(1, GROUP_REQUESTS):
        low = jnp.where(request == r, ends[r - 1], low)
        high = jnp.where(request == r, ends[r], high)
    kpos = key_positions(keys, sources, width)
    return (kpos >= low) & (kpos < high)


def stacked_heads(ref, rows, first, count):
    return jnp.concatenate(
        [ref[rows, span(first + i * HEAD_SIZE, HEAD_SIZE)] for i in range(count)], axis=0
    )


def each_kv_head(width, step):
    if width <= 8:
        for h in range(KEY_VALUE_HEADS):
            step(h)
    else:
        lax.fori_loop(0, KEY_VALUE_HEADS, lambda h, c: (step(h), c)[1], 0)


def peak(exponents):
    return jnp.max(exponents.reshape(-1, 8, exponents.shape[-1]), axis=0)


def picked_rows(facts, pd_size, block_refs):
    row = iota((PADDED_ROWS, DECODE_ROWS), 0)
    column = iota((PADDED_ROWS, DECODE_ROWS), 1)
    total = None
    for k in range(pd_size):
        pick = column < 0
        for r in range(GROUP_REQUESTS):
            slot = facts.slots[r]
            first = jnp.where(facts.group ^ (slot // GROUP_REQUESTS) == k, slot % GROUP_REQUESTS * DECODE_STEPS, -DECODE_ROWS * 4)
            pick = pick | ((row // DECODE_STEPS == r) & (column == first + row - r * DECODE_STEPS))
        part = product(pick.astype(jnp.float32).astype(jnp.bfloat16), block_refs[k][...])
        total = part if total is None else total + part
    return total.astype(jnp.bfloat16)


def pick_matrix(facts):
    row = iota((PADDED_ROWS, PADDED_ROWS), 0)
    column = iota((PADDED_ROWS, PADDED_ROWS), 1)
    pick = column < 0
    for r in range(GROUP_REQUESTS):
        ahead = facts.group ^ (facts.slots[r] // GROUP_REQUESTS)
        pick = pick | (
            (column // DECODE_STEPS == r) & (row == ahead * DECODE_STEPS + column - r * DECODE_STEPS)
        )
    return pick.astype(jnp.float32).astype(jnp.bfloat16)


def fresh_mask():
    row = iota((STACKED, PADDED_ROWS), 0) % PADDED_ROWS
    column = iota((STACKED, PADDED_ROWS), 1)
    return (column // DECODE_STEPS == row // DECODE_STEPS) & (
        column % DECODE_STEPS <= row % DECODE_STEPS
    )


def first_kernel(plan, pd_size, facts_ref, maxima_ref, q_ref, *refs):
    width = plan.size
    kv_refs, refs = refs[: width - 2], refs[width - 2 :]
    block_refs, refs = refs[:pd_size], refs[pd_size:]
    acc_ref, bias_ref, dec_acc_ref, dec_bias_ref, worst_ref, queries_ref, fresh_ref, pick_ref, owner_ref = refs
    tokens = q_ref.shape[0]
    half = tokens // 2
    facts = Facts(facts_ref, width)
    sources = facts.source[:-2]
    pick_ref[...] = pick_matrix(facts)
    slot = iota((8, HEAD_SIZE), 0)
    owner = jnp.zeros_like(slot)
    for p in range(GROUP_REQUESTS):
        owner = jnp.where(slot == p, facts.owner[p], owner)
    owner_ref[...] = owner
    for s in range(width):
        bias_ref[s] = causal_bias(0, tokens, tokens, facts.source[s : s + 1], facts.ends, facts.member, width)
        dec_bias_ref[s] = jnp.where(
            request_mask(facts.ends, tokens, facts.source[s : s + 1], width), 0.0, MASKED
        )
    rows = picked_rows(facts, pd_size, block_refs)
    queries_ref[...] = rows[:, :Q_WIDTH]
    fresh_ref[...] = rows[:, Q_WIDTH:]
    worst_ref[...] = maxima_ref[...]
    new_mask = fresh_mask()
    mask = request_mask(facts.ends, tokens, sources, width)
    spans = ((0, half), (half, tokens))
    biases = [
        causal_bias(s, half, keys, sources, facts.ends, facts.member, width) for s, keys in spans
    ]
    together = max(1, min(HEADS_PER_KV, HEADS_PER_KV * 4 // width))

    def weigh(exponents):
        top = jnp.max(peak(exponents), axis=1, keepdims=True)
        worst_ref[...] = jnp.maximum(worst_ref[...], top)
        return jnp.exp2(exponents).astype(jnp.bfloat16)

    def step(h):
        columns = span(h * HEAD_SIZE, HEAD_SIZE)
        first = h * Q_BLOCK
        queries = stacked_heads(queries_ref, slice(None), first, HEADS_PER_KV)
        k_all = jnp.concatenate([ref[:tokens, columns] for ref in kv_refs], axis=0)
        v_all = with_ones(jnp.concatenate([ref[tokens:, columns] for ref in kv_refs], axis=0))
        new_scores = scores_of(queries, fresh_ref[:, columns]) * EXPONENT
        new_weights = weigh(jnp.where(new_mask, new_scores, MASKED))
        new_values = fresh_ref[:, span(KV_WIDTH + h * HEAD_SIZE, HEAD_SIZE)]
        weights = weigh(jnp.where(mask, scores_of(queries, k_all) * EXPONENT, MASKED))
        dec_acc_ref[h] = product(weights, v_all) + product(new_weights, with_ones(new_values))
        for (start, keys), bias in zip(spans, biases):
            if keys < tokens:
                k_part = jnp.concatenate([ref[:keys, columns] for ref in kv_refs], axis=0)
                v_part = with_ones(
                    jnp.concatenate([ref[tokens : tokens + keys, columns] for ref in kv_refs], axis=0)
                )
            else:
                k_part, v_part = k_all, v_all
            for g in range(0, HEADS_PER_KV, together):
                queries = stacked_heads(
                    q_ref, slice(start, start + half), first + g * HEAD_SIZE, together
                )
                scores = scores_of(queries, k_part).reshape(together, half, bias.shape[1])
                exponents = (scores * EXPONENT + bias[None]).reshape(together * half, bias.shape[1])
                rows = slice(
                    start * HEADS_PER_KV + g * half, start * HEADS_PER_KV + (g + together) * half
                )
                acc_ref[h, rows, :] = product(weigh(exponents), v_part)

    each_kv_head(width, step)


def middle_kernel(plan, acc_ref, bias_ref, dec_acc_ref, dec_bias_ref, worst_ref, queries_ref, q_ref, kv_ref, *refs):
    new_acc_ref, new_dec_acc_ref, new_worst_ref = refs
    piece = plan.size - 2
    tokens = q_ref.shape[0]
    half = tokens // 2
    worst = worst_ref[...]
    for h in range(KEY_VALUE_HEADS):
        columns = slice(h * HEAD_SIZE, (h + 1) * HEAD_SIZE)
        keys, values = kv_ref[:tokens, columns], with_ones(kv_ref[tokens:, columns])
        queries = stacked_heads(queries_ref, slice(None), h * Q_BLOCK, HEADS_PER_KV)
        exponents = scores_of(queries, keys) * EXPONENT + dec_bias_ref[piece]
        worst = jnp.maximum(worst, peak(exponents))
        new_dec_acc_ref[h] = dec_acc_ref[h] + product(jnp.exp2(exponents).astype(jnp.bfloat16), values)
        for start in (0, half):
            bias = bias_ref[piece, start : start + half, :]
            queries = stacked_heads(q_ref, slice(start, start + half), h * Q_BLOCK, HEADS_PER_KV)
            scores = scores_of(queries, keys).reshape(HEADS_PER_KV, half, tokens)
            exponents = (scores * EXPONENT + bias[None]).reshape(HEADS_PER_KV * half, tokens)
            worst = jnp.maximum(worst, peak(exponents))
            rows = slice(start * HEADS_PER_KV, (start + half) * HEADS_PER_KV)
            new_acc_ref[h, rows, :] = acc_ref[h, rows, :] + product(
                jnp.exp2(exponents).astype(jnp.bfloat16), values
            )
    new_worst_ref[...] = worst


def divided(acc):
    return (acc[:, :HEAD_SIZE] * pl.reciprocal(acc[:, HEAD_SIZE:], approx=True)).astype(jnp.bfloat16)


def fold(state, scores_list, values_list):
    top = None if state is None else state[0]
    for scores in scores_list:
        part = jnp.max(scores, axis=1, keepdims=True)
        top = part if top is None else jnp.maximum(top, part)
    acc = None
    for scores, values in zip(scores_list, values_list):
        weights = jnp.exp2((scores - top) * EXPONENT).astype(jnp.bfloat16)
        part = product(weights, with_ones(values))
        acc = part if acc is None else acc + part
    if state is not None:
        acc = acc + state[1] * jnp.exp2((state[0] - top) * EXPONENT)
    return top, acc


def parts_in(width):
    return [range(c, min(c + 4, width)) for c in range(0, width, 4)]


def out_of_range(worst, least):
    return (jnp.max(worst) > LIMIT) | (jnp.min(least) < 2.0**-LIMIT)


def decode_kernel(plan, acc_ref, bias_ref, worst_ref, queries_ref, fresh_ref, pick_ref, *refs):
    width = plan.size
    kv_refs, (out_ref,) = refs[:width], refs[width:]
    tokens = kv_refs[0].shape[0] // 2
    heads = range(KEY_VALUE_HEADS)
    columns = [slice(h * HEAD_SIZE, (h + 1) * HEAD_SIZE) for h in heads]

    def queries_of(h):
        return stacked_heads(queries_ref, slice(None), h * Q_BLOCK, HEADS_PER_KV)

    def send(acc):
        out = [divided(a) for a in acc]
        out = jnp.concatenate(
            [o[g * PADDED_ROWS : (g + 1) * PADDED_ROWS] for o in out for g in range(HEADS_PER_KV)], axis=1
        )
        out_ref[...] = product(pick_ref[...], out).astype(jnp.bfloat16)

    exponents = [
        scores_of(queries_of(h), kv_refs[-1][:tokens, columns[h]]) * EXPONENT + bias_ref[width - 1]
        for h in heads
    ]
    acc = [
        acc_ref[h] + product(jnp.exp2(exponents[h]).astype(jnp.bfloat16), with_ones(kv_refs[-1][tokens:, columns[h]]))
        for h in heads
    ]
    send(acc)
    worst, least = worst_ref[...], None
    for h in heads:
        worst = jnp.maximum(worst, peak(exponents[h]))
        part = jnp.min(acc[h][:, HEAD_SIZE:].reshape(-1, 8, HEAD_SIZE), axis=0)
        least = part if least is None else jnp.minimum(least, part)

    @pl.when(out_of_range(worst, least))
    def _():
        new_mask = fresh_mask()
        again = []
        for h in heads:
            queries = queries_of(h)
            scores = jnp.where(new_mask, scores_of(queries, fresh_ref[:, columns[h]]), MASKED)
            new_columns = slice(KV_WIDTH + h * HEAD_SIZE, KV_WIDTH + (h + 1) * HEAD_SIZE)
            state = fold(None, [scores], [fresh_ref[:, new_columns]])
            for parts in parts_in(width):
                k_part = jnp.concatenate([kv_refs[s][:tokens, columns[h]] for s in parts], axis=0)
                v_part = jnp.concatenate([kv_refs[s][tokens:, columns[h]] for s in parts], axis=0)
                bias = jnp.concatenate([bias_ref[s] for s in parts], axis=1)
                state = fold(state, [scores_of(queries, k_part) + bias], [v_part])
            again.append(state[1])
        send(again)


def prefill_kernel(plan, acc_ref, bias_ref, worst_ref, q_ref, *refs):
    width = plan.size
    kv_refs, refs = refs[:width], refs[width:]
    out_ref, done_ref, sem = refs
    tokens = q_ref.shape[0]
    half = tokens // 2
    def write(h, start, acc):
        out = divided(acc)
        for g in range(HEADS_PER_KV):
            done_ref[start : start + half, span(h * Q_BLOCK + g * HEAD_SIZE, HEAD_SIZE)] = out[
                g * half : (g + 1) * half
            ]

    def copy_out(h):
        part = pl.ds(h * Q_BLOCK, Q_BLOCK)
        return pltpu.make_async_copy(done_ref.at[:, part], out_ref.at[:, part], sem.at[h])

    biases = [bias_ref[width - 1, start : start + half, :] for start in (0, half)]
    worst, least = worst_ref[...], None
    for h in range(KEY_VALUE_HEADS):
        columns = slice(h * HEAD_SIZE, (h + 1) * HEAD_SIZE)
        keys, values = kv_refs[-1][:tokens, columns], with_ones(kv_refs[-1][tokens:, columns])
        for start, bias in zip((0, half), biases):
            queries = stacked_heads(q_ref, slice(start, start + half), h * Q_BLOCK, HEADS_PER_KV)
            scores = scores_of(queries, keys).reshape(HEADS_PER_KV, half, tokens)
            exponents = (scores * EXPONENT + bias[None]).reshape(HEADS_PER_KV * half, tokens)
            worst = jnp.maximum(worst, peak(exponents))
            rows = slice(start * HEADS_PER_KV, (start + half) * HEADS_PER_KV)
            acc = acc_ref[h, rows, :] + product(jnp.exp2(exponents).astype(jnp.bfloat16), values)
            part = jnp.min(acc[:, HEAD_SIZE:].reshape(-1, 8, HEAD_SIZE), axis=0)
            least = part if least is None else jnp.minimum(least, part)
            write(h, start, acc)
        copy_out(h).start()
    redo = out_of_range(worst, least)
    for h in range(KEY_VALUE_HEADS):
        copy_out(h).wait()

    @pl.when(redo)
    def _():
        def step(h, carry):
            columns = span(h * HEAD_SIZE, HEAD_SIZE)
            for start in (0, half):
                queries = stacked_heads(q_ref, slice(start, start + half), h * Q_BLOCK, HEADS_PER_KV)
                state = None
                for parts in parts_in(width):
                    k_part = jnp.concatenate([kv_refs[s][:tokens, columns] for s in parts], axis=0)
                    v_part = jnp.concatenate([kv_refs[s][tokens:, columns] for s in parts], axis=0)
                    bias = jnp.concatenate([bias_ref[s, start : start + half, :] for s in parts], axis=1)
                    scores = scores_of(queries, k_part).reshape(HEADS_PER_KV, half, bias.shape[1])
                    scores = (scores + bias[None]).reshape(HEADS_PER_KV * half, bias.shape[1])
                    state = fold(state, [scores], [v_part])
                write(h, start, state[1])
            return carry

        lax.fori_loop(0, KEY_VALUE_HEADS, step, 0)
        for h in range(KEY_VALUE_HEADS):
            copy_out(h).start()
        for h in range(KEY_VALUE_HEADS):
            copy_out(h).wait()


def cost(rows, keys, exps):
    return pl.CostEstimate(
        flops=32 * rows * keys * Q_WIDTH, bytes_accessed=4 * rows * Q_WIDTH, transcendentals=exps
    )


def call_first(plan, facts, maxima, query, blocks, pieces):
    tokens, width = query.shape[0], plan.size
    rows = HEADS_PER_KV * tokens
    f32, bf16 = jnp.float32, jnp.bfloat16
    every = (width - 2) * tokens
    shapes = [
        jax.ShapeDtypeStruct((KEY_VALUE_HEADS, rows, 2 * HEAD_SIZE), f32),
        jax.ShapeDtypeStruct((width, tokens, tokens), f32),
        jax.ShapeDtypeStruct((KEY_VALUE_HEADS, STACKED, 2 * HEAD_SIZE), f32),
        jax.ShapeDtypeStruct((width, STACKED, tokens), f32),
        jax.ShapeDtypeStruct((8, HEAD_SIZE), f32),
        jax.ShapeDtypeStruct((PADDED_ROWS, Q_WIDTH), bf16),
        jax.ShapeDtypeStruct((PADDED_ROWS, 2 * KV_WIDTH), bf16),
        jax.ShapeDtypeStruct((PADDED_ROWS, PADDED_ROWS), bf16),
        jax.ShapeDtypeStruct((8, HEAD_SIZE), jnp.int32),
    ]
    return pl.pallas_call(
        lambda *refs: first_kernel(plan, len(blocks), *refs),
        in_specs=[SMEM] + [VMEM] * (len(blocks) + width),
        out_specs=[VMEM] * len(shapes),
        out_shape=shapes,
        compiler_params=pltpu.CompilerParams(vmem_limit_bytes=(28 + width) * MIB),
        cost_estimate=cost(tokens, every, tokens * every * QUERY_HEADS),
        name="first_shards",
    )(facts, maxima, query, *pieces, *blocks)


def call_middle(plan, state, query, piece):
    acc, bias, dec_acc, dec_bias, worst, queries = state[:6]
    tokens = query.shape[0]
    new_acc, new_dec_acc, new_worst = pl.pallas_call(
        lambda *refs: middle_kernel(plan, *refs),
        in_specs=[VMEM] * 8,
        out_specs=[VMEM] * 3,
        out_shape=[jax.ShapeDtypeStruct(a.shape, a.dtype) for a in (acc, dec_acc, worst)],
        input_output_aliases={0: 0, 2: 1, 4: 2},
        compiler_params=pltpu.CompilerParams(vmem_limit_bytes=32 * MIB),
        cost_estimate=cost(tokens, tokens, tokens * tokens * QUERY_HEADS),
        name="middle_shard",
    )(acc, bias, dec_acc, dec_bias, worst, queries, query, piece)
    return [new_acc, bias, new_dec_acc, dec_bias, new_worst] + list(state[5:])


def call_decode(plan, state, pieces):
    tokens, width = pieces[0].shape[0] // 2, plan.size
    return pl.pallas_call(
        lambda *refs: decode_kernel(plan, *refs),
        in_specs=[VMEM] * (6 + width),
        out_specs=VMEM,
        out_shape=jax.ShapeDtypeStruct((PADDED_ROWS, Q_WIDTH), jnp.bfloat16),
        compiler_params=pltpu.CompilerParams(vmem_limit_bytes=(28 + width) * MIB),
        cost_estimate=cost(PADDED_ROWS, tokens, PADDED_ROWS * tokens * QUERY_HEADS),
        name="last_shard_decode",
    )(*state[2:8], *pieces)


def call_prefill(plan, state, query, pieces):
    tokens, width = query.shape[0], plan.size
    return pl.pallas_call(
        lambda *refs: prefill_kernel(plan, *refs),
        in_specs=[VMEM] * (4 + width),
        out_specs=ANY,
        out_shape=jax.ShapeDtypeStruct((tokens, Q_WIDTH), jnp.bfloat16),
        scratch_shapes=[
            pltpu.VMEM((tokens, Q_WIDTH), jnp.bfloat16),
            pltpu.SemaphoreType.DMA((KEY_VALUE_HEADS,)),
        ],
        compiler_params=pltpu.CompilerParams(vmem_limit_bytes=(28 + width) * MIB),
        cost_estimate=cost(tokens, tokens, tokens * tokens * QUERY_HEADS),
        name="last_shard_prefill",
    )(*state[:2], state[4], query, *pieces)


def start_maxima(*arrays, flops=5 * 10**9):
    def kernel(*refs):
        refs[-1][...] = jnp.full((8, HEAD_SIZE), MASKED, jnp.float32)

    return pl.pallas_call(
        kernel,
        in_specs=[VMEM] * len(arrays),
        out_specs=VMEM,
        out_shape=jax.ShapeDtypeStruct((8, HEAD_SIZE), jnp.float32),
        cost_estimate=pl.CostEstimate(flops=flops, bytes_accessed=0, transcendentals=0),
        compiler_params=pltpu.CompilerParams(vmem_limit_bytes=MIB),
        name="start_maxima",
    )(*arrays)


def paired(array, k):
    return lax.ppermute(array, "pd", [(g, g ^ k) for g in range(lax.axis_size("pd"))])


def body(
    prompt_query,
    prompt_key,
    prompt_value,
    prompt_lengths,
    decode_slot,
    decoded_query,
    decoded_key,
    decoded_value,
):
    plan = Ring(lax.axis_size("tp"))
    pd_size = lax.axis_size("pd")
    own = jnp.concatenate([decoded_query, decoded_key, decoded_value], axis=2).reshape(
        DECODE_ROWS, Q_WIDTH + 2 * KV_WIDTH
    )
    facts = facts_row(plan, prompt_lengths, decode_slot)
    kv, decoded_query = lax.optimization_barrier(
        (jnp.concatenate([prompt_key, prompt_value], axis=0), decoded_query)
    )
    later_kv, own, facts = lax.optimization_barrier((kv, own, facts))
    pieces, maxima, up, down = [kv], None, kv, later_kv
    for d in range(1, plan.size // 2 + 1):
        if d == 2:
            up, facts = lax.optimization_barrier((up, facts))
        up = plan.step(up, True)
        down = plan.step(down, False) if 2 * d < plan.size else None
        pieces += [up, down]
    pieces = pieces[: plan.size]
    blocks = [own] + [paired(own, k) for k in range(1, pd_size)]
    maxima = start_maxima(pieces[1])

    state = call_first(plan, facts, maxima, prompt_query, blocks, pieces[:-2])
    state = call_middle(plan, state, prompt_query, pieces[-2])
    outgoing = call_decode(plan, state, pieces)
    arrived = [outgoing[:DECODE_STEPS]]
    for k in range(1, pd_size):
        arrived.append(paired(outgoing[k * DECODE_STEPS : (k + 1) * DECODE_STEPS], k))
    pre_out = call_prefill(plan, state, prompt_query, pieces)

    from_block = state[8][:GROUP_REQUESTS, 0]
    dec_out = jnp.zeros((GROUP_REQUESTS, DECODE_STEPS, Q_WIDTH), jnp.bfloat16)
    for k in range(pd_size):
        dec_out = jnp.where((from_block == k)[:, None, None], arrived[k][None], dec_out)
    return (pre_out, dec_out)


def solution(mesh):
    placed = (
        P(("rep", "pd", "tp"), None),
        P(("rep", "pd", "tp"), None),
        P(("rep", "pd", "tp"), None),
        P("rep", None),
        P("rep"),
        P(("rep", "pd"), None, None),
        P(("rep", "pd"), None, None),
        P(("rep", "pd"), None, None),
    )
    return jax.shard_map(
        body,
        mesh=mesh,
        in_specs=placed,
        out_specs=(P(("rep", "pd", "tp"), None), P(("rep", "pd"), None, None)),
        check_vma=False,
    )
```

```python
import math

import jax
import jax.numpy as jnp
from jax import lax
from jax.experimental import pallas as pl
from jax.experimental.pallas import tpu as pltpu
from jax.sharding import PartitionSpec as P

QUERY_HEADS = 32
KEY_VALUE_HEADS = 4
HEAD_SIZE = 128
PAGE = 16
GROUP_REQUESTS = 4
DECODE_STEPS = 2
HEADS_PER_KV = QUERY_HEADS // KEY_VALUE_HEADS
KV_WIDTH = KEY_VALUE_HEADS * HEAD_SIZE
Q_WIDTH = QUERY_HEADS * HEAD_SIZE
Q_BLOCK = HEADS_PER_KV * HEAD_SIZE
DECODE_ROWS = GROUP_REQUESTS * DECODE_STEPS
PADDED_ROWS = 16
STACKED = HEADS_PER_KV * PADDED_ROWS
MIB = 1024 * 1024

MASKED = -1e30
LIMIT = 60.0
EXPONENT = math.log2(math.e) / math.sqrt(HEAD_SIZE)

VMEM = pl.BlockSpec(memory_space=pltpu.VMEM)
SMEM = pl.BlockSpec(memory_space=pltpu.SMEM)
ANY = pl.BlockSpec(memory_space=pl.ANY)
HBM = pl.BlockSpec(memory_space=pltpu.HBM)


class Ring:
    def __init__(self, size):
        self.size = size
        order = [0] + list(range(1, size, 2)) + [i for i in range(size - 1, 0, -1) if i % 2 == 0]
        self.pairs = [(order[i], order[(i + 1) % size]) for i in range(size)]
        self.offsets = [0]
        for d in range(1, size // 2 + 1):
            self.offsets += [-d, d]
        self.offsets = self.offsets[:size]

    def step(self, array, up):
        return lax.ppermute(array, "tp", self.pairs if up else [(b, a) for a, b in self.pairs])


def scores_of(queries, keys):
    return lax.dot_general(
        queries, keys, (((1,), (1,)), ((), ())), preferred_element_type=jnp.float32
    )


def product(left, right):
    return jnp.dot(left, right, preferred_element_type=jnp.float32)


def iota(shape, axis):
    return lax.broadcasted_iota(jnp.int32, shape, axis)


def span(start, size):
    if isinstance(start, int):
        return slice(start, start + size)
    return pl.ds(pl.multiple_of(start, size), size)


def with_ones(values):
    return jnp.concatenate([values, jnp.ones_like(values)], axis=1)


def page_position(offset, member, width):
    return (offset // PAGE * width + member) * PAGE + offset % PAGE


def key_positions(rows, sources, width):
    column = iota((1, len(sources) * rows), 1)
    part = column // rows
    source = jnp.zeros_like(column) + sources[0]
    for b in range(1, len(sources)):
        source = jnp.where(part == b, sources[b], source)
    return page_position(column - part * rows, source, width)


class Facts:
    def __init__(self, ref, width):
        self.width = width
        self.group, self.member = ref[0], ref[1]
        self.slots = [ref[2 + r] for r in range(GROUP_REQUESTS)]
        first = 2 + GROUP_REQUESTS
        self.ends = []
        total = jnp.int32(0)
        for r in range(GROUP_REQUESTS):
            total = total + ref[first + r] * PAGE
            self.ends.append(total)
        first += GROUP_REQUESTS
        self.source = [ref[first + s] for s in range(width)]
        first += width
        self.owner = [ref[first + p] for p in range(GROUP_REQUESTS)]


def facts_row(plan, lengths, slots):
    width, requests = plan.size, slots.shape[0]

    def kernel(lengths_ref, slots_ref, out_ref):
        group, member = lax.axis_index("pd"), lax.axis_index("tp")
        values = [group, member]
        values += [slots_ref[group * GROUP_REQUESTS + r] for r in range(GROUP_REQUESTS)]
        values += [lengths_ref[group, r] for r in range(GROUP_REQUESTS)]
        place = jnp.where(member % 2 == 1, (member + 1) // 2, width - member // 2)
        for offset in plan.offsets:
            before = (place + width + offset) % width
            up = 2 * before - 1
            values.append(jnp.where(before == 0, 0, jnp.where(before <= width // 2, up, 2 * (width - before))))
        for i, value in enumerate(values):
            out_ref[i] = value.astype(jnp.int32)
        for q in range(requests):
            place = slots_ref[q] - group * GROUP_REQUESTS

            @pl.when((place >= 0) & (place < GROUP_REQUESTS))
            def _():
                out_ref[len(values) + place] = group ^ (q // GROUP_REQUESTS)

    length = 2 + 2 * GROUP_REQUESTS + width + GROUP_REQUESTS
    return pl.pallas_call(
        kernel,
        in_specs=[SMEM, SMEM],
        out_specs=SMEM,
        out_shape=jax.ShapeDtypeStruct((length,), jnp.int32),
        cost_estimate=pl.CostEstimate(flops=5 * 10**9, bytes_accessed=0, transcendentals=0),
        name="facts",
    )(lengths, slots)


def causal_bias(start, rows, keys, sources, ends, member, width):
    qpos = page_position(start + iota((rows, 1), 0), member, width)
    low = jnp.zeros_like(qpos)
    for end in ends:
        low = jnp.where(qpos >= end, end, low)
    kpos = key_positions(keys, sources, width)
    return jnp.where((kpos >= low) & (kpos <= qpos), 0.0, MASKED)


def request_mask(ends, keys, sources, width):
    request = iota((STACKED, 1), 0) % PADDED_ROWS // DECODE_STEPS
    low = jnp.zeros_like(request)
    high = jnp.zeros_like(request) + ends[0]
    for r in range(1, GROUP_REQUESTS):
        low = jnp.where(request == r, ends[r - 1], low)
        high = jnp.where(request == r, ends[r], high)
    kpos = key_positions(keys, sources, width)
    return (kpos >= low) & (kpos < high)


def stacked_heads(ref, rows, first, count):
    return jnp.concatenate(
        [ref[rows, span(first + i * HEAD_SIZE, HEAD_SIZE)] for i in range(count)], axis=0
    )


def each_kv_head(width, step):
    if width <= 8:
        for h in range(KEY_VALUE_HEADS):
            step(h)
    else:
        lax.fori_loop(0, KEY_VALUE_HEADS, lambda h, c: (step(h), c)[1], 0)


def peak(exponents):
    return jnp.max(exponents.reshape(-1, 8, exponents.shape[-1]), axis=0)


def picked_rows(facts, pd_size, block_refs):
    row = iota((PADDED_ROWS, DECODE_ROWS), 0)
    column = iota((PADDED_ROWS, DECODE_ROWS), 1)
    total = None
    for k in range(pd_size):
        pick = column < 0
        for r in range(GROUP_REQUESTS):
            slot = facts.slots[r]
            first = jnp.where(facts.group ^ (slot // GROUP_REQUESTS) == k, slot % GROUP_REQUESTS * DECODE_STEPS, -DECODE_ROWS * 4)
            pick = pick | ((row // DECODE_STEPS == r) & (column == first + row - r * DECODE_STEPS))
        part = product(pick.astype(jnp.float32).astype(jnp.bfloat16), block_refs[k][...])
        total = part if total is None else total + part
    return total.astype(jnp.bfloat16)


def pick_matrix(facts):
    row = iota((PADDED_ROWS, PADDED_ROWS), 0)
    column = iota((PADDED_ROWS, PADDED_ROWS), 1)
    pick = column < 0
    for r in range(GROUP_REQUESTS):
        ahead = facts.group ^ (facts.slots[r] // GROUP_REQUESTS)
        pick = pick | (
            (column // DECODE_STEPS == r) & (row == ahead * DECODE_STEPS + column - r * DECODE_STEPS)
        )
    return pick.astype(jnp.float32).astype(jnp.bfloat16)


def fresh_mask():
    row = iota((STACKED, PADDED_ROWS), 0) % PADDED_ROWS
    column = iota((STACKED, PADDED_ROWS), 1)
    return (column // DECODE_STEPS == row // DECODE_STEPS) & (
        column % DECODE_STEPS <= row % DECODE_STEPS
    )


def first_kernel(plan, pd_size, facts_ref, maxima_ref, q_ref, *refs):
    width = plan.size
    k_refs, v_refs, refs = refs[: width - 2], refs[width - 2 : 2 * width - 4], refs[2 * width - 4 :]
    block_refs, refs = refs[:pd_size], refs[pd_size:]
    acc_ref, bias_ref, dec_acc_ref, dec_bias_ref, worst_ref, queries_ref, fresh_ref, pick_ref, owner_ref = refs
    tokens = q_ref.shape[0]
    half = tokens // 2
    facts = Facts(facts_ref, width)
    sources = facts.source[:-2]
    pick_ref[...] = pick_matrix(facts)
    slot = iota((8, HEAD_SIZE), 0)
    owner = jnp.zeros_like(slot)
    for p in range(GROUP_REQUESTS):
        owner = jnp.where(slot == p, facts.owner[p], owner)
    owner_ref[...] = owner
    for s in range(width):
        bias_ref[s] = causal_bias(0, tokens, tokens, facts.source[s : s + 1], facts.ends, facts.member, width)
        dec_bias_ref[s] = jnp.where(
            request_mask(facts.ends, tokens, facts.source[s : s + 1], width), 0.0, MASKED
        )
    rows = picked_rows(facts, pd_size, block_refs)
    queries_ref[...] = rows[:, :Q_WIDTH]
    fresh_ref[...] = rows[:, Q_WIDTH:]
    worst_ref[...] = maxima_ref[...]
    new_mask = fresh_mask()
    mask = request_mask(facts.ends, tokens, sources, width)
    spans = ((0, half), (half, tokens))
    biases = [
        causal_bias(s, half, keys, sources, facts.ends, facts.member, width) for s, keys in spans
    ]
    together = max(1, min(HEADS_PER_KV, HEADS_PER_KV * 4 // width))

    def weigh(exponents):
        top = jnp.max(peak(exponents), axis=1, keepdims=True)
        worst_ref[...] = jnp.maximum(worst_ref[...], top)
        return jnp.exp2(exponents).astype(jnp.bfloat16)

    def step(h):
        columns = span(h * HEAD_SIZE, HEAD_SIZE)
        first = h * Q_BLOCK
        queries = stacked_heads(queries_ref, slice(None), first, HEADS_PER_KV)
        k_all = jnp.concatenate([ref[:, columns] for ref in k_refs], axis=0)
        v_all = with_ones(jnp.concatenate([ref[:, columns] for ref in v_refs], axis=0))
        new_scores = scores_of(queries, fresh_ref[:, columns]) * EXPONENT
        new_weights = weigh(jnp.where(new_mask, new_scores, MASKED))
        new_values = fresh_ref[:, span(KV_WIDTH + h * HEAD_SIZE, HEAD_SIZE)]
        weights = weigh(jnp.where(mask, scores_of(queries, k_all) * EXPONENT, MASKED))
        dec_acc_ref[h] = product(weights, v_all) + product(new_weights, with_ones(new_values))
        for (start, keys), bias in zip(spans, biases):
            if keys < tokens:
                k_part = jnp.concatenate([ref[:keys, columns] for ref in k_refs], axis=0)
                v_part = with_ones(jnp.concatenate([ref[:keys, columns] for ref in v_refs], axis=0))
            else:
                k_part, v_part = k_all, v_all
            for g in range(0, HEADS_PER_KV, together):
                queries = stacked_heads(
                    q_ref, slice(start, start + half), first + g * HEAD_SIZE, together
                )
                scores = scores_of(queries, k_part).reshape(together, half, bias.shape[1])
                exponents = (scores * EXPONENT + bias[None]).reshape(together * half, bias.shape[1])
                rows = slice(
                    start * HEADS_PER_KV + g * half, start * HEADS_PER_KV + (g + together) * half
                )
                acc_ref[h, rows, :] = product(weigh(exponents), v_part)

    each_kv_head(width, step)


def middle_kernel(plan, acc_ref, bias_ref, dec_acc_ref, dec_bias_ref, worst_ref, queries_ref, q_ref, k_ref, v_ref, *refs):
    new_acc_ref, new_dec_acc_ref, new_worst_ref = refs
    piece = plan.size - 2
    tokens = q_ref.shape[0]
    half = tokens // 2
    worst = worst_ref[...]
    for h in range(KEY_VALUE_HEADS):
        columns = slice(h * HEAD_SIZE, (h + 1) * HEAD_SIZE)
        keys, values = k_ref[:, columns], with_ones(v_ref[:, columns])
        queries = stacked_heads(queries_ref, slice(None), h * Q_BLOCK, HEADS_PER_KV)
        exponents = scores_of(queries, keys) * EXPONENT + dec_bias_ref[piece]
        worst = jnp.maximum(worst, peak(exponents))
        new_dec_acc_ref[h] = dec_acc_ref[h] + product(jnp.exp2(exponents).astype(jnp.bfloat16), values)
        for start in (0, half):
            bias = bias_ref[piece, start : start + half, :]
            queries = stacked_heads(q_ref, slice(start, start + half), h * Q_BLOCK, HEADS_PER_KV)
            scores = scores_of(queries, keys).reshape(HEADS_PER_KV, half, tokens)
            exponents = (scores * EXPONENT + bias[None]).reshape(HEADS_PER_KV * half, tokens)
            worst = jnp.maximum(worst, peak(exponents))
            rows = slice(start * HEADS_PER_KV, (start + half) * HEADS_PER_KV)
            new_acc_ref[h, rows, :] = acc_ref[h, rows, :] + product(
                jnp.exp2(exponents).astype(jnp.bfloat16), values
            )
    new_worst_ref[...] = worst


def divided(acc):
    return (acc[:, :HEAD_SIZE] * pl.reciprocal(acc[:, HEAD_SIZE:], approx=True)).astype(jnp.bfloat16)


def fold(state, scores_list, values_list):
    top = None if state is None else state[0]
    for scores in scores_list:
        part = jnp.max(scores, axis=1, keepdims=True)
        top = part if top is None else jnp.maximum(top, part)
    acc = None
    for scores, values in zip(scores_list, values_list):
        weights = jnp.exp2((scores - top) * EXPONENT).astype(jnp.bfloat16)
        part = product(weights, with_ones(values))
        acc = part if acc is None else acc + part
    if state is not None:
        acc = acc + state[1] * jnp.exp2((state[0] - top) * EXPONENT)
    return top, acc


def parts_in(width):
    return [range(c, min(c + 4, width)) for c in range(0, width, 4)]


def out_of_range(worst, least):
    return (jnp.max(worst) > LIMIT) | (jnp.min(least) < 2.0**-LIMIT)


def decode_kernel(plan, acc_ref, bias_ref, worst_ref, queries_ref, fresh_ref, pick_ref, *refs):
    width = plan.size
    k_refs, v_refs, (out_ref,) = refs[:width], refs[width : 2 * width], refs[2 * width :]
    heads = range(KEY_VALUE_HEADS)
    columns = [slice(h * HEAD_SIZE, (h + 1) * HEAD_SIZE) for h in heads]

    def queries_of(h):
        return stacked_heads(queries_ref, slice(None), h * Q_BLOCK, HEADS_PER_KV)

    def send(acc):
        out = [divided(a) for a in acc]
        out = jnp.concatenate(
            [o[g * PADDED_ROWS : (g + 1) * PADDED_ROWS] for o in out for g in range(HEADS_PER_KV)], axis=1
        )
        out_ref[...] = product(pick_ref[...], out).astype(jnp.bfloat16)

    exponents = [
        scores_of(queries_of(h), k_refs[-1][:, columns[h]]) * EXPONENT + bias_ref[width - 1]
        for h in heads
    ]
    acc = [
        acc_ref[h] + product(jnp.exp2(exponents[h]).astype(jnp.bfloat16), with_ones(v_refs[-1][:, columns[h]]))
        for h in heads
    ]
    send(acc)
    worst, least = worst_ref[...], None
    for h in heads:
        worst = jnp.maximum(worst, peak(exponents[h]))
        part = jnp.min(acc[h][:, HEAD_SIZE:].reshape(-1, 8, HEAD_SIZE), axis=0)
        least = part if least is None else jnp.minimum(least, part)

    @pl.when(out_of_range(worst, least))
    def _():
        new_mask = fresh_mask()
        again = []
        for h in heads:
            queries = queries_of(h)
            scores = jnp.where(new_mask, scores_of(queries, fresh_ref[:, columns[h]]), MASKED)
            new_columns = slice(KV_WIDTH + h * HEAD_SIZE, KV_WIDTH + (h + 1) * HEAD_SIZE)
            state = fold(None, [scores], [fresh_ref[:, new_columns]])
            for parts in parts_in(width):
                k_part = jnp.concatenate([k_refs[s][:, columns[h]] for s in parts], axis=0)
                v_part = jnp.concatenate([v_refs[s][:, columns[h]] for s in parts], axis=0)
                bias = jnp.concatenate([bias_ref[s] for s in parts], axis=1)
                state = fold(state, [scores_of(queries, k_part) + bias], [v_part])
            again.append(state[1])
        send(again)


def prefill_kernel(plan, acc_ref, bias_ref, worst_ref, q_ref, *refs):
    width = plan.size
    k_refs, v_refs, refs = refs[:width], refs[width : 2 * width], refs[2 * width :]
    out_ref, done_ref, sem = refs
    tokens = q_ref.shape[0]
    half = tokens // 2
    def write(h, start, acc):
        out = divided(acc)
        for g in range(HEADS_PER_KV):
            done_ref[start : start + half, span(h * Q_BLOCK + g * HEAD_SIZE, HEAD_SIZE)] = out[
                g * half : (g + 1) * half
            ]

    def copy_out(h):
        part = pl.ds(h * Q_BLOCK, Q_BLOCK)
        return pltpu.make_async_copy(done_ref.at[:, part], out_ref.at[:, part], sem.at[h])

    biases = [bias_ref[width - 1, start : start + half, :] for start in (0, half)]
    worst, least = worst_ref[...], None
    for h in range(KEY_VALUE_HEADS):
        columns = slice(h * HEAD_SIZE, (h + 1) * HEAD_SIZE)
        keys, values = k_refs[-1][:, columns], with_ones(v_refs[-1][:, columns])
        for start, bias in zip((0, half), biases):
            queries = stacked_heads(q_ref, slice(start, start + half), h * Q_BLOCK, HEADS_PER_KV)
            scores = scores_of(queries, keys).reshape(HEADS_PER_KV, half, tokens)
            exponents = (scores * EXPONENT + bias[None]).reshape(HEADS_PER_KV * half, tokens)
            worst = jnp.maximum(worst, peak(exponents))
            rows = slice(start * HEADS_PER_KV, (start + half) * HEADS_PER_KV)
            acc = acc_ref[h, rows, :] + product(jnp.exp2(exponents).astype(jnp.bfloat16), values)
            part = jnp.min(acc[:, HEAD_SIZE:].reshape(-1, 8, HEAD_SIZE), axis=0)
            least = part if least is None else jnp.minimum(least, part)
            write(h, start, acc)
        copy_out(h).start()
    redo = out_of_range(worst, least)
    for h in range(KEY_VALUE_HEADS):
        copy_out(h).wait()

    @pl.when(redo)
    def _():
        def step(h, carry):
            columns = span(h * HEAD_SIZE, HEAD_SIZE)
            for start in (0, half):
                queries = stacked_heads(q_ref, slice(start, start + half), h * Q_BLOCK, HEADS_PER_KV)
                state = None
                for parts in parts_in(width):
                    k_part = jnp.concatenate([k_refs[s][:, columns] for s in parts], axis=0)
                    v_part = jnp.concatenate([v_refs[s][:, columns] for s in parts], axis=0)
                    bias = jnp.concatenate([bias_ref[s, start : start + half, :] for s in parts], axis=1)
                    scores = scores_of(queries, k_part).reshape(HEADS_PER_KV, half, bias.shape[1])
                    scores = (scores + bias[None]).reshape(HEADS_PER_KV * half, bias.shape[1])
                    state = fold(state, [scores], [v_part])
                write(h, start, state[1])
            return carry

        lax.fori_loop(0, KEY_VALUE_HEADS, step, 0)
        for h in range(KEY_VALUE_HEADS):
            copy_out(h).start()
        for h in range(KEY_VALUE_HEADS):
            copy_out(h).wait()


def cost(rows, keys, exps):
    return pl.CostEstimate(
        flops=32 * rows * keys * Q_WIDTH, bytes_accessed=4 * rows * Q_WIDTH, transcendentals=exps
    )


def call_first(plan, facts, maxima, query, blocks, keys, values):
    tokens, width = query.shape[0], plan.size
    rows = HEADS_PER_KV * tokens
    f32, bf16 = jnp.float32, jnp.bfloat16
    every = (width - 2) * tokens
    shapes = [
        jax.ShapeDtypeStruct((KEY_VALUE_HEADS, rows, 2 * HEAD_SIZE), f32),
        jax.ShapeDtypeStruct((width, tokens, tokens), f32),
        jax.ShapeDtypeStruct((KEY_VALUE_HEADS, STACKED, 2 * HEAD_SIZE), f32),
        jax.ShapeDtypeStruct((width, STACKED, tokens), f32),
        jax.ShapeDtypeStruct((8, HEAD_SIZE), f32),
        jax.ShapeDtypeStruct((PADDED_ROWS, Q_WIDTH), bf16),
        jax.ShapeDtypeStruct((PADDED_ROWS, 2 * KV_WIDTH), bf16),
        jax.ShapeDtypeStruct((PADDED_ROWS, PADDED_ROWS), bf16),
        jax.ShapeDtypeStruct((8, HEAD_SIZE), jnp.int32),
    ]
    return pl.pallas_call(
        lambda *refs: first_kernel(plan, len(blocks), *refs),
        in_specs=[SMEM] + [VMEM] * (2 + len(blocks) + 2 * (width - 2)),
        out_specs=[VMEM] * len(shapes),
        out_shape=shapes,
        compiler_params=pltpu.CompilerParams(vmem_limit_bytes=(28 + width) * MIB),
        cost_estimate=cost(tokens, every, tokens * every * QUERY_HEADS),
        name="first_shards",
    )(facts, maxima, query, *keys, *values, *blocks)


def call_middle(plan, state, query, key, value):
    acc, bias, dec_acc, dec_bias, worst, queries = state[:6]
    tokens = query.shape[0]
    new_acc, new_dec_acc, new_worst = pl.pallas_call(
        lambda *refs: middle_kernel(plan, *refs),
        in_specs=[VMEM] * 9,
        out_specs=[VMEM] * 3,
        out_shape=[jax.ShapeDtypeStruct(a.shape, a.dtype) for a in (acc, dec_acc, worst)],
        input_output_aliases={0: 0, 2: 1, 4: 2},
        compiler_params=pltpu.CompilerParams(vmem_limit_bytes=32 * MIB),
        cost_estimate=cost(tokens, tokens, tokens * tokens * QUERY_HEADS),
        name="middle_shard",
    )(acc, bias, dec_acc, dec_bias, worst, queries, query, key, value)
    return [new_acc, bias, new_dec_acc, dec_bias, new_worst] + list(state[5:])


def call_decode(plan, state, keys, values):
    tokens, width = keys[0].shape[0], plan.size
    return pl.pallas_call(
        lambda *refs: decode_kernel(plan, *refs),
        in_specs=[VMEM] * (6 + 2 * width),
        out_specs=VMEM,
        out_shape=jax.ShapeDtypeStruct((PADDED_ROWS, Q_WIDTH), jnp.bfloat16),
        compiler_params=pltpu.CompilerParams(vmem_limit_bytes=(28 + width) * MIB),
        cost_estimate=cost(PADDED_ROWS, tokens, PADDED_ROWS * tokens * QUERY_HEADS),
        name="last_shard_decode",
    )(*state[2:8], *keys, *values)


def call_prefill(plan, state, query, keys, values):
    tokens, width = query.shape[0], plan.size
    return pl.pallas_call(
        lambda *refs: prefill_kernel(plan, *refs),
        in_specs=[VMEM] * (4 + 2 * width),
        out_specs=ANY,
        out_shape=jax.ShapeDtypeStruct((tokens, Q_WIDTH), jnp.bfloat16),
        scratch_shapes=[
            pltpu.VMEM((tokens, Q_WIDTH), jnp.bfloat16),
            pltpu.SemaphoreType.DMA((KEY_VALUE_HEADS,)),
        ],
        compiler_params=pltpu.CompilerParams(vmem_limit_bytes=(28 + width) * MIB),
        cost_estimate=cost(tokens, tokens, tokens * tokens * QUERY_HEADS),
        name="last_shard_prefill",
    )(*state[:2], state[4], query, *keys, *values)


def start_maxima(*arrays, flops=5 * 10**9):
    def kernel(*refs):
        refs[-1][...] = jnp.full((8, HEAD_SIZE), MASKED, jnp.float32)

    return pl.pallas_call(
        kernel,
        in_specs=[VMEM] * len(arrays),
        out_specs=VMEM,
        out_shape=jax.ShapeDtypeStruct((8, HEAD_SIZE), jnp.float32),
        cost_estimate=pl.CostEstimate(flops=flops, bytes_accessed=0, transcendentals=0),
        compiler_params=pltpu.CompilerParams(vmem_limit_bytes=MIB),
        name="start_maxima",
    )(*arrays)


def paired(array, k):
    return lax.ppermute(array, "pd", [(g, g ^ k) for g in range(lax.axis_size("pd"))])


def body(
    prompt_query,
    prompt_key,
    prompt_value,
    prompt_lengths,
    decode_slot,
    decoded_query,
    decoded_key,
    decoded_value,
):
    plan = Ring(lax.axis_size("tp"))
    pd_size = lax.axis_size("pd")
    own = jnp.concatenate([decoded_query, decoded_key, decoded_value], axis=2).reshape(
        DECODE_ROWS, Q_WIDTH + 2 * KV_WIDTH
    )
    facts = facts_row(plan, prompt_lengths, decode_slot)
    prompt_key, decoded_query = lax.optimization_barrier((prompt_key, decoded_query))
    later_key, later_value, own, facts = lax.optimization_barrier((prompt_key, prompt_value, own, facts))
    chains = []
    for up, down in ((prompt_key, later_key), (prompt_value, later_value)):
        pieces = [up]
        for d in range(1, plan.size // 2 + 1):
            up = plan.step(up, True)
            down = plan.step(down, False) if 2 * d < plan.size else None
            pieces += [up, down]
        chains.append(pieces[: plan.size])
    keys, values = chains
    blocks = [own] + [paired(own, k) for k in range(1, pd_size)]
    maxima = start_maxima(keys[1], values[1])

    state = call_first(plan, facts, maxima, prompt_query, blocks, keys[:-2], values[:-2])
    state = call_middle(plan, state, prompt_query, keys[-2], values[-2])
    outgoing = call_decode(plan, state, keys, values)
    arrived = [outgoing[:DECODE_STEPS]]
    for k in range(1, pd_size):
        arrived.append(paired(outgoing[k * DECODE_STEPS : (k + 1) * DECODE_STEPS], k))
    pre_out = call_prefill(plan, state, prompt_query, keys, values)

    from_block = state[8][:GROUP_REQUESTS, 0]
    dec_out = jnp.zeros((GROUP_REQUESTS, DECODE_STEPS, Q_WIDTH), jnp.bfloat16)
    for k in range(pd_size):
        dec_out = jnp.where((from_block == k)[:, None, None], arrived[k][None], dec_out)
    return (pre_out, dec_out)


def solution(mesh):
    placed = (
        P(("rep", "pd", "tp"), None),
        P(("rep", "pd", "tp"), None),
        P(("rep", "pd", "tp"), None),
        P("rep", None),
        P("rep"),
        P(("rep", "pd"), None, None),
        P(("rep", "pd"), None, None),
        P(("rep", "pd"), None, None),
    )
    return jax.shard_map(
        body,
        mesh=mesh,
        in_specs=placed,
        out_specs=(P(("rep", "pd", "tp"), None), P(("rep", "pd"), None, None)),
        check_vma=False,
    )
```

```python
import math

import jax
import jax.numpy as jnp
from jax import lax
from jax.experimental import pallas as pl
from jax.experimental.pallas import tpu as pltpu
from jax.sharding import PartitionSpec as P

QUERY_HEADS = 32
KEY_VALUE_HEADS = 4
HEAD_SIZE = 128
PAGE = 16
GROUP_REQUESTS = 4
DECODE_STEPS = 2
HEADS_PER_KV = QUERY_HEADS // KEY_VALUE_HEADS
KV_WIDTH = KEY_VALUE_HEADS * HEAD_SIZE
Q_WIDTH = QUERY_HEADS * HEAD_SIZE
Q_BLOCK = HEADS_PER_KV * HEAD_SIZE
DECODE_ROWS = GROUP_REQUESTS * DECODE_STEPS
PADDED_ROWS = 16
STACKED = HEADS_PER_KV * PADDED_ROWS
MIB = 1024 * 1024

MASKED = -1e30
LIMIT = 60.0
EXPONENT = math.log2(math.e) / math.sqrt(HEAD_SIZE)

VMEM = pl.BlockSpec(memory_space=pltpu.VMEM)
SMEM = pl.BlockSpec(memory_space=pltpu.SMEM)
ANY = pl.BlockSpec(memory_space=pl.ANY)
HBM = pl.BlockSpec(memory_space=pltpu.HBM)


class Ring:
    def __init__(self, size):
        self.size = size
        order = list(range(0, size, 2)) + [i for i in range(size - 1, 0, -1) if i % 2 == 1]
        self.pairs = [(order[i], order[(i + 1) % size]) for i in range(size)]
        self.offsets = [0]
        for d in range(1, size // 2 + 1):
            self.offsets += [-d, d]
        self.offsets = self.offsets[:size]

    def step(self, array, up):
        return lax.ppermute(array, "tp", self.pairs if up else [(b, a) for a, b in self.pairs])


def scores_of(queries, keys):
    return lax.dot_general(
        queries, keys, (((1,), (1,)), ((), ())), preferred_element_type=jnp.float32
    )


def product(left, right):
    return jnp.dot(left, right, preferred_element_type=jnp.float32)


def iota(shape, axis):
    return lax.broadcasted_iota(jnp.int32, shape, axis)


def span(start, size):
    if isinstance(start, int):
        return slice(start, start + size)
    return pl.ds(pl.multiple_of(start, size), size)


def with_ones(values):
    return jnp.concatenate([values, jnp.ones_like(values)], axis=1)


def page_position(offset, member, width):
    return (offset // PAGE * width + member) * PAGE + offset % PAGE


def key_positions(rows, sources, width):
    column = iota((1, len(sources) * rows), 1)
    part = column // rows
    source = jnp.zeros_like(column) + sources[0]
    for b in range(1, len(sources)):
        source = jnp.where(part == b, sources[b], source)
    return page_position(column - part * rows, source, width)


class Facts:
    def __init__(self, ref, width):
        self.width = width
        self.group, self.member = ref[0], ref[1]
        self.slots = [ref[2 + r] for r in range(GROUP_REQUESTS)]
        first = 2 + GROUP_REQUESTS
        self.ends = []
        total = jnp.int32(0)
        for r in range(GROUP_REQUESTS):
            total = total + ref[first + r] * PAGE
            self.ends.append(total)
        first += GROUP_REQUESTS
        self.source = [ref[first + s] for s in range(width)]
        first += width
        self.owner = [ref[first + p] for p in range(GROUP_REQUESTS)]


def facts_row(plan, lengths, slots):
    width, requests = plan.size, slots.shape[0]

    def kernel(lengths_ref, slots_ref, out_ref):
        group, member = lax.axis_index("pd"), lax.axis_index("tp")
        values = [group, member]
        values += [slots_ref[group * GROUP_REQUESTS + r] for r in range(GROUP_REQUESTS)]
        values += [lengths_ref[group, r] for r in range(GROUP_REQUESTS)]
        place = jnp.where(member % 2 == 0, member // 2, width - (member + 1) // 2)
        for offset in plan.offsets:
            before = (place + width + offset) % width
            values.append(jnp.where(2 * before < width, 2 * before, 2 * (width - before) - 1))
        for i, value in enumerate(values):
            out_ref[i] = value.astype(jnp.int32)
        for q in range(requests):
            place = slots_ref[q] - group * GROUP_REQUESTS

            @pl.when((place >= 0) & (place < GROUP_REQUESTS))
            def _():
                out_ref[len(values) + place] = group ^ (q // GROUP_REQUESTS)

    length = 2 + 2 * GROUP_REQUESTS + width + GROUP_REQUESTS
    return pl.pallas_call(
        kernel,
        in_specs=[SMEM, SMEM],
        out_specs=SMEM,
        out_shape=jax.ShapeDtypeStruct((length,), jnp.int32),
        cost_estimate=pl.CostEstimate(flops=5 * 10**9, bytes_accessed=0, transcendentals=0),
        name="facts",
    )(lengths, slots)


def causal_bias(start, rows, keys, sources, ends, member, width):
    qpos = page_position(start + iota((rows, 1), 0), member, width)
    low = jnp.zeros_like(qpos)
    for end in ends:
        low = jnp.where(qpos >= end, end, low)
    kpos = key_positions(keys, sources, width)
    return jnp.where((kpos >= low) & (kpos <= qpos), 0.0, MASKED)


def request_mask(ends, keys, sources, width):
    request = iota((STACKED, 1), 0) % PADDED_ROWS // DECODE_STEPS
    low = jnp.zeros_like(request)
    high = jnp.zeros_like(request) + ends[0]
    for r in range(1, GROUP_REQUESTS):
        low = jnp.where(request == r, ends[r - 1], low)
        high = jnp.where(request == r, ends[r], high)
    kpos = key_positions(keys, sources, width)
    return (kpos >= low) & (kpos < high)


def stacked_heads(ref, rows, first, count):
    return jnp.concatenate(
        [ref[rows, span(first + i * HEAD_SIZE, HEAD_SIZE)] for i in range(count)], axis=0
    )


def each_kv_head(width, step):
    if width <= 8:
        for h in range(KEY_VALUE_HEADS):
            step(h)
    else:
        lax.fori_loop(0, KEY_VALUE_HEADS, lambda h, c: (step(h), c)[1], 0)


def peak(exponents):
    return jnp.max(exponents.reshape(-1, 8, exponents.shape[-1]), axis=0)


def picked_rows(facts, pd_size, block_refs):
    row = iota((PADDED_ROWS, DECODE_ROWS), 0)
    column = iota((PADDED_ROWS, DECODE_ROWS), 1)
    total = None
    for k in range(pd_size):
        pick = column < 0
        for r in range(GROUP_REQUESTS):
            slot = facts.slots[r]
            first = jnp.where(facts.group ^ (slot // GROUP_REQUESTS) == k, slot % GROUP_REQUESTS * DECODE_STEPS, -DECODE_ROWS * 4)
            pick = pick | ((row // DECODE_STEPS == r) & (column == first + row - r * DECODE_STEPS))
        part = product(pick.astype(jnp.float32).astype(jnp.bfloat16), block_refs[k][...])
        total = part if total is None else total + part
    return total.astype(jnp.bfloat16)


def pick_matrix(facts):
    row = iota((PADDED_ROWS, PADDED_ROWS), 0)
    column = iota((PADDED_ROWS, PADDED_ROWS), 1)
    pick = column < 0
    for r in range(GROUP_REQUESTS):
        ahead = facts.group ^ (facts.slots[r] // GROUP_REQUESTS)
        pick = pick | (
            (column // DECODE_STEPS == r) & (row == ahead * DECODE_STEPS + column - r * DECODE_STEPS)
        )
    return pick.astype(jnp.float32).astype(jnp.bfloat16)


def fresh_mask():
    row = iota((STACKED, PADDED_ROWS), 0) % PADDED_ROWS
    column = iota((STACKED, PADDED_ROWS), 1)
    return (column // DECODE_STEPS == row // DECODE_STEPS) & (
        column % DECODE_STEPS <= row % DECODE_STEPS
    )


def first_kernel(plan, pd_size, facts_ref, maxima_ref, q_ref, *refs):
    width = plan.size
    k_refs, v_refs, refs = refs[: width - 2], refs[width - 2 : 2 * width - 4], refs[2 * width - 4 :]
    block_refs, refs = refs[:pd_size], refs[pd_size:]
    acc_ref, bias_ref, dec_acc_ref, dec_bias_ref, worst_ref, queries_ref, fresh_ref, pick_ref, owner_ref = refs
    tokens = q_ref.shape[0]
    half = tokens // 2
    facts = Facts(facts_ref, width)
    sources = facts.source[:-2]
    pick_ref[...] = pick_matrix(facts)
    slot = iota((8, HEAD_SIZE), 0)
    owner = jnp.zeros_like(slot)
    for p in range(GROUP_REQUESTS):
        owner = jnp.where(slot == p, facts.owner[p], owner)
    owner_ref[...] = owner
    for s in range(width):
        bias_ref[s] = causal_bias(0, tokens, tokens, facts.source[s : s + 1], facts.ends, facts.member, width)
        dec_bias_ref[s] = jnp.where(
            request_mask(facts.ends, tokens, facts.source[s : s + 1], width), 0.0, MASKED
        )
    rows = picked_rows(facts, pd_size, block_refs)
    queries_ref[...] = rows[:, :Q_WIDTH]
    fresh_ref[...] = rows[:, Q_WIDTH:]
    worst_ref[...] = maxima_ref[...]
    new_mask = fresh_mask()
    mask = request_mask(facts.ends, tokens, sources, width)
    spans = ((0, half), (half, tokens))
    biases = [
        causal_bias(s, half, keys, sources, facts.ends, facts.member, width) for s, keys in spans
    ]
    together = max(1, min(HEADS_PER_KV, HEADS_PER_KV * 4 // width))

    def weigh(exponents):
        top = jnp.max(peak(exponents), axis=1, keepdims=True)
        worst_ref[...] = jnp.maximum(worst_ref[...], top)
        return jnp.exp2(exponents).astype(jnp.bfloat16)

    def step(h):
        columns = span(h * HEAD_SIZE, HEAD_SIZE)
        first = h * Q_BLOCK
        queries = stacked_heads(queries_ref, slice(None), first, HEADS_PER_KV)
        k_all = jnp.concatenate([ref[:, columns] for ref in k_refs], axis=0)
        v_all = with_ones(jnp.concatenate([ref[:, columns] for ref in v_refs], axis=0))
        new_scores = scores_of(queries, fresh_ref[:, columns]) * EXPONENT
        new_weights = weigh(jnp.where(new_mask, new_scores, MASKED))
        new_values = fresh_ref[:, span(KV_WIDTH + h * HEAD_SIZE, HEAD_SIZE)]
        weights = weigh(jnp.where(mask, scores_of(queries, k_all) * EXPONENT, MASKED))
        dec_acc_ref[h] = product(weights, v_all) + product(new_weights, with_ones(new_values))
        for (start, keys), bias in zip(spans, biases):
            if keys < tokens:
                k_part = jnp.concatenate([ref[:keys, columns] for ref in k_refs], axis=0)
                v_part = with_ones(jnp.concatenate([ref[:keys, columns] for ref in v_refs], axis=0))
            else:
                k_part, v_part = k_all, v_all
            for g in range(0, HEADS_PER_KV, together):
                queries = stacked_heads(
                    q_ref, slice(start, start + half), first + g * HEAD_SIZE, together
                )
                scores = scores_of(queries, k_part).reshape(together, half, bias.shape[1])
                exponents = (scores * EXPONENT + bias[None]).reshape(together * half, bias.shape[1])
                rows = slice(
                    start * HEADS_PER_KV + g * half, start * HEADS_PER_KV + (g + together) * half
                )
                acc_ref[h, rows, :] = product(weigh(exponents), v_part)

    each_kv_head(width, step)


def middle_kernel(plan, acc_ref, bias_ref, dec_acc_ref, dec_bias_ref, worst_ref, queries_ref, q_ref, k_ref, v_ref, *refs):
    new_acc_ref, new_dec_acc_ref, new_worst_ref = refs
    piece = plan.size - 2
    tokens = q_ref.shape[0]
    half = tokens // 2
    worst = worst_ref[...]
    for h in range(KEY_VALUE_HEADS):
        columns = slice(h * HEAD_SIZE, (h + 1) * HEAD_SIZE)
        keys, values = k_ref[:, columns], with_ones(v_ref[:, columns])
        queries = stacked_heads(queries_ref, slice(None), h * Q_BLOCK, HEADS_PER_KV)
        exponents = scores_of(queries, keys) * EXPONENT + dec_bias_ref[piece]
        worst = jnp.maximum(worst, peak(exponents))
        new_dec_acc_ref[h] = dec_acc_ref[h] + product(jnp.exp2(exponents).astype(jnp.bfloat16), values)
        for start in (0, half):
            bias = bias_ref[piece, start : start + half, :]
            queries = stacked_heads(q_ref, slice(start, start + half), h * Q_BLOCK, HEADS_PER_KV)
            scores = scores_of(queries, keys).reshape(HEADS_PER_KV, half, tokens)
            exponents = (scores * EXPONENT + bias[None]).reshape(HEADS_PER_KV * half, tokens)
            worst = jnp.maximum(worst, peak(exponents))
            rows = slice(start * HEADS_PER_KV, (start + half) * HEADS_PER_KV)
            new_acc_ref[h, rows, :] = acc_ref[h, rows, :] + product(
                jnp.exp2(exponents).astype(jnp.bfloat16), values
            )
    new_worst_ref[...] = worst


def divided(acc):
    return (acc[:, :HEAD_SIZE] * pl.reciprocal(acc[:, HEAD_SIZE:], approx=True)).astype(jnp.bfloat16)


def fold(state, scores_list, values_list):
    top = None if state is None else state[0]
    for scores in scores_list:
        part = jnp.max(scores, axis=1, keepdims=True)
        top = part if top is None else jnp.maximum(top, part)
    acc = None
    for scores, values in zip(scores_list, values_list):
        weights = jnp.exp2((scores - top) * EXPONENT).astype(jnp.bfloat16)
        part = product(weights, with_ones(values))
        acc = part if acc is None else acc + part
    if state is not None:
        acc = acc + state[1] * jnp.exp2((state[0] - top) * EXPONENT)
    return top, acc


def parts_in(width):
    return [range(c, min(c + 4, width)) for c in range(0, width, 4)]


def out_of_range(worst, least):
    return (jnp.max(worst) > LIMIT) | (jnp.min(least) < 2.0**-LIMIT)


def decode_kernel(plan, acc_ref, bias_ref, worst_ref, queries_ref, fresh_ref, pick_ref, *refs):
    width = plan.size
    k_refs, v_refs, (out_ref,) = refs[:width], refs[width : 2 * width], refs[2 * width :]
    heads = range(KEY_VALUE_HEADS)
    columns = [slice(h * HEAD_SIZE, (h + 1) * HEAD_SIZE) for h in heads]

    def queries_of(h):
        return stacked_heads(queries_ref, slice(None), h * Q_BLOCK, HEADS_PER_KV)

    def send(acc):
        out = [divided(a) for a in acc]
        out = jnp.concatenate(
            [o[g * PADDED_ROWS : (g + 1) * PADDED_ROWS] for o in out for g in range(HEADS_PER_KV)], axis=1
        )
        out_ref[...] = product(pick_ref[...], out).astype(jnp.bfloat16)

    exponents = [
        scores_of(queries_of(h), k_refs[-1][:, columns[h]]) * EXPONENT + bias_ref[width - 1]
        for h in heads
    ]
    acc = [
        acc_ref[h] + product(jnp.exp2(exponents[h]).astype(jnp.bfloat16), with_ones(v_refs[-1][:, columns[h]]))
        for h in heads
    ]
    send(acc)
    worst, least = worst_ref[...], None
    for h in heads:
        worst = jnp.maximum(worst, peak(exponents[h]))
        part = jnp.min(acc[h][:, HEAD_SIZE:].reshape(-1, 8, HEAD_SIZE), axis=0)
        least = part if least is None else jnp.minimum(least, part)

    @pl.when(out_of_range(worst, least))
    def _():
        new_mask = fresh_mask()
        again = []
        for h in heads:
            queries = queries_of(h)
            scores = jnp.where(new_mask, scores_of(queries, fresh_ref[:, columns[h]]), MASKED)
            new_columns = slice(KV_WIDTH + h * HEAD_SIZE, KV_WIDTH + (h + 1) * HEAD_SIZE)
            state = fold(None, [scores], [fresh_ref[:, new_columns]])
            for parts in parts_in(width):
                k_part = jnp.concatenate([k_refs[s][:, columns[h]] for s in parts], axis=0)
                v_part = jnp.concatenate([v_refs[s][:, columns[h]] for s in parts], axis=0)
                bias = jnp.concatenate([bias_ref[s] for s in parts], axis=1)
                state = fold(state, [scores_of(queries, k_part) + bias], [v_part])
            again.append(state[1])
        send(again)


def prefill_kernel(plan, acc_ref, bias_ref, worst_ref, q_ref, *refs):
    width = plan.size
    k_refs, v_refs, refs = refs[:width], refs[width : 2 * width], refs[2 * width :]
    out_ref, done_ref, sem = refs
    tokens = q_ref.shape[0]
    half = tokens // 2
    def write(h, start, acc):
        out = divided(acc)
        for g in range(HEADS_PER_KV):
            done_ref[start : start + half, span(h * Q_BLOCK + g * HEAD_SIZE, HEAD_SIZE)] = out[
                g * half : (g + 1) * half
            ]

    def copy_out(h):
        part = pl.ds(h * Q_BLOCK, Q_BLOCK)
        return pltpu.make_async_copy(done_ref.at[:, part], out_ref.at[:, part], sem.at[h])

    biases = [bias_ref[width - 1, start : start + half, :] for start in (0, half)]
    worst, least = worst_ref[...], None
    for h in range(KEY_VALUE_HEADS):
        columns = slice(h * HEAD_SIZE, (h + 1) * HEAD_SIZE)
        keys, values = k_refs[-1][:, columns], with_ones(v_refs[-1][:, columns])
        for start, bias in zip((0, half), biases):
            queries = stacked_heads(q_ref, slice(start, start + half), h * Q_BLOCK, HEADS_PER_KV)
            scores = scores_of(queries, keys).reshape(HEADS_PER_KV, half, tokens)
            exponents = (scores * EXPONENT + bias[None]).reshape(HEADS_PER_KV * half, tokens)
            worst = jnp.maximum(worst, peak(exponents))
            rows = slice(start * HEADS_PER_KV, (start + half) * HEADS_PER_KV)
            acc = acc_ref[h, rows, :] + product(jnp.exp2(exponents).astype(jnp.bfloat16), values)
            part = jnp.min(acc[:, HEAD_SIZE:].reshape(-1, 8, HEAD_SIZE), axis=0)
            least = part if least is None else jnp.minimum(least, part)
            write(h, start, acc)
        copy_out(h).start()
    redo = out_of_range(worst, least)
    for h in range(KEY_VALUE_HEADS):
        copy_out(h).wait()

    @pl.when(redo)
    def _():
        def step(h, carry):
            columns = span(h * HEAD_SIZE, HEAD_SIZE)
            for start in (0, half):
                queries = stacked_heads(q_ref, slice(start, start + half), h * Q_BLOCK, HEADS_PER_KV)
                state = None
                for parts in parts_in(width):
                    k_part = jnp.concatenate([k_refs[s][:, columns] for s in parts], axis=0)
                    v_part = jnp.concatenate([v_refs[s][:, columns] for s in parts], axis=0)
                    bias = jnp.concatenate([bias_ref[s, start : start + half, :] for s in parts], axis=1)
                    scores = scores_of(queries, k_part).reshape(HEADS_PER_KV, half, bias.shape[1])
                    scores = (scores + bias[None]).reshape(HEADS_PER_KV * half, bias.shape[1])
                    state = fold(state, [scores], [v_part])
                write(h, start, state[1])
            return carry

        lax.fori_loop(0, KEY_VALUE_HEADS, step, 0)
        for h in range(KEY_VALUE_HEADS):
            copy_out(h).start()
        for h in range(KEY_VALUE_HEADS):
            copy_out(h).wait()


def cost(rows, keys, exps):
    return pl.CostEstimate(
        flops=32 * rows * keys * Q_WIDTH, bytes_accessed=4 * rows * Q_WIDTH, transcendentals=exps
    )


def call_first(plan, facts, maxima, query, blocks, keys, values):
    tokens, width = query.shape[0], plan.size
    rows = HEADS_PER_KV * tokens
    f32, bf16 = jnp.float32, jnp.bfloat16
    every = (width - 2) * tokens
    shapes = [
        jax.ShapeDtypeStruct((KEY_VALUE_HEADS, rows, 2 * HEAD_SIZE), f32),
        jax.ShapeDtypeStruct((width, tokens, tokens), f32),
        jax.ShapeDtypeStruct((KEY_VALUE_HEADS, STACKED, 2 * HEAD_SIZE), f32),
        jax.ShapeDtypeStruct((width, STACKED, tokens), f32),
        jax.ShapeDtypeStruct((8, HEAD_SIZE), f32),
        jax.ShapeDtypeStruct((PADDED_ROWS, Q_WIDTH), bf16),
        jax.ShapeDtypeStruct((PADDED_ROWS, 2 * KV_WIDTH), bf16),
        jax.ShapeDtypeStruct((PADDED_ROWS, PADDED_ROWS), bf16),
        jax.ShapeDtypeStruct((8, HEAD_SIZE), jnp.int32),
    ]
    return pl.pallas_call(
        lambda *refs: first_kernel(plan, len(blocks), *refs),
        in_specs=[SMEM] + [VMEM] * (2 + len(blocks) + 2 * (width - 2)),
        out_specs=[VMEM] * len(shapes),
        out_shape=shapes,
        compiler_params=pltpu.CompilerParams(vmem_limit_bytes=(28 + width) * MIB),
        cost_estimate=cost(tokens, every, tokens * every * QUERY_HEADS),
        name="first_shards",
    )(facts, maxima, query, *keys, *values, *blocks)


def call_middle(plan, state, query, key, value):
    acc, bias, dec_acc, dec_bias, worst, queries = state[:6]
    tokens = query.shape[0]
    new_acc, new_dec_acc, new_worst = pl.pallas_call(
        lambda *refs: middle_kernel(plan, *refs),
        in_specs=[VMEM] * 9,
        out_specs=[VMEM] * 3,
        out_shape=[jax.ShapeDtypeStruct(a.shape, a.dtype) for a in (acc, dec_acc, worst)],
        input_output_aliases={0: 0, 2: 1, 4: 2},
        compiler_params=pltpu.CompilerParams(vmem_limit_bytes=32 * MIB),
        cost_estimate=cost(tokens, tokens, tokens * tokens * QUERY_HEADS),
        name="middle_shard",
    )(acc, bias, dec_acc, dec_bias, worst, queries, query, key, value)
    return [new_acc, bias, new_dec_acc, dec_bias, new_worst] + list(state[5:])


def call_decode(plan, state, keys, values):
    tokens, width = keys[0].shape[0], plan.size
    return pl.pallas_call(
        lambda *refs: decode_kernel(plan, *refs),
        in_specs=[VMEM] * (6 + 2 * width),
        out_specs=VMEM,
        out_shape=jax.ShapeDtypeStruct((PADDED_ROWS, Q_WIDTH), jnp.bfloat16),
        compiler_params=pltpu.CompilerParams(vmem_limit_bytes=(28 + width) * MIB),
        cost_estimate=cost(PADDED_ROWS, tokens, PADDED_ROWS * tokens * QUERY_HEADS),
        name="last_shard_decode",
    )(*state[2:8], *keys, *values)


def call_prefill(plan, state, query, keys, values):
    tokens, width = query.shape[0], plan.size
    return pl.pallas_call(
        lambda *refs: prefill_kernel(plan, *refs),
        in_specs=[VMEM] * (4 + 2 * width),
        out_specs=ANY,
        out_shape=jax.ShapeDtypeStruct((tokens, Q_WIDTH), jnp.bfloat16),
        scratch_shapes=[
            pltpu.VMEM((tokens, Q_WIDTH), jnp.bfloat16),
            pltpu.SemaphoreType.DMA((KEY_VALUE_HEADS,)),
        ],
        compiler_params=pltpu.CompilerParams(vmem_limit_bytes=(28 + width) * MIB),
        cost_estimate=cost(tokens, tokens, tokens * tokens * QUERY_HEADS),
        name="last_shard_prefill",
    )(*state[:2], state[4], query, *keys, *values)


def start_maxima(*arrays, flops=5 * 10**9):
    def kernel(*refs):
        refs[-1][...] = jnp.full((8, HEAD_SIZE), MASKED, jnp.float32)

    return pl.pallas_call(
        kernel,
        in_specs=[VMEM] * len(arrays),
        out_specs=VMEM,
        out_shape=jax.ShapeDtypeStruct((8, HEAD_SIZE), jnp.float32),
        cost_estimate=pl.CostEstimate(flops=flops, bytes_accessed=0, transcendentals=0),
        compiler_params=pltpu.CompilerParams(vmem_limit_bytes=MIB),
        name="start_maxima",
    )(*arrays)


def paired(array, k):
    return lax.ppermute(array, "pd", [(g, g ^ k) for g in range(lax.axis_size("pd"))])


def body(
    prompt_query,
    prompt_key,
    prompt_value,
    prompt_lengths,
    decode_slot,
    decoded_query,
    decoded_key,
    decoded_value,
):
    plan = Ring(lax.axis_size("tp"))
    pd_size = lax.axis_size("pd")
    own = jnp.concatenate([decoded_query, decoded_key, decoded_value], axis=2).reshape(
        DECODE_ROWS, Q_WIDTH + 2 * KV_WIDTH
    )
    facts = facts_row(plan, prompt_lengths, decode_slot)
    prompt_key, decoded_query = lax.optimization_barrier((prompt_key, decoded_query))
    later_key, later_value, own, facts = lax.optimization_barrier((prompt_key, prompt_value, own, facts))
    chains = []
    for up, down in ((prompt_key, later_key), (prompt_value, later_value)):
        pieces = [up]
        for d in range(1, plan.size // 2 + 1):
            up = plan.step(up, True)
            down = plan.step(down, False) if 2 * d < plan.size else None
            pieces += [up, down]
        chains.append(pieces[: plan.size])
    keys, values = chains
    blocks = [own] + [paired(own, k) for k in range(1, pd_size)]
    maxima = start_maxima(keys[1], values[1])

    state = call_first(plan, facts, maxima, prompt_query, blocks, keys[:-2], values[:-2])
    state = call_middle(plan, state, prompt_query, keys[-2], values[-2])
    outgoing = call_decode(plan, state, keys, values)
    arrived = [outgoing[:DECODE_STEPS]]
    for k in range(1, pd_size):
        arrived.append(paired(outgoing[k * DECODE_STEPS : (k + 1) * DECODE_STEPS], k))
    pre_out = call_prefill(plan, state, prompt_query, keys, values)

    from_block = state[8][:GROUP_REQUESTS, 0]
    dec_out = jnp.zeros((GROUP_REQUESTS, DECODE_STEPS, Q_WIDTH), jnp.bfloat16)
    for k in range(pd_size):
        dec_out = jnp.where((from_block == k)[:, None, None], arrived[k][None], dec_out)
    return (pre_out, dec_out)


def solution(mesh):
    placed = (
        P(("rep", "pd", "tp"), None),
        P(("rep", "pd", "tp"), None),
        P(("rep", "pd", "tp"), None),
        P("rep", None),
        P("rep"),
        P(("rep", "pd"), None, None),
        P(("rep", "pd"), None, None),
        P(("rep", "pd"), None, None),
    )
    return jax.shard_map(
        body,
        mesh=mesh,
        in_specs=placed,
        out_specs=(P(("rep", "pd", "tp"), None), P(("rep", "pd"), None, None)),
        check_vma=False,
    )
```

```python
import math

import jax
import jax.numpy as jnp
from jax import lax
from jax.experimental import pallas as pl
from jax.experimental.pallas import tpu as pltpu
from jax.sharding import PartitionSpec as P

QUERY_HEADS = 32
KEY_VALUE_HEADS = 4
HEAD_SIZE = 128
PAGE = 16
GROUP_REQUESTS = 4
DECODE_STEPS = 2
HEADS_PER_KV = QUERY_HEADS // KEY_VALUE_HEADS
KV_WIDTH = KEY_VALUE_HEADS * HEAD_SIZE
Q_WIDTH = QUERY_HEADS * HEAD_SIZE
Q_BLOCK = HEADS_PER_KV * HEAD_SIZE
DECODE_ROWS = GROUP_REQUESTS * DECODE_STEPS
PADDED_ROWS = 16
STACKED = HEADS_PER_KV * PADDED_ROWS
MIB = 1024 * 1024

MASKED = -1e30
LIMIT = 60.0
EXPONENT = math.log2(math.e) / math.sqrt(HEAD_SIZE)

VMEM = pl.BlockSpec(memory_space=pltpu.VMEM)
SMEM = pl.BlockSpec(memory_space=pltpu.SMEM)
ANY = pl.BlockSpec(memory_space=pl.ANY)
HBM = pl.BlockSpec(memory_space=pltpu.HBM)


class Ring:
    def __init__(self, size):
        self.size = size
        order = [0] + list(range(1, size, 2)) + [i for i in range(size - 1, 0, -1) if i % 2 == 0]
        self.pairs = [(order[i], order[(i + 1) % size]) for i in range(size)]
        self.offsets = [0]
        for d in range(1, size // 2 + 1):
            self.offsets += [-d, d]
        self.offsets = self.offsets[:size]

    def step(self, array, up):
        return lax.ppermute(array, "tp", self.pairs if up else [(b, a) for a, b in self.pairs])


def scores_of(queries, keys):
    return lax.dot_general(
        queries, keys, (((1,), (1,)), ((), ())), preferred_element_type=jnp.float32
    )


def product(left, right):
    return jnp.dot(left, right, preferred_element_type=jnp.float32)


def iota(shape, axis):
    return lax.broadcasted_iota(jnp.int32, shape, axis)


def span(start, size):
    if isinstance(start, int):
        return slice(start, start + size)
    return pl.ds(pl.multiple_of(start, size), size)


def with_ones(values):
    return jnp.concatenate([values, jnp.ones_like(values)], axis=1)


def page_position(offset, member, width):
    return (offset // PAGE * width + member) * PAGE + offset % PAGE


def key_positions(rows, sources, width):
    column = iota((1, len(sources) * rows), 1)
    part = column // rows
    source = jnp.zeros_like(column) + sources[0]
    for b in range(1, len(sources)):
        source = jnp.where(part == b, sources[b], source)
    return page_position(column - part * rows, source, width)


class Facts:
    def __init__(self, ref, width):
        self.width = width
        self.group, self.member = ref[0], ref[1]
        self.slots = [ref[2 + r] for r in range(GROUP_REQUESTS)]
        first = 2 + GROUP_REQUESTS
        self.ends = []
        total = jnp.int32(0)
        for r in range(GROUP_REQUESTS):
            total = total + ref[first + r] * PAGE
            self.ends.append(total)
        first += GROUP_REQUESTS
        self.source = [ref[first + s] for s in range(width)]
        first += width
        self.owner = [ref[first + p] for p in range(GROUP_REQUESTS)]


def facts_row(plan, lengths, slots):
    width, requests = plan.size, slots.shape[0]

    def kernel(lengths_ref, slots_ref, out_ref):
        group, member = lax.axis_index("pd"), lax.axis_index("tp")
        values = [group, member]
        values += [slots_ref[group * GROUP_REQUESTS + r] for r in range(GROUP_REQUESTS)]
        values += [lengths_ref[group, r] for r in range(GROUP_REQUESTS)]
        place = jnp.where(member % 2 == 1, (member + 1) // 2, width - member // 2)
        for offset in plan.offsets:
            before = (place + width + offset) % width
            up = 2 * before - 1
            values.append(jnp.where(before == 0, 0, jnp.where(before <= width // 2, up, 2 * (width - before))))
        for i, value in enumerate(values):
            out_ref[i] = value.astype(jnp.int32)
        for q in range(requests):
            place = slots_ref[q] - group * GROUP_REQUESTS

            @pl.when((place >= 0) & (place < GROUP_REQUESTS))
            def _():
                out_ref[len(values) + place] = group ^ (q // GROUP_REQUESTS)

    length = 2 + 2 * GROUP_REQUESTS + width + GROUP_REQUESTS
    return pl.pallas_call(
        kernel,
        in_specs=[SMEM, SMEM],
        out_specs=SMEM,
        out_shape=jax.ShapeDtypeStruct((length,), jnp.int32),
        cost_estimate=pl.CostEstimate(flops=5 * 10**9, bytes_accessed=0, transcendentals=0),
        name="facts",
    )(lengths, slots)


def causal_bias(start, rows, keys, sources, ends, member, width):
    qpos = page_position(start + iota((rows, 1), 0), member, width)
    low = jnp.zeros_like(qpos)
    for end in ends:
        low = jnp.where(qpos >= end, end, low)
    kpos = key_positions(keys, sources, width)
    return jnp.where((kpos >= low) & (kpos <= qpos), 0.0, MASKED)


def request_mask(ends, keys, sources, width):
    request = iota((STACKED, 1), 0) % PADDED_ROWS // DECODE_STEPS
    low = jnp.zeros_like(request)
    high = jnp.zeros_like(request) + ends[0]
    for r in range(1, GROUP_REQUESTS):
        low = jnp.where(request == r, ends[r - 1], low)
        high = jnp.where(request == r, ends[r], high)
    kpos = key_positions(keys, sources, width)
    return (kpos >= low) & (kpos < high)


def stacked_heads(ref, rows, first, count):
    return jnp.concatenate(
        [ref[rows, span(first + i * HEAD_SIZE, HEAD_SIZE)] for i in range(count)], axis=0
    )


def each_kv_head(width, step):
    if width <= 8:
        for h in range(KEY_VALUE_HEADS):
            step(h)
    else:
        lax.fori_loop(0, KEY_VALUE_HEADS, lambda h, c: (step(h), c)[1], 0)


def peak(exponents):
    return jnp.max(exponents.reshape(-1, 8, exponents.shape[-1]), axis=0)


def picked_rows(facts, pd_size, block_refs):
    row = iota((PADDED_ROWS, DECODE_ROWS), 0)
    column = iota((PADDED_ROWS, DECODE_ROWS), 1)
    total = None
    for k in range(pd_size):
        pick = column < 0
        for r in range(GROUP_REQUESTS):
            slot = facts.slots[r]
            first = jnp.where(facts.group ^ (slot // GROUP_REQUESTS) == k, slot % GROUP_REQUESTS * DECODE_STEPS, -DECODE_ROWS * 4)
            pick = pick | ((row // DECODE_STEPS == r) & (column == first + row - r * DECODE_STEPS))
        part = product(pick.astype(jnp.float32).astype(jnp.bfloat16), block_refs[k][...])
        total = part if total is None else total + part
    return total.astype(jnp.bfloat16)


def pick_matrix(facts):
    row = iota((PADDED_ROWS, PADDED_ROWS), 0)
    column = iota((PADDED_ROWS, PADDED_ROWS), 1)
    pick = column < 0
    for r in range(GROUP_REQUESTS):
        ahead = facts.group ^ (facts.slots[r] // GROUP_REQUESTS)
        pick = pick | (
            (column // DECODE_STEPS == r) & (row == ahead * DECODE_STEPS + column - r * DECODE_STEPS)
        )
    return pick.astype(jnp.float32).astype(jnp.bfloat16)


def fresh_mask():
    row = iota((STACKED, PADDED_ROWS), 0) % PADDED_ROWS
    column = iota((STACKED, PADDED_ROWS), 1)
    return (column // DECODE_STEPS == row // DECODE_STEPS) & (
        column % DECODE_STEPS <= row % DECODE_STEPS
    )


def first_kernel(plan, pd_size, facts_ref, maxima_ref, q_ref, *refs):
    width = plan.size
    k_refs, v_refs, refs = refs[: width - 2], refs[width - 2 : 2 * width - 4], refs[2 * width - 4 :]
    block_refs, refs = refs[:pd_size], refs[pd_size:]
    acc_ref, bias_ref, dec_acc_ref, dec_bias_ref, worst_ref, queries_ref, fresh_ref, pick_ref, owner_ref = refs
    tokens = q_ref.shape[0]
    half = tokens // 2
    facts = Facts(facts_ref, width)
    sources = facts.source[:-2]
    pick_ref[...] = pick_matrix(facts)
    slot = iota((8, HEAD_SIZE), 0)
    owner = jnp.zeros_like(slot)
    for p in range(GROUP_REQUESTS):
        owner = jnp.where(slot == p, facts.owner[p], owner)
    owner_ref[...] = owner
    for s in range(width):
        bias_ref[s] = causal_bias(0, tokens, tokens, facts.source[s : s + 1], facts.ends, facts.member, width)
        dec_bias_ref[s] = jnp.where(
            request_mask(facts.ends, tokens, facts.source[s : s + 1], width), 0.0, MASKED
        )
    rows = picked_rows(facts, pd_size, block_refs)
    queries_ref[...] = rows[:, :Q_WIDTH]
    fresh_ref[...] = rows[:, Q_WIDTH:]
    worst_ref[...] = maxima_ref[...]
    new_mask = fresh_mask()
    mask = request_mask(facts.ends, tokens, sources, width)
    spans = ((0, half), (half, tokens))
    biases = [
        causal_bias(s, half, keys, sources, facts.ends, facts.member, width) for s, keys in spans
    ]
    together = max(1, min(HEADS_PER_KV, HEADS_PER_KV * 4 // width))

    def weigh(exponents):
        top = jnp.max(peak(exponents), axis=1, keepdims=True)
        worst_ref[...] = jnp.maximum(worst_ref[...], top)
        return jnp.exp2(exponents).astype(jnp.bfloat16)

    def step(h):
        columns = span(h * HEAD_SIZE, HEAD_SIZE)
        first = h * Q_BLOCK
        queries = stacked_heads(queries_ref, slice(None), first, HEADS_PER_KV)
        k_all = jnp.concatenate([ref[:, columns] for ref in k_refs], axis=0)
        v_all = with_ones(jnp.concatenate([ref[:, columns] for ref in v_refs], axis=0))
        new_scores = scores_of(queries, fresh_ref[:, columns]) * EXPONENT
        new_weights = weigh(jnp.where(new_mask, new_scores, MASKED))
        new_values = fresh_ref[:, span(KV_WIDTH + h * HEAD_SIZE, HEAD_SIZE)]
        weights = weigh(jnp.where(mask, scores_of(queries, k_all) * EXPONENT, MASKED))
        dec_acc_ref[h] = product(weights, v_all) + product(new_weights, with_ones(new_values))
        for (start, keys), bias in zip(spans, biases):
            if keys < tokens:
                k_part = jnp.concatenate([ref[:keys, columns] for ref in k_refs], axis=0)
                v_part = with_ones(jnp.concatenate([ref[:keys, columns] for ref in v_refs], axis=0))
            else:
                k_part, v_part = k_all, v_all
            for g in range(0, HEADS_PER_KV, together):
                queries = stacked_heads(
                    q_ref, slice(start, start + half), first + g * HEAD_SIZE, together
                )
                scores = scores_of(queries, k_part).reshape(together, half, bias.shape[1])
                exponents = (scores * EXPONENT + bias[None]).reshape(together * half, bias.shape[1])
                rows = slice(
                    start * HEADS_PER_KV + g * half, start * HEADS_PER_KV + (g + together) * half
                )
                acc_ref[h, rows, :] = product(weigh(exponents), v_part)

    each_kv_head(width, step)


def middle_kernel(plan, acc_ref, bias_ref, dec_acc_ref, dec_bias_ref, worst_ref, queries_ref, q_ref, k_ref, v_ref, *refs):
    new_acc_ref, new_dec_acc_ref, new_worst_ref = refs
    piece = plan.size - 2
    tokens = q_ref.shape[0]
    half = tokens // 2
    worst = worst_ref[...]
    for h in range(KEY_VALUE_HEADS):
        columns = slice(h * HEAD_SIZE, (h + 1) * HEAD_SIZE)
        keys, values = k_ref[:, columns], with_ones(v_ref[:, columns])
        queries = stacked_heads(queries_ref, slice(None), h * Q_BLOCK, HEADS_PER_KV)
        exponents = scores_of(queries, keys) * EXPONENT + dec_bias_ref[piece]
        worst = jnp.maximum(worst, peak(exponents))
        new_dec_acc_ref[h] = dec_acc_ref[h] + product(jnp.exp2(exponents).astype(jnp.bfloat16), values)
        for start in (0, half):
            bias = bias_ref[piece, start : start + half, :]
            queries = stacked_heads(q_ref, slice(start, start + half), h * Q_BLOCK, HEADS_PER_KV)
            scores = scores_of(queries, keys).reshape(HEADS_PER_KV, half, tokens)
            exponents = (scores * EXPONENT + bias[None]).reshape(HEADS_PER_KV * half, tokens)
            worst = jnp.maximum(worst, peak(exponents))
            rows = slice(start * HEADS_PER_KV, (start + half) * HEADS_PER_KV)
            new_acc_ref[h, rows, :] = acc_ref[h, rows, :] + product(
                jnp.exp2(exponents).astype(jnp.bfloat16), values
            )
    new_worst_ref[...] = worst


def divided(acc):
    return (acc[:, :HEAD_SIZE] * pl.reciprocal(acc[:, HEAD_SIZE:], approx=True)).astype(jnp.bfloat16)


def fold(state, scores_list, values_list):
    top = None if state is None else state[0]
    for scores in scores_list:
        part = jnp.max(scores, axis=1, keepdims=True)
        top = part if top is None else jnp.maximum(top, part)
    acc = None
    for scores, values in zip(scores_list, values_list):
        weights = jnp.exp2((scores - top) * EXPONENT).astype(jnp.bfloat16)
        part = product(weights, with_ones(values))
        acc = part if acc is None else acc + part
    if state is not None:
        acc = acc + state[1] * jnp.exp2((state[0] - top) * EXPONENT)
    return top, acc


def parts_in(width):
    return [range(c, min(c + 4, width)) for c in range(0, width, 4)]


def out_of_range(worst, least):
    return (jnp.max(worst) > LIMIT) | (jnp.min(least) < 2.0**-LIMIT)


def decode_kernel(plan, acc_ref, bias_ref, worst_ref, queries_ref, fresh_ref, pick_ref, *refs):
    width = plan.size
    k_refs, v_refs, (out_ref,) = refs[:width], refs[width : 2 * width], refs[2 * width :]
    heads = range(KEY_VALUE_HEADS)
    columns = [slice(h * HEAD_SIZE, (h + 1) * HEAD_SIZE) for h in heads]

    def queries_of(h):
        return stacked_heads(queries_ref, slice(None), h * Q_BLOCK, HEADS_PER_KV)

    def send(acc):
        out = [divided(a) for a in acc]
        out = jnp.concatenate(
            [o[g * PADDED_ROWS : (g + 1) * PADDED_ROWS] for o in out for g in range(HEADS_PER_KV)], axis=1
        )
        out_ref[...] = product(pick_ref[...], out).astype(jnp.bfloat16)

    exponents = [
        scores_of(queries_of(h), k_refs[-1][:, columns[h]]) * EXPONENT + bias_ref[width - 1]
        for h in heads
    ]
    acc = [
        acc_ref[h] + product(jnp.exp2(exponents[h]).astype(jnp.bfloat16), with_ones(v_refs[-1][:, columns[h]]))
        for h in heads
    ]
    send(acc)
    worst, least = worst_ref[...], None
    for h in heads:
        worst = jnp.maximum(worst, peak(exponents[h]))
        part = jnp.min(acc[h][:, HEAD_SIZE:].reshape(-1, 8, HEAD_SIZE), axis=0)
        least = part if least is None else jnp.minimum(least, part)

    @pl.when(out_of_range(worst, least))
    def _():
        new_mask = fresh_mask()
        again = []
        for h in heads:
            queries = queries_of(h)
            scores = jnp.where(new_mask, scores_of(queries, fresh_ref[:, columns[h]]), MASKED)
            new_columns = slice(KV_WIDTH + h * HEAD_SIZE, KV_WIDTH + (h + 1) * HEAD_SIZE)
            state = fold(None, [scores], [fresh_ref[:, new_columns]])
            for parts in parts_in(width):
                k_part = jnp.concatenate([k_refs[s][:, columns[h]] for s in parts], axis=0)
                v_part = jnp.concatenate([v_refs[s][:, columns[h]] for s in parts], axis=0)
                bias = jnp.concatenate([bias_ref[s] for s in parts], axis=1)
                state = fold(state, [scores_of(queries, k_part) + bias], [v_part])
            again.append(state[1])
        send(again)


def prefill_kernel(plan, acc_ref, bias_ref, worst_ref, q_ref, *refs):
    width = plan.size
    k_refs, v_refs, refs = refs[:width], refs[width : 2 * width], refs[2 * width :]
    out_ref, done_ref, sem = refs
    tokens = q_ref.shape[0]
    half = tokens // 2
    def write(h, start, acc):
        out = divided(acc)
        for g in range(HEADS_PER_KV):
            done_ref[start : start + half, span(h * Q_BLOCK + g * HEAD_SIZE, HEAD_SIZE)] = out[
                g * half : (g + 1) * half
            ]

    def copy_out(h):
        part = pl.ds(h * Q_BLOCK, Q_BLOCK)
        return pltpu.make_async_copy(done_ref.at[:, part], out_ref.at[:, part], sem.at[h])

    biases = [bias_ref[width - 1, start : start + half, :] for start in (0, half)]
    worst, least = worst_ref[...], None
    for h in range(KEY_VALUE_HEADS):
        columns = slice(h * HEAD_SIZE, (h + 1) * HEAD_SIZE)
        keys, values = k_refs[-1][:, columns], with_ones(v_refs[-1][:, columns])
        for start, bias in zip((0, half), biases):
            queries = stacked_heads(q_ref, slice(start, start + half), h * Q_BLOCK, HEADS_PER_KV)
            scores = scores_of(queries, keys).reshape(HEADS_PER_KV, half, tokens)
            exponents = (scores * EXPONENT + bias[None]).reshape(HEADS_PER_KV * half, tokens)
            worst = jnp.maximum(worst, peak(exponents))
            rows = slice(start * HEADS_PER_KV, (start + half) * HEADS_PER_KV)
            acc = acc_ref[h, rows, :] + product(jnp.exp2(exponents).astype(jnp.bfloat16), values)
            part = jnp.min(acc[:, HEAD_SIZE:].reshape(-1, 8, HEAD_SIZE), axis=0)
            least = part if least is None else jnp.minimum(least, part)
            write(h, start, acc)
        copy_out(h).start()
    redo = out_of_range(worst, least)
    for h in range(KEY_VALUE_HEADS):
        copy_out(h).wait()

    @pl.when(redo)
    def _():
        def step(h, carry):
            columns = span(h * HEAD_SIZE, HEAD_SIZE)
            for start in (0, half):
                queries = stacked_heads(q_ref, slice(start, start + half), h * Q_BLOCK, HEADS_PER_KV)
                state = None
                for parts in parts_in(width):
                    k_part = jnp.concatenate([k_refs[s][:, columns] for s in parts], axis=0)
                    v_part = jnp.concatenate([v_refs[s][:, columns] for s in parts], axis=0)
                    bias = jnp.concatenate([bias_ref[s, start : start + half, :] for s in parts], axis=1)
                    scores = scores_of(queries, k_part).reshape(HEADS_PER_KV, half, bias.shape[1])
                    scores = (scores + bias[None]).reshape(HEADS_PER_KV * half, bias.shape[1])
                    state = fold(state, [scores], [v_part])
                write(h, start, state[1])
            return carry

        lax.fori_loop(0, KEY_VALUE_HEADS, step, 0)
        for h in range(KEY_VALUE_HEADS):
            copy_out(h).start()
        for h in range(KEY_VALUE_HEADS):
            copy_out(h).wait()


def cost(rows, keys, exps):
    return pl.CostEstimate(
        flops=32 * rows * keys * Q_WIDTH, bytes_accessed=4 * rows * Q_WIDTH, transcendentals=exps
    )


def call_first(plan, facts, maxima, query, blocks, keys, values):
    tokens, width = query.shape[0], plan.size
    rows = HEADS_PER_KV * tokens
    f32, bf16 = jnp.float32, jnp.bfloat16
    every = (width - 2) * tokens
    shapes = [
        jax.ShapeDtypeStruct((KEY_VALUE_HEADS, rows, 2 * HEAD_SIZE), f32),
        jax.ShapeDtypeStruct((width, tokens, tokens), f32),
        jax.ShapeDtypeStruct((KEY_VALUE_HEADS, STACKED, 2 * HEAD_SIZE), f32),
        jax.ShapeDtypeStruct((width, STACKED, tokens), f32),
        jax.ShapeDtypeStruct((8, HEAD_SIZE), f32),
        jax.ShapeDtypeStruct((PADDED_ROWS, Q_WIDTH), bf16),
        jax.ShapeDtypeStruct((PADDED_ROWS, 2 * KV_WIDTH), bf16),
        jax.ShapeDtypeStruct((PADDED_ROWS, PADDED_ROWS), bf16),
        jax.ShapeDtypeStruct((8, HEAD_SIZE), jnp.int32),
    ]
    return pl.pallas_call(
        lambda *refs: first_kernel(plan, len(blocks), *refs),
        in_specs=[SMEM] + [VMEM] * (2 + len(blocks) + 2 * (width - 2)),
        out_specs=[VMEM] * len(shapes),
        out_shape=shapes,
        compiler_params=pltpu.CompilerParams(vmem_limit_bytes=(28 + width) * MIB),
        cost_estimate=cost(tokens, every, tokens * every * QUERY_HEADS),
        name="first_shards",
    )(facts, maxima, query, *keys, *values, *blocks)


def call_middle(plan, state, query, key, value):
    acc, bias, dec_acc, dec_bias, worst, queries = state[:6]
    tokens = query.shape[0]
    new_acc, new_dec_acc, new_worst = pl.pallas_call(
        lambda *refs: middle_kernel(plan, *refs),
        in_specs=[VMEM] * 9,
        out_specs=[VMEM] * 3,
        out_shape=[jax.ShapeDtypeStruct(a.shape, a.dtype) for a in (acc, dec_acc, worst)],
        input_output_aliases={0: 0, 2: 1, 4: 2},
        compiler_params=pltpu.CompilerParams(vmem_limit_bytes=32 * MIB),
        cost_estimate=cost(tokens, tokens, tokens * tokens * QUERY_HEADS),
        name="middle_shard",
    )(acc, bias, dec_acc, dec_bias, worst, queries, query, key, value)
    return [new_acc, bias, new_dec_acc, dec_bias, new_worst] + list(state[5:])


def call_decode(plan, state, keys, values):
    tokens, width = keys[0].shape[0], plan.size
    return pl.pallas_call(
        lambda *refs: decode_kernel(plan, *refs),
        in_specs=[VMEM] * (6 + 2 * width),
        out_specs=VMEM,
        out_shape=jax.ShapeDtypeStruct((PADDED_ROWS, Q_WIDTH), jnp.bfloat16),
        compiler_params=pltpu.CompilerParams(vmem_limit_bytes=(28 + width) * MIB),
        cost_estimate=cost(PADDED_ROWS, tokens, PADDED_ROWS * tokens * QUERY_HEADS),
        name="last_shard_decode",
    )(*state[2:8], *keys, *values)


def call_prefill(plan, state, query, keys, values):
    tokens, width = query.shape[0], plan.size
    return pl.pallas_call(
        lambda *refs: prefill_kernel(plan, *refs),
        in_specs=[VMEM] * (4 + 2 * width),
        out_specs=ANY,
        out_shape=jax.ShapeDtypeStruct((tokens, Q_WIDTH), jnp.bfloat16),
        scratch_shapes=[
            pltpu.VMEM((tokens, Q_WIDTH), jnp.bfloat16),
            pltpu.SemaphoreType.DMA((KEY_VALUE_HEADS,)),
        ],
        compiler_params=pltpu.CompilerParams(vmem_limit_bytes=(28 + width) * MIB),
        cost_estimate=cost(tokens, tokens, tokens * tokens * QUERY_HEADS),
        name="last_shard_prefill",
    )(*state[:2], state[4], query, *keys, *values)


def start_maxima(*arrays, flops=5 * 10**9):
    def kernel(*refs):
        refs[-1][...] = jnp.full((8, HEAD_SIZE), MASKED, jnp.float32)

    return pl.pallas_call(
        kernel,
        in_specs=[VMEM] * len(arrays),
        out_specs=VMEM,
        out_shape=jax.ShapeDtypeStruct((8, HEAD_SIZE), jnp.float32),
        cost_estimate=pl.CostEstimate(flops=flops, bytes_accessed=0, transcendentals=0),
        compiler_params=pltpu.CompilerParams(vmem_limit_bytes=MIB),
        name="start_maxima",
    )(*arrays)


def paired(array, k):
    return lax.ppermute(array, "pd", [(g, g ^ k) for g in range(lax.axis_size("pd"))])


def body(
    prompt_query,
    prompt_key,
    prompt_value,
    prompt_lengths,
    decode_slot,
    decoded_query,
    decoded_key,
    decoded_value,
):
    plan = Ring(lax.axis_size("tp"))
    pd_size = lax.axis_size("pd")
    own = jnp.concatenate([decoded_query, decoded_key, decoded_value], axis=2).reshape(
        DECODE_ROWS, Q_WIDTH + 2 * KV_WIDTH
    )
    facts = facts_row(plan, prompt_lengths, decode_slot)
    prompt_key, decoded_query = lax.optimization_barrier((prompt_key, decoded_query))
    later_key, later_value = prompt_key, prompt_value
    chains = []
    for up, down in ((prompt_key, later_key), (prompt_value, later_value)):
        pieces = [up]
        for d in range(1, plan.size // 2 + 1):
            up = plan.step(up, True)
            down = plan.step(down, False) if 2 * d < plan.size else None
            pieces += [up, down]
        chains.append(pieces[: plan.size])
    keys, values = chains
    blocks = [own] + [paired(own, k) for k in range(1, pd_size)]
    maxima = start_maxima(keys[1], values[1], keys[2], values[2])

    state = call_first(plan, facts, maxima, prompt_query, blocks, keys[:-2], values[:-2])
    state = call_middle(plan, state, prompt_query, keys[-2], values[-2])
    outgoing = call_decode(plan, state, keys, values)
    arrived = [outgoing[:DECODE_STEPS]]
    for k in range(1, pd_size):
        arrived.append(paired(outgoing[k * DECODE_STEPS : (k + 1) * DECODE_STEPS], k))
    pre_out = call_prefill(plan, state, prompt_query, keys, values)

    from_block = state[8][:GROUP_REQUESTS, 0]
    dec_out = jnp.zeros((GROUP_REQUESTS, DECODE_STEPS, Q_WIDTH), jnp.bfloat16)
    for k in range(pd_size):
        dec_out = jnp.where((from_block == k)[:, None, None], arrived[k][None], dec_out)
    return (pre_out, dec_out)


def solution(mesh):
    placed = (
        P(("rep", "pd", "tp"), None),
        P(("rep", "pd", "tp"), None),
        P(("rep", "pd", "tp"), None),
        P("rep", None),
        P("rep"),
        P(("rep", "pd"), None, None),
        P(("rep", "pd"), None, None),
        P(("rep", "pd"), None, None),
    )
    return jax.shard_map(
        body,
        mesh=mesh,
        in_specs=placed,
        out_specs=(P(("rep", "pd", "tp"), None), P(("rep", "pd"), None, None)),
        check_vma=False,
    )
```

```python
import math

import jax
import jax.numpy as jnp
from jax import lax
from jax.experimental import pallas as pl
from jax.experimental.pallas import tpu as pltpu
from jax.sharding import PartitionSpec as P

QUERY_HEADS = 32
KEY_VALUE_HEADS = 4
HEAD_SIZE = 128
PAGE = 16
GROUP_REQUESTS = 4
DECODE_STEPS = 2
HEADS_PER_KV = QUERY_HEADS // KEY_VALUE_HEADS
KV_WIDTH = KEY_VALUE_HEADS * HEAD_SIZE
Q_WIDTH = QUERY_HEADS * HEAD_SIZE
Q_BLOCK = HEADS_PER_KV * HEAD_SIZE
DECODE_ROWS = GROUP_REQUESTS * DECODE_STEPS
PADDED_ROWS = 16
STACKED = HEADS_PER_KV * PADDED_ROWS
MIB = 1024 * 1024

MASKED = -1e30
LIMIT = 60.0
EXPONENT = math.log2(math.e) / math.sqrt(HEAD_SIZE)

VMEM = pl.BlockSpec(memory_space=pltpu.VMEM)
SMEM = pl.BlockSpec(memory_space=pltpu.SMEM)
ANY = pl.BlockSpec(memory_space=pl.ANY)
HBM = pl.BlockSpec(memory_space=pltpu.HBM)


class Ring:
    def __init__(self, size):
        self.size = size
        order = [0] + list(range(1, size, 2)) + [i for i in range(size - 1, 0, -1) if i % 2 == 0]
        self.pairs = [(order[i], order[(i + 1) % size]) for i in range(size)]
        self.offsets = [0]
        for d in range(1, size // 2 + 1):
            self.offsets += [-d, d]
        self.offsets = self.offsets[:size]

    def step(self, array, up):
        return lax.ppermute(array, "tp", self.pairs if up else [(b, a) for a, b in self.pairs])


def scores_of(queries, keys):
    return lax.dot_general(
        queries, keys, (((1,), (1,)), ((), ())), preferred_element_type=jnp.float32
    )


def product(left, right):
    return jnp.dot(left, right, preferred_element_type=jnp.float32)


def iota(shape, axis):
    return lax.broadcasted_iota(jnp.int32, shape, axis)


def span(start, size):
    if isinstance(start, int):
        return slice(start, start + size)
    return pl.ds(pl.multiple_of(start, size), size)


def with_ones(values):
    return jnp.concatenate([values, jnp.ones_like(values)], axis=1)


def page_position(offset, member, width):
    return (offset // PAGE * width + member) * PAGE + offset % PAGE


def key_positions(rows, sources, width):
    column = iota((1, len(sources) * rows), 1)
    part = column // rows
    source = jnp.zeros_like(column) + sources[0]
    for b in range(1, len(sources)):
        source = jnp.where(part == b, sources[b], source)
    return page_position(column - part * rows, source, width)


class Facts:
    def __init__(self, ref, width):
        self.width = width
        self.group, self.member = ref[0], ref[1]
        self.slots = [ref[2 + r] for r in range(GROUP_REQUESTS)]
        first = 2 + GROUP_REQUESTS
        self.ends = []
        total = jnp.int32(0)
        for r in range(GROUP_REQUESTS):
            total = total + ref[first + r] * PAGE
            self.ends.append(total)
        first += GROUP_REQUESTS
        self.source = [ref[first + s] for s in range(width)]
        first += width
        self.owner = [ref[first + p] for p in range(GROUP_REQUESTS)]


def facts_row(plan, lengths, slots):
    width, requests = plan.size, slots.shape[0]

    def kernel(lengths_ref, slots_ref, out_ref):
        group, member = lax.axis_index("pd"), lax.axis_index("tp")
        values = [group, member]
        values += [slots_ref[group * GROUP_REQUESTS + r] for r in range(GROUP_REQUESTS)]
        values += [lengths_ref[group, r] for r in range(GROUP_REQUESTS)]
        place = jnp.where(member % 2 == 1, (member + 1) // 2, width - member // 2)
        for offset in plan.offsets:
            before = (place + width + offset) % width
            up = 2 * before - 1
            values.append(jnp.where(before == 0, 0, jnp.where(before <= width // 2, up, 2 * (width - before))))
        for i, value in enumerate(values):
            out_ref[i] = value.astype(jnp.int32)
        for q in range(requests):
            place = slots_ref[q] - group * GROUP_REQUESTS

            @pl.when((place >= 0) & (place < GROUP_REQUESTS))
            def _():
                out_ref[len(values) + place] = group ^ (q // GROUP_REQUESTS)

    length = 2 + 2 * GROUP_REQUESTS + width + GROUP_REQUESTS
    return pl.pallas_call(
        kernel,
        in_specs=[SMEM, SMEM],
        out_specs=SMEM,
        out_shape=jax.ShapeDtypeStruct((length,), jnp.int32),
        cost_estimate=pl.CostEstimate(flops=5 * 10**9, bytes_accessed=0, transcendentals=0),
        name="facts",
    )(lengths, slots)


def causal_bias(start, rows, keys, sources, ends, member, width):
    qpos = page_position(start + iota((rows, 1), 0), member, width)
    low = jnp.zeros_like(qpos)
    for end in ends:
        low = jnp.where(qpos >= end, end, low)
    kpos = key_positions(keys, sources, width)
    return jnp.where((kpos >= low) & (kpos <= qpos), 0.0, MASKED)


def request_mask(ends, keys, sources, width):
    request = iota((STACKED, 1), 0) % PADDED_ROWS // DECODE_STEPS
    low = jnp.zeros_like(request)
    high = jnp.zeros_like(request) + ends[0]
    for r in range(1, GROUP_REQUESTS):
        low = jnp.where(request == r, ends[r - 1], low)
        high = jnp.where(request == r, ends[r], high)
    kpos = key_positions(keys, sources, width)
    return (kpos >= low) & (kpos < high)


def stacked_heads(ref, rows, first, count):
    return jnp.concatenate(
        [ref[rows, span(first + i * HEAD_SIZE, HEAD_SIZE)] for i in range(count)], axis=0
    )


def each_kv_head(width, step):
    if width <= 8:
        for h in range(KEY_VALUE_HEADS):
            step(h)
    else:
        lax.fori_loop(0, KEY_VALUE_HEADS, lambda h, c: (step(h), c)[1], 0)


def peak(exponents):
    return jnp.max(exponents.reshape(-1, 8, exponents.shape[-1]), axis=0)


def picked_rows(facts, pd_size, block_refs):
    row = iota((PADDED_ROWS, DECODE_ROWS), 0)
    column = iota((PADDED_ROWS, DECODE_ROWS), 1)
    total = None
    for k in range(pd_size):
        pick = column < 0
        for r in range(GROUP_REQUESTS):
            slot = facts.slots[r]
            first = jnp.where(facts.group ^ (slot // GROUP_REQUESTS) == k, slot % GROUP_REQUESTS * DECODE_STEPS, -DECODE_ROWS * 4)
            pick = pick | ((row // DECODE_STEPS == r) & (column == first + row - r * DECODE_STEPS))
        part = product(pick.astype(jnp.float32).astype(jnp.bfloat16), block_refs[k][...])
        total = part if total is None else total + part
    return total.astype(jnp.bfloat16)


def pick_matrix(facts):
    row = iota((PADDED_ROWS, PADDED_ROWS), 0)
    column = iota((PADDED_ROWS, PADDED_ROWS), 1)
    pick = column < 0
    for r in range(GROUP_REQUESTS):
        ahead = facts.group ^ (facts.slots[r] // GROUP_REQUESTS)
        pick = pick | (
            (column // DECODE_STEPS == r) & (row == ahead * DECODE_STEPS + column - r * DECODE_STEPS)
        )
    return pick.astype(jnp.float32).astype(jnp.bfloat16)


def fresh_mask():
    row = iota((STACKED, PADDED_ROWS), 0) % PADDED_ROWS
    column = iota((STACKED, PADDED_ROWS), 1)
    return (column // DECODE_STEPS == row // DECODE_STEPS) & (
        column % DECODE_STEPS <= row % DECODE_STEPS
    )


def bias_kernel(plan, facts, bias_ref):
    for s in range(plan.size):
        tokens = bias_ref.shape[1]
        bias_ref[s] = causal_bias(
            0, tokens, tokens, facts.source[s : s + 1], facts.ends, facts.member, plan.size
        )


def first_kernel(plan, facts_ref, maxima_ref, q_ref, *refs):
    width = plan.size
    k_refs, v_refs, refs = refs[: width - 2], refs[width - 2 : 2 * width - 4], refs[2 * width - 4 :]
    acc_ref, bias_ref, worst_ref = refs
    tokens = q_ref.shape[0]
    half = tokens // 2
    facts = Facts(facts_ref, width)
    sources = facts.source[:-2]
    bias_kernel(plan, facts, bias_ref)
    worst_ref[...] = maxima_ref[...]
    spans = ((0, half), (half, tokens))
    biases = [
        causal_bias(s, half, keys, sources, facts.ends, facts.member, width) for s, keys in spans
    ]
    together = max(1, min(HEADS_PER_KV, HEADS_PER_KV * 4 // width))

    def step(h):
        columns = span(h * HEAD_SIZE, HEAD_SIZE)
        first = h * Q_BLOCK
        for (start, keys), bias in zip(spans, biases):
            k_part = jnp.concatenate([ref[:keys, columns] for ref in k_refs], axis=0)
            v_part = with_ones(jnp.concatenate([ref[:keys, columns] for ref in v_refs], axis=0))
            for g in range(0, HEADS_PER_KV, together):
                queries = stacked_heads(
                    q_ref, slice(start, start + half), first + g * HEAD_SIZE, together
                )
                scores = scores_of(queries, k_part).reshape(together, half, bias.shape[1])
                exponents = (scores * EXPONENT + bias[None]).reshape(together * half, bias.shape[1])
                rows = slice(
                    start * HEADS_PER_KV + g * half, start * HEADS_PER_KV + (g + together) * half
                )
                worst_ref[...] = jnp.maximum(
                    worst_ref[...], jnp.max(peak(exponents), axis=1, keepdims=True)
                )
                acc_ref[h, rows, :] = product(jnp.exp2(exponents).astype(jnp.bfloat16), v_part)

    each_kv_head(width, step)


def middle_kernel(plan, acc_ref, bias_ref, worst_ref, q_ref, k_ref, v_ref, new_acc_ref, new_worst_ref):
    piece = plan.size - 2
    tokens = q_ref.shape[0]
    half = tokens // 2
    worst = worst_ref[...]
    for h in range(KEY_VALUE_HEADS):
        columns = slice(h * HEAD_SIZE, (h + 1) * HEAD_SIZE)
        keys, values = k_ref[:, columns], with_ones(v_ref[:, columns])
        for start in (0, half):
            bias = bias_ref[piece, start : start + half, :]
            queries = stacked_heads(q_ref, slice(start, start + half), h * Q_BLOCK, HEADS_PER_KV)
            scores = scores_of(queries, keys).reshape(HEADS_PER_KV, half, tokens)
            exponents = (scores * EXPONENT + bias[None]).reshape(HEADS_PER_KV * half, tokens)
            worst = jnp.maximum(worst, peak(exponents))
            rows = slice(start * HEADS_PER_KV, (start + half) * HEADS_PER_KV)
            new_acc_ref[h, rows, :] = acc_ref[h, rows, :] + product(
                jnp.exp2(exponents).astype(jnp.bfloat16), values
            )
    new_worst_ref[...] = worst


def first_decode_kernel(plan, pd_size, facts_ref, worst_ref, *refs):
    width = plan.size
    k_refs, v_refs, refs = refs[: width - 1], refs[width - 1 : 2 * width - 2], refs[2 * width - 2 :]
    block_refs, refs = refs[:pd_size], refs[pd_size:]
    acc_ref, bias_ref, new_worst_ref, queries_ref, fresh_ref, pick_ref, owner_ref = refs
    tokens = k_refs[0].shape[0]
    facts = Facts(facts_ref, width)
    pick_ref[...] = pick_matrix(facts)
    slot = iota((8, HEAD_SIZE), 0)
    owner = jnp.zeros_like(slot)
    for p in range(GROUP_REQUESTS):
        owner = jnp.where(slot == p, facts.owner[p], owner)
    owner_ref[...] = owner
    for s in range(width):
        bias_ref[s] = jnp.where(
            request_mask(facts.ends, tokens, facts.source[s : s + 1], width), 0.0, MASKED
        )
    rows = picked_rows(facts, pd_size, block_refs)
    queries_ref[...] = rows[:, :Q_WIDTH]
    fresh_ref[...] = rows[:, Q_WIDTH:]
    new_mask = fresh_mask()
    worst = worst_ref[...]
    for h in range(KEY_VALUE_HEADS):
        columns = slice(h * HEAD_SIZE, (h + 1) * HEAD_SIZE)
        queries = stacked_heads(rows, slice(None), h * Q_BLOCK, HEADS_PER_KV)
        new_columns = slice(Q_WIDTH + h * HEAD_SIZE, Q_WIDTH + (h + 1) * HEAD_SIZE)
        exponents = jnp.where(new_mask, scores_of(queries, rows[:, new_columns]) * EXPONENT, MASKED)
        worst = jnp.maximum(worst, jnp.max(peak(exponents), axis=1, keepdims=True))
        new_columns = slice(Q_WIDTH + KV_WIDTH + h * HEAD_SIZE, Q_WIDTH + KV_WIDTH + (h + 1) * HEAD_SIZE)
        acc = product(jnp.exp2(exponents).astype(jnp.bfloat16), with_ones(rows[:, new_columns]))
        for parts in parts_in(width - 1):
            k_part = jnp.concatenate([k_refs[s][:, columns] for s in parts], axis=0)
            v_part = jnp.concatenate([v_refs[s][:, columns] for s in parts], axis=0)
            bias = jnp.concatenate([bias_ref[s] for s in parts], axis=1)
            exponents = scores_of(queries, k_part) * EXPONENT + bias
            worst = jnp.maximum(worst, jnp.max(peak(exponents), axis=1, keepdims=True))
            acc += product(jnp.exp2(exponents).astype(jnp.bfloat16), with_ones(v_part))
        acc_ref[h] = acc
    new_worst_ref[...] = worst


def divided(acc):
    return (acc[:, :HEAD_SIZE] * pl.reciprocal(acc[:, HEAD_SIZE:], approx=True)).astype(jnp.bfloat16)


def fold(state, scores_list, values_list):
    top = None if state is None else state[0]
    for scores in scores_list:
        part = jnp.max(scores, axis=1, keepdims=True)
        top = part if top is None else jnp.maximum(top, part)
    acc = None
    for scores, values in zip(scores_list, values_list):
        weights = jnp.exp2((scores - top) * EXPONENT).astype(jnp.bfloat16)
        part = product(weights, with_ones(values))
        acc = part if acc is None else acc + part
    if state is not None:
        acc = acc + state[1] * jnp.exp2((state[0] - top) * EXPONENT)
    return top, acc


def parts_in(width):
    return [range(c, min(c + 4, width)) for c in range(0, width, 4)]


def out_of_range(worst, least):
    return (jnp.max(worst) > LIMIT) | (jnp.min(least) < 2.0**-LIMIT)


def decode_kernel(plan, acc_ref, bias_ref, worst_ref, queries_ref, fresh_ref, pick_ref, *refs):
    width = plan.size
    k_refs, v_refs, (out_ref,) = refs[:width], refs[width : 2 * width], refs[2 * width :]
    heads = range(KEY_VALUE_HEADS)
    columns = [slice(h * HEAD_SIZE, (h + 1) * HEAD_SIZE) for h in heads]

    def queries_of(h):
        return stacked_heads(queries_ref, slice(None), h * Q_BLOCK, HEADS_PER_KV)

    def send(acc):
        out = [divided(a) for a in acc]
        out = jnp.concatenate(
            [o[g * PADDED_ROWS : (g + 1) * PADDED_ROWS] for o in out for g in range(HEADS_PER_KV)], axis=1
        )
        out_ref[...] = product(pick_ref[...], out).astype(jnp.bfloat16)

    exponents = [
        scores_of(queries_of(h), k_refs[-1][:, columns[h]]) * EXPONENT + bias_ref[width - 1]
        for h in heads
    ]
    acc = [
        acc_ref[h] + product(jnp.exp2(exponents[h]).astype(jnp.bfloat16), with_ones(v_refs[-1][:, columns[h]]))
        for h in heads
    ]
    send(acc)
    worst, least = worst_ref[...], None
    for h in heads:
        worst = jnp.maximum(worst, peak(exponents[h]))
        part = jnp.min(acc[h][:, HEAD_SIZE:].reshape(-1, 8, HEAD_SIZE), axis=0)
        least = part if least is None else jnp.minimum(least, part)

    @pl.when(out_of_range(worst, least))
    def _():
        new_mask = fresh_mask()
        again = []
        for h in heads:
            queries = queries_of(h)
            scores = jnp.where(new_mask, scores_of(queries, fresh_ref[:, columns[h]]), MASKED)
            new_columns = slice(KV_WIDTH + h * HEAD_SIZE, KV_WIDTH + (h + 1) * HEAD_SIZE)
            state = fold(None, [scores], [fresh_ref[:, new_columns]])
            for parts in parts_in(width):
                k_part = jnp.concatenate([k_refs[s][:, columns[h]] for s in parts], axis=0)
                v_part = jnp.concatenate([v_refs[s][:, columns[h]] for s in parts], axis=0)
                bias = jnp.concatenate([bias_ref[s] for s in parts], axis=1)
                state = fold(state, [scores_of(queries, k_part) + bias], [v_part])
            again.append(state[1])
        send(again)


def prefill_kernel(plan, acc_ref, bias_ref, worst_ref, q_ref, *refs):
    width = plan.size
    k_refs, v_refs, refs = refs[:width], refs[width : 2 * width], refs[2 * width :]
    out_ref, done_ref, sem = refs
    tokens = q_ref.shape[0]
    half = tokens // 2
    def write(h, start, acc):
        out = divided(acc)
        for g in range(HEADS_PER_KV):
            done_ref[start : start + half, span(h * Q_BLOCK + g * HEAD_SIZE, HEAD_SIZE)] = out[
                g * half : (g + 1) * half
            ]

    def copy_out(h):
        part = pl.ds(h * Q_BLOCK, Q_BLOCK)
        return pltpu.make_async_copy(done_ref.at[:, part], out_ref.at[:, part], sem.at[h])

    biases = [bias_ref[width - 1, start : start + half, :] for start in (0, half)]
    worst, least = worst_ref[...], None
    for h in range(KEY_VALUE_HEADS):
        columns = slice(h * HEAD_SIZE, (h + 1) * HEAD_SIZE)
        keys, values = k_refs[-1][:, columns], with_ones(v_refs[-1][:, columns])
        for start, bias in zip((0, half), biases):
            queries = stacked_heads(q_ref, slice(start, start + half), h * Q_BLOCK, HEADS_PER_KV)
            scores = scores_of(queries, keys).reshape(HEADS_PER_KV, half, tokens)
            exponents = (scores * EXPONENT + bias[None]).reshape(HEADS_PER_KV * half, tokens)
            worst = jnp.maximum(worst, peak(exponents))
            rows = slice(start * HEADS_PER_KV, (start + half) * HEADS_PER_KV)
            acc = acc_ref[h, rows, :] + product(jnp.exp2(exponents).astype(jnp.bfloat16), values)
            part = jnp.min(acc[:, HEAD_SIZE:].reshape(-1, 8, HEAD_SIZE), axis=0)
            least = part if least is None else jnp.minimum(least, part)
            write(h, start, acc)
        copy_out(h).start()
    redo = out_of_range(worst, least)
    for h in range(KEY_VALUE_HEADS):
        copy_out(h).wait()

    @pl.when(redo)
    def _():
        def step(h, carry):
            columns = span(h * HEAD_SIZE, HEAD_SIZE)
            for start in (0, half):
                queries = stacked_heads(q_ref, slice(start, start + half), h * Q_BLOCK, HEADS_PER_KV)
                state = None
                for parts in parts_in(width):
                    k_part = jnp.concatenate([k_refs[s][:, columns] for s in parts], axis=0)
                    v_part = jnp.concatenate([v_refs[s][:, columns] for s in parts], axis=0)
                    bias = jnp.concatenate([bias_ref[s, start : start + half, :] for s in parts], axis=1)
                    scores = scores_of(queries, k_part).reshape(HEADS_PER_KV, half, bias.shape[1])
                    scores = (scores + bias[None]).reshape(HEADS_PER_KV * half, bias.shape[1])
                    state = fold(state, [scores], [v_part])
                write(h, start, state[1])
            return carry

        lax.fori_loop(0, KEY_VALUE_HEADS, step, 0)
        for h in range(KEY_VALUE_HEADS):
            copy_out(h).start()
        for h in range(KEY_VALUE_HEADS):
            copy_out(h).wait()


def cost(rows, keys, exps):
    return pl.CostEstimate(
        flops=32 * rows * keys * Q_WIDTH, bytes_accessed=4 * rows * Q_WIDTH, transcendentals=exps
    )


def call_first(plan, facts, maxima, query, keys, values):
    tokens, width = query.shape[0], plan.size
    rows = HEADS_PER_KV * tokens
    every = (width - 2) * tokens
    shapes = [
        jax.ShapeDtypeStruct((KEY_VALUE_HEADS, rows, 2 * HEAD_SIZE), jnp.float32),
        jax.ShapeDtypeStruct((width, tokens, tokens), jnp.float32),
        jax.ShapeDtypeStruct((8, HEAD_SIZE), jnp.float32),
    ]
    return pl.pallas_call(
        lambda *refs: first_kernel(plan, *refs),
        in_specs=[SMEM] + [VMEM] * (2 + 2 * (width - 2)),
        out_specs=[VMEM] * len(shapes),
        out_shape=shapes,
        compiler_params=pltpu.CompilerParams(vmem_limit_bytes=(28 + width) * MIB),
        cost_estimate=cost(tokens, every, tokens * every * QUERY_HEADS),
        name="first_shards",
    )(facts, maxima, query, *keys, *values)


def call_middle(plan, acc, bias, worst, query, key, value):
    tokens = query.shape[0]
    return pl.pallas_call(
        lambda *refs: middle_kernel(plan, *refs),
        in_specs=[VMEM] * 6,
        out_specs=[VMEM] * 2,
        out_shape=[jax.ShapeDtypeStruct(a.shape, a.dtype) for a in (acc, worst)],
        input_output_aliases={0: 0, 2: 1},
        compiler_params=pltpu.CompilerParams(vmem_limit_bytes=32 * MIB),
        cost_estimate=cost(1, 1, 1),
        name="middle_shard",
    )(acc, bias, worst, query, key, value)


def call_first_decode(plan, facts, worst, keys, values, blocks):
    tokens, width = keys[0].shape[0], plan.size
    f32, bf16 = jnp.float32, jnp.bfloat16
    shapes = [
        jax.ShapeDtypeStruct((KEY_VALUE_HEADS, STACKED, 2 * HEAD_SIZE), f32),
        jax.ShapeDtypeStruct((width, STACKED, tokens), f32),
        jax.ShapeDtypeStruct((8, HEAD_SIZE), f32),
        jax.ShapeDtypeStruct((PADDED_ROWS, Q_WIDTH), bf16),
        jax.ShapeDtypeStruct((PADDED_ROWS, 2 * KV_WIDTH), bf16),
        jax.ShapeDtypeStruct((PADDED_ROWS, PADDED_ROWS), bf16),
        jax.ShapeDtypeStruct((8, HEAD_SIZE), jnp.int32),
    ]
    return pl.pallas_call(
        lambda *refs: first_decode_kernel(plan, len(blocks), *refs),
        in_specs=[SMEM] + [VMEM] * (1 + len(blocks) + 2 * (width - 1)),
        out_specs=[VMEM] * len(shapes),
        out_shape=shapes,
        compiler_params=pltpu.CompilerParams(vmem_limit_bytes=(28 + width) * MIB),
        cost_estimate=cost(1, 1, 1),
        name="first_decode",
    )(facts, worst, *keys, *values, *blocks)


def call_decode(plan, state, keys, values):
    tokens, width = keys[0].shape[0], plan.size
    return pl.pallas_call(
        lambda *refs: decode_kernel(plan, *refs),
        in_specs=[VMEM] * (6 + 2 * width),
        out_specs=VMEM,
        out_shape=jax.ShapeDtypeStruct((PADDED_ROWS, Q_WIDTH), jnp.bfloat16),
        compiler_params=pltpu.CompilerParams(vmem_limit_bytes=(28 + width) * MIB),
        cost_estimate=cost(PADDED_ROWS, tokens, PADDED_ROWS * tokens * QUERY_HEADS),
        name="last_shard_decode",
    )(*state[:6], *keys, *values)


def call_prefill(plan, acc, bias, worst, query, keys, values):
    tokens, width = query.shape[0], plan.size
    return pl.pallas_call(
        lambda *refs: prefill_kernel(plan, *refs),
        in_specs=[VMEM] * (4 + 2 * width),
        out_specs=ANY,
        out_shape=jax.ShapeDtypeStruct((tokens, Q_WIDTH), jnp.bfloat16),
        scratch_shapes=[
            pltpu.VMEM((tokens, Q_WIDTH), jnp.bfloat16),
            pltpu.SemaphoreType.DMA((KEY_VALUE_HEADS,)),
        ],
        compiler_params=pltpu.CompilerParams(vmem_limit_bytes=(28 + width) * MIB),
        cost_estimate=cost(tokens, tokens, tokens * tokens * QUERY_HEADS),
        name="last_shard_prefill",
    )(acc, bias, worst, query, *keys, *values)


def start_maxima(*arrays, flops=5 * 10**9):
    def kernel(*refs):
        refs[-1][...] = jnp.full((8, HEAD_SIZE), MASKED, jnp.float32)

    return pl.pallas_call(
        kernel,
        in_specs=[VMEM] * len(arrays),
        out_specs=VMEM,
        out_shape=jax.ShapeDtypeStruct((8, HEAD_SIZE), jnp.float32),
        cost_estimate=pl.CostEstimate(flops=flops, bytes_accessed=0, transcendentals=0),
        compiler_params=pltpu.CompilerParams(vmem_limit_bytes=MIB),
        name="start_maxima",
    )(*arrays)


def paired(array, k):
    return lax.ppermute(array, "pd", [(g, g ^ k) for g in range(lax.axis_size("pd"))])


def body(
    prompt_query,
    prompt_key,
    prompt_value,
    prompt_lengths,
    decode_slot,
    decoded_query,
    decoded_key,
    decoded_value,
):
    plan = Ring(lax.axis_size("tp"))
    pd_size = lax.axis_size("pd")
    own = jnp.concatenate([decoded_query, decoded_key, decoded_value], axis=2).reshape(
        DECODE_ROWS, Q_WIDTH + 2 * KV_WIDTH
    )
    facts = facts_row(plan, prompt_lengths, decode_slot)
    prompt_key, decoded_query = lax.optimization_barrier((prompt_key, decoded_query))
    later_key, later_value, own, facts = lax.optimization_barrier((prompt_key, prompt_value, own, facts))
    chains = []
    for up, down in ((prompt_key, later_key), (prompt_value, later_value)):
        pieces = [up]
        for d in range(1, plan.size // 2 + 1):
            up = plan.step(up, True)
            down = plan.step(down, False) if 2 * d < plan.size else None
            pieces += [up, down]
        chains.append(pieces[: plan.size])
    keys, values = chains
    own, _ = lax.optimization_barrier((own, (keys[1], values[1])))
    blocks = [own] + [paired(own, k) for k in range(1, pd_size)]
    maxima = start_maxima(keys[1], values[1])

    acc, bias, worst = call_first(plan, facts, maxima, prompt_query, keys[:-2], values[:-2])
    acc, worst = call_middle(plan, acc, bias, worst, prompt_query, keys[-2], values[-2])
    state = call_first_decode(plan, facts, worst, keys[:-1], values[:-1], blocks)
    outgoing = call_decode(plan, state, keys, values)
    arrived = [outgoing[:DECODE_STEPS]]
    for k in range(1, pd_size):
        arrived.append(paired(outgoing[k * DECODE_STEPS : (k + 1) * DECODE_STEPS], k))
    pre_out = call_prefill(plan, acc, bias, state[2], prompt_query, keys, values)

    from_block = state[6][:GROUP_REQUESTS, 0]
    dec_out = jnp.zeros((GROUP_REQUESTS, DECODE_STEPS, Q_WIDTH), jnp.bfloat16)
    for k in range(pd_size):
        dec_out = jnp.where((from_block == k)[:, None, None], arrived[k][None], dec_out)
    return (pre_out, dec_out)


def solution(mesh):
    placed = (
        P(("rep", "pd", "tp"), None),
        P(("rep", "pd", "tp"), None),
        P(("rep", "pd", "tp"), None),
        P("rep", None),
        P("rep"),
        P(("rep", "pd"), None, None),
        P(("rep", "pd"), None, None),
        P(("rep", "pd"), None, None),
    )
    return jax.shard_map(
        body,
        mesh=mesh,
        in_specs=placed,
        out_specs=(P(("rep", "pd", "tp"), None), P(("rep", "pd"), None, None)),
        check_vma=False,
    )
```

```python
import math

import jax
import jax.numpy as jnp
from jax import lax
from jax.experimental import pallas as pl
from jax.experimental.pallas import tpu as pltpu
from jax.sharding import PartitionSpec as P

QUERY_HEADS = 32
KEY_VALUE_HEADS = 4
HEAD_SIZE = 128
PAGE = 16
GROUP_REQUESTS = 4
DECODE_STEPS = 2
HEADS_PER_KV = QUERY_HEADS // KEY_VALUE_HEADS
KV_WIDTH = KEY_VALUE_HEADS * HEAD_SIZE
Q_WIDTH = QUERY_HEADS * HEAD_SIZE
Q_BLOCK = HEADS_PER_KV * HEAD_SIZE
DECODE_ROWS = GROUP_REQUESTS * DECODE_STEPS
PADDED_ROWS = 16
STACKED = HEADS_PER_KV * PADDED_ROWS
MIB = 1024 * 1024

MASKED = -1e30
LIMIT = 60.0
EXPONENT = math.log2(math.e) / math.sqrt(HEAD_SIZE)

VMEM = pl.BlockSpec(memory_space=pltpu.VMEM)
SMEM = pl.BlockSpec(memory_space=pltpu.SMEM)
ANY = pl.BlockSpec(memory_space=pl.ANY)
HBM = pl.BlockSpec(memory_space=pltpu.HBM)


class Ring:
    def __init__(self, size):
        self.size = size
        order = [0] + list(range(1, size, 2)) + [i for i in range(size - 1, 0, -1) if i % 2 == 0]
        self.pairs = [(order[i], order[(i + 1) % size]) for i in range(size)]
        self.offsets = [0]
        for d in range(1, size // 2 + 1):
            self.offsets += [-d, d]
        self.offsets = self.offsets[:size]

    def step(self, array, up):
        return lax.ppermute(array, "tp", self.pairs if up else [(b, a) for a, b in self.pairs])


def scores_of(queries, keys):
    return lax.dot_general(
        queries, keys, (((1,), (1,)), ((), ())), preferred_element_type=jnp.float32
    )


def product(left, right):
    return jnp.dot(left, right, preferred_element_type=jnp.float32)


def iota(shape, axis):
    return lax.broadcasted_iota(jnp.int32, shape, axis)


def span(start, size):
    if isinstance(start, int):
        return slice(start, start + size)
    return pl.ds(pl.multiple_of(start, size), size)


def with_ones(values):
    return jnp.concatenate([values, jnp.ones_like(values)], axis=1)


def page_position(offset, member, width):
    return (offset // PAGE * width + member) * PAGE + offset % PAGE


def key_positions(rows, sources, width):
    column = iota((1, len(sources) * rows), 1)
    part = column // rows
    source = jnp.zeros_like(column) + sources[0]
    for b in range(1, len(sources)):
        source = jnp.where(part == b, sources[b], source)
    return page_position(column - part * rows, source, width)


class Facts:
    def __init__(self, ref, width):
        self.width = width
        self.group, self.member = ref[0], ref[1]
        self.slots = [ref[2 + r] for r in range(GROUP_REQUESTS)]
        first = 2 + GROUP_REQUESTS
        self.ends = []
        total = jnp.int32(0)
        for r in range(GROUP_REQUESTS):
            total = total + ref[first + r] * PAGE
            self.ends.append(total)
        first += GROUP_REQUESTS
        self.source = [ref[first + s] for s in range(width)]
        first += width
        self.owner = [ref[first + p] for p in range(GROUP_REQUESTS)]


def facts_row(plan, lengths, slots):
    width, requests = plan.size, slots.shape[0]

    def kernel(lengths_ref, slots_ref, out_ref):
        group, member = lax.axis_index("pd"), lax.axis_index("tp")
        values = [group, member]
        values += [slots_ref[group * GROUP_REQUESTS + r] for r in range(GROUP_REQUESTS)]
        values += [lengths_ref[group, r] for r in range(GROUP_REQUESTS)]
        place = jnp.where(member % 2 == 1, (member + 1) // 2, width - member // 2)
        for offset in plan.offsets:
            before = (place + width + offset) % width
            up = 2 * before - 1
            values.append(jnp.where(before == 0, 0, jnp.where(before <= width // 2, up, 2 * (width - before))))
        for i, value in enumerate(values):
            out_ref[i] = value.astype(jnp.int32)
        for q in range(requests):
            place = slots_ref[q] - group * GROUP_REQUESTS

            @pl.when((place >= 0) & (place < GROUP_REQUESTS))
            def _():
                out_ref[len(values) + place] = group ^ (q // GROUP_REQUESTS)

    length = 2 + 2 * GROUP_REQUESTS + width + GROUP_REQUESTS
    return pl.pallas_call(
        kernel,
        in_specs=[SMEM, SMEM],
        out_specs=SMEM,
        out_shape=jax.ShapeDtypeStruct((length,), jnp.int32),
        cost_estimate=pl.CostEstimate(flops=5 * 10**9, bytes_accessed=0, transcendentals=0),
        name="facts",
    )(lengths, slots)


def causal_bias(start, rows, keys, sources, ends, member, width):
    qpos = page_position(start + iota((rows, 1), 0), member, width)
    low = jnp.zeros_like(qpos)
    for end in ends:
        low = jnp.where(qpos >= end, end, low)
    kpos = key_positions(keys, sources, width)
    return jnp.where((kpos >= low) & (kpos <= qpos), 0.0, MASKED)


def request_mask(ends, keys, sources, width):
    request = iota((STACKED, 1), 0) % PADDED_ROWS // DECODE_STEPS
    low = jnp.zeros_like(request)
    high = jnp.zeros_like(request) + ends[0]
    for r in range(1, GROUP_REQUESTS):
        low = jnp.where(request == r, ends[r - 1], low)
        high = jnp.where(request == r, ends[r], high)
    kpos = key_positions(keys, sources, width)
    return (kpos >= low) & (kpos < high)


def stacked_heads(ref, rows, first, count):
    return jnp.concatenate(
        [ref[rows, span(first + i * HEAD_SIZE, HEAD_SIZE)] for i in range(count)], axis=0
    )


def each_kv_head(width, step):
    if width <= 8:
        for h in range(KEY_VALUE_HEADS):
            step(h)
    else:
        lax.fori_loop(0, KEY_VALUE_HEADS, lambda h, c: (step(h), c)[1], 0)


def peak(exponents):
    return jnp.max(exponents.reshape(-1, 8, exponents.shape[-1]), axis=0)


def picked_rows(facts, pd_size, block_refs):
    row = iota((PADDED_ROWS, DECODE_ROWS), 0)
    column = iota((PADDED_ROWS, DECODE_ROWS), 1)
    total = None
    for k in range(pd_size):
        pick = column < 0
        for r in range(GROUP_REQUESTS):
            slot = facts.slots[r]
            first = jnp.where(facts.group ^ (slot // GROUP_REQUESTS) == k, slot % GROUP_REQUESTS * DECODE_STEPS, -DECODE_ROWS * 4)
            pick = pick | ((row // DECODE_STEPS == r) & (column == first + row - r * DECODE_STEPS))
        part = product(pick.astype(jnp.float32).astype(jnp.bfloat16), block_refs[k][...])
        total = part if total is None else total + part
    return total.astype(jnp.bfloat16)


def pick_matrix(facts):
    row = iota((PADDED_ROWS, PADDED_ROWS), 0)
    column = iota((PADDED_ROWS, PADDED_ROWS), 1)
    pick = column < 0
    for r in range(GROUP_REQUESTS):
        ahead = facts.group ^ (facts.slots[r] // GROUP_REQUESTS)
        pick = pick | (
            (column // DECODE_STEPS == r) & (row == ahead * DECODE_STEPS + column - r * DECODE_STEPS)
        )
    return pick.astype(jnp.float32).astype(jnp.bfloat16)


def fresh_mask():
    row = iota((STACKED, PADDED_ROWS), 0) % PADDED_ROWS
    column = iota((STACKED, PADDED_ROWS), 1)
    return (column // DECODE_STEPS == row // DECODE_STEPS) & (
        column % DECODE_STEPS <= row % DECODE_STEPS
    )


def first_kernel(plan, pd_size, facts_ref, maxima_ref, q_ref, *refs):
    width = plan.size
    k_refs, v_refs, refs = refs[:1], refs[1:2], refs[2:]
    block_refs, refs = refs[:pd_size], refs[pd_size:]
    acc_ref, bias_ref, dec_acc_ref, dec_bias_ref, worst_ref, queries_ref, fresh_ref, pick_ref, owner_ref = refs
    tokens = q_ref.shape[0]
    half = tokens // 2
    facts = Facts(facts_ref, width)
    sources = facts.source[:1]
    pick_ref[...] = pick_matrix(facts)
    slot = iota((8, HEAD_SIZE), 0)
    owner = jnp.zeros_like(slot)
    for p in range(GROUP_REQUESTS):
        owner = jnp.where(slot == p, facts.owner[p], owner)
    owner_ref[...] = owner
    for s in range(width):
        bias_ref[s] = causal_bias(0, tokens, tokens, facts.source[s : s + 1], facts.ends, facts.member, width)
        dec_bias_ref[s] = jnp.where(
            request_mask(facts.ends, tokens, facts.source[s : s + 1], width), 0.0, MASKED
        )
    rows = picked_rows(facts, pd_size, block_refs)
    queries_ref[...] = rows[:, :Q_WIDTH]
    fresh_ref[...] = rows[:, Q_WIDTH:]
    worst_ref[...] = maxima_ref[...]
    new_mask = fresh_mask()
    mask = request_mask(facts.ends, tokens, sources, width)
    spans = ((0, half), (half, tokens))
    biases = [
        causal_bias(s, half, keys, sources, facts.ends, facts.member, width) for s, keys in spans
    ]
    together = max(1, min(HEADS_PER_KV, HEADS_PER_KV * 4 // width))

    def weigh(exponents):
        top = jnp.max(peak(exponents), axis=1, keepdims=True)
        worst_ref[...] = jnp.maximum(worst_ref[...], top)
        return jnp.exp2(exponents).astype(jnp.bfloat16)

    def step(h):
        columns = span(h * HEAD_SIZE, HEAD_SIZE)
        first = h * Q_BLOCK
        queries = stacked_heads(queries_ref, slice(None), first, HEADS_PER_KV)
        k_all = jnp.concatenate([ref[:, columns] for ref in k_refs], axis=0)
        v_all = with_ones(jnp.concatenate([ref[:, columns] for ref in v_refs], axis=0))
        new_scores = scores_of(queries, fresh_ref[:, columns]) * EXPONENT
        new_weights = weigh(jnp.where(new_mask, new_scores, MASKED))
        new_values = fresh_ref[:, span(KV_WIDTH + h * HEAD_SIZE, HEAD_SIZE)]
        weights = weigh(jnp.where(mask, scores_of(queries, k_all) * EXPONENT, MASKED))
        dec_acc_ref[h] = product(weights, v_all) + product(new_weights, with_ones(new_values))
        for (start, keys), bias in zip(spans, biases):
            if keys < tokens:
                k_part = jnp.concatenate([ref[:keys, columns] for ref in k_refs], axis=0)
                v_part = with_ones(jnp.concatenate([ref[:keys, columns] for ref in v_refs], axis=0))
            else:
                k_part, v_part = k_all, v_all
            for g in range(0, HEADS_PER_KV, together):
                queries = stacked_heads(
                    q_ref, slice(start, start + half), first + g * HEAD_SIZE, together
                )
                scores = scores_of(queries, k_part).reshape(together, half, bias.shape[1])
                exponents = (scores * EXPONENT + bias[None]).reshape(together * half, bias.shape[1])
                rows = slice(
                    start * HEADS_PER_KV + g * half, start * HEADS_PER_KV + (g + together) * half
                )
                acc_ref[h, rows, :] = product(weigh(exponents), v_part)

    each_kv_head(width, step)


def middle_kernel(plan, acc_ref, bias_ref, dec_acc_ref, dec_bias_ref, worst_ref, queries_ref, q_ref, *refs):
    count = plan.size - 2
    k_refs, v_refs, refs = refs[:count], refs[count : 2 * count], refs[2 * count :]
    new_acc_ref, new_dec_acc_ref, new_worst_ref = refs
    tokens = q_ref.shape[0]
    half = tokens // 2
    worst = worst_ref[...]
    for h in range(KEY_VALUE_HEADS):
        columns = slice(h * HEAD_SIZE, (h + 1) * HEAD_SIZE)
        for parts in parts_in(count):
            keys = jnp.concatenate([k_refs[s][:, columns] for s in parts], axis=0)
            values = with_ones(jnp.concatenate([v_refs[s][:, columns] for s in parts], axis=0))
            old_acc_ref, old_dec_acc_ref = acc_ref, dec_acc_ref
            if parts[0] > 0:
                old_acc_ref, old_dec_acc_ref = new_acc_ref, new_dec_acc_ref
            queries = stacked_heads(queries_ref, slice(None), h * Q_BLOCK, HEADS_PER_KV)
            bias = jnp.concatenate([dec_bias_ref[s + 1] for s in parts], axis=1)
            exponents = scores_of(queries, keys) * EXPONENT + bias
            worst = jnp.maximum(worst, jnp.max(peak(exponents), axis=1, keepdims=True))
            new_dec_acc_ref[h] = old_dec_acc_ref[h] + product(
                jnp.exp2(exponents).astype(jnp.bfloat16), values
            )
            for start in (0, half):
                bias = jnp.concatenate([bias_ref[s + 1, start : start + half, :] for s in parts], axis=1)
                queries = stacked_heads(q_ref, slice(start, start + half), h * Q_BLOCK, HEADS_PER_KV)
                scores = scores_of(queries, keys).reshape(HEADS_PER_KV, half, bias.shape[1])
                exponents = (scores * EXPONENT + bias[None]).reshape(HEADS_PER_KV * half, bias.shape[1])
                worst = jnp.maximum(worst, jnp.max(peak(exponents), axis=1, keepdims=True))
                rows = slice(start * HEADS_PER_KV, (start + half) * HEADS_PER_KV)
                new_acc_ref[h, rows, :] = old_acc_ref[h, rows, :] + product(
                    jnp.exp2(exponents).astype(jnp.bfloat16), values
                )
    new_worst_ref[...] = worst


def divided(acc):
    return (acc[:, :HEAD_SIZE] * pl.reciprocal(acc[:, HEAD_SIZE:], approx=True)).astype(jnp.bfloat16)


def fold(state, scores_list, values_list):
    top = None if state is None else state[0]
    for scores in scores_list:
        part = jnp.max(scores, axis=1, keepdims=True)
        top = part if top is None else jnp.maximum(top, part)
    acc = None
    for scores, values in zip(scores_list, values_list):
        weights = jnp.exp2((scores - top) * EXPONENT).astype(jnp.bfloat16)
        part = product(weights, with_ones(values))
        acc = part if acc is None else acc + part
    if state is not None:
        acc = acc + state[1] * jnp.exp2((state[0] - top) * EXPONENT)
    return top, acc


def parts_in(width):
    return [range(c, min(c + 4, width)) for c in range(0, width, 4)]


def out_of_range(worst, least):
    return (jnp.max(worst) > LIMIT) | (jnp.min(least) < 2.0**-LIMIT)


def decode_kernel(plan, acc_ref, bias_ref, worst_ref, queries_ref, fresh_ref, pick_ref, *refs):
    width = plan.size
    k_refs, v_refs, (out_ref,) = refs[:width], refs[width : 2 * width], refs[2 * width :]
    heads = range(KEY_VALUE_HEADS)
    columns = [slice(h * HEAD_SIZE, (h + 1) * HEAD_SIZE) for h in heads]

    def queries_of(h):
        return stacked_heads(queries_ref, slice(None), h * Q_BLOCK, HEADS_PER_KV)

    def send(acc):
        out = [divided(a) for a in acc]
        out = jnp.concatenate(
            [o[g * PADDED_ROWS : (g + 1) * PADDED_ROWS] for o in out for g in range(HEADS_PER_KV)], axis=1
        )
        out_ref[...] = product(pick_ref[...], out).astype(jnp.bfloat16)

    exponents = [
        scores_of(queries_of(h), k_refs[-1][:, columns[h]]) * EXPONENT + bias_ref[width - 1]
        for h in heads
    ]
    acc = [
        acc_ref[h] + product(jnp.exp2(exponents[h]).astype(jnp.bfloat16), with_ones(v_refs[-1][:, columns[h]]))
        for h in heads
    ]
    send(acc)
    worst, least = worst_ref[...], None
    for h in heads:
        worst = jnp.maximum(worst, peak(exponents[h]))
        part = jnp.min(acc[h][:, HEAD_SIZE:].reshape(-1, 8, HEAD_SIZE), axis=0)
        least = part if least is None else jnp.minimum(least, part)

    @pl.when(out_of_range(worst, least))
    def _():
        new_mask = fresh_mask()
        again = []
        for h in heads:
            queries = queries_of(h)
            scores = jnp.where(new_mask, scores_of(queries, fresh_ref[:, columns[h]]), MASKED)
            new_columns = slice(KV_WIDTH + h * HEAD_SIZE, KV_WIDTH + (h + 1) * HEAD_SIZE)
            state = fold(None, [scores], [fresh_ref[:, new_columns]])
            for parts in parts_in(width):
                k_part = jnp.concatenate([k_refs[s][:, columns[h]] for s in parts], axis=0)
                v_part = jnp.concatenate([v_refs[s][:, columns[h]] for s in parts], axis=0)
                bias = jnp.concatenate([bias_ref[s] for s in parts], axis=1)
                state = fold(state, [scores_of(queries, k_part) + bias], [v_part])
            again.append(state[1])
        send(again)


def prefill_kernel(plan, acc_ref, bias_ref, worst_ref, q_ref, *refs):
    width = plan.size
    k_refs, v_refs, refs = refs[:width], refs[width : 2 * width], refs[2 * width :]
    out_ref, done_ref, sem = refs
    tokens = q_ref.shape[0]
    half = tokens // 2
    def write(h, start, acc):
        out = divided(acc)
        for g in range(HEADS_PER_KV):
            done_ref[start : start + half, span(h * Q_BLOCK + g * HEAD_SIZE, HEAD_SIZE)] = out[
                g * half : (g + 1) * half
            ]

    def copy_out(h):
        part = pl.ds(h * Q_BLOCK, Q_BLOCK)
        return pltpu.make_async_copy(done_ref.at[:, part], out_ref.at[:, part], sem.at[h])

    biases = [bias_ref[width - 1, start : start + half, :] for start in (0, half)]
    worst, least = worst_ref[...], None
    for h in range(KEY_VALUE_HEADS):
        columns = slice(h * HEAD_SIZE, (h + 1) * HEAD_SIZE)
        keys, values = k_refs[-1][:, columns], with_ones(v_refs[-1][:, columns])
        for start, bias in zip((0, half), biases):
            queries = stacked_heads(q_ref, slice(start, start + half), h * Q_BLOCK, HEADS_PER_KV)
            scores = scores_of(queries, keys).reshape(HEADS_PER_KV, half, tokens)
            exponents = (scores * EXPONENT + bias[None]).reshape(HEADS_PER_KV * half, tokens)
            worst = jnp.maximum(worst, peak(exponents))
            rows = slice(start * HEADS_PER_KV, (start + half) * HEADS_PER_KV)
            acc = acc_ref[h, rows, :] + product(jnp.exp2(exponents).astype(jnp.bfloat16), values)
            part = jnp.min(acc[:, HEAD_SIZE:].reshape(-1, 8, HEAD_SIZE), axis=0)
            least = part if least is None else jnp.minimum(least, part)
            write(h, start, acc)
        copy_out(h).start()
    redo = out_of_range(worst, least)
    for h in range(KEY_VALUE_HEADS):
        copy_out(h).wait()

    @pl.when(redo)
    def _():
        def step(h, carry):
            columns = span(h * HEAD_SIZE, HEAD_SIZE)
            for start in (0, half):
                queries = stacked_heads(q_ref, slice(start, start + half), h * Q_BLOCK, HEADS_PER_KV)
                state = None
                for parts in parts_in(width):
                    k_part = jnp.concatenate([k_refs[s][:, columns] for s in parts], axis=0)
                    v_part = jnp.concatenate([v_refs[s][:, columns] for s in parts], axis=0)
                    bias = jnp.concatenate([bias_ref[s, start : start + half, :] for s in parts], axis=1)
                    scores = scores_of(queries, k_part).reshape(HEADS_PER_KV, half, bias.shape[1])
                    scores = (scores + bias[None]).reshape(HEADS_PER_KV * half, bias.shape[1])
                    state = fold(state, [scores], [v_part])
                write(h, start, state[1])
            return carry

        lax.fori_loop(0, KEY_VALUE_HEADS, step, 0)
        for h in range(KEY_VALUE_HEADS):
            copy_out(h).start()
        for h in range(KEY_VALUE_HEADS):
            copy_out(h).wait()


def cost(rows, keys, exps):
    return pl.CostEstimate(
        flops=32 * rows * keys * Q_WIDTH, bytes_accessed=4 * rows * Q_WIDTH, transcendentals=exps
    )


def call_first(plan, facts, maxima, query, blocks, keys, values):
    tokens, width = query.shape[0], plan.size
    rows = HEADS_PER_KV * tokens
    f32, bf16 = jnp.float32, jnp.bfloat16
    every = tokens
    shapes = [
        jax.ShapeDtypeStruct((KEY_VALUE_HEADS, rows, 2 * HEAD_SIZE), f32),
        jax.ShapeDtypeStruct((width, tokens, tokens), f32),
        jax.ShapeDtypeStruct((KEY_VALUE_HEADS, STACKED, 2 * HEAD_SIZE), f32),
        jax.ShapeDtypeStruct((width, STACKED, tokens), f32),
        jax.ShapeDtypeStruct((8, HEAD_SIZE), f32),
        jax.ShapeDtypeStruct((PADDED_ROWS, Q_WIDTH), bf16),
        jax.ShapeDtypeStruct((PADDED_ROWS, 2 * KV_WIDTH), bf16),
        jax.ShapeDtypeStruct((PADDED_ROWS, PADDED_ROWS), bf16),
        jax.ShapeDtypeStruct((8, HEAD_SIZE), jnp.int32),
    ]
    return pl.pallas_call(
        lambda *refs: first_kernel(plan, len(blocks), *refs),
        in_specs=[SMEM] + [VMEM] * (4 + len(blocks)),
        out_specs=[VMEM] * len(shapes),
        out_shape=shapes,
        compiler_params=pltpu.CompilerParams(vmem_limit_bytes=(28 + width) * MIB),
        cost_estimate=cost(tokens, every, tokens * every * QUERY_HEADS),
        name="first_shards",
    )(facts, maxima, query, *keys, *values, *blocks)


def call_middle(plan, state, query, keys, values):
    acc, bias, dec_acc, dec_bias, worst, queries = state[:6]
    tokens = query.shape[0]
    new_acc, new_dec_acc, new_worst = pl.pallas_call(
        lambda *refs: middle_kernel(plan, *refs),
        in_specs=[VMEM] * (7 + 2 * len(keys)),
        out_specs=[VMEM] * 3,
        out_shape=[jax.ShapeDtypeStruct(a.shape, a.dtype) for a in (acc, dec_acc, worst)],
        input_output_aliases={0: 0, 2: 1, 4: 2},
        compiler_params=pltpu.CompilerParams(vmem_limit_bytes=32 * MIB),
        cost_estimate=cost(tokens, tokens, tokens * tokens * QUERY_HEADS),
        name="middle_shard",
    )(acc, bias, dec_acc, dec_bias, worst, queries, query, *keys, *values)
    return [new_acc, bias, new_dec_acc, dec_bias, new_worst] + list(state[5:])


def call_decode(plan, state, keys, values):
    tokens, width = keys[0].shape[0], plan.size
    return pl.pallas_call(
        lambda *refs: decode_kernel(plan, *refs),
        in_specs=[VMEM] * (6 + 2 * width),
        out_specs=VMEM,
        out_shape=jax.ShapeDtypeStruct((PADDED_ROWS, Q_WIDTH), jnp.bfloat16),
        compiler_params=pltpu.CompilerParams(vmem_limit_bytes=(28 + width) * MIB),
        cost_estimate=cost(PADDED_ROWS, tokens, PADDED_ROWS * tokens * QUERY_HEADS),
        name="last_shard_decode",
    )(*state[2:8], *keys, *values)


def call_prefill(plan, state, query, keys, values):
    tokens, width = query.shape[0], plan.size
    return pl.pallas_call(
        lambda *refs: prefill_kernel(plan, *refs),
        in_specs=[VMEM] * (4 + 2 * width),
        out_specs=ANY,
        out_shape=jax.ShapeDtypeStruct((tokens, Q_WIDTH), jnp.bfloat16),
        scratch_shapes=[
            pltpu.VMEM((tokens, Q_WIDTH), jnp.bfloat16),
            pltpu.SemaphoreType.DMA((KEY_VALUE_HEADS,)),
        ],
        compiler_params=pltpu.CompilerParams(vmem_limit_bytes=(28 + width) * MIB),
        cost_estimate=cost(tokens, tokens, tokens * tokens * QUERY_HEADS),
        name="last_shard_prefill",
    )(*state[:2], state[4], query, *keys, *values)


def start_maxima(*arrays, flops=5 * 10**9):
    def kernel(*refs):
        refs[-1][...] = jnp.full((8, HEAD_SIZE), MASKED, jnp.float32)

    return pl.pallas_call(
        kernel,
        in_specs=[VMEM] * len(arrays),
        out_specs=VMEM,
        out_shape=jax.ShapeDtypeStruct((8, HEAD_SIZE), jnp.float32),
        cost_estimate=pl.CostEstimate(flops=flops, bytes_accessed=0, transcendentals=0),
        compiler_params=pltpu.CompilerParams(vmem_limit_bytes=MIB),
        name="start_maxima",
    )(*arrays)


def paired(array, k):
    return lax.ppermute(array, "pd", [(g, g ^ k) for g in range(lax.axis_size("pd"))])


def body(
    prompt_query,
    prompt_key,
    prompt_value,
    prompt_lengths,
    decode_slot,
    decoded_query,
    decoded_key,
    decoded_value,
):
    plan = Ring(lax.axis_size("tp"))
    pd_size = lax.axis_size("pd")
    own = jnp.concatenate([decoded_query, decoded_key, decoded_value], axis=2).reshape(
        DECODE_ROWS, Q_WIDTH + 2 * KV_WIDTH
    )
    facts = facts_row(plan, prompt_lengths, decode_slot)
    prompt_key, decoded_query = lax.optimization_barrier((prompt_key, decoded_query))
    later_key, later_value, own, facts = lax.optimization_barrier((prompt_key, prompt_value, own, facts))
    chains = []
    for first, later, way in ((prompt_key, later_key, True), (prompt_value, later_value, False)):
        pieces = [first]
        for d in range(1, plan.size // 2 + 1):
            first = plan.step(first, way)
            later = plan.step(later, not way) if 2 * d < plan.size else None
            pieces += [first, later] if way else [later, first]
        chains.append(pieces[: plan.size - 1] + [first])
    keys, values = chains
    blocks = [own] + [paired(own, k) for k in range(1, pd_size)]
    maxima = start_maxima(keys[1], values[2])

    state = call_first(plan, facts, maxima, prompt_query, blocks, keys[:1], values[:1])
    state = call_middle(plan, state, prompt_query, keys[1:-1], values[1:-1])
    outgoing = call_decode(plan, state, keys, values)
    arrived = [outgoing[:DECODE_STEPS]]
    for k in range(1, pd_size):
        arrived.append(paired(outgoing[k * DECODE_STEPS : (k + 1) * DECODE_STEPS], k))
    pre_out = call_prefill(plan, state, prompt_query, keys, values)

    from_block = state[8][:GROUP_REQUESTS, 0]
    dec_out = jnp.zeros((GROUP_REQUESTS, DECODE_STEPS, Q_WIDTH), jnp.bfloat16)
    for k in range(pd_size):
        dec_out = jnp.where((from_block == k)[:, None, None], arrived[k][None], dec_out)
    return (pre_out, dec_out)


def solution(mesh):
    placed = (
        P(("rep", "pd", "tp"), None),
        P(("rep", "pd", "tp"), None),
        P(("rep", "pd", "tp"), None),
        P("rep", None),
        P("rep"),
        P(("rep", "pd"), None, None),
        P(("rep", "pd"), None, None),
        P(("rep", "pd"), None, None),
    )
    return jax.shard_map(
        body,
        mesh=mesh,
        in_specs=placed,
        out_specs=(P(("rep", "pd", "tp"), None), P(("rep", "pd"), None, None)),
        check_vma=False,
    )
```

```python
import math

import jax
import jax.numpy as jnp
from jax import lax
from jax.experimental import pallas as pl
from jax.experimental.pallas import tpu as pltpu
from jax.sharding import PartitionSpec as P

QUERY_HEADS = 32
KEY_VALUE_HEADS = 4
HEAD_SIZE = 128
PAGE = 16
GROUP_REQUESTS = 4
DECODE_STEPS = 2
HEADS_PER_KV = QUERY_HEADS // KEY_VALUE_HEADS
KV_WIDTH = KEY_VALUE_HEADS * HEAD_SIZE
Q_WIDTH = QUERY_HEADS * HEAD_SIZE
Q_BLOCK = HEADS_PER_KV * HEAD_SIZE
DECODE_ROWS = GROUP_REQUESTS * DECODE_STEPS
PADDED_ROWS = 16
STACKED = HEADS_PER_KV * PADDED_ROWS
MIB = 1024 * 1024

MASKED = -1e30
LIMIT = 60.0
EXPONENT = math.log2(math.e) / math.sqrt(HEAD_SIZE)

VMEM = pl.BlockSpec(memory_space=pltpu.VMEM)
SMEM = pl.BlockSpec(memory_space=pltpu.SMEM)
ANY = pl.BlockSpec(memory_space=pl.ANY)
HBM = pl.BlockSpec(memory_space=pltpu.HBM)


class Ring:
    def __init__(self, size):
        self.size = size
        order = [0] + list(range(1, size, 2)) + [i for i in range(size - 1, 0, -1) if i % 2 == 0]
        self.pairs = [(order[i], order[(i + 1) % size]) for i in range(size)]
        self.offsets = [0]
        for d in range(1, size // 2 + 1):
            self.offsets += [-d, d]
        self.offsets = self.offsets[:size]

    def step(self, array, up):
        return lax.ppermute(array, "tp", self.pairs if up else [(b, a) for a, b in self.pairs])


def scores_of(queries, keys):
    return lax.dot_general(
        queries, keys, (((1,), (1,)), ((), ())), preferred_element_type=jnp.float32
    )


def product(left, right):
    return jnp.dot(left, right, preferred_element_type=jnp.float32)


def iota(shape, axis):
    return lax.broadcasted_iota(jnp.int32, shape, axis)


def span(start, size):
    if isinstance(start, int):
        return slice(start, start + size)
    return pl.ds(pl.multiple_of(start, size), size)


def with_ones(values):
    return jnp.concatenate([values, jnp.ones_like(values)], axis=1)


def page_position(offset, member, width):
    return (offset // PAGE * width + member) * PAGE + offset % PAGE


def key_positions(rows, sources, width):
    column = iota((1, len(sources) * rows), 1)
    part = column // rows
    source = jnp.zeros_like(column) + sources[0]
    for b in range(1, len(sources)):
        source = jnp.where(part == b, sources[b], source)
    return page_position(column - part * rows, source, width)


class Facts:
    def __init__(self, ref, width):
        self.width = width
        self.group, self.member = ref[0], ref[1]
        self.slots = [ref[2 + r] for r in range(GROUP_REQUESTS)]
        first = 2 + GROUP_REQUESTS
        self.ends = []
        total = jnp.int32(0)
        for r in range(GROUP_REQUESTS):
            total = total + ref[first + r] * PAGE
            self.ends.append(total)
        first += GROUP_REQUESTS
        self.source = [ref[first + s] for s in range(width)]
        first += width
        self.owner = [ref[first + p] for p in range(GROUP_REQUESTS)]


def facts_row(plan, lengths, slots):
    width, requests = plan.size, slots.shape[0]

    def kernel(lengths_ref, slots_ref, out_ref):
        group, member = lax.axis_index("pd"), lax.axis_index("tp")
        values = [group, member]
        values += [slots_ref[group * GROUP_REQUESTS + r] for r in range(GROUP_REQUESTS)]
        values += [lengths_ref[group, r] for r in range(GROUP_REQUESTS)]
        place = jnp.where(member % 2 == 1, (member + 1) // 2, width - member // 2)
        for offset in plan.offsets:
            before = (place + width + offset) % width
            up = 2 * before - 1
            values.append(jnp.where(before == 0, 0, jnp.where(before <= width // 2, up, 2 * (width - before))))
        for i, value in enumerate(values):
            out_ref[i] = value.astype(jnp.int32)
        for q in range(requests):
            place = slots_ref[q] - group * GROUP_REQUESTS

            @pl.when((place >= 0) & (place < GROUP_REQUESTS))
            def _():
                out_ref[len(values) + place] = group ^ (q // GROUP_REQUESTS)

    length = 2 + 2 * GROUP_REQUESTS + width + GROUP_REQUESTS
    return pl.pallas_call(
        kernel,
        in_specs=[SMEM, SMEM],
        out_specs=SMEM,
        out_shape=jax.ShapeDtypeStruct((length,), jnp.int32),
        cost_estimate=pl.CostEstimate(flops=5 * 10**9, bytes_accessed=0, transcendentals=0),
        name="facts",
    )(lengths, slots)


def causal_bias(start, rows, keys, sources, ends, member, width):
    qpos = page_position(start + iota((rows, 1), 0), member, width)
    low = jnp.zeros_like(qpos)
    for end in ends:
        low = jnp.where(qpos >= end, end, low)
    kpos = key_positions(keys, sources, width)
    return jnp.where((kpos >= low) & (kpos <= qpos), 0.0, MASKED)


def request_mask(ends, keys, sources, width):
    request = iota((STACKED, 1), 0) % PADDED_ROWS // DECODE_STEPS
    low = jnp.zeros_like(request)
    high = jnp.zeros_like(request) + ends[0]
    for r in range(1, GROUP_REQUESTS):
        low = jnp.where(request == r, ends[r - 1], low)
        high = jnp.where(request == r, ends[r], high)
    kpos = key_positions(keys, sources, width)
    return (kpos >= low) & (kpos < high)


def stacked_heads(ref, rows, first, count):
    return jnp.concatenate(
        [ref[rows, span(first + i * HEAD_SIZE, HEAD_SIZE)] for i in range(count)], axis=0
    )


def each_kv_head(width, step):
    if width <= 8:
        for h in range(KEY_VALUE_HEADS):
            step(h)
    else:
        lax.fori_loop(0, KEY_VALUE_HEADS, lambda h, c: (step(h), c)[1], 0)


def peak(exponents):
    return jnp.max(exponents.reshape(-1, 8, exponents.shape[-1]), axis=0)


def picked_rows(facts, pd_size, block_refs):
    row = iota((PADDED_ROWS, DECODE_ROWS), 0)
    column = iota((PADDED_ROWS, DECODE_ROWS), 1)
    total = None
    for k in range(pd_size):
        pick = column < 0
        for r in range(GROUP_REQUESTS):
            slot = facts.slots[r]
            first = jnp.where(facts.group ^ (slot // GROUP_REQUESTS) == k, slot % GROUP_REQUESTS * DECODE_STEPS, -DECODE_ROWS * 4)
            pick = pick | ((row // DECODE_STEPS == r) & (column == first + row - r * DECODE_STEPS))
        part = product(pick.astype(jnp.float32).astype(jnp.bfloat16), block_refs[k][...])
        total = part if total is None else total + part
    return total.astype(jnp.bfloat16)


def pick_matrix(facts):
    row = iota((PADDED_ROWS, PADDED_ROWS), 0)
    column = iota((PADDED_ROWS, PADDED_ROWS), 1)
    pick = column < 0
    for r in range(GROUP_REQUESTS):
        ahead = facts.group ^ (facts.slots[r] // GROUP_REQUESTS)
        pick = pick | (
            (column // DECODE_STEPS == r) & (row == ahead * DECODE_STEPS + column - r * DECODE_STEPS)
        )
    return pick.astype(jnp.float32).astype(jnp.bfloat16)


def fresh_mask():
    row = iota((STACKED, PADDED_ROWS), 0) % PADDED_ROWS
    column = iota((STACKED, PADDED_ROWS), 1)
    return (column // DECODE_STEPS == row // DECODE_STEPS) & (
        column % DECODE_STEPS <= row % DECODE_STEPS
    )


def first_kernel(plan, pd_size, facts_ref, maxima_ref, q_ref, *refs):
    width = plan.size
    k_refs, v_refs, refs = refs[:1], refs[1:2], refs[2:]
    block_refs, refs = refs[:pd_size], refs[pd_size:]
    acc_ref, bias_ref, dec_acc_ref, dec_bias_ref, worst_ref, queries_ref, fresh_ref, pick_ref, owner_ref = refs
    tokens = q_ref.shape[0]
    half = tokens // 2
    facts = Facts(facts_ref, width)
    sources = facts.source[:1]
    pick_ref[...] = pick_matrix(facts)
    slot = iota((8, HEAD_SIZE), 0)
    owner = jnp.zeros_like(slot)
    for p in range(GROUP_REQUESTS):
        owner = jnp.where(slot == p, facts.owner[p], owner)
    owner_ref[...] = owner
    for s in range(width):
        bias_ref[s] = causal_bias(0, tokens, tokens, facts.source[s : s + 1], facts.ends, facts.member, width)
        dec_bias_ref[s] = jnp.where(
            request_mask(facts.ends, tokens, facts.source[s : s + 1], width), 0.0, MASKED
        )
    rows = picked_rows(facts, pd_size, block_refs)
    queries_ref[...] = rows[:, :Q_WIDTH]
    fresh_ref[...] = rows[:, Q_WIDTH:]
    worst_ref[...] = maxima_ref[...]
    new_mask = fresh_mask()
    mask = request_mask(facts.ends, tokens, sources, width)
    spans = ((0, half), (half, tokens))
    biases = [
        causal_bias(s, half, keys, sources, facts.ends, facts.member, width) for s, keys in spans
    ]
    together = max(1, min(HEADS_PER_KV, HEADS_PER_KV * 4 // width))

    def weigh(exponents):
        top = jnp.max(peak(exponents), axis=1, keepdims=True)
        worst_ref[...] = jnp.maximum(worst_ref[...], top)
        return jnp.exp2(exponents).astype(jnp.bfloat16)

    def step(h):
        columns = span(h * HEAD_SIZE, HEAD_SIZE)
        first = h * Q_BLOCK
        queries = stacked_heads(queries_ref, slice(None), first, HEADS_PER_KV)
        k_all = jnp.concatenate([ref[:, columns] for ref in k_refs], axis=0)
        v_all = with_ones(jnp.concatenate([ref[:, columns] for ref in v_refs], axis=0))
        new_scores = scores_of(queries, fresh_ref[:, columns]) * EXPONENT
        new_weights = weigh(jnp.where(new_mask, new_scores, MASKED))
        new_values = fresh_ref[:, span(KV_WIDTH + h * HEAD_SIZE, HEAD_SIZE)]
        weights = weigh(jnp.where(mask, scores_of(queries, k_all) * EXPONENT, MASKED))
        dec_acc_ref[h] = product(weights, v_all) + product(new_weights, with_ones(new_values))
        for (start, keys), bias in zip(spans, biases):
            if keys < tokens:
                k_part = jnp.concatenate([ref[:keys, columns] for ref in k_refs], axis=0)
                v_part = with_ones(jnp.concatenate([ref[:keys, columns] for ref in v_refs], axis=0))
            else:
                k_part, v_part = k_all, v_all
            for g in range(0, HEADS_PER_KV, together):
                queries = stacked_heads(
                    q_ref, slice(start, start + half), first + g * HEAD_SIZE, together
                )
                scores = scores_of(queries, k_part).reshape(together, half, bias.shape[1])
                exponents = (scores * EXPONENT + bias[None]).reshape(together * half, bias.shape[1])
                rows = slice(
                    start * HEADS_PER_KV + g * half, start * HEADS_PER_KV + (g + together) * half
                )
                acc_ref[h, rows, :] = product(weigh(exponents), v_part)

    each_kv_head(width, step)


def middle_kernel(plan, acc_ref, bias_ref, dec_acc_ref, dec_bias_ref, worst_ref, queries_ref, q_ref, *refs):
    count = plan.size - 2
    k_refs, v_refs, refs = refs[:count], refs[count : 2 * count], refs[2 * count :]
    new_acc_ref, new_dec_acc_ref, new_worst_ref = refs
    tokens = q_ref.shape[0]
    half = tokens // 2
    worst = worst_ref[...]
    for h in range(KEY_VALUE_HEADS):
        columns = slice(h * HEAD_SIZE, (h + 1) * HEAD_SIZE)
        for parts in parts_in(count):
            keys = jnp.concatenate([k_refs[s][:, columns] for s in parts], axis=0)
            values = with_ones(jnp.concatenate([v_refs[s][:, columns] for s in parts], axis=0))
            old_acc_ref, old_dec_acc_ref = acc_ref, dec_acc_ref
            if parts[0] > 0:
                old_acc_ref, old_dec_acc_ref = new_acc_ref, new_dec_acc_ref
            queries = stacked_heads(queries_ref, slice(None), h * Q_BLOCK, HEADS_PER_KV)
            bias = jnp.concatenate([dec_bias_ref[s + 1] for s in parts], axis=1)
            exponents = scores_of(queries, keys) * EXPONENT + bias
            worst = jnp.maximum(worst, jnp.max(peak(exponents), axis=1, keepdims=True))
            new_dec_acc_ref[h] = old_dec_acc_ref[h] + product(
                jnp.exp2(exponents).astype(jnp.bfloat16), values
            )
            for start in (0, half):
                bias = jnp.concatenate([bias_ref[s + 1, start : start + half, :] for s in parts], axis=1)
                queries = stacked_heads(q_ref, slice(start, start + half), h * Q_BLOCK, HEADS_PER_KV)
                scores = scores_of(queries, keys).reshape(HEADS_PER_KV, half, bias.shape[1])
                exponents = (scores * EXPONENT + bias[None]).reshape(HEADS_PER_KV * half, bias.shape[1])
                worst = jnp.maximum(worst, jnp.max(peak(exponents), axis=1, keepdims=True))
                rows = slice(start * HEADS_PER_KV, (start + half) * HEADS_PER_KV)
                new_acc_ref[h, rows, :] = old_acc_ref[h, rows, :] + product(
                    jnp.exp2(exponents).astype(jnp.bfloat16), values
                )
    new_worst_ref[...] = worst


def divided(acc):
    return (acc[:, :HEAD_SIZE] * pl.reciprocal(acc[:, HEAD_SIZE:], approx=True)).astype(jnp.bfloat16)


def fold(state, scores_list, values_list):
    top = None if state is None else state[0]
    for scores in scores_list:
        part = jnp.max(scores, axis=1, keepdims=True)
        top = part if top is None else jnp.maximum(top, part)
    acc = None
    for scores, values in zip(scores_list, values_list):
        weights = jnp.exp2((scores - top) * EXPONENT).astype(jnp.bfloat16)
        part = product(weights, with_ones(values))
        acc = part if acc is None else acc + part
    if state is not None:
        acc = acc + state[1] * jnp.exp2((state[0] - top) * EXPONENT)
    return top, acc


def parts_in(width):
    return [range(c, min(c + 4, width)) for c in range(0, width, 4)]


def out_of_range(worst, least):
    return (jnp.max(worst) > LIMIT) | (jnp.min(least) < 2.0**-LIMIT)


def decode_kernel(plan, acc_ref, bias_ref, worst_ref, queries_ref, fresh_ref, pick_ref, *refs):
    width = plan.size
    k_refs, v_refs, (out_ref,) = refs[:width], refs[width : 2 * width], refs[2 * width :]
    heads = range(KEY_VALUE_HEADS)
    columns = [slice(h * HEAD_SIZE, (h + 1) * HEAD_SIZE) for h in heads]

    def queries_of(h):
        return stacked_heads(queries_ref, slice(None), h * Q_BLOCK, HEADS_PER_KV)

    def send(acc):
        out = [divided(a) for a in acc]
        out = jnp.concatenate(
            [o[g * PADDED_ROWS : (g + 1) * PADDED_ROWS] for o in out for g in range(HEADS_PER_KV)], axis=1
        )
        out_ref[...] = product(pick_ref[...], out).astype(jnp.bfloat16)

    exponents = [
        scores_of(queries_of(h), k_refs[-1][:, columns[h]]) * EXPONENT + bias_ref[width - 1]
        for h in heads
    ]
    acc = [
        acc_ref[h] + product(jnp.exp2(exponents[h]).astype(jnp.bfloat16), with_ones(v_refs[-1][:, columns[h]]))
        for h in heads
    ]
    send(acc)
    worst, least = worst_ref[...], None
    for h in heads:
        worst = jnp.maximum(worst, peak(exponents[h]))
        part = jnp.min(acc[h][:, HEAD_SIZE:].reshape(-1, 8, HEAD_SIZE), axis=0)
        least = part if least is None else jnp.minimum(least, part)

    @pl.when(out_of_range(worst, least))
    def _():
        new_mask = fresh_mask()
        again = []
        for h in heads:
            queries = queries_of(h)
            scores = jnp.where(new_mask, scores_of(queries, fresh_ref[:, columns[h]]), MASKED)
            new_columns = slice(KV_WIDTH + h * HEAD_SIZE, KV_WIDTH + (h + 1) * HEAD_SIZE)
            state = fold(None, [scores], [fresh_ref[:, new_columns]])
            for parts in parts_in(width):
                k_part = jnp.concatenate([k_refs[s][:, columns[h]] for s in parts], axis=0)
                v_part = jnp.concatenate([v_refs[s][:, columns[h]] for s in parts], axis=0)
                bias = jnp.concatenate([bias_ref[s] for s in parts], axis=1)
                state = fold(state, [scores_of(queries, k_part) + bias], [v_part])
            again.append(state[1])
        send(again)


def prefill_kernel(plan, acc_ref, bias_ref, worst_ref, q_ref, *refs):
    width = plan.size
    k_refs, v_refs, refs = refs[:width], refs[width : 2 * width], refs[2 * width :]
    out_ref, done_ref, sem = refs
    tokens = q_ref.shape[0]
    half = tokens // 2
    def write(h, start, acc):
        out = divided(acc)
        for g in range(HEADS_PER_KV):
            done_ref[start : start + half, span(h * Q_BLOCK + g * HEAD_SIZE, HEAD_SIZE)] = out[
                g * half : (g + 1) * half
            ]

    def copy_out(h):
        part = pl.ds(h * Q_BLOCK, Q_BLOCK)
        return pltpu.make_async_copy(done_ref.at[:, part], out_ref.at[:, part], sem.at[h])

    biases = [bias_ref[width - 1, start : start + half, :] for start in (0, half)]
    worst, least = worst_ref[...], None
    for h in range(KEY_VALUE_HEADS):
        columns = slice(h * HEAD_SIZE, (h + 1) * HEAD_SIZE)
        keys, values = k_refs[-1][:, columns], with_ones(v_refs[-1][:, columns])
        for start, bias in zip((0, half), biases):
            queries = stacked_heads(q_ref, slice(start, start + half), h * Q_BLOCK, HEADS_PER_KV)
            scores = scores_of(queries, keys).reshape(HEADS_PER_KV, half, tokens)
            exponents = (scores * EXPONENT + bias[None]).reshape(HEADS_PER_KV * half, tokens)
            worst = jnp.maximum(worst, peak(exponents))
            rows = slice(start * HEADS_PER_KV, (start + half) * HEADS_PER_KV)
            acc = acc_ref[h, rows, :] + product(jnp.exp2(exponents).astype(jnp.bfloat16), values)
            part = jnp.min(acc[:, HEAD_SIZE:].reshape(-1, 8, HEAD_SIZE), axis=0)
            least = part if least is None else jnp.minimum(least, part)
            write(h, start, acc)
        copy_out(h).start()
    redo = out_of_range(worst, least)
    for h in range(KEY_VALUE_HEADS):
        copy_out(h).wait()

    @pl.when(redo)
    def _():
        def step(h, carry):
            columns = span(h * HEAD_SIZE, HEAD_SIZE)
            for start in (0, half):
                queries = stacked_heads(q_ref, slice(start, start + half), h * Q_BLOCK, HEADS_PER_KV)
                state = None
                for parts in parts_in(width):
                    k_part = jnp.concatenate([k_refs[s][:, columns] for s in parts], axis=0)
                    v_part = jnp.concatenate([v_refs[s][:, columns] for s in parts], axis=0)
                    bias = jnp.concatenate([bias_ref[s, start : start + half, :] for s in parts], axis=1)
                    scores = scores_of(queries, k_part).reshape(HEADS_PER_KV, half, bias.shape[1])
                    scores = (scores + bias[None]).reshape(HEADS_PER_KV * half, bias.shape[1])
                    state = fold(state, [scores], [v_part])
                write(h, start, state[1])
            return carry

        lax.fori_loop(0, KEY_VALUE_HEADS, step, 0)
        for h in range(KEY_VALUE_HEADS):
            copy_out(h).start()
        for h in range(KEY_VALUE_HEADS):
            copy_out(h).wait()


def cost(rows, keys, exps):
    return pl.CostEstimate(
        flops=32 * rows * keys * Q_WIDTH, bytes_accessed=4 * rows * Q_WIDTH, transcendentals=exps
    )


def call_first(plan, facts, maxima, query, blocks, keys, values):
    tokens, width = query.shape[0], plan.size
    rows = HEADS_PER_KV * tokens
    f32, bf16 = jnp.float32, jnp.bfloat16
    every = tokens
    shapes = [
        jax.ShapeDtypeStruct((KEY_VALUE_HEADS, rows, 2 * HEAD_SIZE), f32),
        jax.ShapeDtypeStruct((width, tokens, tokens), f32),
        jax.ShapeDtypeStruct((KEY_VALUE_HEADS, STACKED, 2 * HEAD_SIZE), f32),
        jax.ShapeDtypeStruct((width, STACKED, tokens), f32),
        jax.ShapeDtypeStruct((8, HEAD_SIZE), f32),
        jax.ShapeDtypeStruct((PADDED_ROWS, Q_WIDTH), bf16),
        jax.ShapeDtypeStruct((PADDED_ROWS, 2 * KV_WIDTH), bf16),
        jax.ShapeDtypeStruct((PADDED_ROWS, PADDED_ROWS), bf16),
        jax.ShapeDtypeStruct((8, HEAD_SIZE), jnp.int32),
    ]
    return pl.pallas_call(
        lambda *refs: first_kernel(plan, len(blocks), *refs),
        in_specs=[SMEM] + [VMEM] * (4 + len(blocks)),
        out_specs=[VMEM] * len(shapes),
        out_shape=shapes,
        compiler_params=pltpu.CompilerParams(vmem_limit_bytes=(28 + width) * MIB),
        cost_estimate=cost(tokens, every, tokens * every * QUERY_HEADS),
        name="first_shards",
    )(facts, maxima, query, *keys, *values, *blocks)


def call_middle(plan, state, query, keys, values):
    acc, bias, dec_acc, dec_bias, worst, queries = state[:6]
    tokens = query.shape[0]
    new_acc, new_dec_acc, new_worst = pl.pallas_call(
        lambda *refs: middle_kernel(plan, *refs),
        in_specs=[VMEM] * (7 + 2 * len(keys)),
        out_specs=[VMEM] * 3,
        out_shape=[jax.ShapeDtypeStruct(a.shape, a.dtype) for a in (acc, dec_acc, worst)],
        input_output_aliases={0: 0, 2: 1, 4: 2},
        compiler_params=pltpu.CompilerParams(vmem_limit_bytes=32 * MIB),
        cost_estimate=cost(tokens, tokens, tokens * tokens * QUERY_HEADS),
        name="middle_shard",
    )(acc, bias, dec_acc, dec_bias, worst, queries, query, *keys, *values)
    return [new_acc, bias, new_dec_acc, dec_bias, new_worst] + list(state[5:])


def call_decode(plan, state, keys, values):
    tokens, width = keys[0].shape[0], plan.size
    return pl.pallas_call(
        lambda *refs: decode_kernel(plan, *refs),
        in_specs=[VMEM] * (6 + 2 * width),
        out_specs=VMEM,
        out_shape=jax.ShapeDtypeStruct((PADDED_ROWS, Q_WIDTH), jnp.bfloat16),
        compiler_params=pltpu.CompilerParams(vmem_limit_bytes=(28 + width) * MIB),
        cost_estimate=cost(PADDED_ROWS, tokens, PADDED_ROWS * tokens * QUERY_HEADS),
        name="last_shard_decode",
    )(*state[2:8], *keys, *values)


def call_prefill(plan, state, query, keys, values):
    tokens, width = query.shape[0], plan.size
    return pl.pallas_call(
        lambda *refs: prefill_kernel(plan, *refs),
        in_specs=[VMEM] * (4 + 2 * width),
        out_specs=ANY,
        out_shape=jax.ShapeDtypeStruct((tokens, Q_WIDTH), jnp.bfloat16),
        scratch_shapes=[
            pltpu.VMEM((tokens, Q_WIDTH), jnp.bfloat16),
            pltpu.SemaphoreType.DMA((KEY_VALUE_HEADS,)),
        ],
        compiler_params=pltpu.CompilerParams(vmem_limit_bytes=(28 + width) * MIB),
        cost_estimate=cost(tokens, tokens, tokens * tokens * QUERY_HEADS),
        name="last_shard_prefill",
    )(*state[:2], state[4], query, *keys, *values)


def start_maxima(*arrays, flops=5 * 10**9):
    def kernel(*refs):
        refs[-1][...] = jnp.full((8, HEAD_SIZE), MASKED, jnp.float32)

    return pl.pallas_call(
        kernel,
        in_specs=[VMEM] * len(arrays),
        out_specs=VMEM,
        out_shape=jax.ShapeDtypeStruct((8, HEAD_SIZE), jnp.float32),
        cost_estimate=pl.CostEstimate(flops=flops, bytes_accessed=0, transcendentals=0),
        compiler_params=pltpu.CompilerParams(vmem_limit_bytes=MIB),
        name="start_maxima",
    )(*arrays)


def paired(array, k):
    return lax.ppermute(array, "pd", [(g, g ^ k) for g in range(lax.axis_size("pd"))])


def body(
    prompt_query,
    prompt_key,
    prompt_value,
    prompt_lengths,
    decode_slot,
    decoded_query,
    decoded_key,
    decoded_value,
):
    plan = Ring(lax.axis_size("tp"))
    pd_size = lax.axis_size("pd")
    own = jnp.concatenate([decoded_query, decoded_key, decoded_value], axis=2).reshape(
        DECODE_ROWS, Q_WIDTH + 2 * KV_WIDTH
    )
    facts = facts_row(plan, prompt_lengths, decode_slot)
    prompt_key, decoded_query = lax.optimization_barrier((prompt_key, decoded_query))
    later_key, later_value, own, facts = lax.optimization_barrier((prompt_key, prompt_value, own, facts))
    blocks = [own] + [paired(own, k) for k in range(1, pd_size)]
    firsts = [prompt_key, prompt_value]
    laters = [later_key, later_value]
    ways = (True, False)
    keys, values = [prompt_key], [prompt_value]
    maxima = None
    for d in range(1, plan.size // 2 + 1):
        firsts = [plan.step(a, way) for a, way in zip(firsts, ways)]
        if 2 * d < plan.size:
            laters = [plan.step(a, not way) for a, way in zip(laters, ways)]
        if d == 1:
            firsts, blocks = lax.optimization_barrier((firsts, blocks))
            maxima = start_maxima(*firsts)
        if 2 * d < plan.size:
            keys += [firsts[0], laters[0]]
            values += [laters[1], firsts[1]]
        else:
            keys.append(firsts[0])
            values.append(firsts[1])

    state = call_first(plan, facts, maxima, prompt_query, blocks, keys[:1], values[:1])
    state = call_middle(plan, state, prompt_query, keys[1:-1], values[1:-1])
    outgoing = call_decode(plan, state, keys, values)
    arrived = [outgoing[:DECODE_STEPS]]
    for k in range(1, pd_size):
        arrived.append(paired(outgoing[k * DECODE_STEPS : (k + 1) * DECODE_STEPS], k))
    pre_out = call_prefill(plan, state, prompt_query, keys, values)

    from_block = state[8][:GROUP_REQUESTS, 0]
    dec_out = jnp.zeros((GROUP_REQUESTS, DECODE_STEPS, Q_WIDTH), jnp.bfloat16)
    for k in range(pd_size):
        dec_out = jnp.where((from_block == k)[:, None, None], arrived[k][None], dec_out)
    return (pre_out, dec_out)


def solution(mesh):
    placed = (
        P(("rep", "pd", "tp"), None),
        P(("rep", "pd", "tp"), None),
        P(("rep", "pd", "tp"), None),
        P("rep", None),
        P("rep"),
        P(("rep", "pd"), None, None),
        P(("rep", "pd"), None, None),
        P(("rep", "pd"), None, None),
    )
    return jax.shard_map(
        body,
        mesh=mesh,
        in_specs=placed,
        out_specs=(P(("rep", "pd", "tp"), None), P(("rep", "pd"), None, None)),
        check_vma=False,
    )
```

```python
import math

import jax
import jax.numpy as jnp
from jax import lax
from jax.experimental import pallas as pl
from jax.experimental.pallas import tpu as pltpu
from jax.sharding import PartitionSpec as P

QUERY_HEADS = 32
KEY_VALUE_HEADS = 4
HEAD_SIZE = 128
PAGE = 16
GROUP_REQUESTS = 4
DECODE_STEPS = 2
HEADS_PER_KV = QUERY_HEADS // KEY_VALUE_HEADS
KV_WIDTH = KEY_VALUE_HEADS * HEAD_SIZE
Q_WIDTH = QUERY_HEADS * HEAD_SIZE
Q_BLOCK = HEADS_PER_KV * HEAD_SIZE
DECODE_ROWS = GROUP_REQUESTS * DECODE_STEPS
PADDED_ROWS = 16
STACKED = HEADS_PER_KV * PADDED_ROWS
MIB = 1024 * 1024

MASKED = -1e30
LIMIT = 60.0
EXPONENT = math.log2(math.e) / math.sqrt(HEAD_SIZE)

VMEM = pl.BlockSpec(memory_space=pltpu.VMEM)
SMEM = pl.BlockSpec(memory_space=pltpu.SMEM)
ANY = pl.BlockSpec(memory_space=pl.ANY)
HBM = pl.BlockSpec(memory_space=pltpu.HBM)


class Ring:
    def __init__(self, size):
        self.size = size
        order = [0] + list(range(1, size, 2)) + [i for i in range(size - 1, 0, -1) if i % 2 == 0]
        self.pairs = [(order[i], order[(i + 1) % size]) for i in range(size)]
        self.offsets = [0]
        for d in range(1, size // 2 + 1):
            self.offsets += [-d, d]
        self.offsets = self.offsets[:size]

    def step(self, array, up):
        return lax.ppermute(array, "tp", self.pairs if up else [(b, a) for a, b in self.pairs])


def scores_of(queries, keys):
    return lax.dot_general(
        queries, keys, (((1,), (1,)), ((), ())), preferred_element_type=jnp.float32
    )


def product(left, right):
    return jnp.dot(left, right, preferred_element_type=jnp.float32)


def iota(shape, axis):
    return lax.broadcasted_iota(jnp.int32, shape, axis)


def span(start, size):
    if isinstance(start, int):
        return slice(start, start + size)
    return pl.ds(pl.multiple_of(start, size), size)


def with_ones(values):
    return jnp.concatenate([values, jnp.ones_like(values)], axis=1)


def page_position(offset, member, width):
    return (offset // PAGE * width + member) * PAGE + offset % PAGE


def key_positions(rows, sources, width):
    column = iota((1, len(sources) * rows), 1)
    part = column // rows
    source = jnp.zeros_like(column) + sources[0]
    for b in range(1, len(sources)):
        source = jnp.where(part == b, sources[b], source)
    return page_position(column - part * rows, source, width)


class Facts:
    def __init__(self, ref, width):
        self.width = width
        self.group, self.member = ref[0], ref[1]
        self.slots = [ref[2 + r] for r in range(GROUP_REQUESTS)]
        first = 2 + GROUP_REQUESTS
        self.ends = []
        total = jnp.int32(0)
        for r in range(GROUP_REQUESTS):
            total = total + ref[first + r] * PAGE
            self.ends.append(total)
        first += GROUP_REQUESTS
        self.source = [ref[first + s] for s in range(width)]
        first += width
        self.owner = [ref[first + p] for p in range(GROUP_REQUESTS)]


def facts_row(plan, lengths, slots):
    width, requests = plan.size, slots.shape[0]

    def kernel(lengths_ref, slots_ref, out_ref):
        group, member = lax.axis_index("pd"), lax.axis_index("tp")
        values = [group, member]
        values += [slots_ref[group * GROUP_REQUESTS + r] for r in range(GROUP_REQUESTS)]
        values += [lengths_ref[group, r] for r in range(GROUP_REQUESTS)]
        place = jnp.where(member % 2 == 1, (member + 1) // 2, width - member // 2)
        for offset in plan.offsets:
            before = (place + width + offset) % width
            up = 2 * before - 1
            values.append(jnp.where(before == 0, 0, jnp.where(before <= width // 2, up, 2 * (width - before))))
        for i, value in enumerate(values):
            out_ref[i] = value.astype(jnp.int32)
        for q in range(requests):
            place = slots_ref[q] - group * GROUP_REQUESTS

            @pl.when((place >= 0) & (place < GROUP_REQUESTS))
            def _():
                out_ref[len(values) + place] = group ^ (q // GROUP_REQUESTS)

    length = 2 + 2 * GROUP_REQUESTS + width + GROUP_REQUESTS
    return pl.pallas_call(
        kernel,
        in_specs=[SMEM, SMEM],
        out_specs=SMEM,
        out_shape=jax.ShapeDtypeStruct((length,), jnp.int32),
        cost_estimate=pl.CostEstimate(flops=5 * 10**9, bytes_accessed=0, transcendentals=0),
        name="facts",
    )(lengths, slots)


def causal_bias(start, rows, keys, sources, ends, member, width):
    qpos = page_position(start + iota((rows, 1), 0), member, width)
    low = jnp.zeros_like(qpos)
    for end in ends:
        low = jnp.where(qpos >= end, end, low)
    kpos = key_positions(keys, sources, width)
    return jnp.where((kpos >= low) & (kpos <= qpos), 0.0, MASKED)


def request_mask(ends, keys, sources, width):
    request = iota((STACKED, 1), 0) % PADDED_ROWS // DECODE_STEPS
    low = jnp.zeros_like(request)
    high = jnp.zeros_like(request) + ends[0]
    for r in range(1, GROUP_REQUESTS):
        low = jnp.where(request == r, ends[r - 1], low)
        high = jnp.where(request == r, ends[r], high)
    kpos = key_positions(keys, sources, width)
    return (kpos >= low) & (kpos < high)


def stacked_heads(ref, rows, first, count):
    return jnp.concatenate(
        [ref[rows, span(first + i * HEAD_SIZE, HEAD_SIZE)] for i in range(count)], axis=0
    )


def each_kv_head(width, step):
    if width <= 8:
        for h in range(KEY_VALUE_HEADS):
            step(h)
    else:
        lax.fori_loop(0, KEY_VALUE_HEADS, lambda h, c: (step(h), c)[1], 0)


def peak(exponents):
    return jnp.max(exponents.reshape(-1, 8, exponents.shape[-1]), axis=0)


def picked_rows(facts, pd_size, block_refs):
    row = iota((PADDED_ROWS, DECODE_ROWS), 0)
    column = iota((PADDED_ROWS, DECODE_ROWS), 1)
    total = None
    for k in range(pd_size):
        pick = column < 0
        for r in range(GROUP_REQUESTS):
            slot = facts.slots[r]
            first = jnp.where(facts.group ^ (slot // GROUP_REQUESTS) == k, slot % GROUP_REQUESTS * DECODE_STEPS, -DECODE_ROWS * 4)
            pick = pick | ((row // DECODE_STEPS == r) & (column == first + row - r * DECODE_STEPS))
        part = product(pick.astype(jnp.float32).astype(jnp.bfloat16), block_refs[k][...])
        total = part if total is None else total + part
    return total.astype(jnp.bfloat16)


def pick_matrix(facts):
    row = iota((PADDED_ROWS, PADDED_ROWS), 0)
    column = iota((PADDED_ROWS, PADDED_ROWS), 1)
    pick = column < 0
    for r in range(GROUP_REQUESTS):
        ahead = facts.group ^ (facts.slots[r] // GROUP_REQUESTS)
        pick = pick | (
            (column // DECODE_STEPS == r) & (row == ahead * DECODE_STEPS + column - r * DECODE_STEPS)
        )
    return pick.astype(jnp.float32).astype(jnp.bfloat16)


def fresh_mask():
    row = iota((STACKED, PADDED_ROWS), 0) % PADDED_ROWS
    column = iota((STACKED, PADDED_ROWS), 1)
    return (column // DECODE_STEPS == row // DECODE_STEPS) & (
        column % DECODE_STEPS <= row % DECODE_STEPS
    )


def first_kernel(plan, pd_size, facts_ref, maxima_ref, q_ref, *refs):
    width = plan.size
    k_refs, v_refs, refs = refs[:1], refs[1:2], refs[2:]
    block_refs, refs = refs[:pd_size], refs[pd_size:]
    acc_ref, bias_ref, dec_acc_ref, dec_bias_ref, worst_ref, queries_ref, fresh_ref, pick_ref, owner_ref = refs
    tokens = q_ref.shape[0]
    half = tokens // 2
    facts = Facts(facts_ref, width)
    sources = facts.source[:1]
    pick_ref[...] = pick_matrix(facts)
    slot = iota((8, HEAD_SIZE), 0)
    owner = jnp.zeros_like(slot)
    for p in range(GROUP_REQUESTS):
        owner = jnp.where(slot == p, facts.owner[p], owner)
    owner_ref[...] = owner
    for s in range(width):
        bias_ref[s] = causal_bias(0, tokens, tokens, facts.source[s : s + 1], facts.ends, facts.member, width)
        dec_bias_ref[s] = jnp.where(
            request_mask(facts.ends, tokens, facts.source[s : s + 1], width), 0.0, MASKED
        )
    rows = picked_rows(facts, pd_size, block_refs)
    queries_ref[...] = rows[:, :Q_WIDTH]
    fresh_ref[...] = rows[:, Q_WIDTH:]
    worst_ref[...] = maxima_ref[...]
    new_mask = fresh_mask()
    mask = request_mask(facts.ends, tokens, sources, width)
    spans = ((0, half), (half, tokens))
    biases = [
        causal_bias(s, half, keys, sources, facts.ends, facts.member, width) for s, keys in spans
    ]
    together = max(1, min(HEADS_PER_KV, HEADS_PER_KV * 4 // width))

    def weigh(exponents):
        top = jnp.max(peak(exponents), axis=1, keepdims=True)
        worst_ref[...] = jnp.maximum(worst_ref[...], top)
        return jnp.exp2(exponents).astype(jnp.bfloat16)

    def step(h):
        columns = span(h * HEAD_SIZE, HEAD_SIZE)
        first = h * Q_BLOCK
        queries = stacked_heads(queries_ref, slice(None), first, HEADS_PER_KV)
        k_all = jnp.concatenate([ref[:, columns] for ref in k_refs], axis=0)
        v_all = with_ones(jnp.concatenate([ref[:, columns] for ref in v_refs], axis=0))
        new_scores = scores_of(queries, fresh_ref[:, columns]) * EXPONENT
        new_weights = weigh(jnp.where(new_mask, new_scores, MASKED))
        new_values = fresh_ref[:, span(KV_WIDTH + h * HEAD_SIZE, HEAD_SIZE)]
        weights = weigh(jnp.where(mask, scores_of(queries, k_all) * EXPONENT, MASKED))
        dec_acc_ref[h] = product(weights, v_all) + product(new_weights, with_ones(new_values))
        for (start, keys), bias in zip(spans, biases):
            if keys < tokens:
                k_part = jnp.concatenate([ref[:keys, columns] for ref in k_refs], axis=0)
                v_part = with_ones(jnp.concatenate([ref[:keys, columns] for ref in v_refs], axis=0))
            else:
                k_part, v_part = k_all, v_all
            for g in range(0, HEADS_PER_KV, together):
                queries = stacked_heads(
                    q_ref, slice(start, start + half), first + g * HEAD_SIZE, together
                )
                scores = scores_of(queries, k_part).reshape(together, half, bias.shape[1])
                exponents = (scores * EXPONENT + bias[None]).reshape(together * half, bias.shape[1])
                rows = slice(
                    start * HEADS_PER_KV + g * half, start * HEADS_PER_KV + (g + together) * half
                )
                acc_ref[h, rows, :] = product(weigh(exponents), v_part)

    each_kv_head(width, step)


def middle_kernel(plan, acc_ref, bias_ref, dec_acc_ref, dec_bias_ref, worst_ref, queries_ref, q_ref, *refs):
    count = plan.size - 2
    k_refs, v_refs, refs = refs[:count], refs[count : 2 * count], refs[2 * count :]
    new_acc_ref, new_dec_acc_ref, new_worst_ref = refs
    tokens = q_ref.shape[0]
    half = tokens // 2
    worst = worst_ref[...]
    for h in range(KEY_VALUE_HEADS):
        columns = slice(h * HEAD_SIZE, (h + 1) * HEAD_SIZE)
        for parts in parts_in(count):
            keys = jnp.concatenate([k_refs[s][:, columns] for s in parts], axis=0)
            values = with_ones(jnp.concatenate([v_refs[s][:, columns] for s in parts], axis=0))
            old_acc_ref, old_dec_acc_ref = acc_ref, dec_acc_ref
            if parts[0] > 0:
                old_acc_ref, old_dec_acc_ref = new_acc_ref, new_dec_acc_ref
            queries = stacked_heads(queries_ref, slice(None), h * Q_BLOCK, HEADS_PER_KV)
            bias = jnp.concatenate([dec_bias_ref[s + 1] for s in parts], axis=1)
            exponents = scores_of(queries, keys) * EXPONENT + bias
            worst = jnp.maximum(worst, jnp.max(peak(exponents), axis=1, keepdims=True))
            new_dec_acc_ref[h] = old_dec_acc_ref[h] + product(
                jnp.exp2(exponents).astype(jnp.bfloat16), values
            )
            for start in (0, half):
                bias = jnp.concatenate([bias_ref[s + 1, start : start + half, :] for s in parts], axis=1)
                queries = stacked_heads(q_ref, slice(start, start + half), h * Q_BLOCK, HEADS_PER_KV)
                scores = scores_of(queries, keys).reshape(HEADS_PER_KV, half, bias.shape[1])
                exponents = (scores * EXPONENT + bias[None]).reshape(HEADS_PER_KV * half, bias.shape[1])
                worst = jnp.maximum(worst, jnp.max(peak(exponents), axis=1, keepdims=True))
                rows = slice(start * HEADS_PER_KV, (start + half) * HEADS_PER_KV)
                new_acc_ref[h, rows, :] = old_acc_ref[h, rows, :] + product(
                    jnp.exp2(exponents).astype(jnp.bfloat16), values
                )
    new_worst_ref[...] = worst


def divided(acc):
    return (acc[:, :HEAD_SIZE] * pl.reciprocal(acc[:, HEAD_SIZE:], approx=True)).astype(jnp.bfloat16)


def fold(state, scores_list, values_list):
    top = None if state is None else state[0]
    for scores in scores_list:
        part = jnp.max(scores, axis=1, keepdims=True)
        top = part if top is None else jnp.maximum(top, part)
    acc = None
    for scores, values in zip(scores_list, values_list):
        weights = jnp.exp2((scores - top) * EXPONENT).astype(jnp.bfloat16)
        part = product(weights, with_ones(values))
        acc = part if acc is None else acc + part
    if state is not None:
        acc = acc + state[1] * jnp.exp2((state[0] - top) * EXPONENT)
    return top, acc


def parts_in(width):
    return [range(c, min(c + 4, width)) for c in range(0, width, 4)]


def out_of_range(worst, least):
    return (jnp.max(worst) > LIMIT) | (jnp.min(least) < 2.0**-LIMIT)


def decode_kernel(plan, acc_ref, bias_ref, worst_ref, queries_ref, fresh_ref, pick_ref, *refs):
    width = plan.size
    k_refs, v_refs, (out_ref,) = refs[:width], refs[width : 2 * width], refs[2 * width :]
    heads = range(KEY_VALUE_HEADS)
    columns = [slice(h * HEAD_SIZE, (h + 1) * HEAD_SIZE) for h in heads]

    def queries_of(h):
        return stacked_heads(queries_ref, slice(None), h * Q_BLOCK, HEADS_PER_KV)

    def send(acc):
        out = [divided(a) for a in acc]
        out = jnp.concatenate(
            [o[g * PADDED_ROWS : (g + 1) * PADDED_ROWS] for o in out for g in range(HEADS_PER_KV)], axis=1
        )
        out_ref[...] = product(pick_ref[...], out).astype(jnp.bfloat16)

    exponents = [
        scores_of(queries_of(h), k_refs[-1][:, columns[h]]) * EXPONENT + bias_ref[width - 1]
        for h in heads
    ]
    acc = [
        acc_ref[h] + product(jnp.exp2(exponents[h]).astype(jnp.bfloat16), with_ones(v_refs[-1][:, columns[h]]))
        for h in heads
    ]
    send(acc)
    worst, least = worst_ref[...], None
    for h in heads:
        worst = jnp.maximum(worst, peak(exponents[h]))
        part = jnp.min(acc[h][:, HEAD_SIZE:].reshape(-1, 8, HEAD_SIZE), axis=0)
        least = part if least is None else jnp.minimum(least, part)

    @pl.when(out_of_range(worst, least))
    def _():
        new_mask = fresh_mask()
        again = []
        for h in heads:
            queries = queries_of(h)
            scores = jnp.where(new_mask, scores_of(queries, fresh_ref[:, columns[h]]), MASKED)
            new_columns = slice(KV_WIDTH + h * HEAD_SIZE, KV_WIDTH + (h + 1) * HEAD_SIZE)
            state = fold(None, [scores], [fresh_ref[:, new_columns]])
            for parts in parts_in(width):
                k_part = jnp.concatenate([k_refs[s][:, columns[h]] for s in parts], axis=0)
                v_part = jnp.concatenate([v_refs[s][:, columns[h]] for s in parts], axis=0)
                bias = jnp.concatenate([bias_ref[s] for s in parts], axis=1)
                state = fold(state, [scores_of(queries, k_part) + bias], [v_part])
            again.append(state[1])
        send(again)


def prefill_kernel(plan, acc_ref, bias_ref, worst_ref, q_ref, *refs):
    width = plan.size
    k_refs, v_refs, refs = refs[:width], refs[width : 2 * width], refs[2 * width :]
    out_ref, done_ref, sem = refs
    tokens = q_ref.shape[0]
    half = tokens // 2
    def write(h, start, acc):
        out = divided(acc)
        for g in range(HEADS_PER_KV):
            done_ref[start : start + half, span(h * Q_BLOCK + g * HEAD_SIZE, HEAD_SIZE)] = out[
                g * half : (g + 1) * half
            ]

    def copy_out(h):
        part = pl.ds(h * Q_BLOCK, Q_BLOCK)
        return pltpu.make_async_copy(done_ref.at[:, part], out_ref.at[:, part], sem.at[h])

    biases = [bias_ref[width - 1, start : start + half, :] for start in (0, half)]
    worst, least = worst_ref[...], None
    for h in range(KEY_VALUE_HEADS):
        columns = slice(h * HEAD_SIZE, (h + 1) * HEAD_SIZE)
        keys, values = k_refs[-1][:, columns], with_ones(v_refs[-1][:, columns])
        for start, bias in zip((0, half), biases):
            queries = stacked_heads(q_ref, slice(start, start + half), h * Q_BLOCK, HEADS_PER_KV)
            scores = scores_of(queries, keys).reshape(HEADS_PER_KV, half, tokens)
            exponents = (scores * EXPONENT + bias[None]).reshape(HEADS_PER_KV * half, tokens)
            worst = jnp.maximum(worst, peak(exponents))
            rows = slice(start * HEADS_PER_KV, (start + half) * HEADS_PER_KV)
            acc = acc_ref[h, rows, :] + product(jnp.exp2(exponents).astype(jnp.bfloat16), values)
            part = jnp.min(acc[:, HEAD_SIZE:].reshape(-1, 8, HEAD_SIZE), axis=0)
            least = part if least is None else jnp.minimum(least, part)
            write(h, start, acc)
        copy_out(h).start()
    redo = out_of_range(worst, least)
    for h in range(KEY_VALUE_HEADS):
        copy_out(h).wait()

    @pl.when(redo)
    def _():
        def step(h, carry):
            columns = span(h * HEAD_SIZE, HEAD_SIZE)
            for start in (0, half):
                queries = stacked_heads(q_ref, slice(start, start + half), h * Q_BLOCK, HEADS_PER_KV)
                state = None
                for parts in parts_in(width):
                    k_part = jnp.concatenate([k_refs[s][:, columns] for s in parts], axis=0)
                    v_part = jnp.concatenate([v_refs[s][:, columns] for s in parts], axis=0)
                    bias = jnp.concatenate([bias_ref[s, start : start + half, :] for s in parts], axis=1)
                    scores = scores_of(queries, k_part).reshape(HEADS_PER_KV, half, bias.shape[1])
                    scores = (scores + bias[None]).reshape(HEADS_PER_KV * half, bias.shape[1])
                    state = fold(state, [scores], [v_part])
                write(h, start, state[1])
            return carry

        lax.fori_loop(0, KEY_VALUE_HEADS, step, 0)
        for h in range(KEY_VALUE_HEADS):
            copy_out(h).start()
        for h in range(KEY_VALUE_HEADS):
            copy_out(h).wait()


def cost(rows, keys, exps):
    return pl.CostEstimate(
        flops=32 * rows * keys * Q_WIDTH, bytes_accessed=4 * rows * Q_WIDTH, transcendentals=exps
    )


def call_first(plan, facts, maxima, query, blocks, keys, values):
    tokens, width = query.shape[0], plan.size
    rows = HEADS_PER_KV * tokens
    f32, bf16 = jnp.float32, jnp.bfloat16
    every = tokens
    shapes = [
        jax.ShapeDtypeStruct((KEY_VALUE_HEADS, rows, 2 * HEAD_SIZE), f32),
        jax.ShapeDtypeStruct((width, tokens, tokens), f32),
        jax.ShapeDtypeStruct((KEY_VALUE_HEADS, STACKED, 2 * HEAD_SIZE), f32),
        jax.ShapeDtypeStruct((width, STACKED, tokens), f32),
        jax.ShapeDtypeStruct((8, HEAD_SIZE), f32),
        jax.ShapeDtypeStruct((PADDED_ROWS, Q_WIDTH), bf16),
        jax.ShapeDtypeStruct((PADDED_ROWS, 2 * KV_WIDTH), bf16),
        jax.ShapeDtypeStruct((PADDED_ROWS, PADDED_ROWS), bf16),
        jax.ShapeDtypeStruct((8, HEAD_SIZE), jnp.int32),
    ]
    return pl.pallas_call(
        lambda *refs: first_kernel(plan, len(blocks), *refs),
        in_specs=[SMEM] + [VMEM] * (4 + len(blocks)),
        out_specs=[VMEM] * len(shapes),
        out_shape=shapes,
        compiler_params=pltpu.CompilerParams(vmem_limit_bytes=(28 + width) * MIB),
        cost_estimate=cost(tokens, every, tokens * every * QUERY_HEADS),
        name="first_shards",
    )(facts, maxima, query, *keys, *values, *blocks)


def call_middle(plan, state, query, keys, values):
    acc, bias, dec_acc, dec_bias, worst, queries = state[:6]
    tokens = query.shape[0]
    new_acc, new_dec_acc, new_worst = pl.pallas_call(
        lambda *refs: middle_kernel(plan, *refs),
        in_specs=[VMEM] * (7 + 2 * len(keys)),
        out_specs=[VMEM] * 3,
        out_shape=[jax.ShapeDtypeStruct(a.shape, a.dtype) for a in (acc, dec_acc, worst)],
        input_output_aliases={0: 0, 2: 1, 4: 2},
        compiler_params=pltpu.CompilerParams(vmem_limit_bytes=32 * MIB),
        cost_estimate=cost(tokens, tokens, tokens * tokens * QUERY_HEADS),
        name="middle_shard",
    )(acc, bias, dec_acc, dec_bias, worst, queries, query, *keys, *values)
    return [new_acc, bias, new_dec_acc, dec_bias, new_worst] + list(state[5:])


def call_decode(plan, state, keys, values):
    tokens, width = keys[0].shape[0], plan.size
    return pl.pallas_call(
        lambda *refs: decode_kernel(plan, *refs),
        in_specs=[VMEM] * (6 + 2 * width),
        out_specs=VMEM,
        out_shape=jax.ShapeDtypeStruct((PADDED_ROWS, Q_WIDTH), jnp.bfloat16),
        compiler_params=pltpu.CompilerParams(vmem_limit_bytes=(28 + width) * MIB),
        cost_estimate=cost(PADDED_ROWS, tokens, PADDED_ROWS * tokens * QUERY_HEADS),
        name="last_shard_decode",
    )(*state[2:8], *keys, *values)


def call_prefill(plan, state, query, keys, values):
    tokens, width = query.shape[0], plan.size
    return pl.pallas_call(
        lambda *refs: prefill_kernel(plan, *refs),
        in_specs=[VMEM] * (4 + 2 * width),
        out_specs=ANY,
        out_shape=jax.ShapeDtypeStruct((tokens, Q_WIDTH), jnp.bfloat16),
        scratch_shapes=[
            pltpu.VMEM((tokens, Q_WIDTH), jnp.bfloat16),
            pltpu.SemaphoreType.DMA((KEY_VALUE_HEADS,)),
        ],
        compiler_params=pltpu.CompilerParams(vmem_limit_bytes=(28 + width) * MIB),
        cost_estimate=cost(tokens, tokens, tokens * tokens * QUERY_HEADS),
        name="last_shard_prefill",
    )(*state[:2], state[4], query, *keys, *values)


def start_maxima(*arrays, flops=5 * 10**9):
    def kernel(*refs):
        refs[-1][...] = jnp.full((8, HEAD_SIZE), MASKED, jnp.float32)

    return pl.pallas_call(
        kernel,
        in_specs=[VMEM] * len(arrays),
        out_specs=VMEM,
        out_shape=jax.ShapeDtypeStruct((8, HEAD_SIZE), jnp.float32),
        cost_estimate=pl.CostEstimate(flops=flops, bytes_accessed=0, transcendentals=0),
        compiler_params=pltpu.CompilerParams(vmem_limit_bytes=MIB),
        name="start_maxima",
    )(*arrays)


def paired(array, k):
    return lax.ppermute(array, "pd", [(g, g ^ k) for g in range(lax.axis_size("pd"))])


def body(
    prompt_query,
    prompt_key,
    prompt_value,
    prompt_lengths,
    decode_slot,
    decoded_query,
    decoded_key,
    decoded_value,
):
    plan = Ring(lax.axis_size("tp"))
    pd_size = lax.axis_size("pd")
    own = jnp.concatenate([decoded_query, decoded_key, decoded_value], axis=2).reshape(
        DECODE_ROWS, Q_WIDTH + 2 * KV_WIDTH
    )
    facts = facts_row(plan, prompt_lengths, decode_slot)
    prompt_key, decoded_query = lax.optimization_barrier((prompt_key, decoded_query))
    later_key, later_value, own, facts = lax.optimization_barrier((prompt_key, prompt_value, own, facts))
    firsts = [prompt_key, prompt_value]
    laters = [later_key, later_value]
    ways = (True, False)
    keys, values = [prompt_key], [prompt_value]
    maxima = None
    for d in range(1, plan.size // 2 + 1):
        firsts = [plan.step(a, way) for a, way in zip(firsts, ways)]
        if d == 1:
            firsts[0], own, laters[1] = lax.optimization_barrier((firsts[0], own, laters[1]))
            blocks = [own] + [paired(own, k) for k in range(1, pd_size)]
        if 2 * d < plan.size:
            laters = [plan.step(a, not way) for a, way in zip(laters, ways)]
        if d == 1:
            maxima = start_maxima(*firsts)
        if 2 * d < plan.size:
            keys += [firsts[0], laters[0]]
            values += [laters[1], firsts[1]]
        else:
            keys.append(firsts[0])
            values.append(firsts[1])

    state = call_first(plan, facts, maxima, prompt_query, blocks, keys[:1], values[:1])
    state = call_middle(plan, state, prompt_query, keys[1:-1], values[1:-1])
    outgoing = call_decode(plan, state, keys, values)
    arrived = [outgoing[:DECODE_STEPS]]
    for k in range(1, pd_size):
        arrived.append(paired(outgoing[k * DECODE_STEPS : (k + 1) * DECODE_STEPS], k))
    pre_out = call_prefill(plan, state, prompt_query, keys, values)

    from_block = state[8][:GROUP_REQUESTS, 0]
    dec_out = jnp.zeros((GROUP_REQUESTS, DECODE_STEPS, Q_WIDTH), jnp.bfloat16)
    for k in range(pd_size):
        dec_out = jnp.where((from_block == k)[:, None, None], arrived[k][None], dec_out)
    return (pre_out, dec_out)


def solution(mesh):
    placed = (
        P(("rep", "pd", "tp"), None),
        P(("rep", "pd", "tp"), None),
        P(("rep", "pd", "tp"), None),
        P("rep", None),
        P("rep"),
        P(("rep", "pd"), None, None),
        P(("rep", "pd"), None, None),
        P(("rep", "pd"), None, None),
    )
    return jax.shard_map(
        body,
        mesh=mesh,
        in_specs=placed,
        out_specs=(P(("rep", "pd", "tp"), None), P(("rep", "pd"), None, None)),
        check_vma=False,
    )
```

```python
import math

import jax
import jax.numpy as jnp
from jax import lax
from jax.experimental import pallas as pl
from jax.experimental.pallas import tpu as pltpu
from jax.sharding import PartitionSpec as P

QUERY_HEADS = 32
KEY_VALUE_HEADS = 4
HEAD_SIZE = 128
PAGE = 16
GROUP_REQUESTS = 4
DECODE_STEPS = 2
HEADS_PER_KV = QUERY_HEADS // KEY_VALUE_HEADS
KV_WIDTH = KEY_VALUE_HEADS * HEAD_SIZE
Q_WIDTH = QUERY_HEADS * HEAD_SIZE
Q_BLOCK = HEADS_PER_KV * HEAD_SIZE
DECODE_ROWS = GROUP_REQUESTS * DECODE_STEPS
PADDED_ROWS = 16
STACKED = HEADS_PER_KV * PADDED_ROWS
MIB = 1024 * 1024

MASKED = -1e30
LIMIT = 60.0
EXPONENT = math.log2(math.e) / math.sqrt(HEAD_SIZE)

VMEM = pl.BlockSpec(memory_space=pltpu.VMEM)
SMEM = pl.BlockSpec(memory_space=pltpu.SMEM)
ANY = pl.BlockSpec(memory_space=pl.ANY)
HBM = pl.BlockSpec(memory_space=pltpu.HBM)


class Ring:
    def __init__(self, size):
        self.size = size
        order = [0] + list(range(1, size, 2)) + [i for i in range(size - 1, 0, -1) if i % 2 == 0]
        self.pairs = [(order[i], order[(i + 1) % size]) for i in range(size)]
        self.offsets = [0]
        for d in range(1, size // 2 + 1):
            self.offsets += [-d, d]
        self.offsets = self.offsets[:size]

    def step(self, array, up):
        return lax.ppermute(array, "tp", self.pairs if up else [(b, a) for a, b in self.pairs])


def scores_of(queries, keys):
    return lax.dot_general(
        queries, keys, (((1,), (1,)), ((), ())), preferred_element_type=jnp.float32
    )


def product(left, right):
    return jnp.dot(left, right, preferred_element_type=jnp.float32)


def iota(shape, axis):
    return lax.broadcasted_iota(jnp.int32, shape, axis)


def span(start, size):
    if isinstance(start, int):
        return slice(start, start + size)
    return pl.ds(pl.multiple_of(start, size), size)


def with_ones(values):
    return jnp.concatenate([values, jnp.ones_like(values)], axis=1)


def page_position(offset, member, width):
    return (offset // PAGE * width + member) * PAGE + offset % PAGE


def key_positions(rows, sources, width):
    column = iota((1, len(sources) * rows), 1)
    part = column // rows
    source = jnp.zeros_like(column) + sources[0]
    for b in range(1, len(sources)):
        source = jnp.where(part == b, sources[b], source)
    return page_position(column - part * rows, source, width)


class Facts:
    def __init__(self, ref, width):
        self.width = width
        self.group, self.member = ref[0], ref[1]
        self.slots = [ref[2 + r] for r in range(GROUP_REQUESTS)]
        first = 2 + GROUP_REQUESTS
        self.ends = []
        total = jnp.int32(0)
        for r in range(GROUP_REQUESTS):
            total = total + ref[first + r] * PAGE
            self.ends.append(total)
        first += GROUP_REQUESTS
        self.source = [ref[first + s] for s in range(width)]
        first += width
        self.owner = [ref[first + p] for p in range(GROUP_REQUESTS)]


def facts_row(plan, lengths, slots):
    width, requests = plan.size, slots.shape[0]

    def kernel(lengths_ref, slots_ref, out_ref):
        group, member = lax.axis_index("pd"), lax.axis_index("tp")
        values = [group, member]
        values += [slots_ref[group * GROUP_REQUESTS + r] for r in range(GROUP_REQUESTS)]
        values += [lengths_ref[group, r] for r in range(GROUP_REQUESTS)]
        place = jnp.where(member % 2 == 1, (member + 1) // 2, width - member // 2)
        for offset in plan.offsets:
            before = (place + width + offset) % width
            up = 2 * before - 1
            values.append(jnp.where(before == 0, 0, jnp.where(before <= width // 2, up, 2 * (width - before))))
        for i, value in enumerate(values):
            out_ref[i] = value.astype(jnp.int32)
        for q in range(requests):
            place = slots_ref[q] - group * GROUP_REQUESTS

            @pl.when((place >= 0) & (place < GROUP_REQUESTS))
            def _():
                out_ref[len(values) + place] = group ^ (q // GROUP_REQUESTS)

    length = 2 + 2 * GROUP_REQUESTS + width + GROUP_REQUESTS
    return pl.pallas_call(
        kernel,
        in_specs=[SMEM, SMEM],
        out_specs=SMEM,
        out_shape=jax.ShapeDtypeStruct((length,), jnp.int32),
        cost_estimate=pl.CostEstimate(flops=5 * 10**9, bytes_accessed=0, transcendentals=0),
        name="facts",
    )(lengths, slots)


def causal_bias(start, rows, keys, sources, ends, member, width):
    qpos = page_position(start + iota((rows, 1), 0), member, width)
    low = jnp.zeros_like(qpos)
    for end in ends:
        low = jnp.where(qpos >= end, end, low)
    kpos = key_positions(keys, sources, width)
    return jnp.where((kpos >= low) & (kpos <= qpos), 0.0, MASKED)


def request_mask(ends, keys, sources, width):
    request = iota((STACKED, 1), 0) % PADDED_ROWS // DECODE_STEPS
    low = jnp.zeros_like(request)
    high = jnp.zeros_like(request) + ends[0]
    for r in range(1, GROUP_REQUESTS):
        low = jnp.where(request == r, ends[r - 1], low)
        high = jnp.where(request == r, ends[r], high)
    kpos = key_positions(keys, sources, width)
    return (kpos >= low) & (kpos < high)


def stacked_heads(ref, rows, first, count):
    return jnp.concatenate(
        [ref[rows, span(first + i * HEAD_SIZE, HEAD_SIZE)] for i in range(count)], axis=0
    )


def each_kv_head(width, step):
    if width <= 8:
        for h in range(KEY_VALUE_HEADS):
            step(h)
    else:
        lax.fori_loop(0, KEY_VALUE_HEADS, lambda h, c: (step(h), c)[1], 0)


def peak(exponents):
    return jnp.max(exponents.reshape(-1, 8, exponents.shape[-1]), axis=0)


def picked_rows(facts, pd_size, block_refs):
    row = iota((PADDED_ROWS, DECODE_ROWS), 0)
    column = iota((PADDED_ROWS, DECODE_ROWS), 1)
    total = None
    for k in range(pd_size):
        pick = column < 0
        for r in range(GROUP_REQUESTS):
            slot = facts.slots[r]
            first = jnp.where(facts.group ^ (slot // GROUP_REQUESTS) == k, slot % GROUP_REQUESTS * DECODE_STEPS, -DECODE_ROWS * 4)
            pick = pick | ((row // DECODE_STEPS == r) & (column == first + row - r * DECODE_STEPS))
        part = product(pick.astype(jnp.float32).astype(jnp.bfloat16), block_refs[k][...])
        total = part if total is None else total + part
    return total.astype(jnp.bfloat16)


def pick_matrix(facts):
    row = iota((PADDED_ROWS, PADDED_ROWS), 0)
    column = iota((PADDED_ROWS, PADDED_ROWS), 1)
    pick = column < 0
    for r in range(GROUP_REQUESTS):
        ahead = facts.group ^ (facts.slots[r] // GROUP_REQUESTS)
        pick = pick | (
            (column // DECODE_STEPS == r) & (row == ahead * DECODE_STEPS + column - r * DECODE_STEPS)
        )
    return pick.astype(jnp.float32).astype(jnp.bfloat16)


def fresh_mask():
    row = iota((STACKED, PADDED_ROWS), 0) % PADDED_ROWS
    column = iota((STACKED, PADDED_ROWS), 1)
    return (column // DECODE_STEPS == row // DECODE_STEPS) & (
        column % DECODE_STEPS <= row % DECODE_STEPS
    )


def first_kernel(plan, pd_size, facts_ref, maxima_ref, q_ref, *refs):
    width = plan.size
    kv_refs, refs = refs[: width - 2], refs[width - 2 :]
    block_refs, refs = refs[:pd_size], refs[pd_size:]
    acc_ref, bias_ref, dec_acc_ref, dec_bias_ref, worst_ref, queries_ref, fresh_ref, pick_ref, owner_ref = refs
    tokens = q_ref.shape[0]
    half = tokens // 2
    facts = Facts(facts_ref, width)
    sources = facts.source[:-2]
    pick_ref[...] = pick_matrix(facts)
    slot = iota((8, HEAD_SIZE), 0)
    owner = jnp.zeros_like(slot)
    for p in range(GROUP_REQUESTS):
        owner = jnp.where(slot == p, facts.owner[p], owner)
    owner_ref[...] = owner
    for s in range(width):
        bias_ref[s] = causal_bias(0, tokens, tokens, facts.source[s : s + 1], facts.ends, facts.member, width)
        dec_bias_ref[s] = jnp.where(
            request_mask(facts.ends, tokens, facts.source[s : s + 1], width), 0.0, MASKED
        )
    rows = picked_rows(facts, pd_size, block_refs)
    queries_ref[...] = rows[:, :Q_WIDTH]
    fresh_ref[...] = rows[:, Q_WIDTH:]
    worst_ref[...] = maxima_ref[...]
    new_mask = fresh_mask()
    mask = request_mask(facts.ends, tokens, sources, width)
    spans = ((0, half), (half, tokens))
    biases = [
        causal_bias(s, half, keys, sources, facts.ends, facts.member, width) for s, keys in spans
    ]
    together = max(1, min(HEADS_PER_KV, HEADS_PER_KV * 4 // width))

    def weigh(exponents):
        top = jnp.max(peak(exponents), axis=1, keepdims=True)
        worst_ref[...] = jnp.maximum(worst_ref[...], top)
        return jnp.exp2(exponents).astype(jnp.bfloat16)

    def step(h):
        columns = span(h * HEAD_SIZE, HEAD_SIZE)
        first = h * Q_BLOCK
        queries = stacked_heads(queries_ref, slice(None), first, HEADS_PER_KV)
        k_all = jnp.concatenate([ref[:tokens, columns] for ref in kv_refs], axis=0)
        v_all = with_ones(jnp.concatenate([ref[tokens:, columns] for ref in kv_refs], axis=0))
        new_scores = scores_of(queries, fresh_ref[:, columns]) * EXPONENT
        new_weights = weigh(jnp.where(new_mask, new_scores, MASKED))
        new_values = fresh_ref[:, span(KV_WIDTH + h * HEAD_SIZE, HEAD_SIZE)]
        weights = weigh(jnp.where(mask, scores_of(queries, k_all) * EXPONENT, MASKED))
        dec_acc_ref[h] = product(weights, v_all) + product(new_weights, with_ones(new_values))
        for (start, keys), bias in zip(spans, biases):
            if keys < tokens:
                k_part = jnp.concatenate([ref[:keys, columns] for ref in kv_refs], axis=0)
                v_part = with_ones(
                    jnp.concatenate([ref[tokens : tokens + keys, columns] for ref in kv_refs], axis=0)
                )
            else:
                k_part, v_part = k_all, v_all
            for g in range(0, HEADS_PER_KV, together):
                queries = stacked_heads(
                    q_ref, slice(start, start + half), first + g * HEAD_SIZE, together
                )
                scores = scores_of(queries, k_part).reshape(together, half, bias.shape[1])
                exponents = (scores * EXPONENT + bias[None]).reshape(together * half, bias.shape[1])
                rows = slice(
                    start * HEADS_PER_KV + g * half, start * HEADS_PER_KV + (g + together) * half
                )
                acc_ref[h, rows, :] = product(weigh(exponents), v_part)

    each_kv_head(width, step)


def middle_kernel(plan, acc_ref, bias_ref, dec_acc_ref, dec_bias_ref, worst_ref, queries_ref, q_ref, kv_ref, *refs):
    new_acc_ref, new_dec_acc_ref, new_worst_ref = refs
    piece = plan.size - 2
    tokens = q_ref.shape[0]
    half = tokens // 2
    worst = worst_ref[...]
    for h in range(KEY_VALUE_HEADS):
        columns = slice(h * HEAD_SIZE, (h + 1) * HEAD_SIZE)
        keys, values = kv_ref[:tokens, columns], with_ones(kv_ref[tokens:, columns])
        queries = stacked_heads(queries_ref, slice(None), h * Q_BLOCK, HEADS_PER_KV)
        exponents = scores_of(queries, keys) * EXPONENT + dec_bias_ref[piece]
        worst = jnp.maximum(worst, peak(exponents))
        new_dec_acc_ref[h] = dec_acc_ref[h] + product(jnp.exp2(exponents).astype(jnp.bfloat16), values)
        for start in (0, half):
            bias = bias_ref[piece, start : start + half, :]
            queries = stacked_heads(q_ref, slice(start, start + half), h * Q_BLOCK, HEADS_PER_KV)
            scores = scores_of(queries, keys).reshape(HEADS_PER_KV, half, tokens)
            exponents = (scores * EXPONENT + bias[None]).reshape(HEADS_PER_KV * half, tokens)
            worst = jnp.maximum(worst, peak(exponents))
            rows = slice(start * HEADS_PER_KV, (start + half) * HEADS_PER_KV)
            new_acc_ref[h, rows, :] = acc_ref[h, rows, :] + product(
                jnp.exp2(exponents).astype(jnp.bfloat16), values
            )
    new_worst_ref[...] = worst


def divided(acc):
    return (acc[:, :HEAD_SIZE] * pl.reciprocal(acc[:, HEAD_SIZE:], approx=True)).astype(jnp.bfloat16)


def fold(state, scores_list, values_list):
    top = None if state is None else state[0]
    for scores in scores_list:
        part = jnp.max(scores, axis=1, keepdims=True)
        top = part if top is None else jnp.maximum(top, part)
    acc = None
    for scores, values in zip(scores_list, values_list):
        weights = jnp.exp2((scores - top) * EXPONENT).astype(jnp.bfloat16)
        part = product(weights, with_ones(values))
        acc = part if acc is None else acc + part
    if state is not None:
        acc = acc + state[1] * jnp.exp2((state[0] - top) * EXPONENT)
    return top, acc


def parts_in(width):
    return [range(c, min(c + 4, width)) for c in range(0, width, 4)]


def out_of_range(worst, least):
    return (jnp.max(worst) > LIMIT) | (jnp.min(least) < 2.0**-LIMIT)


def decode_kernel(plan, acc_ref, bias_ref, worst_ref, queries_ref, fresh_ref, pick_ref, *refs):
    width = plan.size
    kv_refs, (out_ref,) = refs[:width], refs[width:]
    tokens = kv_refs[0].shape[0] // 2
    heads = range(KEY_VALUE_HEADS)
    columns = [slice(h * HEAD_SIZE, (h + 1) * HEAD_SIZE) for h in heads]

    def queries_of(h):
        return stacked_heads(queries_ref, slice(None), h * Q_BLOCK, HEADS_PER_KV)

    def send(acc):
        out = [divided(a) for a in acc]
        out = jnp.concatenate(
            [o[g * PADDED_ROWS : (g + 1) * PADDED_ROWS] for o in out for g in range(HEADS_PER_KV)], axis=1
        )
        out_ref[...] = product(pick_ref[...], out).astype(jnp.bfloat16)

    exponents = [
        scores_of(queries_of(h), kv_refs[-1][:tokens, columns[h]]) * EXPONENT + bias_ref[width - 1]
        for h in heads
    ]
    acc = [
        acc_ref[h] + product(jnp.exp2(exponents[h]).astype(jnp.bfloat16), with_ones(kv_refs[-1][tokens:, columns[h]]))
        for h in heads
    ]
    send(acc)
    worst, least = worst_ref[...], None
    for h in heads:
        worst = jnp.maximum(worst, peak(exponents[h]))
        part = jnp.min(acc[h][:, HEAD_SIZE:].reshape(-1, 8, HEAD_SIZE), axis=0)
        least = part if least is None else jnp.minimum(least, part)

    @pl.when(out_of_range(worst, least))
    def _():
        new_mask = fresh_mask()
        again = []
        for h in heads:
            queries = queries_of(h)
            scores = jnp.where(new_mask, scores_of(queries, fresh_ref[:, columns[h]]), MASKED)
            new_columns = slice(KV_WIDTH + h * HEAD_SIZE, KV_WIDTH + (h + 1) * HEAD_SIZE)
            state = fold(None, [scores], [fresh_ref[:, new_columns]])
            for parts in parts_in(width):
                k_part = jnp.concatenate([kv_refs[s][:tokens, columns[h]] for s in parts], axis=0)
                v_part = jnp.concatenate([kv_refs[s][tokens:, columns[h]] for s in parts], axis=0)
                bias = jnp.concatenate([bias_ref[s] for s in parts], axis=1)
                state = fold(state, [scores_of(queries, k_part) + bias], [v_part])
            again.append(state[1])
        send(again)


def prefill_kernel(plan, acc_ref, bias_ref, worst_ref, q_ref, *refs):
    width = plan.size
    kv_refs, refs = refs[:width], refs[width:]
    out_ref, done_ref, sem = refs
    tokens = q_ref.shape[0]
    half = tokens // 2
    def write(h, start, acc):
        out = divided(acc)
        for g in range(HEADS_PER_KV):
            done_ref[start : start + half, span(h * Q_BLOCK + g * HEAD_SIZE, HEAD_SIZE)] = out[
                g * half : (g + 1) * half
            ]

    def copy_out(h):
        part = pl.ds(h * Q_BLOCK, Q_BLOCK)
        return pltpu.make_async_copy(done_ref.at[:, part], out_ref.at[:, part], sem.at[h])

    biases = [bias_ref[width - 1, start : start + half, :] for start in (0, half)]
    worst, least = worst_ref[...], None
    for h in range(KEY_VALUE_HEADS):
        columns = slice(h * HEAD_SIZE, (h + 1) * HEAD_SIZE)
        keys, values = kv_refs[-1][:tokens, columns], with_ones(kv_refs[-1][tokens:, columns])
        for start, bias in zip((0, half), biases):
            queries = stacked_heads(q_ref, slice(start, start + half), h * Q_BLOCK, HEADS_PER_KV)
            scores = scores_of(queries, keys).reshape(HEADS_PER_KV, half, tokens)
            exponents = (scores * EXPONENT + bias[None]).reshape(HEADS_PER_KV * half, tokens)
            worst = jnp.maximum(worst, peak(exponents))
            rows = slice(start * HEADS_PER_KV, (start + half) * HEADS_PER_KV)
            acc = acc_ref[h, rows, :] + product(jnp.exp2(exponents).astype(jnp.bfloat16), values)
            part = jnp.min(acc[:, HEAD_SIZE:].reshape(-1, 8, HEAD_SIZE), axis=0)
            least = part if least is None else jnp.minimum(least, part)
            write(h, start, acc)
        copy_out(h).start()
    redo = out_of_range(worst, least)
    for h in range(KEY_VALUE_HEADS):
        copy_out(h).wait()

    @pl.when(redo)
    def _():
        def step(h, carry):
            columns = span(h * HEAD_SIZE, HEAD_SIZE)
            for start in (0, half):
                queries = stacked_heads(q_ref, slice(start, start + half), h * Q_BLOCK, HEADS_PER_KV)
                state = None
                for parts in parts_in(width):
                    k_part = jnp.concatenate([kv_refs[s][:tokens, columns] for s in parts], axis=0)
                    v_part = jnp.concatenate([kv_refs[s][tokens:, columns] for s in parts], axis=0)
                    bias = jnp.concatenate([bias_ref[s, start : start + half, :] for s in parts], axis=1)
                    scores = scores_of(queries, k_part).reshape(HEADS_PER_KV, half, bias.shape[1])
                    scores = (scores + bias[None]).reshape(HEADS_PER_KV * half, bias.shape[1])
                    state = fold(state, [scores], [v_part])
                write(h, start, state[1])
            return carry

        lax.fori_loop(0, KEY_VALUE_HEADS, step, 0)
        for h in range(KEY_VALUE_HEADS):
            copy_out(h).start()
        for h in range(KEY_VALUE_HEADS):
            copy_out(h).wait()


def cost(rows, keys, exps):
    return pl.CostEstimate(
        flops=32 * rows * keys * Q_WIDTH, bytes_accessed=4 * rows * Q_WIDTH, transcendentals=exps
    )


def call_first(plan, facts, maxima, query, blocks, pieces):
    tokens, width = query.shape[0], plan.size
    rows = HEADS_PER_KV * tokens
    f32, bf16 = jnp.float32, jnp.bfloat16
    every = (width - 2) * tokens
    shapes = [
        jax.ShapeDtypeStruct((KEY_VALUE_HEADS, rows, 2 * HEAD_SIZE), f32),
        jax.ShapeDtypeStruct((width, tokens, tokens), f32),
        jax.ShapeDtypeStruct((KEY_VALUE_HEADS, STACKED, 2 * HEAD_SIZE), f32),
        jax.ShapeDtypeStruct((width, STACKED, tokens), f32),
        jax.ShapeDtypeStruct((8, HEAD_SIZE), f32),
        jax.ShapeDtypeStruct((PADDED_ROWS, Q_WIDTH), bf16),
        jax.ShapeDtypeStruct((PADDED_ROWS, 2 * KV_WIDTH), bf16),
        jax.ShapeDtypeStruct((PADDED_ROWS, PADDED_ROWS), bf16),
        jax.ShapeDtypeStruct((8, HEAD_SIZE), jnp.int32),
    ]
    return pl.pallas_call(
        lambda *refs: first_kernel(plan, len(blocks), *refs),
        in_specs=[SMEM] + [VMEM] * (len(blocks) + width),
        out_specs=[VMEM] * len(shapes),
        out_shape=shapes,
        compiler_params=pltpu.CompilerParams(vmem_limit_bytes=(28 + width) * MIB),
        cost_estimate=cost(tokens, every, tokens * every * QUERY_HEADS),
        name="first_shards",
    )(facts, maxima, query, *pieces, *blocks)


def call_middle(plan, state, query, piece):
    acc, bias, dec_acc, dec_bias, worst, queries = state[:6]
    tokens = query.shape[0]
    new_acc, new_dec_acc, new_worst = pl.pallas_call(
        lambda *refs: middle_kernel(plan, *refs),
        in_specs=[VMEM] * 8,
        out_specs=[VMEM] * 3,
        out_shape=[jax.ShapeDtypeStruct(a.shape, a.dtype) for a in (acc, dec_acc, worst)],
        input_output_aliases={0: 0, 2: 1, 4: 2},
        compiler_params=pltpu.CompilerParams(vmem_limit_bytes=32 * MIB),
        cost_estimate=cost(tokens, tokens, tokens * tokens * QUERY_HEADS),
        name="middle_shard",
    )(acc, bias, dec_acc, dec_bias, worst, queries, query, piece)
    return [new_acc, bias, new_dec_acc, dec_bias, new_worst] + list(state[5:])


def call_decode(plan, state, pieces):
    tokens, width = pieces[0].shape[0] // 2, plan.size
    return pl.pallas_call(
        lambda *refs: decode_kernel(plan, *refs),
        in_specs=[VMEM] * (6 + width),
        out_specs=VMEM,
        out_shape=jax.ShapeDtypeStruct((PADDED_ROWS, Q_WIDTH), jnp.bfloat16),
        compiler_params=pltpu.CompilerParams(vmem_limit_bytes=(28 + width) * MIB),
        cost_estimate=cost(PADDED_ROWS, tokens, PADDED_ROWS * tokens * QUERY_HEADS),
        name="last_shard_decode",
    )(*state[2:8], *pieces)


def call_prefill(plan, state, query, pieces):
    tokens, width = query.shape[0], plan.size
    return pl.pallas_call(
        lambda *refs: prefill_kernel(plan, *refs),
        in_specs=[VMEM] * (4 + width),
        out_specs=ANY,
        out_shape=jax.ShapeDtypeStruct((tokens, Q_WIDTH), jnp.bfloat16),
        scratch_shapes=[
            pltpu.VMEM((tokens, Q_WIDTH), jnp.bfloat16),
            pltpu.SemaphoreType.DMA((KEY_VALUE_HEADS,)),
        ],
        compiler_params=pltpu.CompilerParams(vmem_limit_bytes=(28 + width) * MIB),
        cost_estimate=cost(tokens, tokens, tokens * tokens * QUERY_HEADS),
        name="last_shard_prefill",
    )(*state[:2], state[4], query, *pieces)


def start_maxima(*arrays, flops=5 * 10**9):
    def kernel(*refs):
        refs[-1][...] = jnp.full((8, HEAD_SIZE), MASKED, jnp.float32)

    return pl.pallas_call(
        kernel,
        in_specs=[VMEM] * len(arrays),
        out_specs=VMEM,
        out_shape=jax.ShapeDtypeStruct((8, HEAD_SIZE), jnp.float32),
        cost_estimate=pl.CostEstimate(flops=flops, bytes_accessed=0, transcendentals=0),
        compiler_params=pltpu.CompilerParams(vmem_limit_bytes=MIB),
        name="start_maxima",
    )(*arrays)


def paired(array, k):
    return lax.ppermute(array, "pd", [(g, g ^ k) for g in range(lax.axis_size("pd"))])


def body(
    prompt_query,
    prompt_key,
    prompt_value,
    prompt_lengths,
    decode_slot,
    decoded_query,
    decoded_key,
    decoded_value,
):
    plan = Ring(lax.axis_size("tp"))
    pd_size = lax.axis_size("pd")
    own = jnp.concatenate([decoded_query, decoded_key, decoded_value], axis=2).reshape(
        DECODE_ROWS, Q_WIDTH + 2 * KV_WIDTH
    )
    facts = facts_row(plan, prompt_lengths, decode_slot)
    kv, decoded_query = lax.optimization_barrier(
        (jnp.concatenate([prompt_key, prompt_value], axis=0), decoded_query)
    )
    own, facts = lax.optimization_barrier((own, facts))
    pieces, maxima, up, down = [kv], None, kv, kv
    for d in range(1, plan.size // 2 + 1):
        if d == 2:
            up, facts = lax.optimization_barrier((up, facts))
        up = plan.step(up, True)
        if d == 1:
            up, down = lax.optimization_barrier((up, down))
        down = plan.step(down, False) if 2 * d < plan.size else None
        pieces += [up, down]
    pieces = pieces[: plan.size]
    blocks = [own] + [paired(own, k) for k in range(1, pd_size)]
    maxima = start_maxima(pieces[1])

    state = call_first(plan, facts, maxima, prompt_query, blocks, pieces[:-2])
    state = call_middle(plan, state, prompt_query, pieces[-2])
    outgoing = call_decode(plan, state, pieces)
    arrived = [outgoing[:DECODE_STEPS]]
    for k in range(1, pd_size):
        arrived.append(paired(outgoing[k * DECODE_STEPS : (k + 1) * DECODE_STEPS], k))
    pre_out = call_prefill(plan, state, prompt_query, pieces)

    from_block = state[8][:GROUP_REQUESTS, 0]
    dec_out = jnp.zeros((GROUP_REQUESTS, DECODE_STEPS, Q_WIDTH), jnp.bfloat16)
    for k in range(pd_size):
        dec_out = jnp.where((from_block == k)[:, None, None], arrived[k][None], dec_out)
    return (pre_out, dec_out)


def solution(mesh):
    placed = (
        P(("rep", "pd", "tp"), None),
        P(("rep", "pd", "tp"), None),
        P(("rep", "pd", "tp"), None),
        P("rep", None),
        P("rep"),
        P(("rep", "pd"), None, None),
        P(("rep", "pd"), None, None),
        P(("rep", "pd"), None, None),
    )
    return jax.shard_map(
        body,
        mesh=mesh,
        in_specs=placed,
        out_specs=(P(("rep", "pd", "tp"), None), P(("rep", "pd"), None, None)),
        check_vma=False,
    )
```

```python
import math

import jax
import jax.numpy as jnp
from jax import lax
from jax.experimental import pallas as pl
from jax.experimental.pallas import tpu as pltpu
from jax.sharding import PartitionSpec as P

QUERY_HEADS = 32
KEY_VALUE_HEADS = 4
HEAD_SIZE = 128
PAGE = 16
GROUP_REQUESTS = 4
DECODE_STEPS = 2
HEADS_PER_KV = QUERY_HEADS // KEY_VALUE_HEADS
KV_WIDTH = KEY_VALUE_HEADS * HEAD_SIZE
Q_WIDTH = QUERY_HEADS * HEAD_SIZE
Q_BLOCK = HEADS_PER_KV * HEAD_SIZE
DECODE_ROWS = GROUP_REQUESTS * DECODE_STEPS
PADDED_ROWS = 16
STACKED = HEADS_PER_KV * PADDED_ROWS
MIB = 1024 * 1024

MASKED = -1e30
LIMIT = 60.0
EXPONENT = math.log2(math.e) / math.sqrt(HEAD_SIZE)

VMEM = pl.BlockSpec(memory_space=pltpu.VMEM)
SMEM = pl.BlockSpec(memory_space=pltpu.SMEM)
ANY = pl.BlockSpec(memory_space=pl.ANY)
HBM = pl.BlockSpec(memory_space=pltpu.HBM)


class Ring:
    def __init__(self, size):
        self.size = size
        order = [0] + list(range(1, size, 2)) + [i for i in range(size - 1, 0, -1) if i % 2 == 0]
        self.pairs = [(order[i], order[(i + 1) % size]) for i in range(size)]
        self.offsets = [0]
        for d in range(1, size // 2 + 1):
            self.offsets += [-d, d]
        self.offsets = self.offsets[:size]

    def step(self, array, up):
        return lax.ppermute(array, "tp", self.pairs if up else [(b, a) for a, b in self.pairs])


def scores_of(queries, keys):
    return lax.dot_general(
        queries, keys, (((1,), (1,)), ((), ())), preferred_element_type=jnp.float32
    )


def product(left, right):
    return jnp.dot(left, right, preferred_element_type=jnp.float32)


def iota(shape, axis):
    return lax.broadcasted_iota(jnp.int32, shape, axis)


def span(start, size):
    if isinstance(start, int):
        return slice(start, start + size)
    return pl.ds(pl.multiple_of(start, size), size)


def with_ones(values):
    return jnp.concatenate([values, jnp.ones_like(values)], axis=1)


def page_position(offset, member, width):
    return (offset // PAGE * width + member) * PAGE + offset % PAGE


def key_positions(rows, sources, width):
    column = iota((1, len(sources) * rows), 1)
    part = column // rows
    source = jnp.zeros_like(column) + sources[0]
    for b in range(1, len(sources)):
        source = jnp.where(part == b, sources[b], source)
    return page_position(column - part * rows, source, width)


class Facts:
    def __init__(self, ref, width):
        self.width = width
        self.group, self.member = ref[0], ref[1]
        self.slots = [ref[2 + r] for r in range(GROUP_REQUESTS)]
        first = 2 + GROUP_REQUESTS
        self.ends = []
        total = jnp.int32(0)
        for r in range(GROUP_REQUESTS):
            total = total + ref[first + r] * PAGE
            self.ends.append(total)
        first += GROUP_REQUESTS
        self.source = [ref[first + s] for s in range(width)]
        first += width
        self.owner = [ref[first + p] for p in range(GROUP_REQUESTS)]


def facts_row(plan, lengths, slots):
    width, requests = plan.size, slots.shape[0]

    def kernel(lengths_ref, slots_ref, out_ref):
        group, member = lax.axis_index("pd"), lax.axis_index("tp")
        values = [group, member]
        values += [slots_ref[group * GROUP_REQUESTS + r] for r in range(GROUP_REQUESTS)]
        values += [lengths_ref[group, r] for r in range(GROUP_REQUESTS)]
        place = jnp.where(member % 2 == 1, (member + 1) // 2, width - member // 2)
        for offset in plan.offsets:
            before = (place + width + offset) % width
            up = 2 * before - 1
            values.append(jnp.where(before == 0, 0, jnp.where(before <= width // 2, up, 2 * (width - before))))
        for i, value in enumerate(values):
            out_ref[i] = value.astype(jnp.int32)
        for q in range(requests):
            place = slots_ref[q] - group * GROUP_REQUESTS

            @pl.when((place >= 0) & (place < GROUP_REQUESTS))
            def _():
                out_ref[len(values) + place] = group ^ (q // GROUP_REQUESTS)

    length = 2 + 2 * GROUP_REQUESTS + width + GROUP_REQUESTS
    return pl.pallas_call(
        kernel,
        in_specs=[SMEM, SMEM],
        out_specs=SMEM,
        out_shape=jax.ShapeDtypeStruct((length,), jnp.int32),
        cost_estimate=pl.CostEstimate(flops=5 * 10**9, bytes_accessed=0, transcendentals=0),
        name="facts",
    )(lengths, slots)


def causal_bias(start, rows, keys, sources, ends, member, width):
    qpos = page_position(start + iota((rows, 1), 0), member, width)
    low = jnp.zeros_like(qpos)
    for end in ends:
        low = jnp.where(qpos >= end, end, low)
    kpos = key_positions(keys, sources, width)
    return jnp.where((kpos >= low) & (kpos <= qpos), 0.0, MASKED)


def request_mask(ends, keys, sources, width):
    request = iota((STACKED, 1), 0) % PADDED_ROWS // DECODE_STEPS
    low = jnp.zeros_like(request)
    high = jnp.zeros_like(request) + ends[0]
    for r in range(1, GROUP_REQUESTS):
        low = jnp.where(request == r, ends[r - 1], low)
        high = jnp.where(request == r, ends[r], high)
    kpos = key_positions(keys, sources, width)
    return (kpos >= low) & (kpos < high)


def stacked_heads(ref, rows, first, count):
    return jnp.concatenate(
        [ref[rows, span(first + i * HEAD_SIZE, HEAD_SIZE)] for i in range(count)], axis=0
    )


def each_kv_head(width, step):
    if width <= 8:
        for h in range(KEY_VALUE_HEADS):
            step(h)
    else:
        lax.fori_loop(0, KEY_VALUE_HEADS, lambda h, c: (step(h), c)[1], 0)


def peak(exponents):
    return jnp.max(exponents.reshape(-1, 8, exponents.shape[-1]), axis=0)


def picked_rows(facts, pd_size, block_refs):
    row = iota((PADDED_ROWS, DECODE_ROWS), 0)
    column = iota((PADDED_ROWS, DECODE_ROWS), 1)
    total = None
    for k in range(pd_size):
        pick = column < 0
        for r in range(GROUP_REQUESTS):
            slot = facts.slots[r]
            first = jnp.where(facts.group ^ (slot // GROUP_REQUESTS) == k, slot % GROUP_REQUESTS * DECODE_STEPS, -DECODE_ROWS * 4)
            pick = pick | ((row // DECODE_STEPS == r) & (column == first + row - r * DECODE_STEPS))
        part = product(pick.astype(jnp.float32).astype(jnp.bfloat16), block_refs[k][...])
        total = part if total is None else total + part
    return total.astype(jnp.bfloat16)


def pick_matrix(facts):
    row = iota((PADDED_ROWS, PADDED_ROWS), 0)
    column = iota((PADDED_ROWS, PADDED_ROWS), 1)
    pick = column < 0
    for r in range(GROUP_REQUESTS):
        ahead = facts.group ^ (facts.slots[r] // GROUP_REQUESTS)
        pick = pick | (
            (column // DECODE_STEPS == r) & (row == ahead * DECODE_STEPS + column - r * DECODE_STEPS)
        )
    return pick.astype(jnp.float32).astype(jnp.bfloat16)


def fresh_mask():
    row = iota((STACKED, PADDED_ROWS), 0) % PADDED_ROWS
    column = iota((STACKED, PADDED_ROWS), 1)
    return (column // DECODE_STEPS == row // DECODE_STEPS) & (
        column % DECODE_STEPS <= row % DECODE_STEPS
    )


def first_kernel(plan, pd_size, facts_ref, maxima_ref, q_ref, *refs):
    width = plan.size
    kv_refs, refs = refs[: width - 1], refs[width - 1 :]
    block_refs, refs = refs[:pd_size], refs[pd_size:]
    acc_ref, bias_ref, dec_acc_ref, dec_bias_ref, worst_ref, queries_ref, fresh_ref, pick_ref, owner_ref = refs
    tokens = q_ref.shape[0]
    half = tokens // 2
    facts = Facts(facts_ref, width)
    sources = facts.source[:-1]
    pick_ref[...] = pick_matrix(facts)
    slot = iota((8, HEAD_SIZE), 0)
    owner = jnp.zeros_like(slot)
    for p in range(GROUP_REQUESTS):
        owner = jnp.where(slot == p, facts.owner[p], owner)
    owner_ref[...] = owner
    for s in range(width):
        bias_ref[s] = causal_bias(0, tokens, tokens, facts.source[s : s + 1], facts.ends, facts.member, width)
        dec_bias_ref[s] = jnp.where(
            request_mask(facts.ends, tokens, facts.source[s : s + 1], width), 0.0, MASKED
        )
    rows = picked_rows(facts, pd_size, block_refs)
    queries_ref[...] = rows[:, :Q_WIDTH]
    fresh_ref[...] = rows[:, Q_WIDTH:]
    worst_ref[...] = maxima_ref[...]
    new_mask = fresh_mask()
    mask = request_mask(facts.ends, tokens, sources, width)
    spans = ((0, half), (half, tokens))
    biases = [
        causal_bias(s, half, keys, sources, facts.ends, facts.member, width) for s, keys in spans
    ]
    together = max(1, min(HEADS_PER_KV, HEADS_PER_KV * 4 // width))

    def weigh(exponents):
        top = jnp.max(peak(exponents), axis=1, keepdims=True)
        worst_ref[...] = jnp.maximum(worst_ref[...], top)
        return jnp.exp2(exponents).astype(jnp.bfloat16)

    def step(h):
        columns = span(h * HEAD_SIZE, HEAD_SIZE)
        first = h * Q_BLOCK
        queries = stacked_heads(queries_ref, slice(None), first, HEADS_PER_KV)
        k_all = jnp.concatenate([ref[:tokens, columns] for ref in kv_refs], axis=0)
        v_all = with_ones(jnp.concatenate([ref[tokens:, columns] for ref in kv_refs], axis=0))
        new_scores = scores_of(queries, fresh_ref[:, columns]) * EXPONENT
        new_weights = weigh(jnp.where(new_mask, new_scores, MASKED))
        new_values = fresh_ref[:, span(KV_WIDTH + h * HEAD_SIZE, HEAD_SIZE)]
        weights = weigh(jnp.where(mask, scores_of(queries, k_all) * EXPONENT, MASKED))
        dec_acc_ref[h] = product(weights, v_all) + product(new_weights, with_ones(new_values))
        for (start, keys), bias in zip(spans, biases):
            if keys < tokens:
                k_part = jnp.concatenate([ref[:keys, columns] for ref in kv_refs], axis=0)
                v_part = with_ones(
                    jnp.concatenate([ref[tokens : tokens + keys, columns] for ref in kv_refs], axis=0)
                )
            else:
                k_part, v_part = k_all, v_all
            for g in range(0, HEADS_PER_KV, together):
                queries = stacked_heads(
                    q_ref, slice(start, start + half), first + g * HEAD_SIZE, together
                )
                scores = scores_of(queries, k_part).reshape(together, half, bias.shape[1])
                exponents = (scores * EXPONENT + bias[None]).reshape(together * half, bias.shape[1])
                rows = slice(
                    start * HEADS_PER_KV + g * half, start * HEADS_PER_KV + (g + together) * half
                )
                acc_ref[h, rows, :] = product(weigh(exponents), v_part)

    each_kv_head(width, step)


def divided(acc):
    return (acc[:, :HEAD_SIZE] * pl.reciprocal(acc[:, HEAD_SIZE:], approx=True)).astype(jnp.bfloat16)


def fold(state, scores_list, values_list):
    top = None if state is None else state[0]
    for scores in scores_list:
        part = jnp.max(scores, axis=1, keepdims=True)
        top = part if top is None else jnp.maximum(top, part)
    acc = None
    for scores, values in zip(scores_list, values_list):
        weights = jnp.exp2((scores - top) * EXPONENT).astype(jnp.bfloat16)
        part = product(weights, with_ones(values))
        acc = part if acc is None else acc + part
    if state is not None:
        acc = acc + state[1] * jnp.exp2((state[0] - top) * EXPONENT)
    return top, acc


def parts_in(width):
    return [range(c, min(c + 4, width)) for c in range(0, width, 4)]


def out_of_range(worst, least):
    return (jnp.max(worst) > LIMIT) | (jnp.min(least) < 2.0**-LIMIT)


def decode_kernel(plan, acc_ref, bias_ref, worst_ref, queries_ref, fresh_ref, pick_ref, *refs):
    width = plan.size
    kv_refs, (out_ref,) = refs[:width], refs[width:]
    tokens = kv_refs[0].shape[0] // 2
    heads = range(KEY_VALUE_HEADS)
    columns = [slice(h * HEAD_SIZE, (h + 1) * HEAD_SIZE) for h in heads]

    def queries_of(h):
        return stacked_heads(queries_ref, slice(None), h * Q_BLOCK, HEADS_PER_KV)

    def send(acc):
        out = [divided(a) for a in acc]
        out = jnp.concatenate(
            [o[g * PADDED_ROWS : (g + 1) * PADDED_ROWS] for o in out for g in range(HEADS_PER_KV)], axis=1
        )
        out_ref[...] = product(pick_ref[...], out).astype(jnp.bfloat16)

    exponents = [
        scores_of(queries_of(h), kv_refs[-1][:tokens, columns[h]]) * EXPONENT + bias_ref[width - 1]
        for h in heads
    ]
    acc = [
        acc_ref[h] + product(jnp.exp2(exponents[h]).astype(jnp.bfloat16), with_ones(kv_refs[-1][tokens:, columns[h]]))
        for h in heads
    ]
    send(acc)
    worst, least = worst_ref[...], None
    for h in heads:
        worst = jnp.maximum(worst, peak(exponents[h]))
        part = jnp.min(acc[h][:, HEAD_SIZE:].reshape(-1, 8, HEAD_SIZE), axis=0)
        least = part if least is None else jnp.minimum(least, part)

    @pl.when(out_of_range(worst, least))
    def _():
        new_mask = fresh_mask()
        again = []
        for h in heads:
            queries = queries_of(h)
            scores = jnp.where(new_mask, scores_of(queries, fresh_ref[:, columns[h]]), MASKED)
            new_columns = slice(KV_WIDTH + h * HEAD_SIZE, KV_WIDTH + (h + 1) * HEAD_SIZE)
            state = fold(None, [scores], [fresh_ref[:, new_columns]])
            for parts in parts_in(width):
                k_part = jnp.concatenate([kv_refs[s][:tokens, columns[h]] for s in parts], axis=0)
                v_part = jnp.concatenate([kv_refs[s][tokens:, columns[h]] for s in parts], axis=0)
                bias = jnp.concatenate([bias_ref[s] for s in parts], axis=1)
                state = fold(state, [scores_of(queries, k_part) + bias], [v_part])
            again.append(state[1])
        send(again)


def prefill_kernel(plan, acc_ref, bias_ref, worst_ref, q_ref, *refs):
    width = plan.size
    kv_refs, refs = refs[:width], refs[width:]
    out_ref, done_ref, sem = refs
    tokens = q_ref.shape[0]
    half = tokens // 2
    def write(h, start, acc):
        out = divided(acc)
        for g in range(HEADS_PER_KV):
            done_ref[start : start + half, span(h * Q_BLOCK + g * HEAD_SIZE, HEAD_SIZE)] = out[
                g * half : (g + 1) * half
            ]

    def copy_out(h):
        part = pl.ds(h * Q_BLOCK, Q_BLOCK)
        return pltpu.make_async_copy(done_ref.at[:, part], out_ref.at[:, part], sem.at[h])

    biases = [bias_ref[width - 1, start : start + half, :] for start in (0, half)]
    worst, least = worst_ref[...], None
    for h in range(KEY_VALUE_HEADS):
        columns = slice(h * HEAD_SIZE, (h + 1) * HEAD_SIZE)
        keys, values = kv_refs[-1][:tokens, columns], with_ones(kv_refs[-1][tokens:, columns])
        for start, bias in zip((0, half), biases):
            queries = stacked_heads(q_ref, slice(start, start + half), h * Q_BLOCK, HEADS_PER_KV)
            scores = scores_of(queries, keys).reshape(HEADS_PER_KV, half, tokens)
            exponents = (scores * EXPONENT + bias[None]).reshape(HEADS_PER_KV * half, tokens)
            worst = jnp.maximum(worst, peak(exponents))
            rows = slice(start * HEADS_PER_KV, (start + half) * HEADS_PER_KV)
            acc = acc_ref[h, rows, :] + product(jnp.exp2(exponents).astype(jnp.bfloat16), values)
            part = jnp.min(acc[:, HEAD_SIZE:].reshape(-1, 8, HEAD_SIZE), axis=0)
            least = part if least is None else jnp.minimum(least, part)
            write(h, start, acc)
        copy_out(h).start()
    redo = out_of_range(worst, least)
    for h in range(KEY_VALUE_HEADS):
        copy_out(h).wait()

    @pl.when(redo)
    def _():
        def step(h, carry):
            columns = span(h * HEAD_SIZE, HEAD_SIZE)
            for start in (0, half):
                queries = stacked_heads(q_ref, slice(start, start + half), h * Q_BLOCK, HEADS_PER_KV)
                state = None
                for parts in parts_in(width):
                    k_part = jnp.concatenate([kv_refs[s][:tokens, columns] for s in parts], axis=0)
                    v_part = jnp.concatenate([kv_refs[s][tokens:, columns] for s in parts], axis=0)
                    bias = jnp.concatenate([bias_ref[s, start : start + half, :] for s in parts], axis=1)
                    scores = scores_of(queries, k_part).reshape(HEADS_PER_KV, half, bias.shape[1])
                    scores = (scores + bias[None]).reshape(HEADS_PER_KV * half, bias.shape[1])
                    state = fold(state, [scores], [v_part])
                write(h, start, state[1])
            return carry

        lax.fori_loop(0, KEY_VALUE_HEADS, step, 0)
        for h in range(KEY_VALUE_HEADS):
            copy_out(h).start()
        for h in range(KEY_VALUE_HEADS):
            copy_out(h).wait()


def cost(rows, keys, exps):
    return pl.CostEstimate(
        flops=32 * rows * keys * Q_WIDTH, bytes_accessed=4 * rows * Q_WIDTH, transcendentals=exps
    )


def call_first(plan, facts, maxima, query, blocks, pieces):
    tokens, width = query.shape[0], plan.size
    rows = HEADS_PER_KV * tokens
    f32, bf16 = jnp.float32, jnp.bfloat16
    every = (width - 1) * tokens
    shapes = [
        jax.ShapeDtypeStruct((KEY_VALUE_HEADS, rows, 2 * HEAD_SIZE), f32),
        jax.ShapeDtypeStruct((width, tokens, tokens), f32),
        jax.ShapeDtypeStruct((KEY_VALUE_HEADS, STACKED, 2 * HEAD_SIZE), f32),
        jax.ShapeDtypeStruct((width, STACKED, tokens), f32),
        jax.ShapeDtypeStruct((8, HEAD_SIZE), f32),
        jax.ShapeDtypeStruct((PADDED_ROWS, Q_WIDTH), bf16),
        jax.ShapeDtypeStruct((PADDED_ROWS, 2 * KV_WIDTH), bf16),
        jax.ShapeDtypeStruct((PADDED_ROWS, PADDED_ROWS), bf16),
        jax.ShapeDtypeStruct((8, HEAD_SIZE), jnp.int32),
    ]
    return pl.pallas_call(
        lambda *refs: first_kernel(plan, len(blocks), *refs),
        in_specs=[SMEM] + [VMEM] * (2 + len(blocks) + width - 1),
        out_specs=[VMEM] * len(shapes),
        out_shape=shapes,
        compiler_params=pltpu.CompilerParams(vmem_limit_bytes=(28 + width) * MIB),
        cost_estimate=cost(tokens, every, tokens * every * QUERY_HEADS),
        name="first_shards",
    )(facts, maxima, query, *pieces, *blocks)


def call_decode(plan, state, pieces):
    tokens, width = pieces[0].shape[0] // 2, plan.size
    return pl.pallas_call(
        lambda *refs: decode_kernel(plan, *refs),
        in_specs=[VMEM] * (6 + width),
        out_specs=VMEM,
        out_shape=jax.ShapeDtypeStruct((PADDED_ROWS, Q_WIDTH), jnp.bfloat16),
        compiler_params=pltpu.CompilerParams(vmem_limit_bytes=(28 + width) * MIB),
        cost_estimate=cost(PADDED_ROWS, tokens, PADDED_ROWS * tokens * QUERY_HEADS),
        name="last_shard_decode",
    )(*state[2:8], *pieces)


def call_prefill(plan, state, query, pieces):
    tokens, width = query.shape[0], plan.size
    return pl.pallas_call(
        lambda *refs: prefill_kernel(plan, *refs),
        in_specs=[VMEM] * (4 + width),
        out_specs=ANY,
        out_shape=jax.ShapeDtypeStruct((tokens, Q_WIDTH), jnp.bfloat16),
        scratch_shapes=[
            pltpu.VMEM((tokens, Q_WIDTH), jnp.bfloat16),
            pltpu.SemaphoreType.DMA((KEY_VALUE_HEADS,)),
        ],
        compiler_params=pltpu.CompilerParams(vmem_limit_bytes=(28 + width) * MIB),
        cost_estimate=cost(tokens, tokens, tokens * tokens * QUERY_HEADS),
        name="last_shard_prefill",
    )(*state[:2], state[4], query, *pieces)


def stacked(key, value):
    tokens, width = key.shape

    def kernel(k_ref, v_ref, out_ref, sem):
        copies = [
            pltpu.make_async_copy(ref, out_ref.at[pl.ds(i * tokens, tokens), :], sem.at[i])
            for i, ref in enumerate((k_ref, v_ref))
        ]
        for copy in copies:
            copy.start()
        for copy in copies:
            copy.wait()

    return pl.pallas_call(
        kernel,
        in_specs=[HBM, HBM],
        out_specs=HBM,
        out_shape=jax.ShapeDtypeStruct((2 * tokens, width), key.dtype),
        scratch_shapes=[pltpu.SemaphoreType.DMA((2,))],
        compiler_params=pltpu.CompilerParams(vmem_limit_bytes=60 * MIB),
        name="stacked",
    )(key, value)


def start_maxima(*arrays, flops=5 * 10**9):
    def kernel(*refs):
        refs[-1][...] = jnp.full((8, HEAD_SIZE), MASKED, jnp.float32)

    return pl.pallas_call(
        kernel,
        in_specs=[VMEM] * len(arrays),
        out_specs=VMEM,
        out_shape=jax.ShapeDtypeStruct((8, HEAD_SIZE), jnp.float32),
        cost_estimate=pl.CostEstimate(flops=flops, bytes_accessed=0, transcendentals=0),
        compiler_params=pltpu.CompilerParams(vmem_limit_bytes=MIB),
        name="start_maxima",
    )(*arrays)


def paired(array, k):
    return lax.ppermute(array, "pd", [(g, g ^ k) for g in range(lax.axis_size("pd"))])


def body(
    prompt_query,
    prompt_key,
    prompt_value,
    prompt_lengths,
    decode_slot,
    decoded_query,
    decoded_key,
    decoded_value,
):
    plan = Ring(lax.axis_size("tp"))
    pd_size = lax.axis_size("pd")
    own = jnp.concatenate([decoded_query, decoded_key, decoded_value], axis=2).reshape(
        DECODE_ROWS, Q_WIDTH + 2 * KV_WIDTH
    )
    facts = facts_row(plan, prompt_lengths, decode_slot)
    kv, decoded_query = lax.optimization_barrier(
        (stacked(prompt_key, prompt_value), decoded_query)
    )
    later_kv, own = lax.optimization_barrier((kv, own))
    pieces, maxima, up, down = [kv], None, kv, later_kv
    for d in range(1, plan.size // 2 + 1):
        if d == 2:
            up, facts = lax.optimization_barrier((up, facts))
        up = plan.step(up, True)
        down = plan.step(down, False) if 2 * d < plan.size else None
        pieces += [up, down]
    pieces = pieces[: plan.size]
    blocks = [own] + [paired(own, k) for k in range(1, pd_size)]
    maxima = start_maxima(pieces[1])

    state = call_first(plan, facts, maxima, prompt_query, blocks, pieces[:-1])
    outgoing = call_decode(plan, state, pieces)
    arrived = [outgoing[:DECODE_STEPS]]
    for k in range(1, pd_size):
        arrived.append(paired(outgoing[k * DECODE_STEPS : (k + 1) * DECODE_STEPS], k))
    pre_out = call_prefill(plan, state, prompt_query, pieces)

    from_block = state[8][:GROUP_REQUESTS, 0]
    dec_out = jnp.zeros((GROUP_REQUESTS, DECODE_STEPS, Q_WIDTH), jnp.bfloat16)
    for k in range(pd_size):
        dec_out = jnp.where((from_block == k)[:, None, None], arrived[k][None], dec_out)
    return (pre_out, dec_out)


def solution(mesh):
    placed = (
        P(("rep", "pd", "tp"), None),
        P(("rep", "pd", "tp"), None),
        P(("rep", "pd", "tp"), None),
        P("rep", None),
        P("rep"),
        P(("rep", "pd"), None, None),
        P(("rep", "pd"), None, None),
        P(("rep", "pd"), None, None),
    )
    return jax.shard_map(
        body,
        mesh=mesh,
        in_specs=placed,
        out_specs=(P(("rep", "pd", "tp"), None), P(("rep", "pd"), None, None)),
        check_vma=False,
    )
```
